32 devices in a mesh: dp: 4 (over z), expert: 2 (over x), tensor: 4 (over y, core).
Axes of the slice: x: 2, y: 2, z: 4, core: 2. Of those that a mesh axis runs over, the one named last changes fastest.
Arguments:
- hidden_in: bfloat16 [16384, 768], P(('dp', 'expert')), may hold values from -6 to 6
- prev_logits: bfloat16 [16384, 6], P(('dp', 'expert')), may hold values from -4 to 4
- routes: int32 [16384, 2], P(('dp', 'expert')), may hold values from 0 to 5, all different within a row; in each aligned block of 2048 rows (0 to 2047, 2048 to 4095, ...) at most 1024 rows name the same one
- block_ids: int32 [8, 2048], P(('dp', 'expert')), may hold values from 0 to 11, never falling along the last dimension, each value on 1 to 256 neighbouring positions
- cotangent: bfloat16 [16384, 768], P(('dp', 'expert')), may hold values from -6 to 6
- gain_attn: bfloat16 [768], replicated, may hold values from 0.5 to 1.5
- w_qkv: bfloat16 [768, 2304], P(None, 'tensor'), may hold values from -0.21875 to 0.21875
- w_out: bfloat16 [768, 768], P('tensor'), may hold values from -3 to 3
- gain_moe: bfloat16 [768], replicated, may hold values from 0.5 to 1.5
- w_router: bfloat16 [768, 6], replicated, may hold values from -0.15625 to 0.15625
- w_prev: bfloat16 [6, 6], replicated, may hold values from -2.5 to 2.5
- w_const: bfloat16 [2, 768, 2], replicated, may hold values from -0.21875 to 0.21875
- v_const: bfloat16 [2, 768], replicated, may hold values from -16 to 16
- w_gate_up: bfloat16 [2, 768, 2, 2048], P('expert', None, None, 'tensor'), may hold values from -0.21875 to 0.21875
- w_down: bfloat16 [2, 2048, 768], P('expert', 'tensor'), may hold values from -1.25 to 1.25
Outputs:
- output: float32 [16384, 768], P(('dp', 'expert'))
- grad_input: float32 [16384, 768], P(('dp', 'expert'))
- grad_prev: float32 [16384, 6], P(('dp', 'expert'))
- grad_gain_attn: float32 [768], replicated
- grad_qkv: float32 [768, 2304], P(('dp', 'expert'), 'tensor')
- grad_out: float32 [768, 768], P('tensor', ('dp', 'expert'))
- grad_gain_moe: float32 [768], replicated
- grad_router: float32 [768, 6], replicated
- grad_prev_weight: float32 [6, 6], replicated
- grad_const_weight: float32 [2, 768, 2], replicated
- grad_const_vector: float32 [2, 768], replicated
- grad_gate_up: float32 [2, 768, 2, 2048], P('expert', 'dp', None, 'tensor')
- grad_down: float32 [2, 2048, 768], P('expert', 'tensor', 'dp')
- loss: float32 [], replicated
- expert_load: float32 [2, 6], replicated
The draws below stay inside these ranges and needn't reach their ends.
Inputs may be any that keep to these rules, and one draw needn't show every extreme that they name: Within the 2048 rows of one device no expert is named by more than 1024 routes, a bound that some block reaches; the two experts of a token differ. `block_ids`: within a sequence block ids never fall, each block has 1 to 256 positions, and one has exactly 256.
All inputs are finite; a program needn't handle non-finite values.
Results may differ from the reference program's by a relative error of at most 0.023.
Values may be sent and summed in bfloat16 or wider, within the bound.
A program may use at most 320 MiB of HBM per device.

```python
import math
import jax
import jax.numpy as jnp
import numpy as np
from jax import lax

D = 768
HEADS = 12
HEAD_DIM = 64
FF = 2048
FFN_EXPERTS = 2
NE = 6
LEN = 2048
MAXBLOCK = 256
BLOCKS = 12
TOK = 2048
TOKENS = 16384
NSEQ = 8
CAP = 1024


def draw_prev_logits(key, part):
    group_count = TOKENS // TOK
    offsets = jax.random.uniform(jax.random.fold_in(key, 11), (group_count, 1, NE), jnp.float32, -2.0, 2.0)
    noise_key = jax.random.fold_in(key, 12)
    noise = jnp.clip(0.5 * jax.random.normal(noise_key, (group_count, TOK, NE), jnp.float32), -2.0, 2.0)
    return (offsets + noise).reshape(TOKENS, NE).astype(jnp.bfloat16)


def block_scale(stream_key, extent, shards, smallest, top_value):
    def one(dim, shards_of):
        steps = jax.random.uniform(jax.random.fold_in(jax.random.fold_in(stream_key, 6), dim), (shards_of,), jnp.float32, smallest / len(shards), top_value / len(shards))
        return jnp.repeat(jnp.exp(steps), extent[dim] // shards_of).reshape((-1,) + (1,) * (len(extent) - dim - 1))

    loudness = one(*shards[0])
    for cut in shards[1:]:
        loudness = loudness * one(*cut)
    return loudness


def length_profile(count, total, bound, lean):
    weights = [(1 << 20) // math.isqrt(rank ** lean) + 1 for rank in range(2, count + 1)]
    surplus, counts = total - bound - (count - 1), [1] * (count - 1)
    while surplus > 0:
        movable = [i for i in range(count - 1) if counts[i] < bound]
        pool, budget = sum([weights[i] for i in movable]), surplus
        for i in movable:
            more = min(bound - counts[i], max(1, budget * weights[i] // pool), surplus)
            counts[i] = counts[i] + more
            surplus = surplus - more
    return np.array([bound] + counts)


def ragged(rng, count, total, bound, skew):
    if count == 2:
        one = jax.random.randint(rng, (), max(1, total - bound), min(bound, total - 1) + 1)
        return jnp.stack([one, total - one])
    lengths = jnp.asarray(length_profile(count, total, bound, skew), jnp.int32)
    twos = (count - 1) // 2
    source_of, taker = lengths[1:1 + 2 * twos:2], lengths[2:2 + 2 * twos:2]
    slack = jnp.minimum(source_of - 1, bound - taker)
    shifted = jax.random.randint(jax.random.fold_in(rng, 1), (twos,), 0, 1 << 20) % (slack + 1)
    lengths = lengths.at[1:1 + 2 * twos:2].set(source_of - shifted).at[2:2 + 2 * twos:2].set(taker + shifted)
    return lengths[jax.random.permutation(jax.random.fold_in(rng, 2), count)]


def shared_out(own_key, own, number, rows, number_of, top, most, lean):
    ranking = jax.random.permutation(own_key, number_of)
    crowded, usual = portions_of(number_of, rows * top, most, lean, True), portions_of(number_of, rows * top, most, lean, False)
    places = jnp.arange(number_of)

    def named(tallies, turn):
        used = int((tallies > 0).sum())
        fixed = max(1, used // 4)
        shifted = fixed + (places - fixed + turn * (used - fixed)) % max(1, number_of - fixed)
        return jnp.zeros((number_of,), jnp.int32).at[ranking[jnp.where(places < fixed, places, shifted)]].set(jnp.asarray(tallies, jnp.int32))

    tallies = jnp.where(number % 4 == 0, named(crowded, number // 4), named(usual, number - number // 4 - 1))
    mixed = jax.random.permutation(jax.random.fold_in(own, 3), number_of)
    source_of, receiver = mixed[0:number_of // 2 * 2:2], mixed[1:number_of // 2 * 2:2]
    slack = jnp.minimum(tallies[source_of] - 1, most - tallies[receiver]) // 2
    slack = jnp.where((source_of == ranking[0]) | (receiver == ranking[0]) | (tallies[receiver] == 0), 0, jnp.maximum(slack, 0))
    shifted = jax.random.randint(jax.random.fold_in(own, 4), (number_of // 2,), 0, 1 << 20) % (slack + 1)
    tallies = tallies.at[source_of].add(-shifted).at[receiver].add(shifted)
    labels = jnp.searchsorted(jnp.cumsum(tallies), jnp.arange(rows * top), side="right").astype(jnp.int32)
    listing = labels.reshape(top, rows).T
    listing = listing[jax.random.permutation(jax.random.fold_in(own, 1), rows)]
    turn = jax.random.randint(jax.random.fold_in(own, 2), (rows, 1), 0, top)
    return jnp.take_along_axis(listing, (jnp.arange(top)[None, :] + turn) % top, axis=1)


def portions_of(amount, total, limit, skew, full):
    weights = [(1 << 20) // math.isqrt(standing ** skew) + 1 for standing in range(1, amount + 1)]
    largest = limit if full else min(limit, max(-(-total // amount), total * weights[0] // sum(weights)))
    least = 1 if total - largest >= amount - 1 else 0
    counts, spare = [largest] + [least] * (amount - 1), total - largest - least * (amount - 1)
    while spare > 0:
        free = [i for i in range(1, amount) if counts[i] < largest] or [i for i in range(1, amount) if counts[i] < limit]
        whole, budget = sum([weights[i] for i in free]), spare
        for i in free:
            addition = min(limit - counts[i], max(1, budget * weights[i] // whole), spare)
            counts[i] = counts[i] + addition
            spare = spare - addition
    return np.array(counts)


def gaussian(key, extent, spread, bound, split=(), kind=jnp.bfloat16):
    loudness = block_scale(key, extent, split, -0.22, 0.18) if split else 1.0
    array = jax.random.normal(key, extent, jnp.float32) * spread * loudness
    return jnp.minimum(jnp.maximum(array, -bound), bound).astype(kind)


def setup_inputs(seed: int = 0) -> dict:
    keys = jax.random.split(jax.random.key(seed), 16)
    hidden_in = gaussian(keys[0], (TOKENS, D), 1.0, 6.0, ((0, 8),))
    prev_logits = draw_prev_logits(jax.random.fold_in(keys[15], 71), 0)
    routes_keys = jax.random.split(jax.random.fold_in(keys[2], 1), TOKENS // TOK)
    routes_turns = jax.random.permutation(jax.random.fold_in(keys[2], 3), TOKENS // TOK)
    routes = jax.vmap(lambda own, number: shared_out(jax.random.fold_in(keys[2], 2), own, number, TOK, NE, 2, CAP, 1))(routes_keys, routes_turns).reshape((TOKENS, 2))
    block_ids = jax.vmap(lambda own: jnp.searchsorted(jnp.cumsum(ragged(own, BLOCKS, LEN, MAXBLOCK, 0)), jnp.arange(LEN), side="right"))(jax.random.split(keys[3], NSEQ)).reshape((NSEQ, LEN)).astype(jnp.int32)
    cotangent = gaussian(keys[4], (TOKENS, D), 1.0, 6.0, ((0, 8),))
    gain_attn = jnp.clip(1.0 + 0.1 * jax.random.normal(keys[5], (D,), jnp.float32), 0.5, 1.5).astype(jnp.bfloat16)
    w_qkv = gaussian(keys[6], (D, 3 * HEADS * HEAD_DIM), D ** -0.5, 0.21875, ((1, 4),))
    w_out = gaussian(keys[7], (HEADS * HEAD_DIM, D), 0.5, 3.0, ((0, 4),))
    gain_moe = jnp.clip(1.0 + 0.1 * jax.random.normal(keys[8], (D,), jnp.float32), 0.5, 1.5).astype(jnp.bfloat16)
    w_router = gaussian(keys[9], (D, NE), 0.025, 0.15625)
    w_prev = gaussian(keys[10], (NE, NE), NE ** -0.5, 2.5)
    w_const = gaussian(keys[11], (2, D, 2), D ** -0.5, 0.21875)
    v_const = gaussian(keys[12], (2, D), 3.0, 16.0)
    w_gate_up = gaussian(keys[13], (FFN_EXPERTS, D, 2, FF), D ** -0.5, 0.21875, ((0, 2), (3, 4)))
    w_down = gaussian(keys[14], (FFN_EXPERTS, FF, D), 0.2, 1.25, ((0, 2), (1, 4)))
    return dict(hidden_in=hidden_in, prev_logits=prev_logits, routes=routes, block_ids=block_ids, cotangent=cotangent, gain_attn=gain_attn, w_qkv=w_qkv, w_out=w_out, gain_moe=gain_moe, w_router=w_router, w_prev=w_prev, w_const=w_const, v_const=v_const, w_gate_up=w_gate_up, w_down=w_down)


EPSILON = 1e-06
AUX_WEIGHT = 0.01
SCORE_SCALE = 0.125
HIGHEST = lax.Precision.HIGHEST

@jax.custom_vjp
def low(v):
    return lax.optimization_barrier(v.astype(jnp.bfloat16)).astype(jnp.float32)

@jax.custom_vjp
def low_back(v):
    return v

def low_keep(v):
    return (low(v), None)

def low_pass(kept, grad):
    return (grad,)

def back_keep(v):
    return (v, None)

def back_low(kept, grad):
    return (low(grad),)
low.defvjp(low_keep, low_pass)
low_back.defvjp(back_keep, back_low)

def exact_dot(left_side, right_side):
    return jnp.dot(left_side, right_side, precision=HIGHEST, preferred_element_type=jnp.float32)

def rms_factor(values):
    return lax.rsqrt(lax.optimization_barrier(jnp.mean(values * values, axis=-1, keepdims=True)) + EPSILON)

def attend_sequence(arguments):
    qkv_part, block_row = arguments
    queries = qkv_part[:, :, 0]
    key_rows = qkv_part[:, :, 1]
    value_rows = qkv_part[:, :, 2]
    scores = low_back(jnp.einsum('qhd,khd->hqk', queries, key_rows, precision=HIGHEST) * SCORE_SCALE)
    allowed = block_row[None, :] <= block_row[:, None]
    scores = jnp.where(allowed[None], scores, -1e+30)
    weights = low(jax.nn.softmax(scores, axis=-1))
    return low_back(low(jnp.einsum('hqk,khd->qhd', weights, value_rows, precision=HIGHEST)))

def route_slots(group_routes, expert_count, capacity, type_count):
    flat_routes = group_routes.reshape(-1)
    one_hot = (flat_routes[:, None] == jnp.arange(type_count, dtype=jnp.int32)[None, :]).astype(jnp.int32)
    ranks = jnp.cumsum(one_hot, axis=0) - 1
    slots = lax.optimization_barrier(jnp.sum(ranks * one_hot, axis=1))
    return jnp.where(flat_routes < expert_count, flat_routes * capacity + slots, expert_count * capacity).astype(jnp.int32)

def group_slots(group_routes):
    return route_slots(group_routes, FFN_EXPERTS, CAP, NE)

def pick_rows(row_table, row_index):
    return row_table[row_index]

def expert_branch(arguments):
    expert_rows, weights_gate_up, weights_down = arguments
    gate_up = low_back(jnp.einsum('rd,dgf->rgf', expert_rows, weights_gate_up, precision=HIGHEST))
    hidden = low(jax.nn.silu(gate_up[:, 0]) * gate_up[:, 1])
    return low(low_back(exact_dot(hidden, weights_down)))

def forward(inputs, prev_values, gain_attn, w_qkv, w_out, gain_moe, w_router, w_prev, w_const, v_const, w_gate_up, w_down, routes, block_ids):
    tok_total, model_width = inputs.shape
    seq_total, length = block_ids.shape
    normed_in = low(inputs * rms_factor(inputs) * gain_attn)
    qkv_rows = low_back(low(exact_dot(normed_in, w_qkv)))
    qkv_split = qkv_rows.reshape(seq_total, length, HEADS, 3, HEAD_DIM)
    mixed_heads = lax.map(jax.checkpoint(attend_sequence), (qkv_split, block_ids)).reshape(tok_total, HEADS * HEAD_DIM)
    residual = inputs + low_back(exact_dot(mixed_heads, w_out))
    moe_in = low(residual * rms_factor(residual) * gain_moe)
    logits = exact_dot(moe_in, w_router) + exact_dot(prev_values, w_prev)
    route_probs = jax.nn.softmax(logits, axis=-1)
    type_ids = jnp.arange(NE, dtype=jnp.int32)
    choose = (routes[:, :, None] == type_ids[None, None, :]).astype(jnp.float32)
    gate_values = lax.optimization_barrier(jnp.sum(choose * route_probs[:, None, :], axis=-1))
    count_all = lax.optimization_barrier(jnp.sum(choose, axis=(0, 1)))
    prob_all = lax.optimization_barrier(jnp.sum(route_probs, axis=0))
    load_share = count_all / (2.0 * tok_total)
    balance_loss = NE * jnp.sum(load_share * prob_all / tok_total)
    load_stats = jnp.stack([count_all / (2.0 * TOK), prob_all / TOK])
    group_count = tok_total // TOK
    destination = jax.vmap(group_slots)(routes.reshape(group_count, TOK, 2))
    token_of = jnp.arange(group_count, dtype=jnp.int32)[:, None] * TOK + jnp.arange(2 * TOK, dtype=jnp.int32)[None, :] // 2
    row_table = jnp.full((group_count, FFN_EXPERTS * CAP + 1), tok_total, dtype=jnp.int32)
    row_table = row_table.at[jnp.arange(group_count, dtype=jnp.int32)[:, None], destination].set(token_of)
    slot_tokens = row_table[:, :-1].reshape(group_count, FFN_EXPERTS, CAP).transpose(1, 0, 2).reshape(FFN_EXPERTS, group_count * CAP)
    padded_in = jnp.concatenate([moe_in, jnp.zeros((1, model_width), moe_in.dtype)], axis=0)
    expert_in = low_back(padded_in[slot_tokens])
    expert_out = lax.map(jax.checkpoint(expert_branch), (expert_in, w_gate_up, w_down))
    out_table = expert_out.reshape(FFN_EXPERTS, group_count, CAP, model_width).transpose(1, 0, 2, 3)
    out_table = out_table.reshape(group_count, FFN_EXPERTS * CAP, model_width)
    out_table = jnp.concatenate([out_table, jnp.zeros((group_count, 1, model_width), out_table.dtype)], axis=1)
    ffn_values = jax.vmap(pick_rows)(out_table, destination).reshape(tok_total, 2, model_width)
    const_logits = jnp.einsum('td,cdk->tck', moe_in, w_const, precision=HIGHEST)
    const_mix = jax.nn.softmax(const_logits, axis=-1)
    const_values = const_mix[:, :, 0:1] * moe_in[:, None, :] + const_mix[:, :, 1:2] * v_const[None]
    copy_mask = choose[:, :, FFN_EXPERTS + 1]
    first_const = choose[:, :, FFN_EXPERTS + 2]
    second_const = choose[:, :, FFN_EXPERTS + 3]
    route_values = ffn_values + copy_mask[..., None] * moe_in[:, None, :]
    route_values = route_values + first_const[..., None] * const_values[:, None, 0] + second_const[..., None] * const_values[:, None, 1]
    output = residual + lax.optimization_barrier(jnp.sum(gate_values[..., None] * route_values, axis=1))
    return ((output, balance_loss), load_stats)

def reference(hidden_in, prev_logits, routes, block_ids, cotangent, gain_attn, w_qkv, w_out, gain_moe, w_router, w_prev, w_const, v_const, w_gate_up, w_down):
    floats = [array_item.astype(jnp.float32) for array_item in (hidden_in, prev_logits, gain_attn, w_qkv, w_out, gain_moe, w_router, w_prev, w_const, v_const, w_gate_up, w_down)]

    def run_layer(*arrays):
        return forward(*arrays, routes, block_ids)
    (output, balance_loss), pullback, load_stats = jax.vjp(run_layer, *floats, has_aux=True)
    gradients = pullback((cotangent.astype(jnp.float32), jnp.asarray(AUX_WEIGHT, dtype=balance_loss.dtype)))
    return (output, gradients[0], gradients[1], gradients[2], gradients[3], gradients[4], gradients[5], gradients[6], gradients[7], gradients[8], gradients[9], gradients[10], gradients[11], balance_loss, load_stats)
```

```python
import functools

import jax
import jax.numpy as jnp
from jax import lax
from jax.experimental import pallas as pl
from jax.experimental.pallas import tpu as pltpu
from jax.sharding import PartitionSpec as P

HEAD_DIM = 64
EPSILON = 1e-06
AUX_WEIGHT = 0.01
SCORE_SCALE = 0.125
MAX_BLOCK = 256
LANES = 128
QB = 256
TB = 256
NEG = -1e30
F32 = jnp.float32
BF16 = jnp.bfloat16
VMEM_LIMIT = 48 * 1024 * 1024


def params(**more):
    return pltpu.CompilerParams(vmem_limit_bytes=VMEM_LIMIT, **more)


def nn(a, b):
    return lax.dot_general(a, b, (((1,), (0,)), ((), ())), preferred_element_type=F32)


def nt(a, b):
    return lax.dot_general(a, b, (((1,), (1,)), ((), ())), preferred_element_type=F32)


def tn(a, b):
    return lax.dot_general(a, b, (((0,), (0,)), ((), ())), preferred_element_type=F32)


def split_hi_lo(a):
    hi = a.astype(BF16)
    return hi, (a - hi.astype(F32)).astype(BF16)


def rms_factor(values):
    return lax.rsqrt(jnp.mean(values * values, axis=-1, keepdims=True) + EPSILON)


def swap(a, axis, bit):
    n = lax.axis_size(axis)
    return lax.ppermute(a, axis, [(i, i ^ bit) for i in range(n)])


def sum_over(a, axes):
    for axis in axes:
        bit = 1
        while bit < lax.axis_size(axis):
            a = a + swap(a, axis, bit)
            bit *= 2
    return a


def attn_fwd_kernel(heads, x_ref, gain_ref, wt_ref, bq_ref, bk_ref, h1_ref, qkvt_ref, ot_ref, lse_ref, kn_ref):
    tokens = x_ref.shape[0]
    win = min(2 * QB, tokens)

    def project(i, carry):
        rows = pl.ds(pl.multiple_of(i * TB, TB), TB)
        xb = x_ref[rows, :].astype(F32)
        h1 = (xb * rms_factor(xb) * gain_ref[...]).astype(BF16)
        h1_ref[rows, :] = h1
        qkvt = nt(wt_ref[...], h1)
        for h in range(heads):
            base = h * 3 * HEAD_DIM
            q = qkvt[base : base + HEAD_DIM].astype(BF16).astype(F32) * SCORE_SCALE
            k = qkvt[base + HEAD_DIM : base + 2 * HEAD_DIM].astype(BF16)
            v = qkvt[base + 2 * HEAD_DIM : base + 3 * HEAD_DIM].astype(BF16)
            qkvt_ref[base : base + HEAD_DIM, rows] = q.astype(BF16)
            qkvt_ref[base + HEAD_DIM : base + 2 * HEAD_DIM, rows] = k
            qkvt_ref[base + 2 * HEAD_DIM : base + 3 * HEAD_DIM, rows] = v
            kn_ref[h, rows, :] = k.astype(F32).T.astype(BF16)
        return carry

    lax.fori_loop(0, tokens // TB, project, 0)

    def query_block(i, carry):
        q0 = pl.multiple_of(i * QB, QB)
        w0 = pl.multiple_of(jnp.minimum(q0, tokens - win), QB)
        cols = pl.ds(q0, QB)
        allowed = bk_ref[pl.ds(w0, win), :] <= bq_ref[:, cols]
        state = []
        for h in range(heads):
            base = h * 3 * HEAD_DIM
            qt = qkvt_ref[base : base + HEAD_DIM, cols]
            s = nn(kn_ref[h, pl.ds(w0, win), :], qt)
            s = jnp.where(allowed, s, NEG)
            m = jnp.max(s, axis=0, keepdims=True)
            p = jnp.exp(s - m)
            total = jnp.sum(p, axis=0, keepdims=True)
            vt = qkvt_ref[base + 2 * HEAD_DIM : base + 3 * HEAD_DIM, pl.ds(w0, win)]
            acc = nn(vt, p.astype(BF16))
            state += [m, total, acc]

        def chunk(c, state):
            keys = pl.ds(pl.multiple_of(c * QB, QB), QB)
            new = []
            for h in range(heads):
                base = h * 3 * HEAD_DIM
                m, total, acc = state[3 * h : 3 * h + 3]
                qt = qkvt_ref[base : base + HEAD_DIM, cols]
                s = nn(kn_ref[h, keys, :], qt)
                m_new = jnp.maximum(m, jnp.max(s, axis=0, keepdims=True))
                p = jnp.exp(s - m_new)
                alpha = jnp.exp(m - m_new)
                total = total * alpha + jnp.sum(p, axis=0, keepdims=True)
                vt = qkvt_ref[base + 2 * HEAD_DIM : base + 3 * HEAD_DIM, keys]
                acc = acc * alpha + nn(vt, p.astype(BF16))
                new += [m_new, total, acc]
            return new

        state = lax.fori_loop(0, w0 // QB, chunk, state)
        for h in range(heads):
            m, total, acc = state[3 * h : 3 * h + 3]
            ot_ref[h * HEAD_DIM : (h + 1) * HEAD_DIM, cols] = (acc / total).astype(BF16)
            lse_ref[h : h + 1, cols] = m + jnp.log(total)
        return carry

    lax.fori_loop(0, tokens // QB, query_block, 0)


def attention_forward(x, gain, w_t, bq, bk, heads):
    tokens, width = x.shape
    cols = w_t.shape[0]
    lse_rows = -(-heads // 8) * 8
    return pl.pallas_call(
        functools.partial(attn_fwd_kernel, heads),
        name="attn_fwd",
        out_shape=(
            jax.ShapeDtypeStruct((tokens, width), BF16),
            jax.ShapeDtypeStruct((cols, tokens), BF16),
            jax.ShapeDtypeStruct((heads * HEAD_DIM, tokens), BF16),
            jax.ShapeDtypeStruct((lse_rows, tokens), F32),
        ),
        scratch_shapes=[pltpu.VMEM((heads, tokens, HEAD_DIM), BF16)],
        compiler_params=params(),
        cost_estimate=pl.CostEstimate(flops=20_000_000_000, bytes_accessed=12_000_000, transcendentals=9_000_000),
    )(x, gain, w_t, bq, bk)


def attn_bwd_kernel(heads, da_ref, wo_ref, qkvt_ref, ot_ref, lse_ref, bq_ref, bk_ref, dqkvt_ref, dot_ref, delta_ref, kn_ref, vn_ref, dk_ref, dv_ref):
    tokens = da_ref.shape[0]
    win = min(2 * QB, tokens)

    def project(i, carry):
        rows = pl.ds(pl.multiple_of(i * TB, TB), TB)
        dot = nt(wo_ref[...], da_ref[rows, :]).astype(BF16)
        dot_ref[:, rows] = dot
        prod = dot.astype(F32) * ot_ref[:, rows].astype(F32)
        for h in range(heads):
            base = h * 3 * HEAD_DIM
            delta_ref[h : h + 1, rows] = jnp.sum(prod[h * HEAD_DIM : (h + 1) * HEAD_DIM], axis=0, keepdims=True)
            kn_ref[h, rows, :] = qkvt_ref[base + HEAD_DIM : base + 2 * HEAD_DIM, rows].astype(F32).T.astype(BF16)
            vn_ref[h, rows, :] = qkvt_ref[base + 2 * HEAD_DIM : base + 3 * HEAD_DIM, rows].astype(F32).T.astype(BF16)
        return carry

    lax.fori_loop(0, tokens // TB, project, 0)
    dk_ref[...] = jnp.zeros_like(dk_ref)
    dv_ref[...] = jnp.zeros_like(dv_ref)

    def query_block(i, carry):
        q0 = pl.multiple_of(i * QB, QB)
        w0 = pl.multiple_of(jnp.minimum(q0, tokens - win), QB)
        cols = pl.ds(q0, QB)

        def tile(h, keys, allowed):
            base = h * 3 * HEAD_DIM
            qt = qkvt_ref[base : base + HEAD_DIM, cols]
            dot = dot_ref[h * HEAD_DIM : (h + 1) * HEAD_DIM, cols]
            s = nn(kn_ref[h, keys, :], qt)
            p = jnp.exp(s - lse_ref[h : h + 1, cols])
            if allowed is not None:
                p = jnp.where(allowed, p, 0.0)
            dp = nn(vn_ref[h, keys, :], dot)
            ds = (p * (dp - delta_ref[h : h + 1, cols])).astype(BF16)
            dv_ref[h, :, keys] += nt(dot, p.astype(BF16))
            dk_ref[h, :, keys] += nt(qt, ds)
            kt = qkvt_ref[base + HEAD_DIM : base + 2 * HEAD_DIM, keys]
            return nn(kt, ds)

        dq = []
        allowed = bk_ref[pl.ds(w0, win), :] <= bq_ref[:, cols]
        for h in range(heads):
            dq.append(tile(h, pl.ds(w0, win), allowed))

        def chunk(c, dq):
            keys = pl.ds(pl.multiple_of(c * QB, QB), QB)
            return [dq[h] + tile(h, keys, None) for h in range(heads)]

        dq = lax.fori_loop(0, w0 // QB, chunk, dq)
        for h in range(heads):
            base = h * 3 * HEAD_DIM
            dqkvt_ref[base : base + HEAD_DIM, cols] = (dq[h] * SCORE_SCALE).astype(BF16)
        return carry

    lax.fori_loop(0, tokens // QB, query_block, 0)
    for h in range(heads):
        base = h * 3 * HEAD_DIM
        dqkvt_ref[base + HEAD_DIM : base + 2 * HEAD_DIM, :] = dk_ref[h].astype(BF16)
        dqkvt_ref[base + 2 * HEAD_DIM : base + 3 * HEAD_DIM, :] = dv_ref[h].astype(BF16)


def attention_backward(da, w_out, qkvt, ot, lse, bq, bk, heads):
    tokens = da.shape[0]
    cols = qkvt.shape[0]
    return pl.pallas_call(
        functools.partial(attn_bwd_kernel, heads),
        name="attn_bwd",
        out_shape=jax.ShapeDtypeStruct((cols, tokens), BF16),
        scratch_shapes=[
            pltpu.VMEM((heads * HEAD_DIM, tokens), BF16),
            pltpu.VMEM((lse.shape[0], tokens), F32),
            pltpu.VMEM((heads, tokens, HEAD_DIM), BF16),
            pltpu.VMEM((heads, tokens, HEAD_DIM), BF16),
            pltpu.VMEM((heads, HEAD_DIM, tokens), F32),
            pltpu.VMEM((heads, HEAD_DIM, tokens), F32),
        ],
        compiler_params=params(),
        cost_estimate=pl.CostEstimate(flops=40_000_000_000, bytes_accessed=10_000_000, transcendentals=9_000_000),
    )(da, w_out, qkvt, ot, lse, bq, bk)


def lane_iota(rows):
    return lax.broadcasted_iota(jnp.int32, (rows, LANES), 1)


def column(values, lane, number):
    return jnp.sum(jnp.where(lane == number, values, 0.0), axis=1, keepdims=True)


def routing(logits, aux, types):
    lane = lane_iota(logits.shape[0])
    is_type = lane < types
    shown = jnp.where(is_type, logits, NEG)
    e = jnp.exp(shown - jnp.max(shown, axis=1, keepdims=True))
    probs = e / jnp.sum(e, axis=1, keepdims=True)
    aux = aux.astype(F32)
    first = column(aux, lane, types).astype(jnp.int32)
    second = column(aux, lane, types + 1).astype(jnp.int32)
    mask = jnp.where((lane == first) | (lane == second), 1.0, 0.0)
    return lane, probs, mask


def const_mix(logits, lane, types, c):
    l0 = column(logits, lane, types + 2 * c)
    l1 = column(logits, lane, types + 2 * c + 1)
    top = jnp.maximum(l0, l1)
    e0, e1 = jnp.exp(l0 - top), jnp.exp(l1 - top)
    total = e0 + e1
    return e0 / total, e1 / total


def post_attn_kernel(types, group, idx_ref, x_ref, *refs):
    ots, wos = refs[:group], refs[group : 2 * group]
    gain_ref, wcat_ref, aux_ref, wprev_ref = refs[2 * group : 2 * group + 4]
    x1_ref, h2_ref, lg_ref, ps_ref, wo_scr, ot_scr = refs[2 * group + 4 :]
    rows = ots[0].shape[0]
    me = idx_ref[0]

    @pl.when(pl.program_id(0) == 0)
    def _():
        for m in range(group):
            wo_scr[pl.ds(pl.multiple_of((me ^ m) * rows, HEAD_DIM), rows), :] = wos[m][...]
        ps_ref[...] = jnp.zeros_like(ps_ref)

    for m in range(group):
        ot_scr[pl.ds(pl.multiple_of((me ^ m) * rows, HEAD_DIM), rows), :] = ots[m][...]
    x1 = x_ref[...].astype(F32) + tn(ot_scr[...], wo_scr[...])
    x1_ref[...] = x1
    h2 = (x1 * rms_factor(x1) * gain_ref[...]).astype(BF16)
    h2_ref[...] = h2
    lg = nn(h2, wcat_ref[...]) + nn(aux_ref[...], wprev_ref[...])
    lg_ref[...] = lg
    _, probs, _ = routing(lg, aux_ref[...], types)
    ps_ref[0:1, :] += jnp.sum(probs, axis=0, keepdims=True)


def post_attention(me, x, ots, wos, gain, wcat, aux, wprev, types):
    tokens, width = x.shape
    rows = ots[0].shape[0]
    group = len(ots)
    block = lambda i, *_: (i, 0)
    fixed = lambda i, *_: (0, 0)
    grid_spec = pltpu.PrefetchScalarGridSpec(
        num_scalar_prefetch=1,
        grid=(tokens // TB,),
        in_specs=[pl.BlockSpec((TB, width), block)]
        + [pl.BlockSpec((rows, TB), lambda i, *_: (0, i))] * group
        + [pl.BlockSpec((rows, width), fixed)] * group
        + [
            pl.BlockSpec((1, width), fixed),
            pl.BlockSpec((width, LANES), fixed),
            pl.BlockSpec((TB, LANES), block),
            pl.BlockSpec((LANES, LANES), fixed),
        ],
        out_specs=[
            pl.BlockSpec((TB, width), block),
            pl.BlockSpec((TB, width), block),
            pl.BlockSpec((TB, LANES), block),
            pl.BlockSpec((8, LANES), fixed),
        ],
        scratch_shapes=[pltpu.VMEM((group * rows, width), BF16), pltpu.VMEM((group * rows, TB), BF16)],
    )
    return pl.pallas_call(
        functools.partial(post_attn_kernel, types, group),
        name="post_attn",
        grid_spec=grid_spec,
        out_shape=(
            jax.ShapeDtypeStruct((tokens, width), F32),
            jax.ShapeDtypeStruct((tokens, width), BF16),
            jax.ShapeDtypeStruct((tokens, LANES), F32),
            jax.ShapeDtypeStruct((8, LANES), F32),
        ),
        compiler_params=params(),
        cost_estimate=pl.CostEstimate(flops=3_000_000_000, bytes_accessed=20_000_000, transcendentals=300_000),
    )(me, x, *ots, *wos, gain, wcat, aux, wprev)


def expert_kernel(types, experts, halves, idx_ref, h2_ref, dy_ref, lg_ref, aux_ref, *refs):
    wgus, wds = refs[:experts], refs[experts : 2 * experts]
    eye_ref = refs[2 * experts]
    keep_ref, send_ref, gh_ref, du_ref, dlt_ref, acc_ref = refs[2 * experts + 1 :]
    me, half = idx_ref[0], idx_ref[1]
    hidden = wds[0].shape[0]
    h2, dy = h2_ref[...], dy_ref[...]
    lane, probs, mask = routing(lg_ref[...], aux_ref[...], types)
    gates = probs * mask
    dprobs = jnp.zeros_like(probs)
    for s in range(experts):
        e = me ^ s
        gate_col = column(gates, lane, e)
        u = nn(h2, wgus[s][...])
        dhr = nt(dy, wds[s][...])
        g, up = u[:, :hidden], u[:, hidden:]
        sig = 1.0 / (1.0 + jnp.exp(-g))
        silu = g * sig
        hid = silu * up
        gh_ref[e, :, :] = (hid * gate_col).astype(BF16)
        dg = jnp.sum(hid * dhr, axis=1, keepdims=True)
        dprobs = dprobs + jnp.where(lane == e, dg * mask, 0.0)
        dh = dhr * gate_col
        dgate = dh * up * sig * (1.0 + g * (1.0 - sig))
        dup = dh * silu
        du_ref[e, :, :hidden] = dgate.astype(BF16)
        du_ref[e, :, hidden:] = dup.astype(BF16)
        part = nt(du_ref[e, :, :], wgus[s][...])
        if s == 0:
            acc_ref[...] = part
        else:
            acc_ref[...] += part
    dlog = probs * (dprobs - jnp.sum(probs * dprobs, axis=1, keepdims=True))
    hi, lo = split_hi_lo(dlog)
    dlt_ref[...] = nt(eye_ref[...], hi) + nt(eye_ref[...], lo)
    half_cols = acc_ref.shape[1] // halves
    keep_ref[...] = acc_ref[:, pl.ds(pl.multiple_of(half * half_cols, LANES), half_cols)].astype(BF16)
    send_ref[...] = acc_ref[:, pl.ds(pl.multiple_of((1 - half) * half_cols, LANES), half_cols)].astype(BF16)


def experts_pass(idx, h2, dy, lg, aux, wgus, wds, eye, types):
    tokens, width = h2.shape
    experts = len(wgus)
    hidden = wds[0].shape[0]
    erows = eye.shape[0]
    block = lambda i, *_: (i, 0)
    fixed = lambda i, *_: (0, 0)
    grid_spec = pltpu.PrefetchScalarGridSpec(
        num_scalar_prefetch=1,
        grid=(tokens // TB,),
        in_specs=[
            pl.BlockSpec((TB, width), block),
            pl.BlockSpec((TB, width), block),
            pl.BlockSpec((TB, LANES), block),
            pl.BlockSpec((TB, LANES), block),
        ]
        + [pl.BlockSpec((width, 2 * hidden), fixed, pipeline_mode=pl.Buffered(1))] * experts
        + [pl.BlockSpec((hidden, width), fixed, pipeline_mode=pl.Buffered(1))] * experts
        + [pl.BlockSpec((erows, LANES), fixed)],
        out_specs=[
            pl.BlockSpec((TB, width // 2), block),
            pl.BlockSpec((TB, width // 2), block),
            pl.BlockSpec((experts, TB, hidden), lambda i, *_: (0, i, 0)),
            pl.BlockSpec((experts, TB, 2 * hidden), lambda i, *_: (0, i, 0)),
            pl.BlockSpec((erows, TB), lambda i, *_: (0, i)),
        ],
        scratch_shapes=[pltpu.VMEM((TB, width), F32)],
    )
    return pl.pallas_call(
        functools.partial(expert_kernel, types, experts, 2),
        name="experts",
        grid_spec=grid_spec,
        out_shape=(
            jax.ShapeDtypeStruct((tokens, width // 2), BF16),
            jax.ShapeDtypeStruct((tokens, width // 2), BF16),
            jax.ShapeDtypeStruct((experts, tokens, hidden), BF16),
            jax.ShapeDtypeStruct((experts, tokens, 2 * hidden), BF16),
            jax.ShapeDtypeStruct((erows, tokens), F32),
        ),
        compiler_params=params(),
        cost_estimate=pl.CostEstimate(flops=16_000_000_000, bytes_accessed=30_000_000, transcendentals=2_000_000),
    )(idx, h2, dy, lg, aux, *wgus, *wds, eye)


def down_kernel(experts, idx_ref, gh_ref, *refs):
    wds, (keep_ref, send_ref, acc_ref) = refs[:experts], refs[experts:]
    me, half = idx_ref[0], idx_ref[1]
    for s in range(experts):
        part = nn(gh_ref[me ^ s, :, :], wds[s][...])
        if s == 0:
            acc_ref[...] = part
        else:
            acc_ref[...] += part
    half_cols = keep_ref.shape[1]
    keep_ref[...] = acc_ref[:, pl.ds(pl.multiple_of(half * half_cols, LANES), half_cols)].astype(BF16)
    send_ref[...] = acc_ref[:, pl.ds(pl.multiple_of((1 - half) * half_cols, LANES), half_cols)].astype(BF16)


def down_pass(idx, gh, wds):
    experts, tokens, hidden = gh.shape
    width = wds[0].shape[1]
    block = lambda i, *_: (i, 0)
    fixed = lambda i, *_: (0, 0)
    grid_spec = pltpu.PrefetchScalarGridSpec(
        num_scalar_prefetch=1,
        grid=(tokens // TB,),
        in_specs=[pl.BlockSpec((experts, TB, hidden), lambda i, *_: (0, i, 0))]
        + [pl.BlockSpec((hidden, width), fixed, pipeline_mode=pl.Buffered(1))] * experts,
        out_specs=[pl.BlockSpec((TB, width // 2), block)] * 2,
        scratch_shapes=[pltpu.VMEM((TB, width), F32)],
    )
    return pl.pallas_call(
        functools.partial(down_kernel, experts),
        name="down",
        grid_spec=grid_spec,
        out_shape=(jax.ShapeDtypeStruct((tokens, width // 2), BF16),) * 2,
        compiler_params=params(),
        cost_estimate=pl.CostEstimate(flops=3_500_000_000, bytes_accessed=9_000_000, transcendentals=0),
    )(idx, gh, *wds)


def middle_kernel(types, ffn, total_tokens, idx_ref, mine_ref, theirs_ref, x1_ref, dy_ref, lg_ref, aux_ref, dlt_ref, eye_ref, count_ref, gain_ref, wcat_ref, vt_ref, wprevt_ref, dx1_ref, da_ref, gp_ref, g1_ref, g2_ref, g3_ref, g4_ref, scr_ref):
    half = idx_ref[1]
    half_cols = mine_ref.shape[1]
    scr_ref[:, pl.ds(pl.multiple_of(half * half_cols, LANES), half_cols)] = mine_ref[...]
    scr_ref[:, pl.ds(pl.multiple_of((1 - half) * half_cols, LANES), half_cols)] = theirs_ref[...]
    first = pl.program_id(0) == 0

    @pl.when(first)
    def _():
        for ref in (g1_ref, g2_ref, g3_ref, g4_ref):
            ref[...] = jnp.zeros_like(ref)

    gain = gain_ref[...]
    x1 = x1_ref[...]
    r2 = rms_factor(x1)
    n2 = x1 * r2
    h2 = (n2 * gain).astype(BF16)
    dyb = dy_ref[...]
    dy = dyb.astype(F32)
    lg = lg_ref[...]
    lane, probs, mask = routing(lg, aux_ref[...], types)
    gates = probs * mask
    a = jnp.sum(dy * h2.astype(F32), axis=1, keepdims=True)
    b = nn(dyb, vt_ref[...])
    coef = column(gates, lane, ffn + 1)
    dprobs = jnp.where(lane == ffn + 1, a, 0.0)
    dlc = jnp.zeros_like(probs)
    vcoef = jnp.zeros_like(probs)
    for c in range(2):
        m0, m1 = const_mix(lg, lane, types, c)
        g = column(gates, lane, ffn + 2 + c)
        bc = column(b, lane, c)
        dprobs = dprobs + jnp.where(lane == ffn + 2 + c, m0 * a + m1 * bc, 0.0)
        dm0, dm1 = g * a, g * bc
        inner = m0 * dm0 + m1 * dm1
        dlc = dlc + jnp.where(lane == types + 2 * c, m0 * (dm0 - inner), 0.0)
        dlc = dlc + jnp.where(lane == types + 2 * c + 1, m1 * (dm1 - inner), 0.0)
        coef = coef + g * m0
        vcoef = vcoef + jnp.where(lane == c, g * m1, 0.0)
    dprobs = dprobs * mask + count_ref[...] * (AUX_WEIGHT * types / (2.0 * total_tokens * total_tokens))
    dlog = probs * (dprobs - jnp.sum(probs * dprobs, axis=1, keepdims=True))
    hi, lo = split_hi_lo(dlt_ref[...])
    dl = dlog + dlc + tn(hi, eye_ref[...]) + tn(lo, eye_ref[...])
    dhi, dlo = split_hi_lo(dl)
    dh2 = scr_ref[...].astype(F32) + coef * dy + nt(dhi, wcat_ref[...]) + nt(dlo, wcat_ref[...])
    dn2 = dh2 * gain
    dx1 = dy + r2 * (dn2 - n2 * jnp.mean(dn2 * n2, axis=1, keepdims=True))
    dx1_ref[...] = dx1
    da_ref[...] = dx1.astype(BF16)
    gp_ref[...] = nn(dhi, wprevt_ref[...]) + nn(dlo, wprevt_ref[...])
    g1_ref[...] += tn(dhi, h2) + tn(dlo, h2)
    vhi, vlo = split_hi_lo(vcoef)
    g2_ref[...] += tn(vhi, dyb) + tn(vlo, dyb)
    g3_ref[0:1, :] += jnp.sum(dh2 * n2, axis=0, keepdims=True)
    g4_ref[...] += tn(aux_ref[...], dhi) + tn(aux_ref[...], dlo)


def middle_pass(idx, mine, theirs, x1, dy, lg, aux, dlt, eye, count, gain, wcat, vt, wprevt, types, ffn, total_tokens):
    tokens, width = x1.shape
    erows = dlt.shape[0]
    block = lambda i, *_: (i, 0)
    fixed = lambda i, *_: (0, 0)
    grid_spec = pltpu.PrefetchScalarGridSpec(
        num_scalar_prefetch=1,
        grid=(tokens // TB,),
        in_specs=[
            pl.BlockSpec((TB, width // 2), block),
            pl.BlockSpec((TB, width // 2), block),
            pl.BlockSpec((TB, width), block),
            pl.BlockSpec((TB, width), block),
            pl.BlockSpec((TB, LANES), block),
            pl.BlockSpec((TB, LANES), block),
            pl.BlockSpec((erows, TB), lambda i, *_: (0, i)),
            pl.BlockSpec((erows, LANES), fixed),
            pl.BlockSpec((1, LANES), fixed),
            pl.BlockSpec((1, width), fixed),
            pl.BlockSpec((width, LANES), fixed),
            pl.BlockSpec((width, LANES), fixed),
            pl.BlockSpec((LANES, LANES), fixed),
        ],
        out_specs=[
            pl.BlockSpec((TB, width), block),
            pl.BlockSpec((TB, width), block),
            pl.BlockSpec((TB, LANES), block),
            pl.BlockSpec((LANES, width), fixed),
            pl.BlockSpec((LANES, width), fixed),
            pl.BlockSpec((8, width), fixed),
            pl.BlockSpec((LANES, LANES), fixed),
        ],
        scratch_shapes=[pltpu.VMEM((TB, width), BF16)],
    )
    return pl.pallas_call(
        functools.partial(middle_kernel, types, ffn, total_tokens),
        name="middle",
        grid_spec=grid_spec,
        out_shape=(
            jax.ShapeDtypeStruct((tokens, width), F32),
            jax.ShapeDtypeStruct((tokens, width), BF16),
            jax.ShapeDtypeStruct((tokens, LANES), F32),
            jax.ShapeDtypeStruct((LANES, width), F32),
            jax.ShapeDtypeStruct((LANES, width), F32),
            jax.ShapeDtypeStruct((8, width), F32),
            jax.ShapeDtypeStruct((LANES, LANES), F32),
        ),
        compiler_params=params(),
        cost_estimate=pl.CostEstimate(flops=4_000_000_000, bytes_accessed=25_000_000, transcendentals=300_000),
    )(idx, mine, theirs, x1, dy, lg, aux, dlt, eye, count, gain, wcat, vt, wprevt)


def output_kernel(types, ffn, idx_ref, mine_ref, theirs_ref, x1_ref, h2_ref, lg_ref, aux_ref, v_ref, out_ref, scr_ref):
    half = idx_ref[1]
    half_cols = mine_ref.shape[1]
    scr_ref[:, pl.ds(pl.multiple_of(half * half_cols, LANES), half_cols)] = mine_ref[...]
    scr_ref[:, pl.ds(pl.multiple_of((1 - half) * half_cols, LANES), half_cols)] = theirs_ref[...]
    lg = lg_ref[...]
    lane, probs, mask = routing(lg, aux_ref[...], types)
    gates = probs * mask
    coef = column(gates, lane, ffn + 1)
    out = x1_ref[...] + scr_ref[...].astype(F32)
    for c in range(2):
        m0, m1 = const_mix(lg, lane, types, c)
        g = column(gates, lane, ffn + 2 + c)
        coef = coef + g * m0
        out = out + (g * m1) * v_ref[c : c + 1, :]
    out_ref[...] = out + coef * h2_ref[...].astype(F32)


def output_pass(idx, mine, theirs, x1, h2, lg, aux, v, types, ffn):
    tokens, width = x1.shape
    block = lambda i, *_: (i, 0)
    fixed = lambda i, *_: (0, 0)
    grid_spec = pltpu.PrefetchScalarGridSpec(
        num_scalar_prefetch=1,
        grid=(tokens // TB,),
        in_specs=[
            pl.BlockSpec((TB, width // 2), block),
            pl.BlockSpec((TB, width // 2), block),
            pl.BlockSpec((TB, width), block),
            pl.BlockSpec((TB, width), block),
            pl.BlockSpec((TB, LANES), block),
            pl.BlockSpec((TB, LANES), block),
            pl.BlockSpec((8, width), fixed),
        ],
        out_specs=pl.BlockSpec((TB, width), block),
        scratch_shapes=[pltpu.VMEM((TB, width), BF16)],
    )
    return pl.pallas_call(
        functools.partial(output_kernel, types, ffn),
        name="output",
        grid_spec=grid_spec,
        out_shape=jax.ShapeDtypeStruct((tokens, width), F32),
        compiler_params=params(),
        cost_estimate=pl.CostEstimate(flops=20_000_000, bytes_accessed=22_000_000, transcendentals=300_000),
    )(idx, mine, theirs, x1, h2, lg, aux, v)


def last_kernel(idx_ref, mine_ref, theirs_ref, x_ref, dx1_ref, gain_ref, out_ref, scr_ref):
    half = idx_ref[1]
    half_cols = mine_ref.shape[1]
    scr_ref[:, pl.ds(pl.multiple_of(half * half_cols, LANES), half_cols)] = mine_ref[...]
    scr_ref[:, pl.ds(pl.multiple_of((1 - half) * half_cols, LANES), half_cols)] = theirs_ref[...]
    x = x_ref[...].astype(F32)
    r1 = rms_factor(x)
    n1 = x * r1
    dn1 = scr_ref[...].astype(F32) * gain_ref[...]
    out_ref[...] = dx1_ref[...] + r1 * (dn1 - n1 * jnp.mean(dn1 * n1, axis=1, keepdims=True))


def last_pass(idx, mine, theirs, x, dx1, gain):
    tokens, width = x.shape
    block = lambda i, *_: (i, 0)
    fixed = lambda i, *_: (0, 0)
    grid_spec = pltpu.PrefetchScalarGridSpec(
        num_scalar_prefetch=1,
        grid=(tokens // TB,),
        in_specs=[
            pl.BlockSpec((TB, width // 2), block),
            pl.BlockSpec((TB, width // 2), block),
            pl.BlockSpec((TB, width), block),
            pl.BlockSpec((TB, width), block),
            pl.BlockSpec((1, width), fixed),
        ],
        out_specs=pl.BlockSpec((TB, width), block),
        scratch_shapes=[pltpu.VMEM((TB, width), BF16)],
    )
    return pl.pallas_call(
        last_kernel,
        name="last",
        grid_spec=grid_spec,
        out_shape=jax.ShapeDtypeStruct((tokens, width), F32),
        compiler_params=params(),
        cost_estimate=pl.CostEstimate(flops=20_000_000, bytes_accessed=20_000_000, transcendentals=2_000),
    )(idx, mine, theirs, x, dx1, gain)


def group_sum(keep, send):
    part = (keep.astype(F32) + swap(send, "tensor", 1).astype(F32)).astype(BF16)
    bit = 2
    while bit < lax.axis_size("tensor"):
        part = (part.astype(F32) + swap(part, "tensor", bit).astype(F32)).astype(BF16)
        bit *= 2
    return part, swap(part, "tensor", 1)


def gather_group(a):
    out = [a]
    bit = lax.axis_size("tensor") // 2
    parts = {0: a}
    while bit:
        parts.update({m | bit: swap(p, "tensor", bit) for m, p in list(parts.items())})
        bit //= 2
    return [parts[m] for m in range(len(parts))]


def per_device(hidden_in, prev_logits, routes, block_ids, cotangent, gain_attn, w_qkv, w_out, gain_moe, w_router, w_prev, w_const, v_const, w_gate_up, w_down):
    tokens, width = hidden_in.shape
    types = w_router.shape[1]
    experts = lax.axis_size("expert")
    heads = w_out.shape[0] // HEAD_DIM
    hidden = w_down.shape[1]
    total_tokens = tokens * lax.axis_size(("dp", "expert"))
    t_index, x_index = lax.axis_index("tensor"), lax.axis_index("expert")
    t_idx = jnp.stack([t_index, t_index % 2]).astype(jnp.int32)
    x_idx = jnp.stack([x_index, t_index % 2]).astype(jnp.int32)

    wgu, wd = w_gate_up[0].reshape(width, 2 * hidden), w_down[0]
    wgus = [wgu] + [swap(wgu, "expert", s) for s in range(1, experts)]
    wds = [wd] + [swap(wd, "expert", s) for s in range(1, experts)]
    wos = gather_group(w_out)
    gain_first = gain_attn.astype(F32)[None]
    gain_second = gain_moe.astype(F32)[None]
    consts = w_const.transpose(1, 0, 2).reshape(width, 4)
    wcat = jnp.pad(jnp.concatenate([w_router, consts], axis=1), ((0, 0), (0, LANES - types - 4)))
    aux = jnp.concatenate([prev_logits, routes.astype(BF16)], axis=1)
    aux = jnp.pad(aux, ((0, 0), (0, LANES - types - 2)))
    wprev = jnp.pad(w_prev, ((0, LANES - types), (0, LANES - types)))
    wprevt = jnp.pad(w_prev.T, ((0, LANES - types), (0, LANES - types)))
    vt = jnp.pad(v_const.T, ((0, 0), (0, LANES - 2)))
    vrows = jnp.pad(v_const.astype(F32), ((0, 6), (0, 0)))
    erows = -(-types // 16) * 16
    eye = jnp.eye(erows, LANES, dtype=BF16)
    lanes = jnp.arange(LANES, dtype=jnp.int32)
    chosen = (routes[:, :, None] == lanes[None, None, :]).astype(F32)
    count = sum_over(jnp.sum(chosen, axis=(0, 1))[None], ("expert", "dp"))
    bq, bk = block_ids, block_ids.reshape(tokens, 1)

    h1, qkvt, ot, lse = attention_forward(hidden_in, gain_first, w_qkv.T, bq, bk, heads)
    ots = gather_group(ot)
    x1, h2, lg, prob_part = post_attention(t_idx, hidden_in, ots, wos, gain_second, wcat, aux, wprev, types)
    keep, send, gh, du, dlt = experts_pass(x_idx, h2, cotangent, lg, aux, wgus, wds, eye, types)
    mine, theirs = group_sum(keep, send)
    dlt = sum_over(dlt, ("tensor",))
    fkeep, fsend = down_pass(x_idx, gh, wds)
    grad_gate_up = jnp.einsum("td,etf->edf", h2, du, preferred_element_type=F32).astype(BF16)
    grad_down = jnp.einsum("td,etf->edf", cotangent, gh, preferred_element_type=F32).astype(BF16)
    fmine, ftheirs = group_sum(fkeep, fsend)
    dx1, da, gp, g1, g2, g3, g4 = middle_pass(
        x_idx, mine, theirs, x1, cotangent, lg, aux, dlt, eye, count, gain_second, wcat, vt, wprevt, types, experts, total_tokens
    )
    srows = -(-(types + 4) // 8) * 8
    prow = -(-types // 8) * 8
    small = jnp.concatenate(
        [
            g1[:srows],
            g2[:8],
            g3,
            jnp.pad(g4[:prow], ((0, 0), (0, width - LANES))),
            jnp.pad(prob_part, ((0, 0), (0, width - LANES))),
        ],
        axis=0,
    )
    small = sum_over(small, ("expert", "dp"))
    grad_out = lax.dot_general(ot, da, (((1,), (0,)), ((), ())), preferred_element_type=F32)
    dqkvt = attention_backward(da, w_out, qkvt, ot, lse, bq, bk, heads)
    output = output_pass(x_idx, fmine, ftheirs, x1, h2, lg, aux, vrows, types, experts)

    dh1 = lax.dot_general(dqkvt, w_qkv, (((0,), (1,)), ((), ())), preferred_element_type=F32).astype(BF16)
    core = t_index % 2
    half_cols = width // 2
    last_mine, last_theirs = group_sum(
        lax.dynamic_slice_in_dim(dh1, core * half_cols, half_cols, 1),
        lax.dynamic_slice_in_dim(dh1, (1 - core) * half_cols, half_cols, 1),
    )
    grad_qkv = lax.dot_general(h1, dqkvt, (((0,), (1,)), ((), ())), preferred_element_type=F32)
    gain_part = jnp.sum(grad_qkv * w_qkv.astype(F32), axis=1)
    grad_gain = sum_over(gain_part[None], ("tensor", "expert", "dp"))[0] / gain_first[0]
    grad_input = last_pass(x_idx, last_mine, last_theirs, hidden_in, dx1, gain_first)

    grad_gate_up = lax.psum_scatter(grad_gate_up, "expert", scatter_dimension=0, tiled=True)
    grad_gate_up = lax.psum_scatter(grad_gate_up, "dp", scatter_dimension=1, tiled=True).astype(F32)
    grad_down = lax.psum_scatter(grad_down, "expert", scatter_dimension=0, tiled=True)
    grad_down = lax.psum_scatter(grad_down, "dp", scatter_dimension=1, tiled=True).astype(F32)
    grad_qkv = lax.psum_scatter(grad_qkv, ("dp", "expert"), scatter_dimension=0, tiled=True)
    grad_out = lax.psum_scatter(grad_out, ("dp", "expert"), scatter_dimension=1, tiled=True)

    prob_all = small[srows + 16 + prow, :types]
    count_all = count[0, :types]
    balance_loss = types * jnp.sum((count_all / (2.0 * total_tokens)) * prob_all / total_tokens)
    load = jnp.stack([count_all / (2.0 * tokens), prob_all / tokens])
    return (
        output,
        grad_input,
        gp[:, :types],
        grad_gain,
        grad_qkv,
        grad_out,
        small[srows + 8],
        small[:types].T,
        small[srows + 16 : srows + 16 + types, :types],
        small[types : types + 4].reshape(2, 2, width).transpose(0, 2, 1),
        small[srows : srows + 2],
        grad_gate_up.reshape(1, -1, 2, hidden),
        grad_down.transpose(0, 2, 1),
        balance_loss,
        load,
    )


def solution(mesh):
    tok = P(("dp", "expert"), None)
    return jax.shard_map(
        per_device,
        mesh=mesh,
        in_specs=(
            tok,
            tok,
            tok,
            tok,
            tok,
            P(),
            P(None, "tensor"),
            P("tensor", None),
            P(),
            P(),
            P(),
            P(),
            P(),
            P("expert", None, None, "tensor"),
            P("expert", "tensor", None),
        ),
        out_specs=(
            tok,
            tok,
            tok,
            P(),
            P(("dp", "expert"), "tensor"),
            P("tensor", ("dp", "expert")),
            P(),
            P(),
            P(),
            P(),
            P(),
            P("expert", "dp", None, "tensor"),
            P("expert", "tensor", "dp"),
            P(),
            P(),
        ),
        check_vma=False,
    )
```

```python
import functools

import jax
import jax.numpy as jnp
from jax import lax
from jax.experimental import pallas as pl
from jax.experimental.pallas import tpu as pltpu
from jax.sharding import PartitionSpec as P

HEAD_DIM = 64
EPSILON = 1e-06
AUX_WEIGHT = 0.01
SCORE_SCALE = 0.125
MAX_BLOCK = 256
LANES = 128
QB = 256
QF = 512
TB = 256
NEG = -1e30
F32 = jnp.float32
BF16 = jnp.bfloat16
MESH = pl.DeviceIdType.MESH
VMEM_LIMIT = 48 * 1024 * 1024
COST = pl.CostEstimate(flops=1000, bytes_accessed=1000, transcendentals=0)


def params(**more):
    return pltpu.CompilerParams(vmem_limit_bytes=VMEM_LIMIT, **more)


def nn(a, b):
    return lax.dot_general(a, b, (((1,), (0,)), ((), ())), preferred_element_type=F32)


def nt(a, b):
    return lax.dot_general(a, b, (((1,), (1,)), ((), ())), preferred_element_type=F32)


def tn(a, b):
    return lax.dot_general(a, b, (((0,), (0,)), ((), ())), preferred_element_type=F32)


def split_hi_lo(a):
    hi = a.astype(BF16)
    return hi, (a - hi.astype(F32)).astype(BF16)


def rms_factor(values):
    return lax.rsqrt(jnp.mean(values * values, axis=-1, keepdims=True) + EPSILON)


def swap(a, axis, bit):
    n = lax.axis_size(axis)
    return lax.ppermute(a, axis, [(i, i ^ bit) for i in range(n)])


def sum_over(a, axes):
    for axis in axes:
        bit = 1
        while bit < lax.axis_size(axis):
            a = a + swap(a, axis, bit)
            bit *= 2
    return a


def key_range(q0, rows, tokens):
    return min(tokens, q0 + rows + MAX_BLOCK)


def attn_fwd_kernel(heads, x_ref, gain_ref, wt_ref, bq_ref, bk_ref, h1_ref, qkvt_ref, ot_ref, lse_ref, kn_ref):
    tokens = x_ref.shape[0]
    d = HEAD_DIM
    for r0 in range(0, tokens, QF):
        rows = slice(r0, r0 + QF)
        xb = x_ref[rows, :].astype(F32)
        h1 = (xb * rms_factor(xb) * gain_ref[...]).astype(BF16)
        h1_ref[rows, :] = h1
        qkvt = nt(wt_ref[...], h1)
        for h in range(heads):
            base = h * 3 * d
            q = qkvt[base : base + d].astype(BF16).astype(F32) * SCORE_SCALE
            qkvt_ref[base : base + d, rows] = q.astype(BF16)
            qkvt_ref[base + d : base + 3 * d, rows] = qkvt[base + d : base + 3 * d].astype(BF16)
            kn_ref[h, rows, :] = qkvt[base + d : base + 2 * d].T.astype(BF16)
    for h in range(heads):
        base = h * 3 * d
        for q0 in range(0, tokens, QF):
            cols = slice(q0, q0 + QF)
            top = key_range(q0, QF, tokens)
            s = nn(kn_ref[h, :top, :], qkvt_ref[base : base + d, cols])
            parts = [jnp.where(bk_ref[q0:top, :] <= bq_ref[:, cols], s[q0:], NEG)]
            if q0:
                parts = [s[:q0]] + parts
            m = functools.reduce(jnp.maximum, [jnp.max(a, axis=0, keepdims=True) for a in parts])
            ps = [jnp.exp(a - m) for a in parts]
            total = functools.reduce(jnp.add, [jnp.sum(p, axis=0, keepdims=True) for p in ps])
            p = jnp.concatenate([p.astype(BF16) for p in ps], axis=0)
            acc = nn(qkvt_ref[base + 2 * d : base + 3 * d, :top], p)
            ot_ref[h * d : (h + 1) * d, cols] = (acc / total).astype(BF16)
            lse_ref[h : h + 1, cols] = m + jnp.log(total)


def attention_forward(x, gain, w_t, bq, bk, heads):
    tokens, width = x.shape
    cols = w_t.shape[0]
    lse_rows = -(-heads // 8) * 8
    return pl.pallas_call(
        functools.partial(attn_fwd_kernel, heads),
        name="attn_fwd",
        out_shape=(
            jax.ShapeDtypeStruct((tokens, width), BF16),
            jax.ShapeDtypeStruct((cols, tokens), BF16),
            jax.ShapeDtypeStruct((heads * HEAD_DIM, tokens), BF16),
            jax.ShapeDtypeStruct((lse_rows, tokens), F32),
        ),
        scratch_shapes=[pltpu.VMEM((heads, tokens, HEAD_DIM), BF16)],
        compiler_params=params(),
        cost_estimate=COST,
    )(x, gain, w_t, bq, bk)


CHUNK = 256


def neighbours():
    t = lax.axis_index("tensor")
    return t % 2, {"tensor": t + 1 - 2 * (t % 2)}, {"tensor": (t + 2) % 4}


def greet(devices):
    barrier = pltpu.get_barrier_semaphore()
    for device in devices:
        pl.semaphore_signal(barrier, inc=1, device_id=device, device_id_type=MESH)
    pl.semaphore_wait(barrier, len(devices))


def each(count, step):
    def body(i, carry):
        step(i)
        return carry

    lax.fori_loop(0, count, body, 0)


class GroupSum:
    def __init__(self, keep, send, first, second, result, sems):
        self.keep, self.send, self.first, self.second, self.result, self.sems = keep, send, first, second, result, sems
        self.half, self.partner, self.other = neighbours()

    def rows(self, i):
        return pl.ds(pl.multiple_of(i * CHUNK, CHUNK), CHUNK)

    def copy(self, stage, i, src, dst, device):
        return pltpu.make_async_remote_copy(
            src_ref=src,
            dst_ref=dst,
            send_sem=self.sems.at[0, stage, i],
            recv_sem=self.sems.at[1, stage, i],
            device_id=device,
            device_id_type=MESH,
        )

    def to_partner(self, i):
        r = self.rows(i)
        return self.copy(0, i, self.send.at[r, :], self.first.at[r, :], self.partner)

    def to_other(self, i):
        r = self.rows(i)
        return self.copy(1, i, self.keep.at[r, :], self.second.at[r, :], self.other)

    def back(self, i):
        place = self.result.at[self.half, self.rows(i), :]
        return self.copy(2, i, place, place, self.partner)

    def pair(self, i):
        self.to_partner(i).wait_recv()
        r = self.rows(i)
        self.keep[r, :] = (self.keep[r, :].astype(F32) + self.first[r, :].astype(F32)).astype(BF16)
        self.to_other(i).start()

    def finish(self, i):
        self.to_other(i).wait_recv()
        r = self.rows(i)
        self.result[self.half, r, :] = (self.keep[r, :].astype(F32) + self.second[r, :].astype(F32)).astype(BF16)
        self.back(i).start()

    def close(self, i):
        self.back(i).wait_recv()
        self.to_partner(i).wait_send()
        self.to_other(i).wait_send()
        self.back(i).wait_send()


def sum_scratch(tokens, half_cols, sends=True):
    return [pltpu.VMEM((tokens, half_cols), BF16)] * (4 if sends else 3) + [pltpu.SemaphoreType.DMA((2, 3, tokens // CHUNK))]


def attn_bwd_kernel(heads, da_ref, wo_ref, qkvt_ref, ot_ref, lse_ref, bq_ref, bk_ref, wq_ref, fkeep_ref, fsend_ref, dqkvt_ref, dres_ref, fres_ref, dot_ref, delta_ref, kn_ref, vn_ref, dk_ref, dv_ref, *scratch):
    tokens = da_ref.shape[0]
    d = HEAD_DIM
    chunks = tokens // CHUNK
    dkeep, dsend, dfirst, dsecond, dsems, fsum, ffirst, fsecond, fsems = scratch
    dh = GroupSum(dkeep, dsend, dfirst, dsecond, dres_ref, dsems)
    ff = GroupSum(fsum, fsend_ref, ffirst, fsecond, fres_ref, fsems)
    half, partner, other = neighbours()
    greet((partner, other))
    each(chunks, lambda i: ff.to_partner(i).start())
    fsum[...] = fkeep_ref[...]

    def project(i):
        rows = pl.ds(pl.multiple_of(i * CHUNK, CHUNK), CHUNK)
        dot = nt(wo_ref[...], da_ref[rows, :]).astype(BF16)
        dot_ref[:, rows] = dot
        prod = dot.astype(F32) * ot_ref[:, rows].astype(F32)
        for h in range(heads):
            base = h * 3 * d
            delta_ref[h : h + 1, rows] = jnp.sum(prod[h * d : (h + 1) * d], axis=0, keepdims=True)
            kn_ref[h, rows, :] = qkvt_ref[base + d : base + 2 * d, rows].astype(F32).T.astype(BF16)
            vn_ref[h, rows, :] = qkvt_ref[base + 2 * d : base + 3 * d, rows].astype(F32).T.astype(BF16)

    each(chunks, project)
    each(chunks, ff.pair)
    dk_ref[...] = jnp.zeros_like(dk_ref)
    dv_ref[...] = jnp.zeros_like(dv_ref)

    def head(h):
        base = pl.multiple_of(h * 3 * d, d)
        qrows, krows, vrows = pl.ds(base, d), pl.ds(base + d, d), pl.ds(base + 2 * d, d)
        orows = pl.ds(pl.multiple_of(h * d, d), d)
        for q0 in range(0, tokens, QB):
            cols = slice(q0, q0 + QB)
            top = key_range(q0, QB, tokens)
            qt = qkvt_ref[qrows, cols]
            dot = dot_ref[orows, cols]
            s = nn(kn_ref[h, :top, :], qt)
            p = jnp.exp(s - lse_ref[pl.ds(h, 1), cols])
            last = jnp.where(bk_ref[q0:top, :] <= bq_ref[:, cols], p[q0:], 0.0)
            p = jnp.concatenate([p[:q0], last], axis=0) if q0 else last
            dp = nn(vn_ref[h, :top, :], dot)
            ds = (p * (dp - delta_ref[pl.ds(h, 1), cols])).astype(BF16)
            dv_ref[h, :, :top] += nt(dot, p.astype(BF16))
            dk_ref[h, :, :top] += nt(qt, ds)
            dq = nn(qkvt_ref[krows, :top], ds)
            dqkvt_ref[qrows, cols] = (dq * SCORE_SCALE).astype(BF16)
        dqkvt_ref[krows, :] = dk_ref[h].astype(BF16)
        dqkvt_ref[vrows, :] = dv_ref[h].astype(BF16)

    each(heads, head)

    def input_grad(i):
        r = dh.rows(i)
        dqkv = dqkvt_ref[:, r]
        dsend[r, :] = tn(dqkv, wq_ref[1 - half]).astype(BF16)
        dh.to_partner(i).start()
        dkeep[r, :] = tn(dqkv, wq_ref[half]).astype(BF16)
        dh.pair(i)

    each(chunks, input_grad)
    each(chunks, ff.finish)
    each(chunks, dh.finish)
    each(chunks, ff.close)
    each(chunks, dh.close)


def attention_backward(da, w_out, qkvt, ot, lse, bq, bk, w_halves, fkeep, fsend, heads):
    tokens, width = da.shape
    cols = qkvt.shape[0]
    return pl.pallas_call(
        functools.partial(attn_bwd_kernel, heads),
        name="attn_bwd",
        out_shape=(
            jax.ShapeDtypeStruct((cols, tokens), BF16),
            jax.ShapeDtypeStruct((2, tokens, width // 2), BF16),
            jax.ShapeDtypeStruct((2, tokens, width // 2), BF16),
        ),
        scratch_shapes=[
            pltpu.VMEM((heads * HEAD_DIM, tokens), BF16),
            pltpu.VMEM((lse.shape[0], tokens), F32),
            pltpu.VMEM((heads, tokens, HEAD_DIM), BF16),
            pltpu.VMEM((heads, tokens, HEAD_DIM), BF16),
            pltpu.VMEM((heads, HEAD_DIM, tokens), F32),
            pltpu.VMEM((heads, HEAD_DIM, tokens), F32),
        ]
        + sum_scratch(tokens, width // 2)
        + sum_scratch(tokens, width // 2, False),
        compiler_params=params(collective_id=1, has_side_effects=True),
        cost_estimate=COST,
    )(da, w_out, qkvt, ot, lse, bq, bk, w_halves, fkeep, fsend)


def lane_iota(rows):
    return lax.broadcasted_iota(jnp.int32, (rows, LANES), 1)


def column(values, lane, number):
    return jnp.sum(jnp.where(lane == number, values, 0.0), axis=1, keepdims=True)


def routing(logits, aux, types):
    lane = lane_iota(logits.shape[0])
    is_type = lane < types
    shown = jnp.where(is_type, logits, NEG)
    e = jnp.exp(shown - jnp.max(shown, axis=1, keepdims=True))
    probs = e / jnp.sum(e, axis=1, keepdims=True)
    aux = aux.astype(F32)
    first = column(aux, lane, types).astype(jnp.int32)
    second = column(aux, lane, types + 1).astype(jnp.int32)
    mask = jnp.where((lane == first) | (lane == second), 1.0, 0.0)
    return lane, probs, mask


def const_mix(logits, lane, types, c):
    l0 = column(logits, lane, types + 2 * c)
    l1 = column(logits, lane, types + 2 * c + 1)
    top = jnp.maximum(l0, l1)
    e0, e1 = jnp.exp(l0 - top), jnp.exp(l1 - top)
    total = e0 + e1
    return e0 / total, e1 / total


def post_attn_kernel(types, group, idx_ref, x_ref, *refs):
    ots, wos = refs[:group], refs[group : 2 * group]
    gain_ref, wcat_ref, aux_ref, wprev_ref = refs[2 * group : 2 * group + 4]
    x1_ref, h2_ref, lg_ref, ps_ref, wo_scr, ot_scr = refs[2 * group + 4 :]
    rows = ots[0].shape[0]
    me = idx_ref[0]

    @pl.when(pl.program_id(0) == 0)
    def _():
        for m in range(group):
            wo_scr[pl.ds(pl.multiple_of((me ^ m) * rows, HEAD_DIM), rows), :] = wos[m][...]
        ps_ref[...] = jnp.zeros_like(ps_ref)

    for m in range(group):
        ot_scr[pl.ds(pl.multiple_of((me ^ m) * rows, HEAD_DIM), rows), :] = ots[m][...]
    x1 = x_ref[...].astype(F32) + tn(ot_scr[...], wo_scr[...])
    x1_ref[...] = x1
    h2 = (x1 * rms_factor(x1) * gain_ref[...]).astype(BF16)
    h2_ref[...] = h2
    lg = nn(h2, wcat_ref[...]) + nn(aux_ref[...], wprev_ref[...])
    lg_ref[...] = lg
    _, probs, _ = routing(lg, aux_ref[...], types)
    ps_ref[0:1, :] += jnp.sum(probs, axis=0, keepdims=True)


def post_attention(me, x, ots, wos, gain, wcat, aux, wprev, types):
    tokens, width = x.shape
    rows = ots[0].shape[0]
    group = len(ots)
    block = lambda i, *_: (i, 0)
    fixed = lambda i, *_: (0, 0)
    grid_spec = pltpu.PrefetchScalarGridSpec(
        num_scalar_prefetch=1,
        grid=(tokens // TB,),
        in_specs=[pl.BlockSpec((TB, width), block)]
        + [pl.BlockSpec((rows, TB), lambda i, *_: (0, i))] * group
        + [pl.BlockSpec((rows, width), fixed)] * group
        + [
            pl.BlockSpec((1, width), fixed),
            pl.BlockSpec((width, LANES), fixed),
            pl.BlockSpec((TB, LANES), block),
            pl.BlockSpec((LANES, LANES), fixed),
        ],
        out_specs=[
            pl.BlockSpec((TB, width), block),
            pl.BlockSpec((TB, width), block),
            pl.BlockSpec((TB, LANES), block),
            pl.BlockSpec((8, LANES), fixed),
        ],
        scratch_shapes=[pltpu.VMEM((group * rows, width), BF16), pltpu.VMEM((group * rows, TB), BF16)],
    )
    return pl.pallas_call(
        functools.partial(post_attn_kernel, types, group),
        name="post_attn",
        grid_spec=grid_spec,
        out_shape=(
            jax.ShapeDtypeStruct((tokens, width), F32),
            jax.ShapeDtypeStruct((tokens, width), BF16),
            jax.ShapeDtypeStruct((tokens, LANES), F32),
            jax.ShapeDtypeStruct((8, LANES), F32),
        ),
        compiler_params=params(),
        cost_estimate=COST,
    )(me, x, *ots, *wos, gain, wcat, aux, wprev)


def expert_kernel(types, experts, halves, idx_ref, h2_ref, dy_ref, lg_ref, aux_ref, *refs):
    wgus, wds = refs[:experts], refs[experts : 2 * experts]
    eye_ref = refs[2 * experts]
    keep_ref, send_ref, gh_ref, du_ref, dlt_ref, acc_ref = refs[2 * experts + 1 :]
    me, half = idx_ref[0], idx_ref[1]
    hidden = wds[0].shape[0]
    h2, dy = h2_ref[...], dy_ref[...]
    lane, probs, mask = routing(lg_ref[...], aux_ref[...], types)
    gates = probs * mask
    dprobs = jnp.zeros_like(probs)
    for s in range(experts):
        e = me ^ s
        gate_col = column(gates, lane, e)
        u = nn(h2, wgus[s][...])
        dhr = nt(dy, wds[s][...])
        g, up = u[:, :hidden], u[:, hidden:]
        sig = 1.0 / (1.0 + jnp.exp(-g))
        silu = g * sig
        hid = silu * up
        gh_ref[s, :, :] = (hid * gate_col).astype(BF16)
        dg = jnp.sum(hid * dhr, axis=1, keepdims=True)
        dprobs = dprobs + jnp.where(lane == e, dg * mask, 0.0)
        dh = dhr * gate_col
        dgate = dh * up * sig * (1.0 + g * (1.0 - sig))
        dup = dh * silu
        du_ref[s, :, :hidden] = dgate.astype(BF16)
        du_ref[s, :, hidden:] = dup.astype(BF16)
        part = nt(du_ref[s, :, :], wgus[s][...])
        if s == 0:
            acc_ref[...] = part
        else:
            acc_ref[...] += part
    dlog = probs * (dprobs - jnp.sum(probs * dprobs, axis=1, keepdims=True))
    hi, lo = split_hi_lo(dlog)
    dlt_ref[...] = nt(eye_ref[...], hi) + nt(eye_ref[...], lo)
    half_cols = acc_ref.shape[1] // halves
    keep_ref[...] = acc_ref[:, pl.ds(pl.multiple_of(half * half_cols, LANES), half_cols)].astype(BF16)
    send_ref[...] = acc_ref[:, pl.ds(pl.multiple_of((1 - half) * half_cols, LANES), half_cols)].astype(BF16)


def experts_pass(idx, h2, dy, lg, aux, wgus, wds, eye, types):
    tokens, width = h2.shape
    experts = len(wgus)
    hidden = wds[0].shape[0]
    erows = eye.shape[0]
    block = lambda i, *_: (i, 0)
    fixed = lambda i, *_: (0, 0)
    grid_spec = pltpu.PrefetchScalarGridSpec(
        num_scalar_prefetch=1,
        grid=(tokens // TB,),
        in_specs=[
            pl.BlockSpec((TB, width), block),
            pl.BlockSpec((TB, width), block),
            pl.BlockSpec((TB, LANES), block),
            pl.BlockSpec((TB, LANES), block),
        ]
        + [pl.BlockSpec((width, 2 * hidden), fixed, pipeline_mode=pl.Buffered(1))] * experts
        + [pl.BlockSpec((hidden, width), fixed, pipeline_mode=pl.Buffered(1))] * experts
        + [pl.BlockSpec((erows, LANES), fixed)],
        out_specs=[
            pl.BlockSpec((TB, width // 2), block),
            pl.BlockSpec((TB, width // 2), block),
            pl.BlockSpec((experts, TB, hidden), lambda i, *_: (0, i, 0)),
            pl.BlockSpec((experts, TB, 2 * hidden), lambda i, *_: (0, i, 0)),
            pl.BlockSpec((erows, TB), lambda i, *_: (0, i)),
        ],
        scratch_shapes=[pltpu.VMEM((TB, width), F32)],
    )
    return pl.pallas_call(
        functools.partial(expert_kernel, types, experts, 2),
        name="experts",
        grid_spec=grid_spec,
        out_shape=(
            jax.ShapeDtypeStruct((tokens, width // 2), BF16),
            jax.ShapeDtypeStruct((tokens, width // 2), BF16),
            jax.ShapeDtypeStruct((experts, tokens, hidden), BF16),
            jax.ShapeDtypeStruct((experts, tokens, 2 * hidden), BF16),
            jax.ShapeDtypeStruct((erows, tokens), F32),
        ),
        compiler_params=params(),
        cost_estimate=COST,
    )(idx, h2, dy, lg, aux, *wgus, *wds, eye)


def down_kernel(experts, idx_ref, gh_ref, *refs):
    wds, (keep_ref, send_ref, acc_ref) = refs[:experts], refs[experts:]
    me, half = idx_ref[0], idx_ref[1]
    for s in range(experts):
        part = nn(gh_ref[s, :, :], wds[s][...])
        if s == 0:
            acc_ref[...] = part
        else:
            acc_ref[...] += part
    half_cols = keep_ref.shape[1]
    keep_ref[...] = acc_ref[:, pl.ds(pl.multiple_of(half * half_cols, LANES), half_cols)].astype(BF16)
    send_ref[...] = acc_ref[:, pl.ds(pl.multiple_of((1 - half) * half_cols, LANES), half_cols)].astype(BF16)


def down_pass(idx, gh, wds):
    experts, tokens, hidden = gh.shape
    width = wds[0].shape[1]
    block = lambda i, *_: (i, 0)
    fixed = lambda i, *_: (0, 0)
    grid_spec = pltpu.PrefetchScalarGridSpec(
        num_scalar_prefetch=1,
        grid=(tokens // TB,),
        in_specs=[pl.BlockSpec((experts, TB, hidden), lambda i, *_: (0, i, 0))]
        + [pl.BlockSpec((hidden, width), fixed, pipeline_mode=pl.Buffered(1))] * experts,
        out_specs=[pl.BlockSpec((TB, width // 2), block)] * 2,
        scratch_shapes=[pltpu.VMEM((TB, width), F32)],
    )
    return pl.pallas_call(
        functools.partial(down_kernel, experts),
        name="down",
        grid_spec=grid_spec,
        out_shape=(jax.ShapeDtypeStruct((tokens, width // 2), BF16),) * 2,
        compiler_params=params(),
        cost_estimate=COST,
    )(idx, gh, *wds)


def middle_kernel(types, ffn, total_tokens, idx_ref, mine_ref, theirs_ref, x1_ref, dy_ref, lg_ref, aux_ref, dlt_ref, eye_ref, count_ref, gain_ref, wcat_ref, vt_ref, wprevt_ref, dx1_ref, da_ref, gp_ref, g1_ref, g2_ref, g3_ref, g4_ref, scr_ref):
    half = idx_ref[1]
    half_cols = mine_ref.shape[1]
    scr_ref[:, pl.ds(pl.multiple_of(half * half_cols, LANES), half_cols)] = mine_ref[...]
    scr_ref[:, pl.ds(pl.multiple_of((1 - half) * half_cols, LANES), half_cols)] = theirs_ref[...]
    first = pl.program_id(0) == 0

    @pl.when(first)
    def _():
        for ref in (g1_ref, g2_ref, g3_ref, g4_ref):
            ref[...] = jnp.zeros_like(ref)

    gain = gain_ref[...]
    x1 = x1_ref[...]
    r2 = rms_factor(x1)
    n2 = x1 * r2
    h2 = (n2 * gain).astype(BF16)
    dyb = dy_ref[...]
    dy = dyb.astype(F32)
    lg = lg_ref[...]
    lane, probs, mask = routing(lg, aux_ref[...], types)
    gates = probs * mask
    a = jnp.sum(dy * h2.astype(F32), axis=1, keepdims=True)
    b = nn(dyb, vt_ref[...])
    coef = column(gates, lane, ffn + 1)
    dprobs = jnp.where(lane == ffn + 1, a, 0.0)
    dlc = jnp.zeros_like(probs)
    vcoef = jnp.zeros_like(probs)
    for c in range(2):
        m0, m1 = const_mix(lg, lane, types, c)
        g = column(gates, lane, ffn + 2 + c)
        bc = column(b, lane, c)
        dprobs = dprobs + jnp.where(lane == ffn + 2 + c, m0 * a + m1 * bc, 0.0)
        dm0, dm1 = g * a, g * bc
        inner = m0 * dm0 + m1 * dm1
        dlc = dlc + jnp.where(lane == types + 2 * c, m0 * (dm0 - inner), 0.0)
        dlc = dlc + jnp.where(lane == types + 2 * c + 1, m1 * (dm1 - inner), 0.0)
        coef = coef + g * m0
        vcoef = vcoef + jnp.where(lane == c, g * m1, 0.0)
    dprobs = dprobs * mask + count_ref[...] * (AUX_WEIGHT * types / (2.0 * total_tokens * total_tokens))
    dlog = probs * (dprobs - jnp.sum(probs * dprobs, axis=1, keepdims=True))
    hi, lo = split_hi_lo(dlt_ref[...])
    dl = dlog + dlc + tn(hi, eye_ref[...]) + tn(lo, eye_ref[...])
    dhi, dlo = split_hi_lo(dl)
    dh2 = scr_ref[...].astype(F32) + coef * dy + nt(dhi, wcat_ref[...]) + nt(dlo, wcat_ref[...])
    dn2 = dh2 * gain
    dx1 = dy + r2 * (dn2 - n2 * jnp.mean(dn2 * n2, axis=1, keepdims=True))
    dx1_ref[...] = dx1
    da_ref[...] = dx1.astype(BF16)
    gp_ref[...] = nn(dhi, wprevt_ref[...]) + nn(dlo, wprevt_ref[...])
    g1_ref[...] += tn(dhi, h2) + tn(dlo, h2)
    vhi, vlo = split_hi_lo(vcoef)
    g2_ref[...] += tn(vhi, dyb) + tn(vlo, dyb)
    g3_ref[0:1, :] += jnp.sum(dh2 * n2, axis=0, keepdims=True)
    g4_ref[...] += tn(aux_ref[...], dhi) + tn(aux_ref[...], dlo)


def middle_pass(idx, mine, theirs, x1, dy, lg, aux, dlt, eye, count, gain, wcat, vt, wprevt, types, ffn, total_tokens):
    tokens, width = x1.shape
    erows = dlt.shape[0]
    block = lambda i, *_: (i, 0)
    fixed = lambda i, *_: (0, 0)
    grid_spec = pltpu.PrefetchScalarGridSpec(
        num_scalar_prefetch=1,
        grid=(tokens // TB,),
        in_specs=[
            pl.BlockSpec((TB, width // 2), block),
            pl.BlockSpec((TB, width // 2), block),
            pl.BlockSpec((TB, width), block),
            pl.BlockSpec((TB, width), block),
            pl.BlockSpec((TB, LANES), block),
            pl.BlockSpec((TB, LANES), block),
            pl.BlockSpec((erows, TB), lambda i, *_: (0, i)),
            pl.BlockSpec((erows, LANES), fixed),
            pl.BlockSpec((1, LANES), fixed),
            pl.BlockSpec((1, width), fixed),
            pl.BlockSpec((width, LANES), fixed),
            pl.BlockSpec((width, LANES), fixed),
            pl.BlockSpec((LANES, LANES), fixed),
        ],
        out_specs=[
            pl.BlockSpec((TB, width), block),
            pl.BlockSpec((TB, width), block),
            pl.BlockSpec((TB, LANES), block),
            pl.BlockSpec((LANES, width), fixed),
            pl.BlockSpec((LANES, width), fixed),
            pl.BlockSpec((8, width), fixed),
            pl.BlockSpec((LANES, LANES), fixed),
        ],
        scratch_shapes=[pltpu.VMEM((TB, width), BF16)],
    )
    return pl.pallas_call(
        functools.partial(middle_kernel, types, ffn, total_tokens),
        name="middle",
        grid_spec=grid_spec,
        out_shape=(
            jax.ShapeDtypeStruct((tokens, width), F32),
            jax.ShapeDtypeStruct((tokens, width), BF16),
            jax.ShapeDtypeStruct((tokens, LANES), F32),
            jax.ShapeDtypeStruct((LANES, width), F32),
            jax.ShapeDtypeStruct((LANES, width), F32),
            jax.ShapeDtypeStruct((8, width), F32),
            jax.ShapeDtypeStruct((LANES, LANES), F32),
        ),
        compiler_params=params(),
        cost_estimate=COST,
    )(idx, mine, theirs, x1, dy, lg, aux, dlt, eye, count, gain, wcat, vt, wprevt)


def output_kernel(types, ffn, f_ref, x1_ref, h2_ref, lg_ref, aux_ref, v_ref, out_ref):
    halves = jnp.concatenate([f_ref[0], f_ref[1]], axis=1)
    lg = lg_ref[...]
    lane, probs, mask = routing(lg, aux_ref[...], types)
    gates = probs * mask
    coef = column(gates, lane, ffn + 1)
    out = x1_ref[...] + halves.astype(F32)
    for c in range(2):
        m0, m1 = const_mix(lg, lane, types, c)
        g = column(gates, lane, ffn + 2 + c)
        coef = coef + g * m0
        out = out + (g * m1) * v_ref[c : c + 1, :]
    out_ref[...] = out + coef * h2_ref[...].astype(F32)


def output_pass(f, x1, h2, lg, aux, v, types, ffn):
    tokens, width = x1.shape
    block = lambda i: (i, 0)
    return pl.pallas_call(
        functools.partial(output_kernel, types, ffn),
        name="output",
        grid=(tokens // TB,),
        in_specs=[
            pl.BlockSpec((2, TB, width // 2), lambda i: (0, i, 0)),
            pl.BlockSpec((TB, width), block),
            pl.BlockSpec((TB, width), block),
            pl.BlockSpec((TB, LANES), block),
            pl.BlockSpec((TB, LANES), block),
            pl.BlockSpec((8, width), lambda i: (0, 0)),
        ],
        out_specs=pl.BlockSpec((TB, width), block),
        out_shape=jax.ShapeDtypeStruct((tokens, width), F32),
        compiler_params=params(),
        cost_estimate=COST,
    )(f, x1, h2, lg, aux, v)


def last_kernel(d_ref, x_ref, dx1_ref, gain_ref, out_ref):
    halves = jnp.concatenate([d_ref[0], d_ref[1]], axis=1)
    x = x_ref[...].astype(F32)
    r1 = rms_factor(x)
    n1 = x * r1
    dn1 = halves.astype(F32) * gain_ref[...]
    out_ref[...] = dx1_ref[...] + r1 * (dn1 - n1 * jnp.mean(dn1 * n1, axis=1, keepdims=True))


def last_pass(dh1, x, dx1, gain):
    tokens, width = x.shape
    block = lambda i: (i, 0)
    return pl.pallas_call(
        last_kernel,
        name="last",
        grid=(tokens // TB,),
        in_specs=[
            pl.BlockSpec((2, TB, width // 2), lambda i: (0, i, 0)),
            pl.BlockSpec((TB, width), block),
            pl.BlockSpec((TB, width), block),
            pl.BlockSpec((1, width), lambda i: (0, 0)),
        ],
        out_specs=pl.BlockSpec((TB, width), block),
        out_shape=jax.ShapeDtypeStruct((tokens, width), F32),
        compiler_params=params(),
        cost_estimate=COST,
    )(dh1, x, dx1, gain)


def tie(value, *others):
    return lax.optimization_barrier((value, *others))[0]


def add_all(own, got):
    total = own.astype(F32)
    for g in got:
        total = total + g.astype(F32)
    return total.astype(BF16)


def pair_sum(keep, send):
    return (keep.astype(F32) + swap(send, "tensor", 1).astype(F32)).astype(BF16)


def group_sum(part):
    bit = 2
    while bit < lax.axis_size("tensor"):
        got = swap(part, "tensor", bit)
        part = (part.astype(F32) + got.astype(F32)).astype(BF16)
        bit *= 2
    return part, swap(part, "tensor", 1), got


def scatter_sum(a, axes):
    steps = []
    for axis in axes:
        bits = lax.axis_size(axis).bit_length() - 1
        steps += [(axis, b) for b in reversed(range(bits))]
    a = a.reshape((2,) * len(steps) + (-1, a.shape[-1]))
    order = [s for axis in reversed(axes) for s in reversed(steps) if s[0] == axis]
    left = list(steps)
    for axis, bit in order:
        dim = left.index((axis, bit))
        mine = (lax.axis_index(axis) >> bit) & 1
        got = swap(lax.dynamic_index_in_dim(a, 1 - mine, dim, keepdims=False), axis, 1 << bit)
        a = (lax.dynamic_index_in_dim(a, mine, dim, keepdims=False).astype(F32) + got.astype(F32)).astype(BF16)
        left.remove((axis, bit))
    return a


def gather_group(a):
    out = [a]
    bit = lax.axis_size("tensor") // 2
    parts = {0: a}
    while bit:
        parts.update({m | bit: swap(p, "tensor", bit) for m, p in list(parts.items())})
        bit //= 2
    return [parts[m] for m in range(len(parts))]


def per_device(hidden_in, prev_logits, routes, block_ids, cotangent, gain_attn, w_qkv, w_out, gain_moe, w_router, w_prev, w_const, v_const, w_gate_up, w_down):
    tokens, width = hidden_in.shape
    types = w_router.shape[1]
    experts = lax.axis_size("expert")
    heads = w_out.shape[0] // HEAD_DIM
    hidden = w_down.shape[1]
    total_tokens = tokens * lax.axis_size(("dp", "expert"))
    t_index, x_index = lax.axis_index("tensor"), lax.axis_index("expert")
    t_idx = jnp.stack([t_index, t_index % 2]).astype(jnp.int32)
    x_idx = jnp.stack([x_index, t_index % 2]).astype(jnp.int32)

    wgus = [w_gate_up[0]] + [swap(w_gate_up[0], "expert", s) for s in range(1, experts)]
    wgus = [w.reshape(width, 2 * hidden) for w in wgus]
    wds = [w_down[0]] + [swap(w_down[0], "expert", s) for s in range(1, experts)]
    wos = gather_group(w_out)
    gain_first = gain_attn.astype(F32)[None]
    gain_second = gain_moe.astype(F32)[None]
    consts = w_const.transpose(1, 0, 2).reshape(width, 4)
    wcat = jnp.pad(jnp.concatenate([w_router, consts], axis=1), ((0, 0), (0, LANES - types - 4)))
    aux = jnp.concatenate([prev_logits, routes.astype(BF16)], axis=1)
    aux = jnp.pad(aux, ((0, 0), (0, LANES - types - 2)))
    wprev = jnp.pad(w_prev, ((0, LANES - types), (0, LANES - types)))
    wprevt = jnp.pad(w_prev.T, ((0, LANES - types), (0, LANES - types)))
    vt = jnp.pad(v_const.T, ((0, 0), (0, LANES - 2)))
    vrows = jnp.pad(v_const.astype(F32), ((0, 6), (0, 0)))
    erows = -(-types // 16) * 16
    eye = jnp.eye(erows, LANES, dtype=BF16)
    lanes = jnp.arange(LANES, dtype=jnp.int32)
    chosen = (routes[:, :, None] == lanes[None, None, :]).astype(F32)
    count = jnp.sum(chosen, axis=(0, 1))[None]
    bq, bk = block_ids, block_ids.reshape(tokens, 1)

    h1, qkvt, ot, lse = attention_forward(hidden_in, gain_first, w_qkv.T, bq, bk, heads)
    ots = gather_group(ot)
    x1, h2, lg, prob_part = post_attention(t_idx, hidden_in, ots, wos, gain_second, wcat, aux, wprev, types)
    keep, send, gh, du, dlt = experts_pass(x_idx, h2, cotangent, lg, aux, wgus, wds, eye, types)
    dx_part = pair_sum(keep, send)
    mine, theirs, dx_got = group_sum(dx_part)
    dlt = sum_over(tie(dlt, dx_part), ("tensor",))
    count = sum_over(tie(count, dx_part), ("expert", "dp"))

    gh, du, h2_late = tie((gh, du, h2), dx_part)
    fkeep, fsend = down_pass(x_idx, gh, wds)
    order = list(range(1, experts)) + [0]
    gu_parts, down_parts = {}, {}
    for e in order:
        gu_parts[e] = tn(h2_late, du[e]).astype(BF16)
    for e in order:
        down_parts[e] = tn(cotangent, gh[e]).astype(BF16)
    gu_got = [swap(gu_parts[e], "expert", e) for e in range(1, experts)]
    down_got = [swap(down_parts[e], "expert", e) for e in range(1, experts)]

    dx1, da, gp, g1, g2, g3, g4 = middle_pass(
        x_idx, mine, theirs, x1, cotangent, lg, aux, dlt, eye, count, gain_second, wcat, vt, wprevt, types, experts, total_tokens
    )
    gu_got = tie(gu_got, da)
    gu_total = add_all(gu_parts[0], gu_got)
    srows = -(-(types + 4) // 8) * 8
    prow = -(-types // 8) * 8
    small = jnp.concatenate(
        [
            g1[:srows],
            g2[:8],
            g3,
            jnp.pad(g4[:prow], ((0, 0), (0, width - LANES))),
            jnp.pad(prob_part, ((0, 0), (0, width - LANES))),
        ],
        axis=0,
    )
    w_halves = w_qkv.T.reshape(-1, 2, width // 2).transpose(1, 0, 2)
    dqkvt, dh1, f = attention_backward(tie(da, gu_total), w_out, qkvt, ot, lse, bq, bk, w_halves, fkeep, fsend, heads)
    small, gu_total, down_got = tie((small, gu_total, down_got), dqkvt)
    dqkvt_late, da_late = dqkvt, tie(da, dqkvt)
    grad_qkv = lax.dot_general(h1, dqkvt_late, (((0,), (1,)), ((), ())), preferred_element_type=F32)
    gain_part = jnp.sum(grad_qkv * w_qkv.astype(F32), axis=1)
    grad_qkv = scatter_sum(grad_qkv.astype(BF16), ("dp", "expert")).astype(F32)
    grad_gate_up = scatter_sum(gu_total, ("dp",)).astype(F32)
    grad_down = scatter_sum(add_all(down_parts[0], down_got), ("dp",)).astype(F32)
    grad_out = lax.dot_general(da_late, ot, (((0,), (1,)), ((), ())), preferred_element_type=F32)
    grad_out = scatter_sum(grad_out.astype(BF16), ("dp", "expert")).astype(F32).T
    small = sum_over(small, ("expert", "dp"))
    gain_part = sum_over(gain_part[None], ("expert", "dp"))
    output = output_pass(f, x1, h2, lg, aux, vrows, types, experts)
    grad_gain = sum_over(gain_part, ("tensor",))[0] / gain_first[0]
    grad_input = last_pass(dh1, hidden_in, dx1, gain_first)

    prob_all = small[srows + 16 + prow, :types]
    count_all = count[0, :types]
    balance_loss = types * jnp.sum((count_all / (2.0 * total_tokens)) * prob_all / total_tokens)
    load = jnp.stack([count_all / (2.0 * tokens), prob_all / tokens])
    return (
        output,
        grad_input,
        gp[:, :types],
        grad_gain,
        grad_qkv,
        grad_out,
        small[srows + 8],
        small[:types].T,
        small[srows + 16 : srows + 16 + types, :types],
        small[types : types + 4].reshape(2, 2, width).transpose(0, 2, 1),
        small[srows : srows + 2],
        grad_gate_up.reshape(1, -1, 2, hidden),
        grad_down.T[None],
        balance_loss,
        load,
    )


def solution(mesh):
    tok = P(("dp", "expert"), None)
    return jax.shard_map(
        per_device,
        mesh=mesh,
        in_specs=(
            tok,
            tok,
            tok,
            tok,
            tok,
            P(),
            P(None, "tensor"),
            P("tensor", None),
            P(),
            P(),
            P(),
            P(),
            P(),
            P("expert", None, None, "tensor"),
            P("expert", "tensor", None),
        ),
        out_specs=(
            tok,
            tok,
            tok,
            P(),
            P(("dp", "expert"), "tensor"),
            P("tensor", ("dp", "expert")),
            P(),
            P(),
            P(),
            P(),
            P(),
            P("expert", "dp", None, "tensor"),
            P("expert", "tensor", "dp"),
            P(),
            P(),
        ),
        check_vma=False,
    )
```

```python
import functools

import jax
import jax.numpy as jnp
from jax import lax
from jax.experimental import pallas as pl
from jax.experimental.pallas import tpu as pltpu
from jax.sharding import PartitionSpec as P

HEAD_DIM = 64
EPSILON = 1e-06
AUX_WEIGHT = 0.01
SCORE_SCALE = 0.125
MAX_BLOCK = 256
LANES = 128
QB = 256
QF = 512
TB = 256
NEG = -1e30
F32 = jnp.float32
BF16 = jnp.bfloat16
MESH = pl.DeviceIdType.MESH
VMEM_LIMIT = 48 * 1024 * 1024
COST = pl.CostEstimate(flops=1000, bytes_accessed=1000, transcendentals=0)


def params(**more):
    return pltpu.CompilerParams(vmem_limit_bytes=VMEM_LIMIT, **more)


def nn(a, b):
    return lax.dot_general(a, b, (((1,), (0,)), ((), ())), preferred_element_type=F32)


def nt(a, b):
    return lax.dot_general(a, b, (((1,), (1,)), ((), ())), preferred_element_type=F32)


def tn(a, b):
    return lax.dot_general(a, b, (((0,), (0,)), ((), ())), preferred_element_type=F32)


def split_hi_lo(a):
    hi = a.astype(BF16)
    return hi, (a - hi.astype(F32)).astype(BF16)


def rms_factor(values):
    return lax.rsqrt(jnp.mean(values * values, axis=-1, keepdims=True) + EPSILON)


def swap(a, axis, bit):
    n = lax.axis_size(axis)
    return lax.ppermute(a, axis, [(i, i ^ bit) for i in range(n)])


def sum_over(a, axes):
    for axis in axes:
        bit = 1
        while bit < lax.axis_size(axis):
            a = a + swap(a, axis, bit)
            bit *= 2
    return a


def key_range(q0, rows, tokens):
    return min(tokens, q0 + rows + MAX_BLOCK)


def attn_fwd_kernel(heads, x_ref, gain_ref, wt_ref, bq_ref, bk_ref, h1_ref, qkvt_ref, ot_ref, lse_ref, kn_ref):
    tokens = x_ref.shape[0]
    d = HEAD_DIM
    for r0 in range(0, tokens, QF):
        rows = slice(r0, r0 + QF)
        xb = x_ref[rows, :].astype(F32)
        h1 = (xb * rms_factor(xb) * gain_ref[...]).astype(BF16)
        h1_ref[rows, :] = h1
        qkvt = nt(wt_ref[...], h1)
        for h in range(heads):
            base = h * 3 * d
            q = qkvt[base : base + d].astype(BF16).astype(F32) * SCORE_SCALE
            qkvt_ref[base : base + d, rows] = q.astype(BF16)
            qkvt_ref[base + d : base + 3 * d, rows] = qkvt[base + d : base + 3 * d].astype(BF16)
            kn_ref[h, rows, :] = qkvt[base + d : base + 2 * d].T.astype(BF16)
    for h in range(heads):
        base = h * 3 * d
        for q0 in range(0, tokens, QF):
            cols = slice(q0, q0 + QF)
            top = key_range(q0, QF, tokens)
            s = nn(kn_ref[h, :top, :], qkvt_ref[base : base + d, cols])
            parts = [jnp.where(bk_ref[q0:top, :] <= bq_ref[:, cols], s[q0:], NEG)]
            if q0:
                parts = [s[:q0]] + parts
            m = functools.reduce(jnp.maximum, [jnp.max(a, axis=0, keepdims=True) for a in parts])
            ps = [jnp.exp(a - m) for a in parts]
            total = functools.reduce(jnp.add, [jnp.sum(p, axis=0, keepdims=True) for p in ps])
            p = jnp.concatenate([p.astype(BF16) for p in ps], axis=0)
            acc = nn(qkvt_ref[base + 2 * d : base + 3 * d, :top], p)
            ot_ref[h * d : (h + 1) * d, cols] = (acc / total).astype(BF16)
            lse_ref[h : h + 1, cols] = m + jnp.log(total)


def attention_forward(x, gain, w_t, bq, bk, heads):
    tokens, width = x.shape
    cols = w_t.shape[0]
    lse_rows = -(-heads // 8) * 8
    return pl.pallas_call(
        functools.partial(attn_fwd_kernel, heads),
        name="attn_fwd",
        out_shape=(
            jax.ShapeDtypeStruct((tokens, width), BF16),
            jax.ShapeDtypeStruct((cols, tokens), BF16),
            jax.ShapeDtypeStruct((heads * HEAD_DIM, tokens), BF16),
            jax.ShapeDtypeStruct((lse_rows, tokens), F32),
        ),
        scratch_shapes=[pltpu.VMEM((heads, tokens, HEAD_DIM), BF16)],
        compiler_params=params(),
        cost_estimate=COST,
    )(x, gain, w_t, bq, bk)


CHUNK = 256


def neighbours():
    t = lax.axis_index("tensor")
    return t % 2, {"tensor": t + 1 - 2 * (t % 2)}, {"tensor": (t + 2) % 4}


def greet(devices):
    barrier = pltpu.get_barrier_semaphore()
    for device in devices:
        pl.semaphore_signal(barrier, inc=1, device_id=device, device_id_type=MESH)
    pl.semaphore_wait(barrier, len(devices))


def each(count, step):
    def body(i, carry):
        step(i)
        return carry

    lax.fori_loop(0, count, body, 0)


class GroupSum:
    def __init__(self, keep, send, first, second, result, sems):
        self.keep, self.send, self.first, self.second, self.result, self.sems = keep, send, first, second, result, sems
        self.half, self.partner, self.other = neighbours()

    def rows(self, i):
        return pl.ds(pl.multiple_of(i * CHUNK, CHUNK), CHUNK)

    def copy(self, stage, i, src, dst, device):
        return pltpu.make_async_remote_copy(
            src_ref=src,
            dst_ref=dst,
            send_sem=self.sems.at[0, stage, i],
            recv_sem=self.sems.at[1, stage, i],
            device_id=device,
            device_id_type=MESH,
        )

    def to_partner(self, i):
        r = self.rows(i)
        return self.copy(0, i, self.send.at[r, :], self.first.at[r, :], self.partner)

    def to_other(self, i):
        r = self.rows(i)
        return self.copy(1, i, self.keep.at[r, :], self.second.at[r, :], self.other)

    def back(self, i):
        place = self.result.at[self.half, self.rows(i), :]
        return self.copy(2, i, place, place, self.partner)

    def pair(self, i):
        self.to_partner(i).wait_recv()
        r = self.rows(i)
        self.keep[r, :] = (self.keep[r, :].astype(F32) + self.first[r, :].astype(F32)).astype(BF16)
        self.to_other(i).start()

    def finish(self, i):
        self.to_other(i).wait_recv()
        r = self.rows(i)
        self.result[self.half, r, :] = (self.keep[r, :].astype(F32) + self.second[r, :].astype(F32)).astype(BF16)
        self.back(i).start()

    def close(self, i):
        self.back(i).wait_recv()
        self.to_partner(i).wait_send()
        self.to_other(i).wait_send()
        self.back(i).wait_send()


class SmallSum:
    def __init__(self, part, first, second, sems):
        self.part, self.first, self.second, self.sems = part, first, second, sems
        _, self.partner, self.other = neighbours()

    def copy(self, stage, i, landing, device):
        return pltpu.make_async_remote_copy(
            src_ref=self.part.at[stage, i],
            dst_ref=landing.at[i],
            send_sem=self.sems.at[0, stage, i],
            recv_sem=self.sems.at[1, stage, i],
            device_id=device,
            device_id_type=MESH,
        )

    def start(self, i):
        self.copy(0, i, self.first, self.partner).start()

    def pair(self, i):
        self.copy(0, i, self.first, self.partner).wait_recv()
        self.part[1, i] = self.part[0, i] + self.first[i]
        self.copy(1, i, self.second, self.other).start()

    def finish(self, i):
        self.copy(1, i, self.second, self.other).wait_recv()
        self.copy(0, i, self.first, self.partner).wait_send()
        self.copy(1, i, self.second, self.other).wait_send()
        return self.part[1, i] + self.second[i]


def sum_scratch(tokens, half_cols, sends=True):
    return [pltpu.VMEM((tokens, half_cols), BF16)] * (4 if sends else 3) + [pltpu.SemaphoreType.DMA((2, 3, tokens // CHUNK))]


def attn_bwd_kernel(heads, fused, da_ref, wo_ref, qkvt_ref, ot_ref, lse_ref, bq_ref, bk_ref, wq_ref, h1_ref, *refs):
    if fused:
        gu_ref, down_ref = refs[:2]
        dres_ref, gain_ref, gsum_ref, gusum_ref, dosum_ref = refs[2:7]
        scratch = refs[7:]
    else:
        dres_ref, gain_ref, gsum_ref = refs[:3]
        scratch = refs[3:]
    dqkvt_ref, dot_ref, delta_ref, kn_ref, vn_ref, dk_ref, dv_ref, dkeep, dsend, dfirst, dsecond, dsems = scratch[:12]
    tokens, width = da_ref.shape
    d = HEAD_DIM
    cols_all = dqkvt_ref.shape[0]
    chunks = tokens // CHUNK
    dh = GroupSum(dkeep, dsend, dfirst, dsecond, dres_ref, dsems)
    half, partner, other = neighbours()
    if fused:
        glocal, grecv, gsems, xg, xd, og, od, zg, zd, xsems, lsems, zsems = scratch[12:]
        hidden = xd.shape[2]
        nz = lax.axis_size("dp")
        z, x = lax.axis_index("dp"), lax.axis_index("expert")
        block = width // nz
        small = width // (2 * nz)
        across = {"expert": 1 - x}
        peers = [(k, j) for k in range(nz) for j in range(2) if k + j]
        devices = [{"dp": (z + k) % nz, "expert": (x + j) % 2} for k, j in peers]
        greet([partner, other] + devices)

        def block_rows(k):
            return pl.ds(pl.multiple_of(((z + 1 + k) % nz) * block, block), block)

        def x_copies(k):
            pairs = (
                (gu_ref.at[block_rows(k), pl.ds(2 * hidden, 2 * hidden)], xg.at[k]),
                (down_ref.at[block_rows(k), pl.ds(hidden, hidden)], xd.at[k]),
            )
            return [
                pltpu.make_async_remote_copy(
                    src_ref=src, dst_ref=dst, send_sem=xsems.at[0, n, k], recv_sem=xsems.at[1, n, k], device_id=across, device_id_type=MESH
                )
                for n, (src, dst) in enumerate(pairs)
            ]

        def local_copies(k):
            return [
                pltpu.make_async_copy(gu_ref.at[block_rows(k), pl.ds(0, 2 * hidden)], og.at[k], lsems.at[0, k]),
                pltpu.make_async_copy(down_ref.at[block_rows(k), pl.ds(0, hidden)], od.at[k], lsems.at[1, k]),
            ]

        def z_copies(k):
            return [
                pltpu.make_async_remote_copy(
                    src_ref=own.at[k],
                    dst_ref=land.at[k],
                    send_sem=zsems.at[0, n, k],
                    recv_sem=zsems.at[1, n, k],
                    device_id={"dp": (z + 1 + k) % nz},
                    device_id_type=MESH,
                )
                for n, (own, land) in enumerate(((og, zg), (od, zd)))
            ]

        def pass_on(k):
            for c in local_copies(k):
                c.wait()
            for c in x_copies(k):
                c.wait_recv()
            og[k] = (og[k].astype(F32) + xg[k].astype(F32)).astype(BF16)
            od[k] = (od[k].astype(F32) + xd[k].astype(F32)).astype(BF16)
            if k < nz - 1:
                for c in z_copies(k):
                    c.start()

        def g_copies():
            return [
                pltpu.make_async_remote_copy(
                    src_ref=glocal.at[pl.ds(pl.multiple_of((((z + k) % nz) * 2 + (x + j) % 2) * small, small), small), :],
                    dst_ref=grecv.at[n],
                    send_sem=gsems.at[0, n],
                    recv_sem=gsems.at[1, n],
                    device_id=devices[n],
                    device_id_type=MESH,
                )
                for n, (k, j) in enumerate(peers)
            ]

        for k in range(nz):
            for c in x_copies(k) + local_copies(k):
                c.start()
    else:
        glocal = gsum_ref
        greet([partner, other])

    def project(i):
        rows = pl.ds(pl.multiple_of(i * CHUNK, CHUNK), CHUNK)
        dot = nt(wo_ref[...], da_ref[rows, :]).astype(BF16)
        dot_ref[:, rows] = dot
        prod = dot.astype(F32) * ot_ref[:, rows].astype(F32)
        for h in range(heads):
            base = h * 3 * d
            delta_ref[h : h + 1, rows] = jnp.sum(prod[h * d : (h + 1) * d], axis=0, keepdims=True)
            kn_ref[h, rows, :] = qkvt_ref[base + d : base + 2 * d, rows].astype(F32).T.astype(BF16)
            vn_ref[h, rows, :] = qkvt_ref[base + 2 * d : base + 3 * d, rows].astype(F32).T.astype(BF16)

    each(chunks, project)
    dk_ref[...] = jnp.zeros_like(dk_ref)
    dv_ref[...] = jnp.zeros_like(dv_ref)

    def query_block(q0):
        def head(h):
            base = pl.multiple_of(h * 3 * d, d)
            orows = pl.ds(pl.multiple_of(h * d, d), d)
            cols = slice(q0, q0 + QB)
            top = key_range(q0, QB, tokens)
            qt = qkvt_ref[pl.ds(base, d), cols]
            dot = dot_ref[orows, cols]
            s = nn(kn_ref[h, :top, :], qt)
            p = jnp.exp(s - lse_ref[pl.ds(h, 1), cols])
            last = jnp.where(bk_ref[q0:top, :] <= bq_ref[:, cols], p[q0:], 0.0)
            p = jnp.concatenate([p[:q0], last], axis=0) if q0 else last
            dp = nn(vn_ref[h, :top, :], dot)
            ds = (p * (dp - delta_ref[pl.ds(h, 1), cols])).astype(BF16)
            dv_ref[h, :, :top] += nt(dot, p.astype(BF16))
            dk_ref[h, :, :top] += nt(qt, ds)
            dq = nn(qkvt_ref[pl.ds(base + d, d), :top], ds)
            dqkvt_ref[pl.ds(base, d), cols] = (dq * SCORE_SCALE).astype(BF16)

        each(heads, head)

    def input_grad(i):
        r = dh.rows(i)
        for h in range(heads):
            base = h * 3 * d
            dqkvt_ref[base + d : base + 2 * d, r] = dk_ref[h, :, r].astype(BF16)
            dqkvt_ref[base + 2 * d : base + 3 * d, r] = dv_ref[h, :, r].astype(BF16)
        dqkv = dqkvt_ref[:, r]
        dsend[r, :] = tn(dqkv, wq_ref[1 - half]).astype(BF16)
        dh.to_partner(i).start()
        dkeep[r, :] = tn(dqkv, wq_ref[half]).astype(BF16)
        dh.pair(i)

    for i in reversed(range(chunks)):
        query_block(i * QB)
        if i + 1 < chunks:
            input_grad(i + 1)
        if fused and i == chunks - 4:
            pass_on(0)
    input_grad(0)
    if fused:
        pass_on(1)
    gain = jnp.zeros((1, width), F32)
    for c0 in range(0, cols_all, 3 * d):
        part = nn(dqkvt_ref[c0 : c0 + 3 * d, :], h1_ref[...])
        w = jnp.concatenate([wq_ref[0, c0 : c0 + 3 * d, :], wq_ref[1, c0 : c0 + 3 * d, :]], axis=1)
        gain = gain + jnp.sum(part * w.astype(F32), axis=0, keepdims=True)
        glocal[:, c0 : c0 + 3 * d] = part.T.astype(BF16)
    gain_ref[...] = jnp.broadcast_to(gain, gain_ref.shape)
    glocal[:, cols_all:] = nn(ot_ref[...], da_ref[...]).T.astype(BF16)
    if fused:
        for c in g_copies():
            c.start()
        for k in range(2, nz):
            pass_on(k)
    each(chunks, lambda i: dh.finish(chunks - 1 - i))
    if fused:
        mine = z * 2 + x
        total = glocal[pl.ds(pl.multiple_of(mine * small, small), small), :].astype(F32)
        for n, c in enumerate(g_copies()):
            c.wait_recv()
            total = total + grecv[n].astype(F32)
        gsum_ref[...] = total
        tg, td = og[nz - 1].astype(F32), od[nz - 1].astype(F32)
        for k in range(nz - 1):
            for c in z_copies(k):
                c.wait_recv()
            tg, td = tg + zg[k].astype(F32), td + zd[k].astype(F32)
        gusum_ref[...] = tg
        dosum_ref[...] = td
        for c in g_copies():
            c.wait_send()
        for k in range(nz):
            for c in x_copies(k) + (z_copies(k) if k < nz - 1 else []):
                c.wait_send()
    each(chunks, dh.close)


def attention_backward(da, w_out, qkvt, ot, lse, bq, bk, w_halves, h1, heads, gu=None, down=None):
    tokens, width = da.shape
    cols = qkvt.shape[0]
    fused = gu is not None
    out_shape = [jax.ShapeDtypeStruct((2, tokens, width // 2), BF16), jax.ShapeDtypeStruct((8, width), F32)]
    vmem = pl.BlockSpec(memory_space=pltpu.VMEM)
    in_specs = [vmem] * 9
    operands = [da, w_out, qkvt, ot, lse, bq, bk, w_halves, h1]
    rows = w_out.shape[0]
    scratch = [
        pltpu.VMEM((cols, tokens), BF16),
        pltpu.VMEM((rows, tokens), BF16),
        pltpu.VMEM((lse.shape[0], tokens), F32),
        pltpu.VMEM((heads, tokens, HEAD_DIM), BF16),
        pltpu.VMEM((heads, tokens, HEAD_DIM), BF16),
        pltpu.VMEM((heads, HEAD_DIM, tokens), F32),
        pltpu.VMEM((heads, HEAD_DIM, tokens), F32),
    ] + sum_scratch(tokens, width // 2)
    if fused:
        nz = lax.axis_size("dp")
        hidden = down.shape[1] // 2
        block, small = width // nz, width // (2 * nz)
        others = 2 * nz - 1
        operands += [gu, down]
        in_specs += [pl.BlockSpec(memory_space=pl.ANY)] * 2
        out_shape += [
            jax.ShapeDtypeStruct((small, cols + rows), F32),
            jax.ShapeDtypeStruct((block, 2 * hidden), F32),
            jax.ShapeDtypeStruct((block, hidden), F32),
        ]
        scratch += [
            pltpu.VMEM((width, cols + rows), BF16),
            pltpu.VMEM((others, small, cols + rows), BF16),
            pltpu.SemaphoreType.DMA((2, others)),
            pltpu.VMEM((nz, block, 2 * hidden), BF16),
            pltpu.VMEM((nz, block, hidden), BF16),
            pltpu.VMEM((nz, block, 2 * hidden), BF16),
            pltpu.VMEM((nz, block, hidden), BF16),
            pltpu.VMEM((nz - 1, block, 2 * hidden), BF16),
            pltpu.VMEM((nz - 1, block, hidden), BF16),
            pltpu.SemaphoreType.DMA((2, 2, nz)),
            pltpu.SemaphoreType.DMA((2, nz)),
            pltpu.SemaphoreType.DMA((2, 2, nz)),
        ]
    else:
        out_shape += [jax.ShapeDtypeStruct((width, cols + rows), BF16)]
    return pl.pallas_call(
        functools.partial(attn_bwd_kernel, heads, fused),
        name="attn_bwd",
        in_specs=in_specs,
        out_shape=out_shape,
        scratch_shapes=scratch,
        compiler_params=params(collective_id=1, has_side_effects=True),
        cost_estimate=COST,
    )(*operands)


def lane_iota(rows):
    return lax.broadcasted_iota(jnp.int32, (rows, LANES), 1)


def column(values, lane, number):
    return jnp.sum(jnp.where(lane == number, values, 0.0), axis=1, keepdims=True)


def routing(logits, aux, types):
    lane = lane_iota(logits.shape[0])
    is_type = lane < types
    shown = jnp.where(is_type, logits, NEG)
    e = jnp.exp(shown - jnp.max(shown, axis=1, keepdims=True))
    probs = e / jnp.sum(e, axis=1, keepdims=True)
    aux = aux.astype(F32)
    first = column(aux, lane, types).astype(jnp.int32)
    second = column(aux, lane, types + 1).astype(jnp.int32)
    mask = jnp.where((lane == first) | (lane == second), 1.0, 0.0)
    return lane, probs, mask


def const_mix(logits, lane, types, c):
    l0 = column(logits, lane, types + 2 * c)
    l1 = column(logits, lane, types + 2 * c + 1)
    top = jnp.maximum(l0, l1)
    e0, e1 = jnp.exp(l0 - top), jnp.exp(l1 - top)
    total = e0 + e1
    return e0 / total, e1 / total


def post_attn_kernel(types, group, idx_ref, x_ref, *refs):
    ots, wos = refs[:group], refs[group : 2 * group]
    gain_ref, wcat_ref, aux_ref, wprev_ref = refs[2 * group : 2 * group + 4]
    x1_ref, h2_ref, lg_ref, ps_ref, wo_scr, ot_scr = refs[2 * group + 4 :]
    rows = ots[0].shape[0]
    me = idx_ref[0]

    @pl.when(pl.program_id(0) == 0)
    def _():
        for m in range(group):
            wo_scr[pl.ds(pl.multiple_of((me ^ m) * rows, HEAD_DIM), rows), :] = wos[m][...]
        ps_ref[...] = jnp.zeros_like(ps_ref)

    for m in range(group):
        ot_scr[pl.ds(pl.multiple_of((me ^ m) * rows, HEAD_DIM), rows), :] = ots[m][...]
    x1 = x_ref[...].astype(F32) + tn(ot_scr[...], wo_scr[...])
    x1_ref[...] = x1
    h2 = (x1 * rms_factor(x1) * gain_ref[...]).astype(BF16)
    h2_ref[...] = h2
    lg = nn(h2, wcat_ref[...]) + nn(aux_ref[...], wprev_ref[...])
    lg_ref[...] = lg
    _, probs, _ = routing(lg, aux_ref[...], types)
    ps_ref[0:1, :] += jnp.sum(probs, axis=0, keepdims=True)


def post_attention(me, x, ots, wos, gain, wcat, aux, wprev, types):
    tokens, width = x.shape
    rows = ots[0].shape[0]
    group = len(ots)
    block = lambda i, *_: (i, 0)
    fixed = lambda i, *_: (0, 0)
    grid_spec = pltpu.PrefetchScalarGridSpec(
        num_scalar_prefetch=1,
        grid=(tokens // TB,),
        in_specs=[pl.BlockSpec((TB, width), block)]
        + [pl.BlockSpec((rows, TB), lambda i, *_: (0, i))] * group
        + [pl.BlockSpec((rows, width), fixed)] * group
        + [
            pl.BlockSpec((1, width), fixed),
            pl.BlockSpec((width, LANES), fixed),
            pl.BlockSpec((TB, LANES), block),
            pl.BlockSpec((LANES, LANES), fixed),
        ],
        out_specs=[
            pl.BlockSpec((TB, width), block),
            pl.BlockSpec((TB, width), block),
            pl.BlockSpec((TB, LANES), block),
            pl.BlockSpec((8, LANES), fixed),
        ],
        scratch_shapes=[pltpu.VMEM((group * rows, width), BF16), pltpu.VMEM((group * rows, TB), BF16)],
    )
    return pl.pallas_call(
        functools.partial(post_attn_kernel, types, group),
        name="post_attn",
        grid_spec=grid_spec,
        out_shape=(
            jax.ShapeDtypeStruct((tokens, width), F32),
            jax.ShapeDtypeStruct((tokens, width), BF16),
            jax.ShapeDtypeStruct((tokens, LANES), F32),
            jax.ShapeDtypeStruct((8, LANES), F32),
        ),
        compiler_params=params(),
        cost_estimate=COST,
    )(me, x, *ots, *wos, gain, wcat, aux, wprev)


def expert_kernel(types, experts, halves, idx_ref, h2_ref, dy_ref, lg_ref, aux_ref, *refs):
    wgus, wds = refs[:experts], refs[experts : 2 * experts]
    eye_ref = refs[2 * experts]
    keep_ref, send_ref, gh_ref, du_ref, dlt_ref, acc_ref = refs[2 * experts + 1 :]
    me, half = idx_ref[0], idx_ref[1]
    hidden = wds[0].shape[0]
    h2, dy = h2_ref[...], dy_ref[...]
    lane, probs, mask = routing(lg_ref[...], aux_ref[...], types)
    gates = probs * mask
    dprobs = jnp.zeros_like(probs)
    for s in range(experts):
        e = me ^ s
        gate_col = column(gates, lane, e)
        u = nn(h2, wgus[s][...])
        dhr = nt(dy, wds[s][...])
        g, up = u[:, :hidden], u[:, hidden:]
        sig = 1.0 / (1.0 + jnp.exp(-g))
        silu = g * sig
        hid = silu * up
        gh_ref[s, :, :] = (hid * gate_col).astype(BF16)
        dg = jnp.sum(hid * dhr, axis=1, keepdims=True)
        dprobs = dprobs + jnp.where(lane == e, dg * mask, 0.0)
        dh = dhr * gate_col
        dgate = dh * up * sig * (1.0 + g * (1.0 - sig))
        dup = dh * silu
        du_ref[s, :, :hidden] = dgate.astype(BF16)
        du_ref[s, :, hidden:] = dup.astype(BF16)
        part = nt(du_ref[s, :, :], wgus[s][...])
        if s == 0:
            acc_ref[...] = part
        else:
            acc_ref[...] += part
    dlog = probs * (dprobs - jnp.sum(probs * dprobs, axis=1, keepdims=True))
    hi, lo = split_hi_lo(dlog)
    dlt_ref[...] = nt(eye_ref[...], hi) + nt(eye_ref[...], lo)
    half_cols = acc_ref.shape[1] // halves
    keep_ref[...] = acc_ref[:, pl.ds(pl.multiple_of(half * half_cols, LANES), half_cols)].astype(BF16)
    send_ref[...] = acc_ref[:, pl.ds(pl.multiple_of((1 - half) * half_cols, LANES), half_cols)].astype(BF16)


def experts_pass(idx, h2, dy, lg, aux, wgus, wds, eye, types):
    tokens, width = h2.shape
    experts = len(wgus)
    hidden = wds[0].shape[0]
    erows = eye.shape[0]
    block = lambda i, *_: (i, 0)
    fixed = lambda i, *_: (0, 0)
    grid_spec = pltpu.PrefetchScalarGridSpec(
        num_scalar_prefetch=1,
        grid=(tokens // TB,),
        in_specs=[
            pl.BlockSpec((TB, width), block),
            pl.BlockSpec((TB, width), block),
            pl.BlockSpec((TB, LANES), block),
            pl.BlockSpec((TB, LANES), block),
        ]
        + [pl.BlockSpec((width, 2 * hidden), fixed, pipeline_mode=pl.Buffered(1))] * experts
        + [pl.BlockSpec((hidden, width), fixed, pipeline_mode=pl.Buffered(1))] * experts
        + [pl.BlockSpec((erows, LANES), fixed)],
        out_specs=[
            pl.BlockSpec((TB, width // 2), block),
            pl.BlockSpec((TB, width // 2), block),
            pl.BlockSpec((experts, TB, hidden), lambda i, *_: (0, i, 0)),
            pl.BlockSpec((experts, TB, 2 * hidden), lambda i, *_: (0, i, 0)),
            pl.BlockSpec((erows, TB), lambda i, *_: (0, i)),
        ],
        scratch_shapes=[pltpu.VMEM((TB, width), F32)],
    )
    return pl.pallas_call(
        functools.partial(expert_kernel, types, experts, 2),
        name="experts",
        grid_spec=grid_spec,
        out_shape=(
            jax.ShapeDtypeStruct((tokens, width // 2), BF16),
            jax.ShapeDtypeStruct((tokens, width // 2), BF16),
            jax.ShapeDtypeStruct((experts, tokens, hidden), BF16),
            jax.ShapeDtypeStruct((experts, tokens, 2 * hidden), BF16),
            jax.ShapeDtypeStruct((erows, tokens), F32),
        ),
        compiler_params=params(),
        cost_estimate=COST,
    )(idx, h2, dy, lg, aux, *wgus, *wds, eye)


def down_kernel(experts, idx_ref, gh_ref, *refs):
    wds, (keep_ref, send_ref, acc_ref) = refs[:experts], refs[experts:]
    me, half = idx_ref[0], idx_ref[1]
    for s in range(experts):
        part = nn(gh_ref[s, :, :], wds[s][...])
        if s == 0:
            acc_ref[...] = part
        else:
            acc_ref[...] += part
    half_cols = keep_ref.shape[1]
    keep_ref[...] = acc_ref[:, pl.ds(pl.multiple_of(half * half_cols, LANES), half_cols)].astype(BF16)
    send_ref[...] = acc_ref[:, pl.ds(pl.multiple_of((1 - half) * half_cols, LANES), half_cols)].astype(BF16)


def down_pass(idx, gh, wds):
    experts, tokens, hidden = gh.shape
    width = wds[0].shape[1]
    block = lambda i, *_: (i, 0)
    fixed = lambda i, *_: (0, 0)
    grid_spec = pltpu.PrefetchScalarGridSpec(
        num_scalar_prefetch=1,
        grid=(tokens // TB,),
        in_specs=[pl.BlockSpec((experts, TB, hidden), lambda i, *_: (0, i, 0))]
        + [pl.BlockSpec((hidden, width), fixed, pipeline_mode=pl.Buffered(1))] * experts,
        out_specs=[pl.BlockSpec((TB, width // 2), block)] * 2,
        scratch_shapes=[pltpu.VMEM((TB, width), F32)],
    )
    return pl.pallas_call(
        functools.partial(down_kernel, experts),
        name="down",
        grid_spec=grid_spec,
        out_shape=(jax.ShapeDtypeStruct((tokens, width // 2), BF16),) * 2,
        compiler_params=params(),
        cost_estimate=COST,
    )(idx, gh, *wds)


def middle_kernel(types, ffn, total_tokens, idx_ref, mine_ref, theirs_ref, x1_ref, dy_ref, lg_ref, aux_ref, dlt_ref, eye_ref, count_ref, gain_ref, wcat_ref, vt_ref, wprevt_ref, dx1_ref, da_ref, gp_ref, g1_ref, g2_ref, g3_ref, g4_ref, scr_ref):
    half = idx_ref[1]
    half_cols = mine_ref.shape[1]
    scr_ref[:, pl.ds(pl.multiple_of(half * half_cols, LANES), half_cols)] = mine_ref[...]
    scr_ref[:, pl.ds(pl.multiple_of((1 - half) * half_cols, LANES), half_cols)] = theirs_ref[...]
    first = pl.program_id(0) == 0

    @pl.when(first)
    def _():
        for ref in (g1_ref, g2_ref, g3_ref, g4_ref):
            ref[...] = jnp.zeros_like(ref)

    gain = gain_ref[...]
    x1 = x1_ref[...]
    r2 = rms_factor(x1)
    n2 = x1 * r2
    h2 = (n2 * gain).astype(BF16)
    dyb = dy_ref[...]
    dy = dyb.astype(F32)
    lg = lg_ref[...]
    lane, probs, mask = routing(lg, aux_ref[...], types)
    gates = probs * mask
    a = jnp.sum(dy * h2.astype(F32), axis=1, keepdims=True)
    b = nn(dyb, vt_ref[...])
    coef = column(gates, lane, ffn + 1)
    dprobs = jnp.where(lane == ffn + 1, a, 0.0)
    dlc = jnp.zeros_like(probs)
    vcoef = jnp.zeros_like(probs)
    for c in range(2):
        m0, m1 = const_mix(lg, lane, types, c)
        g = column(gates, lane, ffn + 2 + c)
        bc = column(b, lane, c)
        dprobs = dprobs + jnp.where(lane == ffn + 2 + c, m0 * a + m1 * bc, 0.0)
        dm0, dm1 = g * a, g * bc
        inner = m0 * dm0 + m1 * dm1
        dlc = dlc + jnp.where(lane == types + 2 * c, m0 * (dm0 - inner), 0.0)
        dlc = dlc + jnp.where(lane == types + 2 * c + 1, m1 * (dm1 - inner), 0.0)
        coef = coef + g * m0
        vcoef = vcoef + jnp.where(lane == c, g * m1, 0.0)
    dprobs = dprobs * mask + count_ref[...] * (AUX_WEIGHT * types / (2.0 * total_tokens * total_tokens))
    dlog = probs * (dprobs - jnp.sum(probs * dprobs, axis=1, keepdims=True))
    hi, lo = split_hi_lo(dlt_ref[...])
    dl = dlog + dlc + tn(hi, eye_ref[...]) + tn(lo, eye_ref[...])
    dhi, dlo = split_hi_lo(dl)
    dh2 = scr_ref[...].astype(F32) + coef * dy + nt(dhi, wcat_ref[...]) + nt(dlo, wcat_ref[...])
    dn2 = dh2 * gain
    dx1 = dy + r2 * (dn2 - n2 * jnp.mean(dn2 * n2, axis=1, keepdims=True))
    dx1_ref[...] = dx1
    da_ref[...] = dx1.astype(BF16)
    gp_ref[...] = nn(dhi, wprevt_ref[...]) + nn(dlo, wprevt_ref[...])
    g1_ref[...] += tn(dhi, h2) + tn(dlo, h2)
    vhi, vlo = split_hi_lo(vcoef)
    g2_ref[...] += tn(vhi, dyb) + tn(vlo, dyb)
    g3_ref[0:1, :] += jnp.sum(dh2 * n2, axis=0, keepdims=True)
    g4_ref[...] += tn(aux_ref[...], dhi) + tn(aux_ref[...], dlo)


def middle_pass(idx, mine, theirs, x1, dy, lg, aux, dlt, eye, count, gain, wcat, vt, wprevt, types, ffn, total_tokens):
    tokens, width = x1.shape
    erows = dlt.shape[0]
    block = lambda i, *_: (i, 0)
    fixed = lambda i, *_: (0, 0)
    grid_spec = pltpu.PrefetchScalarGridSpec(
        num_scalar_prefetch=1,
        grid=(tokens // TB,),
        in_specs=[
            pl.BlockSpec((TB, width // 2), block),
            pl.BlockSpec((TB, width // 2), block),
            pl.BlockSpec((TB, width), block),
            pl.BlockSpec((TB, width), block),
            pl.BlockSpec((TB, LANES), block),
            pl.BlockSpec((TB, LANES), block),
            pl.BlockSpec((erows, TB), lambda i, *_: (0, i)),
            pl.BlockSpec((erows, LANES), fixed),
            pl.BlockSpec((1, LANES), fixed),
            pl.BlockSpec((1, width), fixed),
            pl.BlockSpec((width, LANES), fixed),
            pl.BlockSpec((width, LANES), fixed),
            pl.BlockSpec((LANES, LANES), fixed),
        ],
        out_specs=[
            pl.BlockSpec((TB, width), block),
            pl.BlockSpec((TB, width), block),
            pl.BlockSpec((TB, LANES), block),
            pl.BlockSpec((LANES, width), fixed),
            pl.BlockSpec((LANES, width), fixed),
            pl.BlockSpec((8, width), fixed),
            pl.BlockSpec((LANES, LANES), fixed),
        ],
        scratch_shapes=[pltpu.VMEM((TB, width), BF16)],
    )
    return pl.pallas_call(
        functools.partial(middle_kernel, types, ffn, total_tokens),
        name="middle",
        grid_spec=grid_spec,
        out_shape=(
            jax.ShapeDtypeStruct((tokens, width), F32),
            jax.ShapeDtypeStruct((tokens, width), BF16),
            jax.ShapeDtypeStruct((tokens, LANES), F32),
            jax.ShapeDtypeStruct((LANES, width), F32),
            jax.ShapeDtypeStruct((LANES, width), F32),
            jax.ShapeDtypeStruct((8, width), F32),
            jax.ShapeDtypeStruct((LANES, LANES), F32),
        ),
        compiler_params=params(),
        cost_estimate=COST,
    )(idx, mine, theirs, x1, dy, lg, aux, dlt, eye, count, gain, wcat, vt, wprevt)


def layer_kernel(types, experts, total_tokens, blocks, h2_ref, dy_ref, lg_ref, aux_ref, x1_ref, *refs):
    wgus, wds = refs[:experts], refs[experts : 2 * experts]
    eye_ref, count_ref, gain_ref, wcat_ref, vt_ref, wprevt_ref = refs[2 * experts : 2 * experts + 6]
    dx1_ref, da_ref, gp_ref, fout_ref, gu_ref, down_ref, g1_ref, g2_ref, g3_ref, g4_ref = refs[2 * experts + 6 : 2 * experts + 16]
    scratch = refs[2 * experts + 16 :]
    acc_gu, acc_down, du_ref, gh_ref, dres, fres = scratch[:6]
    dkeep, dsend, dfirst, dsecond, dsems, fkeep, fsend, ffirst, fsecond, fsems, lpart, lfirst, lsecond, lsems = scratch[6:]
    step = pl.program_id(0)
    hidden = wds[0].shape[0]
    lrows = lpart.shape[2]
    me = lax.axis_index("expert")
    half, partner, other = neighbours()
    half_cols = dkeep.shape[1]
    dx = GroupSum(dkeep, dsend, dfirst, dsecond, dres, dsems)
    ff = GroupSum(fkeep, fsend, ffirst, fsecond, fres, fsems)
    small = SmallSum(lpart, lfirst, lsecond, lsems)

    @pl.when(step == 0)
    def _():
        greet((partner, other))
        for ref in (acc_gu, acc_down, g1_ref, g2_ref, g3_ref, g4_ref):
            ref[...] = jnp.zeros_like(ref)

    def own_cols(which):
        return pl.ds(pl.multiple_of(which * half_cols, LANES), half_cols)

    @pl.when(step < blocks)
    def _():
        i = step
        h2, dy = h2_ref[...], dy_ref[...]
        lane, probs, mask = routing(lg_ref[...], aux_ref[...], types)
        gates = probs * mask
        dprobs = jnp.zeros_like(probs)
        for s in range(experts):
            e = (me + s) % experts
            gate_col = column(gates, lane, e)
            u = nn(h2, wgus[s][...])
            dhr = nt(dy, wds[s][...])
            g, up = u[:, :hidden], u[:, hidden:]
            sig = 1.0 / (1.0 + jnp.exp(-g))
            silu = g * sig
            hid = silu * up
            gh_ref[:, s * hidden : (s + 1) * hidden] = (hid * gate_col).astype(BF16)
            dg = jnp.sum(hid * dhr, axis=1, keepdims=True)
            dprobs = dprobs + jnp.where(lane == e, dg * mask, 0.0)
            dh = dhr * gate_col
            base = 2 * s * hidden
            du_ref[:, base : base + hidden] = (dh * up * sig * (1.0 + g * (1.0 - sig))).astype(BF16)
            du_ref[:, base + hidden : base + 2 * hidden] = (dh * silu).astype(BF16)
        dlog = probs * (dprobs - jnp.sum(probs * dprobs, axis=1, keepdims=True))
        hi, lo = split_hi_lo(dlog)
        lpart[0, i] = (nt(eye_ref[...], hi) + nt(eye_ref[...], lo))[:lrows]
        small.start(i)
        rows = dx.rows(i)
        for which, place in ((1 - half, dsend), (half, dkeep)):
            cols = own_cols(which)
            total = nt(du_ref[:, : 2 * hidden], wgus[0][cols, :])
            for s in range(1, experts):
                total = total + nt(du_ref[:, 2 * s * hidden : 2 * (s + 1) * hidden], wgus[s][cols, :])
            place[rows, :] = total.astype(BF16)
            if place is dsend:
                dx.to_partner(i).start()
        for which, place in ((1 - half, fsend), (half, fkeep)):
            cols = own_cols(which)
            total = nn(gh_ref[:, :hidden], wds[0][:, cols])
            for s in range(1, experts):
                total = total + nn(gh_ref[:, s * hidden : (s + 1) * hidden], wds[s][:, cols])
            place[rows, :] = total.astype(BF16)
            if place is fsend:
                ff.to_partner(i).start()
        small.pair(i)
        dx.pair(i)
        acc_gu[...] += tn(h2, du_ref[...])
        ff.pair(i)
        acc_down[...] += tn(dy, gh_ref[...])

    @pl.when(step == blocks)
    def _():
        gu_ref[...] = acc_gu[...].astype(BF16)
        down_ref[...] = acc_down[...].astype(BF16)
        dx.finish(0)

    @pl.when(step >= blocks)
    def _():
        i = step - blocks

        @pl.when(i + 1 < blocks)
        def _():
            dx.finish(i + 1)

        ff.finish(i)
        rows = dx.rows(i)
        dlt = small.finish(i)
        gain = gain_ref[...]
        x1 = x1_ref[...]
        r2 = rms_factor(x1)
        n2 = x1 * r2
        h2 = h2_ref[...]
        dyb = dy_ref[...]
        dy = dyb.astype(F32)
        lg = lg_ref[...]
        lane, probs, mask = routing(lg, aux_ref[...], types)
        gates = probs * mask
        a = jnp.sum(dy * h2.astype(F32), axis=1, keepdims=True)
        b = nn(dyb, vt_ref[...])
        coef = column(gates, lane, experts + 1)
        dprobs = jnp.where(lane == experts + 1, a, 0.0)
        dlc = jnp.zeros_like(probs)
        vcoef = jnp.zeros_like(probs)
        for c in range(2):
            m0, m1 = const_mix(lg, lane, types, c)
            g = column(gates, lane, experts + 2 + c)
            bc = column(b, lane, c)
            dprobs = dprobs + jnp.where(lane == experts + 2 + c, m0 * a + m1 * bc, 0.0)
            dm0, dm1 = g * a, g * bc
            inner = m0 * dm0 + m1 * dm1
            dlc = dlc + jnp.where(lane == types + 2 * c, m0 * (dm0 - inner), 0.0)
            dlc = dlc + jnp.where(lane == types + 2 * c + 1, m1 * (dm1 - inner), 0.0)
            coef = coef + g * m0
            vcoef = vcoef + jnp.where(lane == c, g * m1, 0.0)
        dprobs = dprobs * mask + count_ref[...] * (AUX_WEIGHT * types / (2.0 * total_tokens * total_tokens))
        dlog = probs * (dprobs - jnp.sum(probs * dprobs, axis=1, keepdims=True))
        hi, lo = split_hi_lo(dlt)
        eye = eye_ref[:lrows, :]
        dl = dlog + dlc + tn(hi, eye) + tn(lo, eye)
        dhi, dlo = split_hi_lo(dl)
        vhi, vlo = split_hi_lo(vcoef)
        gp_ref[...] = nn(dhi, wprevt_ref[...]) + nn(dlo, wprevt_ref[...])
        g1_ref[...] += tn(dhi, h2) + tn(dlo, h2)
        g2_ref[...] += tn(vhi, dyb) + tn(vlo, dyb)
        g4_ref[...] += tn(aux_ref[...], dhi) + tn(aux_ref[...], dlo)
        dh2 = coef * dy + nt(dhi, wcat_ref[...]) + nt(dlo, wcat_ref[...])
        dx.close(i)
        dh2 = dh2 + jnp.concatenate([dres[0, rows, :], dres[1, rows, :]], axis=1).astype(F32)
        g3_ref[0:1, :] += jnp.sum(dh2 * n2, axis=0, keepdims=True)
        dn2 = dh2 * gain
        dx1 = dy + r2 * (dn2 - n2 * jnp.mean(dn2 * n2, axis=1, keepdims=True))
        dx1_ref[...] = dx1
        da_ref[...] = dx1.astype(BF16)
        ff.close(i)
        fout_ref[...] = fres[:, rows, :]


def layer_pass(h2, dy, lg, aux, x1, wgus, wds, eye, count, gain, wcat, vt, wprevt, types, total_tokens):
    tokens, width = h2.shape
    experts = len(wgus)
    hidden = wds[0].shape[0]
    blocks = tokens // CHUNK
    lrows = -(-types // 8) * 8
    both = lambda i: (i % blocks, 0)
    late = lambda i: (jnp.maximum(i - blocks, 0), 0)
    fixed = lambda i: (0, 0)
    once = dict(pipeline_mode=pl.Buffered(1))
    small_sums = [
        pltpu.VMEM((2, blocks, lrows, CHUNK), F32),
        pltpu.VMEM((blocks, lrows, CHUNK), F32),
        pltpu.VMEM((blocks, lrows, CHUNK), F32),
        pltpu.SemaphoreType.DMA((2, 2, blocks)),
    ]
    return pl.pallas_call(
        functools.partial(layer_kernel, types, experts, total_tokens, blocks),
        name="layer",
        grid=(2 * blocks,),
        in_specs=[
            pl.BlockSpec((CHUNK, width), both),
            pl.BlockSpec((CHUNK, width), both),
            pl.BlockSpec((CHUNK, LANES), both),
            pl.BlockSpec((CHUNK, LANES), both),
            pl.BlockSpec((CHUNK, width), late),
        ]
        + [pl.BlockSpec((width, 2 * hidden), fixed, **once)] * experts
        + [pl.BlockSpec((hidden, width), fixed, **once)] * experts
        + [
            pl.BlockSpec(eye.shape, fixed),
            pl.BlockSpec((1, LANES), fixed),
            pl.BlockSpec((1, width), fixed),
            pl.BlockSpec((width, LANES), fixed),
            pl.BlockSpec((width, LANES), fixed),
            pl.BlockSpec((LANES, LANES), fixed),
        ],
        out_specs=[
            pl.BlockSpec((CHUNK, width), late),
            pl.BlockSpec((CHUNK, width), late),
            pl.BlockSpec((CHUNK, LANES), late),
            pl.BlockSpec((2, CHUNK, width // 2), lambda i: (0, jnp.maximum(i - blocks, 0), 0)),
            pl.BlockSpec((width, 2 * experts * hidden), fixed, **once),
            pl.BlockSpec((width, experts * hidden), fixed, **once),
            pl.BlockSpec((LANES, width), fixed),
            pl.BlockSpec((LANES, width), fixed),
            pl.BlockSpec((8, width), fixed),
            pl.BlockSpec((LANES, LANES), fixed),
        ],
        out_shape=(
            jax.ShapeDtypeStruct((tokens, width), F32),
            jax.ShapeDtypeStruct((tokens, width), BF16),
            jax.ShapeDtypeStruct((tokens, LANES), F32),
            jax.ShapeDtypeStruct((2, tokens, width // 2), BF16),
            jax.ShapeDtypeStruct((width, 2 * experts * hidden), BF16),
            jax.ShapeDtypeStruct((width, experts * hidden), BF16),
            jax.ShapeDtypeStruct((LANES, width), F32),
            jax.ShapeDtypeStruct((LANES, width), F32),
            jax.ShapeDtypeStruct((8, width), F32),
            jax.ShapeDtypeStruct((LANES, LANES), F32),
        ),
        scratch_shapes=[
            pltpu.VMEM((width, 2 * experts * hidden), F32),
            pltpu.VMEM((width, experts * hidden), F32),
            pltpu.VMEM((CHUNK, 2 * experts * hidden), BF16),
            pltpu.VMEM((CHUNK, experts * hidden), BF16),
            pltpu.VMEM((2, tokens, width // 2), BF16),
            pltpu.VMEM((2, tokens, width // 2), BF16),
        ]
        + sum_scratch(tokens, width // 2)
        + sum_scratch(tokens, width // 2)
        + small_sums,
        compiler_params=params(collective_id=2, has_side_effects=True),
        cost_estimate=COST,
    )(h2, dy, lg, aux, x1, *wgus, *wds, eye, count, gain, wcat, vt, wprevt)


def output_kernel(types, ffn, f_ref, x1_ref, h2_ref, lg_ref, aux_ref, v_ref, out_ref):
    halves = jnp.concatenate([f_ref[0], f_ref[1]], axis=1)
    lg = lg_ref[...]
    lane, probs, mask = routing(lg, aux_ref[...], types)
    gates = probs * mask
    coef = column(gates, lane, ffn + 1)
    out = x1_ref[...] + halves.astype(F32)
    for c in range(2):
        m0, m1 = const_mix(lg, lane, types, c)
        g = column(gates, lane, ffn + 2 + c)
        coef = coef + g * m0
        out = out + (g * m1) * v_ref[c : c + 1, :]
    out_ref[...] = out + coef * h2_ref[...].astype(F32)


def output_pass(f, x1, h2, lg, aux, v, types, ffn):
    tokens, width = x1.shape
    block = lambda i: (i, 0)
    return pl.pallas_call(
        functools.partial(output_kernel, types, ffn),
        name="output",
        grid=(tokens // TB,),
        in_specs=[
            pl.BlockSpec((2, TB, width // 2), lambda i: (0, i, 0)),
            pl.BlockSpec((TB, width), block),
            pl.BlockSpec((TB, width), block),
            pl.BlockSpec((TB, LANES), block),
            pl.BlockSpec((TB, LANES), block),
            pl.BlockSpec((8, width), lambda i: (0, 0)),
        ],
        out_specs=pl.BlockSpec((TB, width), block),
        out_shape=jax.ShapeDtypeStruct((tokens, width), F32),
        compiler_params=params(),
        cost_estimate=COST,
    )(f, x1, h2, lg, aux, v)


def last_kernel(d_ref, x_ref, dx1_ref, gain_ref, out_ref):
    halves = jnp.concatenate([d_ref[0], d_ref[1]], axis=1)
    x = x_ref[...].astype(F32)
    r1 = rms_factor(x)
    n1 = x * r1
    dn1 = halves.astype(F32) * gain_ref[...]
    out_ref[...] = dx1_ref[...] + r1 * (dn1 - n1 * jnp.mean(dn1 * n1, axis=1, keepdims=True))


def last_pass(dh1, x, dx1, gain):
    tokens, width = x.shape
    block = lambda i: (i, 0)
    return pl.pallas_call(
        last_kernel,
        name="last",
        grid=(tokens // TB,),
        in_specs=[
            pl.BlockSpec((2, TB, width // 2), lambda i: (0, i, 0)),
            pl.BlockSpec((TB, width), block),
            pl.BlockSpec((TB, width), block),
            pl.BlockSpec((1, width), lambda i: (0, 0)),
        ],
        out_specs=pl.BlockSpec((TB, width), block),
        out_shape=jax.ShapeDtypeStruct((tokens, width), F32),
        compiler_params=params(),
        cost_estimate=COST,
    )(dh1, x, dx1, gain)


def tie(value, *others):
    return lax.optimization_barrier((value, *others))[0]


def add_all(own, got):
    total = own.astype(F32)
    for g in got:
        total = total + g.astype(F32)
    return total.astype(BF16)


def pair_sum(keep, send):
    return (keep.astype(F32) + swap(send, "tensor", 1).astype(F32)).astype(BF16)


def group_sum(part):
    bit = 2
    while bit < lax.axis_size("tensor"):
        part = (part.astype(F32) + swap(part, "tensor", bit).astype(F32)).astype(BF16)
        bit *= 2
    return part, swap(part, "tensor", 1)


def scatter_sum(a, axes):
    steps = []
    for axis in axes:
        bits = lax.axis_size(axis).bit_length() - 1
        steps += [(axis, b) for b in reversed(range(bits))]
    a = a.reshape((2,) * len(steps) + (-1, a.shape[-1]))
    order = [s for axis in reversed(axes) for s in reversed(steps) if s[0] == axis]
    left = list(steps)
    for axis, bit in order:
        dim = left.index((axis, bit))
        mine = (lax.axis_index(axis) >> bit) & 1
        got = swap(lax.dynamic_index_in_dim(a, 1 - mine, dim, keepdims=False), axis, 1 << bit)
        a = (lax.dynamic_index_in_dim(a, mine, dim, keepdims=False).astype(F32) + got.astype(F32)).astype(BF16)
        left.remove((axis, bit))
    return a


def gather_group(a):
    out = [a]
    bit = lax.axis_size("tensor") // 2
    parts = {0: a}
    while bit:
        parts.update({m | bit: swap(p, "tensor", bit) for m, p in list(parts.items())})
        bit //= 2
    return [parts[m] for m in range(len(parts))]


def per_device(hidden_in, prev_logits, routes, block_ids, cotangent, gain_attn, w_qkv, w_out, gain_moe, w_router, w_prev, w_const, v_const, w_gate_up, w_down):
    tokens, width = hidden_in.shape
    types = w_router.shape[1]
    experts = lax.axis_size("expert")
    heads = w_out.shape[0] // HEAD_DIM
    hidden = w_down.shape[1]
    total_tokens = tokens * lax.axis_size(("dp", "expert"))
    t_index, x_index = lax.axis_index("tensor"), lax.axis_index("expert")
    t_idx = jnp.stack([t_index, t_index % 2]).astype(jnp.int32)
    x_idx = jnp.stack([x_index, t_index % 2]).astype(jnp.int32)

    wgus = [w_gate_up[0]] + [swap(w_gate_up[0], "expert", s) for s in range(1, experts)]
    wgus = [w.reshape(width, 2 * hidden) for w in wgus]
    wds = [w_down[0]] + [swap(w_down[0], "expert", s) for s in range(1, experts)]
    wos = gather_group(w_out)
    gain_first = gain_attn.astype(F32)[None]
    gain_second = gain_moe.astype(F32)[None]
    consts = w_const.transpose(1, 0, 2).reshape(width, 4)
    wcat = jnp.pad(jnp.concatenate([w_router, consts], axis=1), ((0, 0), (0, LANES - types - 4)))
    aux = jnp.concatenate([prev_logits, routes.astype(BF16)], axis=1)
    aux = jnp.pad(aux, ((0, 0), (0, LANES - types - 2)))
    wprev = jnp.pad(w_prev, ((0, LANES - types), (0, LANES - types)))
    wprevt = jnp.pad(w_prev.T, ((0, LANES - types), (0, LANES - types)))
    vt = jnp.pad(v_const.T, ((0, 0), (0, LANES - 2)))
    vrows = jnp.pad(v_const.astype(F32), ((0, 6), (0, 0)))
    erows = -(-types // 16) * 16
    eye = jnp.eye(erows, LANES, dtype=BF16)
    lanes = jnp.arange(LANES, dtype=jnp.int32)
    chosen = (routes[:, :, None] == lanes[None, None, :]).astype(F32)
    count = jnp.sum(chosen, axis=(0, 1))[None]
    bq, bk = block_ids, block_ids.reshape(tokens, 1)

    w_halves = w_qkv.T.reshape(-1, 2, width // 2).transpose(1, 0, 2)

    h1, qkvt, ot, lse = attention_forward(hidden_in, gain_first, w_qkv.T, bq, bk, heads)
    ots = gather_group(ot)
    x1, h2, lg, prob_part = post_attention(t_idx, hidden_in, ots, wos, gain_second, wcat, aux, wprev, types)
    count = sum_over(tie(count, wds[-1]), ("expert", "dp"))
    if experts == 2:
        dx1, da, gp, f, gu, down, g1, g2, g3, g4 = layer_pass(
            h2, cotangent, lg, aux, x1, wgus, wds, eye, count, gain_second, wcat, vt, wprevt, types, total_tokens
        )
        dh1, gain_part, grads, grad_gate_up, grad_down = attention_backward(
            da, w_out, qkvt, ot, lse, bq, bk, w_halves, h1, heads, gu, down
        )
    else:
        keep, send, gh, du, dlt = experts_pass(x_idx, h2, cotangent, lg, aux, wgus, wds, eye, types)
        mine, theirs = group_sum(pair_sum(keep, send))
        dlt = sum_over(dlt, ("tensor",))
        fkeep, fsend = down_pass(x_idx, gh, wds)
        gu_parts = [tn(h2, du[e]).astype(BF16) for e in range(experts)]
        down_parts = [tn(cotangent, gh[e]).astype(BF16) for e in range(experts)]
        f_mine, f_theirs = group_sum(pair_sum(fkeep, fsend))
        first, second = jnp.where(t_index % 2 == 0, f_mine, f_theirs), jnp.where(t_index % 2 == 0, f_theirs, f_mine)
        f = jnp.stack([first, second])
        dx1, da, gp, g1, g2, g3, g4 = middle_pass(
            x_idx, mine, theirs, x1, cotangent, lg, aux, dlt, eye, count, gain_second, wcat, vt, wprevt, types, experts, total_tokens
        )
        dh1, gain_part, grads = attention_backward(da, w_out, qkvt, ot, lse, bq, bk, w_halves, h1, heads)
        grads = scatter_sum(grads, ("dp", "expert")).astype(F32)
        gu_got = [swap(gu_parts[e], "expert", e) for e in range(1, experts)]
        down_got = [swap(down_parts[e], "expert", e) for e in range(1, experts)]
        grad_gate_up = scatter_sum(add_all(gu_parts[0], gu_got), ("dp",)).astype(F32)
        grad_down = scatter_sum(add_all(down_parts[0], down_got), ("dp",)).astype(F32)

    srows = -(-(types + 4) // 8) * 8
    prow = -(-types // 8) * 8
    small = jnp.concatenate(
        [
            g1[:srows],
            g2[:8],
            g3,
            jnp.pad(g4[:prow], ((0, 0), (0, width - LANES))),
            jnp.pad(prob_part, ((0, 0), (0, width - LANES))),
            gain_part,
        ],
        axis=0,
    )
    small = sum_over(small, ("expert", "dp"))
    grad_gain = sum_over(small[srows + 24 + prow :], ("tensor",))[0] / gain_first[0]
    grad_input = last_pass(dh1, hidden_in, dx1, gain_first)
    output = output_pass(f, x1, h2, lg, aux, vrows, types, experts)
    grad_qkv, grad_out = grads[:, : w_qkv.shape[1]], grads[:, w_qkv.shape[1] :].T

    prob_all = small[srows + 16 + prow, :types]
    count_all = count[0, :types]
    balance_loss = types * jnp.sum((count_all / (2.0 * total_tokens)) * prob_all / total_tokens)
    load = jnp.stack([count_all / (2.0 * tokens), prob_all / tokens])
    return (
        output,
        grad_input,
        gp[:, :types],
        grad_gain,
        grad_qkv,
        grad_out,
        small[srows + 8],
        small[:types].T,
        small[srows + 16 : srows + 16 + types, :types],
        small[types : types + 4].reshape(2, 2, width).transpose(0, 2, 1),
        small[srows : srows + 2],
        grad_gate_up.reshape(1, -1, 2, hidden),
        grad_down.T[None],
        balance_loss,
        load,
    )


def solution(mesh):
    tok = P(("dp", "expert"), None)
    return jax.shard_map(
        per_device,
        mesh=mesh,
        in_specs=(
            tok,
            tok,
            tok,
            tok,
            tok,
            P(),
            P(None, "tensor"),
            P("tensor", None),
            P(),
            P(),
            P(),
            P(),
            P(),
            P("expert", None, None, "tensor"),
            P("expert", "tensor", None),
        ),
        out_specs=(
            tok,
            tok,
            tok,
            P(),
            P(("dp", "expert"), "tensor"),
            P("tensor", ("dp", "expert")),
            P(),
            P(),
            P(),
            P(),
            P(),
            P("expert", "dp", None, "tensor"),
            P("expert", "tensor", "dp"),
            P(),
            P(),
        ),
        check_vma=False,
    )
```

```python
import functools

import jax
import jax.numpy as jnp
from jax import lax
from jax.experimental import pallas as pl
from jax.experimental.pallas import tpu as pltpu
from jax.sharding import PartitionSpec as P

HEAD_DIM = 64
EPSILON = 1e-06
AUX_WEIGHT = 0.01
SCORE_SCALE = 0.125
MAX_BLOCK = 256
LANES = 128
QB = 256
QF = 512
TB = 256
NEG = -1e30
F32 = jnp.float32
BF16 = jnp.bfloat16
MESH = pl.DeviceIdType.MESH
VMEM_LIMIT = 52 * 1024 * 1024
COST = pl.CostEstimate(flops=1000, bytes_accessed=1000, transcendentals=0)


def params(**more):
    return pltpu.CompilerParams(vmem_limit_bytes=VMEM_LIMIT, **more)


def nn(a, b):
    return lax.dot_general(a, b, (((1,), (0,)), ((), ())), preferred_element_type=F32)


def nt(a, b):
    return lax.dot_general(a, b, (((1,), (1,)), ((), ())), preferred_element_type=F32)


def tn(a, b):
    return lax.dot_general(a, b, (((0,), (0,)), ((), ())), preferred_element_type=F32)


def split_hi_lo(a):
    hi = a.astype(BF16)
    return hi, (a - hi.astype(F32)).astype(BF16)


def rms_factor(values):
    return lax.rsqrt(jnp.mean(values * values, axis=-1, keepdims=True) + EPSILON)


def swap(a, axis, bit):
    n = lax.axis_size(axis)
    return lax.ppermute(a, axis, [(i, i ^ bit) for i in range(n)])


def sum_over(a, axes):
    for axis in axes:
        bit = 1
        while bit < lax.axis_size(axis):
            a = a + swap(a, axis, bit)
            bit *= 2
    return a


def key_range(q0, rows, tokens):
    return min(tokens, q0 + rows + MAX_BLOCK)


def project_rows(r0, heads, x_ref, gain_ref, wt_ref, h1_ref, qkvt_ref, kn_ref):
    d = HEAD_DIM
    rows = slice(r0, r0 + QF)
    xb = x_ref[rows, :].astype(F32)
    h1 = (xb * rms_factor(xb) * gain_ref[...]).astype(BF16)
    h1_ref[rows, :] = h1
    qkvt = nt(wt_ref[...], h1)
    for h in range(heads):
        base = h * 3 * d
        q = qkvt[base : base + d].astype(BF16).astype(F32) * SCORE_SCALE
        qkvt_ref[base : base + d, rows] = q.astype(BF16)
        qkvt_ref[base + d : base + 3 * d, rows] = qkvt[base + d : base + 3 * d].astype(BF16)
        kn_ref[h, rows, :] = qkvt[base + d : base + 2 * d].T.astype(BF16)


def attend_rows(q0, h, bq_ref, bk_ref, qkvt_ref, kn_ref, lse_ref):
    tokens = qkvt_ref.shape[1]
    d = HEAD_DIM
    base = h * 3 * d
    cols = slice(q0, q0 + QF)
    top = key_range(q0, QF, tokens)
    s = nn(kn_ref[h, :top, :], qkvt_ref[base : base + d, cols])
    parts = [jnp.where(bk_ref[q0:top, :] <= bq_ref[:, cols], s[q0:], NEG)]
    if q0:
        parts = [s[:q0]] + parts
    m = functools.reduce(jnp.maximum, [jnp.max(a, axis=0, keepdims=True) for a in parts])
    ps = [jnp.exp(a - m) for a in parts]
    total = functools.reduce(jnp.add, [jnp.sum(p, axis=0, keepdims=True) for p in ps])
    p = jnp.concatenate([p.astype(BF16) for p in ps], axis=0)
    acc = nn(qkvt_ref[base + 2 * d : base + 3 * d, :top], p)
    lse_ref[h : h + 1, cols] = m + jnp.log(total)
    return (acc / total).astype(BF16)


def attn_fwd_kernel(heads, x_ref, gain_ref, wt_ref, bq_ref, bk_ref, h1_ref, qkvt_ref, ot_ref, lse_ref, kn_ref):
    tokens = x_ref.shape[0]
    d = HEAD_DIM
    for r0 in range(0, tokens, QF):
        project_rows(r0, heads, x_ref, gain_ref, wt_ref, h1_ref, qkvt_ref, kn_ref)
    for h in range(heads):
        for q0 in range(0, tokens, QF):
            ot_ref[h * d : (h + 1) * d, q0 : q0 + QF] = attend_rows(q0, h, bq_ref, bk_ref, qkvt_ref, kn_ref, lse_ref)


def attention_forward(x, gain, w_t, bq, bk, heads):
    tokens, width = x.shape
    cols = w_t.shape[0]
    lse_rows = -(-heads // 8) * 8
    return pl.pallas_call(
        functools.partial(attn_fwd_kernel, heads),
        name="attn_fwd",
        out_shape=(
            jax.ShapeDtypeStruct((tokens, width), BF16),
            jax.ShapeDtypeStruct((cols, tokens), BF16),
            jax.ShapeDtypeStruct((heads * HEAD_DIM, tokens), BF16),
            jax.ShapeDtypeStruct((lse_rows, tokens), F32),
        ),
        scratch_shapes=[pltpu.VMEM((heads, tokens, HEAD_DIM), BF16)],
        compiler_params=params(),
        cost_estimate=COST,
    )(x, gain, w_t, bq, bk)


CHUNK = 256


def neighbours():
    t = lax.axis_index("tensor")
    return t % 2, {"tensor": t + 1 - 2 * (t % 2)}, {"tensor": (t + 2) % 4}


def greet(devices):
    barrier = pltpu.get_barrier_semaphore()
    for device in devices:
        pl.semaphore_signal(barrier, inc=1, device_id=device, device_id_type=MESH)
    pl.semaphore_wait(barrier, len(devices))


def each(count, step):
    def body(i, carry):
        step(i)
        return carry

    lax.fori_loop(0, count, body, 0)


class GroupSum:
    def __init__(self, keep, send, first, second, result, sems):
        self.keep, self.send, self.first, self.second, self.result, self.sems = keep, send, first, second, result, sems
        self.half, self.partner, self.other = neighbours()

    def rows(self, i):
        return pl.ds(pl.multiple_of(i * CHUNK, CHUNK), CHUNK)

    def copy(self, stage, i, src, dst, device):
        return pltpu.make_async_remote_copy(
            src_ref=src,
            dst_ref=dst,
            send_sem=self.sems.at[0, stage, i],
            recv_sem=self.sems.at[1, stage, i],
            device_id=device,
            device_id_type=MESH,
        )

    def to_partner(self, i):
        r = self.rows(i)
        return self.copy(0, i, self.send.at[r, :], self.first.at[r, :], self.partner)

    def to_other(self, i):
        r = self.rows(i)
        return self.copy(1, i, self.keep.at[r, :], self.second.at[r, :], self.other)

    def back(self, i):
        place = self.result.at[self.half, self.rows(i), :]
        return self.copy(2, i, place, place, self.partner)

    def pair(self, i):
        self.to_partner(i).wait_recv()
        r = self.rows(i)
        self.keep[r, :] = (self.keep[r, :].astype(F32) + self.first[r, :].astype(F32)).astype(BF16)
        self.to_other(i).start()

    def finish(self, i):
        self.to_other(i).wait_recv()
        r = self.rows(i)
        self.result[self.half, r, :] = (self.keep[r, :].astype(F32) + self.second[r, :].astype(F32)).astype(BF16)
        self.back(i).start()

    def close(self, i):
        self.back(i).wait_recv()
        self.to_partner(i).wait_send()
        self.to_other(i).wait_send()
        self.back(i).wait_send()


class SmallSum:
    def __init__(self, part, first, second, sems):
        self.part, self.first, self.second, self.sems = part, first, second, sems
        _, self.partner, self.other = neighbours()

    def copy(self, stage, i, landing, device):
        return pltpu.make_async_remote_copy(
            src_ref=self.part.at[stage, i],
            dst_ref=landing.at[i],
            send_sem=self.sems.at[0, stage, i],
            recv_sem=self.sems.at[1, stage, i],
            device_id=device,
            device_id_type=MESH,
        )

    def start(self, i):
        self.copy(0, i, self.first, self.partner).start()

    def pair(self, i):
        self.copy(0, i, self.first, self.partner).wait_recv()
        self.part[1, i] = self.part[0, i] + self.first[i]
        self.copy(1, i, self.second, self.other).start()

    def finish(self, i):
        self.copy(1, i, self.second, self.other).wait_recv()
        self.copy(0, i, self.first, self.partner).wait_send()
        self.copy(1, i, self.second, self.other).wait_send()
        return self.part[1, i] + self.second[i]


class HopSum:
    def __init__(self, partial, landed, sems, devices):
        self.partial, self.landed, self.sems, self.devices = partial, landed, sems, devices

    def hop(self, n):
        return pltpu.make_async_remote_copy(
            src_ref=self.partial.at[n],
            dst_ref=self.landed.at[n],
            send_sem=self.sems.at[0, n],
            recv_sem=self.sems.at[1, n],
            device_id=self.devices[n],
            device_id_type=MESH,
        )

    def start(self):
        self.hop(0).start()

    def add(self, n):
        self.hop(n).wait_recv()
        total = self.partial[n] + self.landed[n]
        if n + 1 < len(self.devices):
            self.partial[n + 1] = total
            self.hop(n + 1).start()
        return total

    def close(self):
        for n in range(len(self.devices)):
            self.hop(n).wait_send()


def hop_scratch(hops, rows, width):
    return [pltpu.VMEM((hops, rows, width), F32), pltpu.VMEM((hops, rows, width), F32), pltpu.SemaphoreType.DMA((2, hops))]


def depth_place():
    z = lax.axis_index("dp")
    low, high = z % 2, z // 2
    order = [2 * (1 - high) + 1 - low, 2 * high + 1 - low, 2 * (1 - high) + low, z]
    return {"dp": z + 1 - 2 * low}, {"dp": (z + 2) % 4}, order


class DepthSum:
    def __init__(self, own, across, landed, xsems, zsems, sources, device):
        self.own, self.across, self.landed, self.xsems, self.zsems = own, across, landed, xsems, zsems
        self.sources, self.device = sources, device
        self.near, self.far, _ = depth_place()

    def x_copy(self, k):
        return pltpu.make_async_remote_copy(
            src_ref=self.sources[k],
            dst_ref=self.across.at[k],
            send_sem=self.xsems.at[0, k],
            recv_sem=self.xsems.at[1, k],
            device_id=self.device,
            device_id_type=MESH,
        )

    def z_copy(self, k):
        return pltpu.make_async_remote_copy(
            src_ref=self.own.at[k],
            dst_ref=self.landed.at[k],
            send_sem=self.zsems.at[0, k],
            recv_sem=self.zsems.at[1, k],
            device_id=self.near if k < 2 else self.far,
            device_id_type=MESH,
        )

    def pass_on(self, k):
        total = self.own[k].astype(F32)
        if self.sources[k] is not None:
            self.x_copy(k).wait_recv()
            total = total + self.across[k].astype(F32)
        for came in {2: (0,), 3: (1, 2)}.get(k, ()):
            self.z_copy(came).wait_recv()
            total = total + self.landed[came].astype(F32)
        if k < 3:
            self.own[k] = total.astype(BF16)
            self.z_copy(k).start()
        return total

    def close(self):
        for k in range(4):
            if self.sources[k] is not None:
                self.x_copy(k).wait_send()
            if k < 3:
                self.z_copy(k).wait_send()


def depth_scratch(rows, cols):
    return [
        pltpu.VMEM((4, rows, cols), BF16),
        pltpu.VMEM((4, rows, cols), BF16),
        pltpu.VMEM((3, rows, cols), BF16),
        pltpu.SemaphoreType.DMA((2, 4)),
        pltpu.SemaphoreType.DMA((2, 3)),
    ]


def sum_scratch(tokens, half_cols, sends=True):
    return [pltpu.VMEM((tokens, half_cols), BF16)] * (4 if sends else 3) + [pltpu.SemaphoreType.DMA((2, 3, tokens // CHUNK))]


def attn_bwd_kernel(heads, fused, da_ref, wo_ref, qkvt_ref, ot_ref, lse_ref, bq_ref, bk_ref, wq_ref, h1_ref, *refs):
    if fused:
        gu_ref, down_ref, small_ref = refs[:3]
        dres_ref, gain_ref, gsum_ref, gusum_ref, dosum_ref, smallsum_ref = refs[3:9]
        scratch = refs[9:]
    else:
        dres_ref, gain_ref, gsum_ref = refs[:3]
        scratch = refs[3:]
    dqkvt_ref, dot_ref, delta_ref, kn_ref, vn_ref, dk_ref, dv_ref, dkeep, dsend, dfirst, dsecond, dsems = scratch[:12]
    tokens, width = da_ref.shape
    d = HEAD_DIM
    cols_all = dqkvt_ref.shape[0]
    chunks = tokens // CHUNK
    dh = GroupSum(dkeep, dsend, dfirst, dsecond, dres_ref, dsems)
    half, partner, other = neighbours()
    if fused:
        glocal, *rest = scratch[12:]
        gparts, uparts, dparts, sparts, nparts, (lsems,) = rest[:5], rest[5:10], rest[10:15], rest[15:18], rest[18:21], rest[21:]
        hidden = dparts[0].shape[2]
        x = lax.axis_index("expert")
        near, far, order = depth_place()
        block, piece = width // 4, width // 8
        across = {"expert": 1 - x}
        greet([partner, other, across, near, far])

        def block_rows(k):
            return pl.ds(pl.multiple_of(order[k] * block, block), block)

        def pieces(k, place):
            return pl.ds(pl.multiple_of(order[k] * block + place * piece, piece), piece)

        gate_up = DepthSum(*uparts, [None] * 2 + [gu_ref.at[block_rows(k), pl.ds(2 * hidden, 2 * hidden)] for k in range(2, 4)], across)
        down = DepthSum(*dparts, [None] * 2 + [down_ref.at[block_rows(k), pl.ds(hidden, hidden)] for k in range(2, 4)], across)
        attn = DepthSum(*gparts, [glocal.at[pieces(k, 1 - x), :] for k in range(4)], across)
        small = HopSum(*sparts, [across, near, far])
        total_gain = HopSum(*nparts, [partner, across, near, far, other])

        def local_copies(k):
            return [
                pltpu.make_async_copy(gu_ref.at[block_rows(k), pl.ds(0, 2 * hidden)], gate_up.own.at[k], lsems.at[0, k]),
                pltpu.make_async_copy(down_ref.at[block_rows(k), pl.ds(0, hidden)], down.own.at[k], lsems.at[1, k]),
            ]

        def pass_on(k):
            for c in local_copies(k):
                c.wait()
            return gate_up.pass_on(k), down.pass_on(k)

        small.partial[0] = small_ref[...]
        small.start()
        for k in range(4):
            for c in local_copies(k):
                c.start()
            if k >= 2:
                gate_up.x_copy(k).start()
                down.x_copy(k).start()
    else:
        glocal = gsum_ref
        greet([partner, other])

    def project(i):
        rows = pl.ds(pl.multiple_of(i * CHUNK, CHUNK), CHUNK)
        dot = nt(wo_ref[...], da_ref[rows, :]).astype(BF16)
        dot_ref[:, rows] = dot
        prod = dot.astype(F32) * ot_ref[:, rows].astype(F32)
        for h in range(heads):
            base = h * 3 * d
            delta_ref[h : h + 1, rows] = jnp.sum(prod[h * d : (h + 1) * d], axis=0, keepdims=True)
            kn_ref[h, rows, :] = qkvt_ref[base + d : base + 2 * d, rows].astype(F32).T.astype(BF16)
            vn_ref[h, rows, :] = qkvt_ref[base + 2 * d : base + 3 * d, rows].astype(F32).T.astype(BF16)

    each(chunks, project)
    dk_ref[...] = jnp.zeros_like(dk_ref)
    dv_ref[...] = jnp.zeros_like(dv_ref)

    def query_block(q0):
        def head(h):
            base = pl.multiple_of(h * 3 * d, d)
            orows = pl.ds(pl.multiple_of(h * d, d), d)
            cols = slice(q0, q0 + QB)
            top = key_range(q0, QB, tokens)
            qt = qkvt_ref[pl.ds(base, d), cols]
            dot = dot_ref[orows, cols]
            s = nn(kn_ref[h, :top, :], qt)
            p = jnp.exp(s - lse_ref[pl.ds(h, 1), cols])
            last = jnp.where(bk_ref[q0:top, :] <= bq_ref[:, cols], p[q0:], 0.0)
            p = jnp.concatenate([p[:q0], last], axis=0) if q0 else last
            dp = nn(vn_ref[h, :top, :], dot)
            ds = (p * (dp - delta_ref[pl.ds(h, 1), cols])).astype(BF16)
            dv_ref[h, :, :top] += nt(dot, p.astype(BF16))
            dk_ref[h, :, :top] += nt(qt, ds)
            dq = nn(qkvt_ref[pl.ds(base + d, d), :top], ds)
            dqkvt_ref[pl.ds(base, d), cols] = (dq * SCORE_SCALE).astype(BF16)

        each(heads, head)

    def input_grad(i):
        r = dh.rows(i)
        for h in range(heads):
            base = h * 3 * d
            dqkvt_ref[base + d : base + 2 * d, r] = dk_ref[h, :, r].astype(BF16)
            dqkvt_ref[base + 2 * d : base + 3 * d, r] = dv_ref[h, :, r].astype(BF16)
        dqkv = dqkvt_ref[:, r]
        dsend[r, :] = tn(dqkv, wq_ref[1 - half]).astype(BF16)
        dh.to_partner(i).start()
        dkeep[r, :] = tn(dqkv, wq_ref[half]).astype(BF16)
        dh.pair(i)

    if fused:
        pass_on(0)
        pass_on(1)
        small.add(0)
    for i in reversed(range(chunks)):
        query_block(i * QB)
        if i + 1 < chunks:
            input_grad(i + 1)
        if fused and i == chunks - 3:
            small.add(1)
            pass_on(2)
        if fused and i == 1:
            smallsum_ref[...] = small.add(2)
    input_grad(0)
    gain = jnp.zeros((1, width), F32)
    for c0 in range(0, cols_all, 3 * d):
        part = nn(dqkvt_ref[c0 : c0 + 3 * d, :], h1_ref[...])
        w = jnp.concatenate([wq_ref[0, c0 : c0 + 3 * d, :], wq_ref[1, c0 : c0 + 3 * d, :]], axis=1)
        gain = gain + jnp.sum(part * w.astype(F32), axis=0, keepdims=True)
        glocal[:, c0 : c0 + 3 * d] = part.T.astype(BF16)
    gain = jnp.broadcast_to(gain, gain_ref.shape)
    glocal[:, cols_all:] = nn(ot_ref[...], da_ref[...]).T.astype(BF16)
    if fused:
        total_gain.partial[0] = gain
        total_gain.start()
        for k in range(4):
            attn.x_copy(k).start()
            attn.own[k] = glocal[pieces(k, x), :]
        total_gain.add(0)
        each(4, lambda i: dh.finish(chunks - 1 - i))
        attn.pass_on(0)
        attn.pass_on(1)
        total_gain.add(1)
        each(2, lambda i: dh.finish(chunks - 5 - i))
        total_gain.add(2)
        gusum_ref[...], dosum_ref[...] = pass_on(3)
        attn.pass_on(2)
        total_gain.add(3)
        each(chunks - 6, lambda i: dh.finish(chunks - 7 - i))
        gsum_ref[...] = attn.pass_on(3)
        gain_ref[...] = total_gain.add(4)
        for part in (gate_up, down, attn, small, total_gain):
            part.close()
    else:
        gain_ref[...] = gain
        each(chunks, lambda i: dh.finish(chunks - 1 - i))
    each(chunks, dh.close)


def attention_backward(da, w_out, qkvt, ot, lse, bq, bk, w_halves, h1, heads, gu=None, down=None, small=None):
    tokens, width = da.shape
    cols = qkvt.shape[0]
    fused = gu is not None
    out_shape = [jax.ShapeDtypeStruct((2, tokens, width // 2), BF16), jax.ShapeDtypeStruct((8, width), F32)]
    vmem = pl.BlockSpec(memory_space=pltpu.VMEM)
    in_specs = [vmem] * 9
    operands = [da, w_out, qkvt, ot, lse, bq, bk, w_halves, h1]
    rows = w_out.shape[0]
    scratch = [
        pltpu.VMEM((cols, tokens), BF16),
        pltpu.VMEM((rows, tokens), BF16),
        pltpu.VMEM((lse.shape[0], tokens), F32),
        pltpu.VMEM((heads, tokens, HEAD_DIM), BF16),
        pltpu.VMEM((heads, tokens, HEAD_DIM), BF16),
        pltpu.VMEM((heads, HEAD_DIM, tokens), F32),
        pltpu.VMEM((heads, HEAD_DIM, tokens), F32),
    ] + sum_scratch(tokens, width // 2)
    if fused:
        hidden = down.shape[1] // 2
        operands += [gu, down, small]
        in_specs += [pl.BlockSpec(memory_space=pl.ANY)] * 2 + [vmem]
        out_shape += [
            jax.ShapeDtypeStruct((width // 8, cols + rows), F32),
            jax.ShapeDtypeStruct((width // 4, 2 * hidden), F32),
            jax.ShapeDtypeStruct((width // 4, hidden), F32),
            jax.ShapeDtypeStruct(small.shape, F32),
        ]
        scratch += [pltpu.VMEM((width, cols + rows), BF16)]
        scratch += depth_scratch(width // 8, cols + rows)
        scratch += depth_scratch(width // 4, 2 * hidden) + depth_scratch(width // 4, hidden)
        scratch += hop_scratch(3, small.shape[0], width) + hop_scratch(5, 8, width)
        scratch += [pltpu.SemaphoreType.DMA((2, 4))]
    else:
        out_shape += [jax.ShapeDtypeStruct((width, cols + rows), BF16)]
    return pl.pallas_call(
        functools.partial(attn_bwd_kernel, heads, fused),
        name="attn_bwd",
        in_specs=in_specs,
        out_shape=out_shape,
        scratch_shapes=scratch,
        compiler_params=params(collective_id=1, has_side_effects=True),
        cost_estimate=COST,
    )(*operands)


def lane_iota(rows):
    return lax.broadcasted_iota(jnp.int32, (rows, LANES), 1)


def column(values, lane, number):
    return jnp.sum(jnp.where(lane == number, values, 0.0), axis=1, keepdims=True)


def routing(logits, aux, types):
    lane = lane_iota(logits.shape[0])
    is_type = lane < types
    shown = jnp.where(is_type, logits, NEG)
    e = jnp.exp(shown - jnp.max(shown, axis=1, keepdims=True))
    probs = e / jnp.sum(e, axis=1, keepdims=True)
    aux = aux.astype(F32)
    first = column(aux, lane, types).astype(jnp.int32)
    second = column(aux, lane, types + 1).astype(jnp.int32)
    mask = jnp.where((lane == first) | (lane == second), 1.0, 0.0)
    return lane, probs, mask


def const_mix(logits, lane, types, c):
    l0 = column(logits, lane, types + 2 * c)
    l1 = column(logits, lane, types + 2 * c + 1)
    top = jnp.maximum(l0, l1)
    e0, e1 = jnp.exp(l0 - top), jnp.exp(l1 - top)
    total = e0 + e1
    return e0 / total, e1 / total


def post_attn_kernel(types, group, idx_ref, x_ref, *refs):
    ots, wos = refs[:group], refs[group : 2 * group]
    gain_ref, wcat_ref, aux_ref, wprev_ref = refs[2 * group : 2 * group + 4]
    x1_ref, h2_ref, lg_ref, ps_ref, wo_scr, ot_scr = refs[2 * group + 4 :]
    rows = ots[0].shape[0]
    me = idx_ref[0]

    @pl.when(pl.program_id(0) == 0)
    def _():
        for m in range(group):
            wo_scr[pl.ds(pl.multiple_of((me ^ m) * rows, HEAD_DIM), rows), :] = wos[m][...]
        ps_ref[...] = jnp.zeros_like(ps_ref)

    for m in range(group):
        ot_scr[pl.ds(pl.multiple_of((me ^ m) * rows, HEAD_DIM), rows), :] = ots[m][...]
    x1 = x_ref[...].astype(F32) + tn(ot_scr[...], wo_scr[...])
    x1_ref[...] = x1
    h2 = (x1 * rms_factor(x1) * gain_ref[...]).astype(BF16)
    h2_ref[...] = h2
    lg = nn(h2, wcat_ref[...]) + nn(aux_ref[...], wprev_ref[...])
    lg_ref[...] = lg
    _, probs, _ = routing(lg, aux_ref[...], types)
    ps_ref[0:1, :] += jnp.sum(probs, axis=0, keepdims=True)


def post_attention(me, x, ots, wos, gain, wcat, aux, wprev, types):
    tokens, width = x.shape
    rows = ots[0].shape[0]
    group = len(ots)
    block = lambda i, *_: (i, 0)
    fixed = lambda i, *_: (0, 0)
    grid_spec = pltpu.PrefetchScalarGridSpec(
        num_scalar_prefetch=1,
        grid=(tokens // TB,),
        in_specs=[pl.BlockSpec((TB, width), block)]
        + [pl.BlockSpec((rows, TB), lambda i, *_: (0, i))] * group
        + [pl.BlockSpec((rows, width), fixed)] * group
        + [
            pl.BlockSpec((1, width), fixed),
            pl.BlockSpec((width, LANES), fixed),
            pl.BlockSpec((TB, LANES), block),
            pl.BlockSpec((LANES, LANES), fixed),
        ],
        out_specs=[
            pl.BlockSpec((TB, width), block),
            pl.BlockSpec((TB, width), block),
            pl.BlockSpec((TB, LANES), block),
            pl.BlockSpec((8, LANES), fixed),
        ],
        scratch_shapes=[pltpu.VMEM((group * rows, width), BF16), pltpu.VMEM((group * rows, TB), BF16)],
    )
    return pl.pallas_call(
        functools.partial(post_attn_kernel, types, group),
        name="post_attn",
        grid_spec=grid_spec,
        out_shape=(
            jax.ShapeDtypeStruct((tokens, width), F32),
            jax.ShapeDtypeStruct((tokens, width), BF16),
            jax.ShapeDtypeStruct((tokens, LANES), F32),
            jax.ShapeDtypeStruct((8, LANES), F32),
        ),
        compiler_params=params(),
        cost_estimate=COST,
    )(me, x, *ots, *wos, gain, wcat, aux, wprev)


def front_kernel(heads, types, x_ref, gain_ref, wt_ref, bq_ref, bk_ref, wo_ref, gain2_ref, wcat_ref, aux_ref, wprev_ref, part_ref, wgu_ref, wd_ref, h1_ref, qkvt_ref, ot_ref, lse_ref, x1_ref, h2_ref, lg_ref, ps_ref, count_ref, pgu_ref, pd_ref, *scratch):
    kn_ref, oall, wall, osems, wsems, esems, *counts = scratch
    tokens, width = x_ref.shape
    rows = ot_ref.shape[0]
    d = HEAD_DIM
    t = lax.axis_index("tensor")
    half, partner, other = neighbours()
    near, far, _ = depth_place()
    across = {"expert": 1 - lax.axis_index("expert")}
    low = lax.axis_index("dp") % 2
    greet([partner, other, across, near, far])
    count = HopSum(*counts, [across, near, far])
    count.partial[0] = part_ref[...]
    count.start()

    mine = pl.ds(pl.multiple_of(t * rows, d), rows)
    others = pl.ds(pl.multiple_of(((t + 2) % 4) * rows, d), rows)

    def spread(ref, cols, sems, n):
        return [
            pltpu.make_async_remote_copy(
                src_ref=ref.at[place, cols],
                dst_ref=ref.at[place, cols],
                send_sem=sems.at[0, stage, n],
                recv_sem=sems.at[1, stage, n],
                device_id=device,
                device_id_type=MESH,
            )
            for stage, (place, device) in enumerate(((mine, partner), (mine, other), (others, partner)))
        ]

    pieces = []
    for ref, land in ((wgu_ref, pgu_ref), (wd_ref, pd_ref)):
        step = ref.shape[0] // 4
        for n in range(2):
            pieces.append((ref, land, pl.ds(pl.multiple_of((2 * low + n) * step, step), step)))

    def weight_copy(n, stage):
        ref, land, place = pieces[n]
        return pltpu.make_async_remote_copy(
            src_ref=(land if stage else ref).at[place, :],
            dst_ref=land.at[place, :],
            send_sem=esems.at[0, stage, n],
            recv_sem=esems.at[1, stage, n],
            device_id=near if stage else across,
            device_id_type=MESH,
        )

    def weight_on(n):
        weight_copy(n, 0).wait_recv()
        weight_copy(n, 1).start()

    for n in range(4):
        weight_copy(n, 0).start()
    wall[mine, :] = wo_ref[...]
    every = slice(None)
    for c in spread(wall, every, wsems, 0)[:2]:
        c.start()

    for r0 in range(0, tokens, QF):
        project_rows(r0, heads, x_ref, gain_ref, wt_ref, h1_ref, qkvt_ref, kn_ref)
    count.add(0)
    ps_ref[...] = jnp.zeros_like(ps_ref)

    def block_cols(n):
        return slice(n * QF, (n + 1) * QF)

    def attend(n):
        o = jnp.concatenate([attend_rows(n * QF, h, bq_ref, bk_ref, qkvt_ref, kn_ref, lse_ref) for h in range(heads)], axis=0)
        ot_ref[:, block_cols(n)] = o
        oall[mine, block_cols(n)] = o
        for c in spread(oall, block_cols(n), osems, n)[:2]:
            c.start()

    def onward(ref, cols, sems, n):
        copies = spread(ref, cols, sems, n)
        copies[1].wait_recv()
        copies[2].start()

    def post(n):
        copies = spread(oall, block_cols(n), osems, n)
        copies[0].wait_recv()
        copies[2].wait_recv()
        for r0 in range(n * QF, (n + 1) * QF, TB):
            r = slice(r0, r0 + TB)
            x1 = x_ref[r, :].astype(F32) + tn(oall[:, r], wall[...])
            x1_ref[r, :] = x1
            h2 = (x1 * rms_factor(x1) * gain2_ref[...]).astype(BF16)
            h2_ref[r, :] = h2
            lg = nn(h2, wcat_ref[...]) + nn(aux_ref[r, :], wprev_ref[...])
            lg_ref[r, :] = lg
            _, probs, _ = routing(lg, aux_ref[r, :], types)
            ps_ref[0:1, :] += jnp.sum(probs, axis=0, keepdims=True)

    blocks = tokens // QF
    for n in range(blocks):
        attend(n)
        if n == 0:
            onward(wall, every, wsems, 0)
            count.add(1)
        if n == 1:
            weight_on(0)
            count_ref[...] = count.add(2)
        if n == 2:
            copies = spread(wall, every, wsems, 0)
            copies[0].wait_recv()
            copies[2].wait_recv()
            weight_on(1)
        if n >= 1:
            onward(oall, block_cols(n - 1), osems, n - 1)
        if n >= 2:
            post(n - 2)
    onward(oall, block_cols(blocks - 1), osems, blocks - 1)
    weight_on(2)
    post(blocks - 2)
    weight_on(3)
    post(blocks - 1)
    for n in range(4):
        weight_copy(n, 1).wait_recv()
        for stage in range(2):
            weight_copy(n, stage).wait_send()
    for c in spread(wall, every, wsems, 0):
        c.wait_send()
    for n in range(blocks):
        for c in spread(oall, block_cols(n), osems, n):
            c.wait_send()
    count.close()


def front_pass(x, gain, w_t, bq, bk, w_out, gain2, wcat, aux, wprev, part, wgu, wd, heads, types):
    tokens, width = x.shape
    cols, rows = w_t.shape[0], w_out.shape[0]
    lse_rows = -(-heads // 8) * 8
    blocks = tokens // QF
    vmem = pl.BlockSpec(memory_space=pltpu.VMEM)
    anywhere = pl.BlockSpec(memory_space=pl.ANY)
    return pl.pallas_call(
        functools.partial(front_kernel, heads, types),
        name="front",
        in_specs=[vmem] * 11 + [anywhere] * 2,
        out_specs=[vmem] * 9 + [anywhere] * 2,
        out_shape=(
            jax.ShapeDtypeStruct((tokens, width), BF16),
            jax.ShapeDtypeStruct((cols, tokens), BF16),
            jax.ShapeDtypeStruct((rows, tokens), BF16),
            jax.ShapeDtypeStruct((lse_rows, tokens), F32),
            jax.ShapeDtypeStruct((tokens, width), F32),
            jax.ShapeDtypeStruct((tokens, width), BF16),
            jax.ShapeDtypeStruct((tokens, LANES), F32),
            jax.ShapeDtypeStruct((8, LANES), F32),
            jax.ShapeDtypeStruct(part.shape, F32),
            jax.ShapeDtypeStruct(wgu.shape, BF16),
            jax.ShapeDtypeStruct(wd.shape, BF16),
        ),
        scratch_shapes=[
            pltpu.VMEM((heads, tokens, HEAD_DIM), BF16),
            pltpu.VMEM((4 * rows, tokens), BF16),
            pltpu.VMEM((4 * rows, width), BF16),
            pltpu.SemaphoreType.DMA((2, 3, blocks)),
            pltpu.SemaphoreType.DMA((2, 3, 1)),
            pltpu.SemaphoreType.DMA((2, 2, 4)),
        ]
        + hop_scratch(3, *part.shape),
        compiler_params=params(collective_id=3, has_side_effects=True),
        cost_estimate=COST,
    )(x, gain, w_t, bq, bk, w_out, gain2, wcat, aux, wprev, part, wgu, wd)


def expert_kernel(types, experts, halves, idx_ref, h2_ref, dy_ref, lg_ref, aux_ref, *refs):
    wgus, wds = refs[:experts], refs[experts : 2 * experts]
    eye_ref = refs[2 * experts]
    keep_ref, send_ref, gh_ref, du_ref, dlt_ref, acc_ref = refs[2 * experts + 1 :]
    me, half = idx_ref[0], idx_ref[1]
    hidden = wds[0].shape[0]
    h2, dy = h2_ref[...], dy_ref[...]
    lane, probs, mask = routing(lg_ref[...], aux_ref[...], types)
    gates = probs * mask
    dprobs = jnp.zeros_like(probs)
    for s in range(experts):
        e = me ^ s
        gate_col = column(gates, lane, e)
        u = nn(h2, wgus[s][...])
        dhr = nt(dy, wds[s][...])
        g, up = u[:, :hidden], u[:, hidden:]
        sig = 1.0 / (1.0 + jnp.exp(-g))
        silu = g * sig
        hid = silu * up
        gh_ref[s, :, :] = (hid * gate_col).astype(BF16)
        dg = jnp.sum(hid * dhr, axis=1, keepdims=True)
        dprobs = dprobs + jnp.where(lane == e, dg * mask, 0.0)
        dh = dhr * gate_col
        dgate = dh * up * sig * (1.0 + g * (1.0 - sig))
        dup = dh * silu
        du_ref[s, :, :hidden] = dgate.astype(BF16)
        du_ref[s, :, hidden:] = dup.astype(BF16)
        part = nt(du_ref[s, :, :], wgus[s][...])
        if s == 0:
            acc_ref[...] = part
        else:
            acc_ref[...] += part
    dlog = probs * (dprobs - jnp.sum(probs * dprobs, axis=1, keepdims=True))
    hi, lo = split_hi_lo(dlog)
    dlt_ref[...] = nt(eye_ref[...], hi) + nt(eye_ref[...], lo)
    half_cols = acc_ref.shape[1] // halves
    keep_ref[...] = acc_ref[:, pl.ds(pl.multiple_of(half * half_cols, LANES), half_cols)].astype(BF16)
    send_ref[...] = acc_ref[:, pl.ds(pl.multiple_of((1 - half) * half_cols, LANES), half_cols)].astype(BF16)


def experts_pass(idx, h2, dy, lg, aux, wgus, wds, eye, types):
    tokens, width = h2.shape
    experts = len(wgus)
    hidden = wds[0].shape[0]
    erows = eye.shape[0]
    block = lambda i, *_: (i, 0)
    fixed = lambda i, *_: (0, 0)
    grid_spec = pltpu.PrefetchScalarGridSpec(
        num_scalar_prefetch=1,
        grid=(tokens // TB,),
        in_specs=[
            pl.BlockSpec((TB, width), block),
            pl.BlockSpec((TB, width), block),
            pl.BlockSpec((TB, LANES), block),
            pl.BlockSpec((TB, LANES), block),
        ]
        + [pl.BlockSpec((width, 2 * hidden), fixed, pipeline_mode=pl.Buffered(1))] * experts
        + [pl.BlockSpec((hidden, width), fixed, pipeline_mode=pl.Buffered(1))] * experts
        + [pl.BlockSpec((erows, LANES), fixed)],
        out_specs=[
            pl.BlockSpec((TB, width // 2), block),
            pl.BlockSpec((TB, width // 2), block),
            pl.BlockSpec((experts, TB, hidden), lambda i, *_: (0, i, 0)),
            pl.BlockSpec((experts, TB, 2 * hidden), lambda i, *_: (0, i, 0)),
            pl.BlockSpec((erows, TB), lambda i, *_: (0, i)),
        ],
        scratch_shapes=[pltpu.VMEM((TB, width), F32)],
    )
    return pl.pallas_call(
        functools.partial(expert_kernel, types, experts, 2),
        name="experts",
        grid_spec=grid_spec,
        out_shape=(
            jax.ShapeDtypeStruct((tokens, width // 2), BF16),
            jax.ShapeDtypeStruct((tokens, width // 2), BF16),
            jax.ShapeDtypeStruct((experts, tokens, hidden), BF16),
            jax.ShapeDtypeStruct((experts, tokens, 2 * hidden), BF16),
            jax.ShapeDtypeStruct((erows, tokens), F32),
        ),
        compiler_params=params(),
        cost_estimate=COST,
    )(idx, h2, dy, lg, aux, *wgus, *wds, eye)


def down_kernel(experts, idx_ref, gh_ref, *refs):
    wds, (keep_ref, send_ref, acc_ref) = refs[:experts], refs[experts:]
    me, half = idx_ref[0], idx_ref[1]
    for s in range(experts):
        part = nn(gh_ref[s, :, :], wds[s][...])
        if s == 0:
            acc_ref[...] = part
        else:
            acc_ref[...] += part
    half_cols = keep_ref.shape[1]
    keep_ref[...] = acc_ref[:, pl.ds(pl.multiple_of(half * half_cols, LANES), half_cols)].astype(BF16)
    send_ref[...] = acc_ref[:, pl.ds(pl.multiple_of((1 - half) * half_cols, LANES), half_cols)].astype(BF16)


def down_pass(idx, gh, wds):
    experts, tokens, hidden = gh.shape
    width = wds[0].shape[1]
    block = lambda i, *_: (i, 0)
    fixed = lambda i, *_: (0, 0)
    grid_spec = pltpu.PrefetchScalarGridSpec(
        num_scalar_prefetch=1,
        grid=(tokens // TB,),
        in_specs=[pl.BlockSpec((experts, TB, hidden), lambda i, *_: (0, i, 0))]
        + [pl.BlockSpec((hidden, width), fixed, pipeline_mode=pl.Buffered(1))] * experts,
        out_specs=[pl.BlockSpec((TB, width // 2), block)] * 2,
        scratch_shapes=[pltpu.VMEM((TB, width), F32)],
    )
    return pl.pallas_call(
        functools.partial(down_kernel, experts),
        name="down",
        grid_spec=grid_spec,
        out_shape=(jax.ShapeDtypeStruct((tokens, width // 2), BF16),) * 2,
        compiler_params=params(),
        cost_estimate=COST,
    )(idx, gh, *wds)


def middle_kernel(types, ffn, total_tokens, idx_ref, mine_ref, theirs_ref, x1_ref, dy_ref, lg_ref, aux_ref, dlt_ref, eye_ref, count_ref, gain_ref, wcat_ref, vt_ref, wprevt_ref, dx1_ref, da_ref, gp_ref, g1_ref, g2_ref, g3_ref, g4_ref, scr_ref):
    half = idx_ref[1]
    half_cols = mine_ref.shape[1]
    scr_ref[:, pl.ds(pl.multiple_of(half * half_cols, LANES), half_cols)] = mine_ref[...]
    scr_ref[:, pl.ds(pl.multiple_of((1 - half) * half_cols, LANES), half_cols)] = theirs_ref[...]
    first = pl.program_id(0) == 0

    @pl.when(first)
    def _():
        for ref in (g1_ref, g2_ref, g3_ref, g4_ref):
            ref[...] = jnp.zeros_like(ref)

    gain = gain_ref[...]
    x1 = x1_ref[...]
    r2 = rms_factor(x1)
    n2 = x1 * r2
    h2 = (n2 * gain).astype(BF16)
    dyb = dy_ref[...]
    dy = dyb.astype(F32)
    lg = lg_ref[...]
    lane, probs, mask = routing(lg, aux_ref[...], types)
    gates = probs * mask
    a = jnp.sum(dy * h2.astype(F32), axis=1, keepdims=True)
    b = nn(dyb, vt_ref[...])
    coef = column(gates, lane, ffn + 1)
    dprobs = jnp.where(lane == ffn + 1, a, 0.0)
    dlc = jnp.zeros_like(probs)
    vcoef = jnp.zeros_like(probs)
    for c in range(2):
        m0, m1 = const_mix(lg, lane, types, c)
        g = column(gates, lane, ffn + 2 + c)
        bc = column(b, lane, c)
        dprobs = dprobs + jnp.where(lane == ffn + 2 + c, m0 * a + m1 * bc, 0.0)
        dm0, dm1 = g * a, g * bc
        inner = m0 * dm0 + m1 * dm1
        dlc = dlc + jnp.where(lane == types + 2 * c, m0 * (dm0 - inner), 0.0)
        dlc = dlc + jnp.where(lane == types + 2 * c + 1, m1 * (dm1 - inner), 0.0)
        coef = coef + g * m0
        vcoef = vcoef + jnp.where(lane == c, g * m1, 0.0)
    dprobs = dprobs * mask + count_ref[...] * (AUX_WEIGHT * types / (2.0 * total_tokens * total_tokens))
    dlog = probs * (dprobs - jnp.sum(probs * dprobs, axis=1, keepdims=True))
    hi, lo = split_hi_lo(dlt_ref[...])
    dl = dlog + dlc + tn(hi, eye_ref[...]) + tn(lo, eye_ref[...])
    dhi, dlo = split_hi_lo(dl)
    dh2 = scr_ref[...].astype(F32) + coef * dy + nt(dhi, wcat_ref[...]) + nt(dlo, wcat_ref[...])
    dn2 = dh2 * gain
    dx1 = dy + r2 * (dn2 - n2 * jnp.mean(dn2 * n2, axis=1, keepdims=True))
    dx1_ref[...] = dx1
    da_ref[...] = dx1.astype(BF16)
    gp_ref[...] = nn(dhi, wprevt_ref[...]) + nn(dlo, wprevt_ref[...])
    g1_ref[...] += tn(dhi, h2) + tn(dlo, h2)
    vhi, vlo = split_hi_lo(vcoef)
    g2_ref[...] += tn(vhi, dyb) + tn(vlo, dyb)
    g3_ref[0:1, :] += jnp.sum(dh2 * n2, axis=0, keepdims=True)
    g4_ref[...] += tn(aux_ref[...], dhi) + tn(aux_ref[...], dlo)


def middle_pass(idx, mine, theirs, x1, dy, lg, aux, dlt, eye, count, gain, wcat, vt, wprevt, types, ffn, total_tokens):
    tokens, width = x1.shape
    erows = dlt.shape[0]
    block = lambda i, *_: (i, 0)
    fixed = lambda i, *_: (0, 0)
    grid_spec = pltpu.PrefetchScalarGridSpec(
        num_scalar_prefetch=1,
        grid=(tokens // TB,),
        in_specs=[
            pl.BlockSpec((TB, width // 2), block),
            pl.BlockSpec((TB, width // 2), block),
            pl.BlockSpec((TB, width), block),
            pl.BlockSpec((TB, width), block),
            pl.BlockSpec((TB, LANES), block),
            pl.BlockSpec((TB, LANES), block),
            pl.BlockSpec((erows, TB), lambda i, *_: (0, i)),
            pl.BlockSpec((erows, LANES), fixed),
            pl.BlockSpec((1, LANES), fixed),
            pl.BlockSpec((1, width), fixed),
            pl.BlockSpec((width, LANES), fixed),
            pl.BlockSpec((width, LANES), fixed),
            pl.BlockSpec((LANES, LANES), fixed),
        ],
        out_specs=[
            pl.BlockSpec((TB, width), block),
            pl.BlockSpec((TB, width), block),
            pl.BlockSpec((TB, LANES), block),
            pl.BlockSpec((LANES, width), fixed),
            pl.BlockSpec((LANES, width), fixed),
            pl.BlockSpec((8, width), fixed),
            pl.BlockSpec((LANES, LANES), fixed),
        ],
        scratch_shapes=[pltpu.VMEM((TB, width), BF16)],
    )
    return pl.pallas_call(
        functools.partial(middle_kernel, types, ffn, total_tokens),
        name="middle",
        grid_spec=grid_spec,
        out_shape=(
            jax.ShapeDtypeStruct((tokens, width), F32),
            jax.ShapeDtypeStruct((tokens, width), BF16),
            jax.ShapeDtypeStruct((tokens, LANES), F32),
            jax.ShapeDtypeStruct((LANES, width), F32),
            jax.ShapeDtypeStruct((LANES, width), F32),
            jax.ShapeDtypeStruct((8, width), F32),
            jax.ShapeDtypeStruct((LANES, LANES), F32),
        ),
        compiler_params=params(),
        cost_estimate=COST,
    )(idx, mine, theirs, x1, dy, lg, aux, dlt, eye, count, gain, wcat, vt, wprevt)


def layer_kernel(types, experts, total_tokens, blocks, h2_ref, dy_ref, lg_ref, aux_ref, x1_ref, *refs):
    wgus, wds = refs[:experts], refs[experts : 2 * experts]
    eye_ref, count_ref, gain_ref, wcat_ref, vt_ref, wprevt_ref = refs[2 * experts : 2 * experts + 6]
    dx1_ref, da_ref, gp_ref, fout_ref, gu_ref, down_ref, g1_ref, g2_ref, g3_ref, g4_ref = refs[2 * experts + 6 : 2 * experts + 16]
    scratch = refs[2 * experts + 16 :]
    acc_gu, acc_down, du_ref, gh_ref, dres, fres = scratch[:6]
    dkeep, dsend, dfirst, dsecond, dsems, fkeep, fsend, ffirst, fsecond, fsems, lpart, lfirst, lsecond, lsems = scratch[6:20]
    xg, xd, xsems = scratch[20:]
    step = pl.program_id(0)
    hidden = wds[0].shape[0]
    lrows = lpart.shape[2]
    me = lax.axis_index("expert")
    half, partner, other = neighbours()
    half_cols = dkeep.shape[1]
    dx = GroupSum(dkeep, dsend, dfirst, dsecond, dres, dsems)
    ff = GroupSum(fkeep, fsend, ffirst, fsecond, fres, fsems)
    small = SmallSum(lpart, lfirst, lsecond, lsems)
    across = {"expert": 1 - me}
    _, _, order = depth_place()
    block = gu_ref.shape[0] // 4
    first_rows = [pl.ds(pl.multiple_of(order[k] * block, block), block) for k in range(2)]

    def first_copies(k):
        return [
            pltpu.make_async_remote_copy(
                src_ref=src.at[first_rows[k], pl.ds(cols, cols)],
                dst_ref=dst.at[k],
                send_sem=xsems.at[0, n, k],
                recv_sem=xsems.at[1, n, k],
                device_id=across,
                device_id_type=MESH,
            )
            for n, (src, dst, cols) in enumerate(((gu_ref, xg, 2 * hidden), (down_ref, xd, hidden)))
        ]

    @pl.when(step == 0)
    def _():
        greet((partner, other, across))
        for ref in (acc_gu, acc_down, g1_ref, g2_ref, g3_ref, g4_ref):
            ref[...] = jnp.zeros_like(ref)

    def own_cols(which):
        return pl.ds(pl.multiple_of(which * half_cols, LANES), half_cols)

    @pl.when(step < blocks)
    def _():
        i = step
        h2, dy = h2_ref[...], dy_ref[...]
        lane, probs, mask = routing(lg_ref[...], aux_ref[...], types)
        gates = probs * mask
        dprobs = jnp.zeros_like(probs)
        for s in range(experts):
            e = (me + s) % experts
            gate_col = column(gates, lane, e)
            u = nn(h2, wgus[s][...])
            dhr = nt(dy, wds[s][...])
            g, up = u[:, :hidden], u[:, hidden:]
            sig = 1.0 / (1.0 + jnp.exp(-g))
            silu = g * sig
            hid = silu * up
            gh_ref[:, s * hidden : (s + 1) * hidden] = (hid * gate_col).astype(BF16)
            dg = jnp.sum(hid * dhr, axis=1, keepdims=True)
            dprobs = dprobs + jnp.where(lane == e, dg * mask, 0.0)
            dh = dhr * gate_col
            base = 2 * s * hidden
            du_ref[:, base : base + hidden] = (dh * up * sig * (1.0 + g * (1.0 - sig))).astype(BF16)
            du_ref[:, base + hidden : base + 2 * hidden] = (dh * silu).astype(BF16)
        dlog = probs * (dprobs - jnp.sum(probs * dprobs, axis=1, keepdims=True))
        hi, lo = split_hi_lo(dlog)
        lpart[0, i] = (nt(eye_ref[...], hi) + nt(eye_ref[...], lo))[:lrows]
        small.start(i)
        rows = dx.rows(i)
        for which, place in ((1 - half, dsend), (half, dkeep)):
            cols = own_cols(which)
            total = nt(du_ref[:, : 2 * hidden], wgus[0][cols, :])
            for s in range(1, experts):
                total = total + nt(du_ref[:, 2 * s * hidden : 2 * (s + 1) * hidden], wgus[s][cols, :])
            place[rows, :] = total.astype(BF16)
            if place is dsend:
                dx.to_partner(i).start()
        for which, place in ((1 - half, fsend), (half, fkeep)):
            cols = own_cols(which)
            total = nn(gh_ref[:, :hidden], wds[0][:, cols])
            for s in range(1, experts):
                total = total + nn(gh_ref[:, s * hidden : (s + 1) * hidden], wds[s][:, cols])
            place[rows, :] = total.astype(BF16)
            if place is fsend:
                ff.to_partner(i).start()
        small.pair(i)
        dx.pair(i)
        acc_gu[...] += tn(h2, du_ref[...])
        ff.pair(i)
        acc_down[...] += tn(dy, gh_ref[...])

    @pl.when(step == blocks)
    def _():
        gu_ref[...] = acc_gu[...].astype(BF16)
        down_ref[...] = acc_down[...].astype(BF16)
        for c in first_copies(0) + first_copies(1):
            c.start()
        dx.finish(0)

    @pl.when(step >= blocks)
    def _():
        i = step - blocks

        @pl.when(i + 1 < blocks)
        def _():
            dx.finish(i + 1)

        ff.finish(i)
        rows = dx.rows(i)
        dlt = small.finish(i)
        gain = gain_ref[...]
        x1 = x1_ref[...]
        r2 = rms_factor(x1)
        n2 = x1 * r2
        h2 = h2_ref[...]
        dyb = dy_ref[...]
        dy = dyb.astype(F32)
        lg = lg_ref[...]
        lane, probs, mask = routing(lg, aux_ref[...], types)
        gates = probs * mask
        a = jnp.sum(dy * h2.astype(F32), axis=1, keepdims=True)
        b = nn(dyb, vt_ref[...])
        coef = column(gates, lane, experts + 1)
        dprobs = jnp.where(lane == experts + 1, a, 0.0)
        dlc = jnp.zeros_like(probs)
        vcoef = jnp.zeros_like(probs)
        for c in range(2):
            m0, m1 = const_mix(lg, lane, types, c)
            g = column(gates, lane, experts + 2 + c)
            bc = column(b, lane, c)
            dprobs = dprobs + jnp.where(lane == experts + 2 + c, m0 * a + m1 * bc, 0.0)
            dm0, dm1 = g * a, g * bc
            inner = m0 * dm0 + m1 * dm1
            dlc = dlc + jnp.where(lane == types + 2 * c, m0 * (dm0 - inner), 0.0)
            dlc = dlc + jnp.where(lane == types + 2 * c + 1, m1 * (dm1 - inner), 0.0)
            coef = coef + g * m0
            vcoef = vcoef + jnp.where(lane == c, g * m1, 0.0)
        dprobs = dprobs * mask + count_ref[...] * (AUX_WEIGHT * types / (2.0 * total_tokens * total_tokens))
        dlog = probs * (dprobs - jnp.sum(probs * dprobs, axis=1, keepdims=True))
        hi, lo = split_hi_lo(dlt)
        eye = eye_ref[:lrows, :]
        dl = dlog + dlc + tn(hi, eye) + tn(lo, eye)
        dhi, dlo = split_hi_lo(dl)
        vhi, vlo = split_hi_lo(vcoef)
        gp_ref[...] = nn(dhi, wprevt_ref[...]) + nn(dlo, wprevt_ref[...])
        g1_ref[...] += tn(dhi, h2) + tn(dlo, h2)
        g2_ref[...] += tn(vhi, dyb) + tn(vlo, dyb)
        g4_ref[...] += tn(aux_ref[...], dhi) + tn(aux_ref[...], dlo)
        dh2 = coef * dy + nt(dhi, wcat_ref[...]) + nt(dlo, wcat_ref[...])
        dx.close(i)
        dh2 = dh2 + jnp.concatenate([dres[0, rows, :], dres[1, rows, :]], axis=1).astype(F32)
        g3_ref[0:1, :] += jnp.sum(dh2 * n2, axis=0, keepdims=True)
        dn2 = dh2 * gain
        dx1 = dy + r2 * (dn2 - n2 * jnp.mean(dn2 * n2, axis=1, keepdims=True))
        dx1_ref[...] = dx1
        da_ref[...] = dx1.astype(BF16)
        ff.close(i)
        fout_ref[...] = fres[:, rows, :]

    @pl.when(step == 2 * blocks - 1)
    def _():
        for k in range(2):
            for c, ref, got in zip(first_copies(k), (gu_ref, down_ref), (xg, xd)):
                c.wait()
                own = (first_rows[k], slice(0, got.shape[2]))
                ref[own] = (ref[own].astype(F32) + got[k].astype(F32)).astype(BF16)


def layer_pass(h2, dy, lg, aux, x1, wgus, wds, eye, count, gain, wcat, vt, wprevt, types, total_tokens):
    tokens, width = h2.shape
    experts = len(wgus)
    hidden = wds[0].shape[0]
    blocks = tokens // CHUNK
    lrows = -(-types // 8) * 8
    both = lambda i: (i % blocks, 0)
    late = lambda i: (jnp.maximum(i - blocks, 0), 0)
    fixed = lambda i: (0, 0)
    once = dict(pipeline_mode=pl.Buffered(1))
    small_sums = [
        pltpu.VMEM((2, blocks, lrows, CHUNK), F32),
        pltpu.VMEM((blocks, lrows, CHUNK), F32),
        pltpu.VMEM((blocks, lrows, CHUNK), F32),
        pltpu.SemaphoreType.DMA((2, 2, blocks)),
    ]
    return pl.pallas_call(
        functools.partial(layer_kernel, types, experts, total_tokens, blocks),
        name="layer",
        grid=(2 * blocks,),
        in_specs=[
            pl.BlockSpec((CHUNK, width), both),
            pl.BlockSpec((CHUNK, width), both),
            pl.BlockSpec((CHUNK, LANES), both),
            pl.BlockSpec((CHUNK, LANES), both),
            pl.BlockSpec((CHUNK, width), late),
        ]
        + [pl.BlockSpec((width, 2 * hidden), fixed, **once)] * experts
        + [pl.BlockSpec((hidden, width), fixed, **once)] * experts
        + [
            pl.BlockSpec(eye.shape, fixed),
            pl.BlockSpec((1, LANES), fixed),
            pl.BlockSpec((1, width), fixed),
            pl.BlockSpec((width, LANES), fixed),
            pl.BlockSpec((width, LANES), fixed),
            pl.BlockSpec((LANES, LANES), fixed),
        ],
        out_specs=[
            pl.BlockSpec((CHUNK, width), late),
            pl.BlockSpec((CHUNK, width), late),
            pl.BlockSpec((CHUNK, LANES), late),
            pl.BlockSpec((2, CHUNK, width // 2), lambda i: (0, jnp.maximum(i - blocks, 0), 0)),
            pl.BlockSpec((width, 2 * experts * hidden), fixed, **once),
            pl.BlockSpec((width, experts * hidden), fixed, **once),
            pl.BlockSpec((LANES, width), fixed),
            pl.BlockSpec((LANES, width), fixed),
            pl.BlockSpec((8, width), fixed),
            pl.BlockSpec((LANES, LANES), fixed),
        ],
        out_shape=(
            jax.ShapeDtypeStruct((tokens, width), F32),
            jax.ShapeDtypeStruct((tokens, width), BF16),
            jax.ShapeDtypeStruct((tokens, LANES), F32),
            jax.ShapeDtypeStruct((2, tokens, width // 2), BF16),
            jax.ShapeDtypeStruct((width, 2 * experts * hidden), BF16),
            jax.ShapeDtypeStruct((width, experts * hidden), BF16),
            jax.ShapeDtypeStruct((LANES, width), F32),
            jax.ShapeDtypeStruct((LANES, width), F32),
            jax.ShapeDtypeStruct((8, width), F32),
            jax.ShapeDtypeStruct((LANES, LANES), F32),
        ),
        scratch_shapes=[
            pltpu.VMEM((width, 2 * experts * hidden), F32),
            pltpu.VMEM((width, experts * hidden), F32),
            pltpu.VMEM((CHUNK, 2 * experts * hidden), BF16),
            pltpu.VMEM((CHUNK, experts * hidden), BF16),
            pltpu.VMEM((2, tokens, width // 2), BF16),
            pltpu.VMEM((2, tokens, width // 2), BF16),
        ]
        + sum_scratch(tokens, width // 2)
        + sum_scratch(tokens, width // 2)
        + small_sums
        + [
            pltpu.VMEM((2, width // 4, 2 * hidden), BF16),
            pltpu.VMEM((2, width // 4, hidden), BF16),
            pltpu.SemaphoreType.DMA((2, 2, 2)),
        ],
        compiler_params=params(collective_id=2, has_side_effects=True),
        cost_estimate=COST,
    )(h2, dy, lg, aux, x1, *wgus, *wds, eye, count, gain, wcat, vt, wprevt)


def output_kernel(types, ffn, f_ref, x1_ref, h2_ref, lg_ref, aux_ref, v_ref, out_ref):
    halves = jnp.concatenate([f_ref[0], f_ref[1]], axis=1)
    lg = lg_ref[...]
    lane, probs, mask = routing(lg, aux_ref[...], types)
    gates = probs * mask
    coef = column(gates, lane, ffn + 1)
    out = x1_ref[...] + halves.astype(F32)
    for c in range(2):
        m0, m1 = const_mix(lg, lane, types, c)
        g = column(gates, lane, ffn + 2 + c)
        coef = coef + g * m0
        out = out + (g * m1) * v_ref[c : c + 1, :]
    out_ref[...] = out + coef * h2_ref[...].astype(F32)


def output_pass(f, x1, h2, lg, aux, v, types, ffn):
    tokens, width = x1.shape
    block = lambda i: (i, 0)
    return pl.pallas_call(
        functools.partial(output_kernel, types, ffn),
        name="output",
        grid=(tokens // TB,),
        in_specs=[
            pl.BlockSpec((2, TB, width // 2), lambda i: (0, i, 0)),
            pl.BlockSpec((TB, width), block),
            pl.BlockSpec((TB, width), block),
            pl.BlockSpec((TB, LANES), block),
            pl.BlockSpec((TB, LANES), block),
            pl.BlockSpec((8, width), lambda i: (0, 0)),
        ],
        out_specs=pl.BlockSpec((TB, width), block),
        out_shape=jax.ShapeDtypeStruct((tokens, width), F32),
        compiler_params=params(),
        cost_estimate=COST,
    )(f, x1, h2, lg, aux, v)


def last_kernel(d_ref, x_ref, dx1_ref, gain_ref, out_ref):
    halves = jnp.concatenate([d_ref[0], d_ref[1]], axis=1)
    x = x_ref[...].astype(F32)
    r1 = rms_factor(x)
    n1 = x * r1
    dn1 = halves.astype(F32) * gain_ref[...]
    out_ref[...] = dx1_ref[...] + r1 * (dn1 - n1 * jnp.mean(dn1 * n1, axis=1, keepdims=True))


def last_pass(dh1, x, dx1, gain):
    tokens, width = x.shape
    block = lambda i: (i, 0)
    return pl.pallas_call(
        last_kernel,
        name="last",
        grid=(tokens // TB,),
        in_specs=[
            pl.BlockSpec((2, TB, width // 2), lambda i: (0, i, 0)),
            pl.BlockSpec((TB, width), block),
            pl.BlockSpec((TB, width), block),
            pl.BlockSpec((1, width), lambda i: (0, 0)),
        ],
        out_specs=pl.BlockSpec((TB, width), block),
        out_shape=jax.ShapeDtypeStruct((tokens, width), F32),
        compiler_params=params(),
        cost_estimate=COST,
    )(dh1, x, dx1, gain)


def tie(value, *others):
    return lax.optimization_barrier((value, *others))[0]


def add_all(own, got):
    total = own.astype(F32)
    for g in got:
        total = total + g.astype(F32)
    return total.astype(BF16)


def pair_sum(keep, send):
    return (keep.astype(F32) + swap(send, "tensor", 1).astype(F32)).astype(BF16)


def group_sum(part):
    bit = 2
    while bit < lax.axis_size("tensor"):
        part = (part.astype(F32) + swap(part, "tensor", bit).astype(F32)).astype(BF16)
        bit *= 2
    return part, swap(part, "tensor", 1)


def scatter_sum(a, axes):
    steps = []
    for axis in axes:
        bits = lax.axis_size(axis).bit_length() - 1
        steps += [(axis, b) for b in reversed(range(bits))]
    a = a.reshape((2,) * len(steps) + (-1, a.shape[-1]))
    order = [s for axis in reversed(axes) for s in reversed(steps) if s[0] == axis]
    left = list(steps)
    for axis, bit in order:
        dim = left.index((axis, bit))
        mine = (lax.axis_index(axis) >> bit) & 1
        got = swap(lax.dynamic_index_in_dim(a, 1 - mine, dim, keepdims=False), axis, 1 << bit)
        a = (lax.dynamic_index_in_dim(a, mine, dim, keepdims=False).astype(F32) + got.astype(F32)).astype(BF16)
        left.remove((axis, bit))
    return a


def gather_group(a):
    out = [a]
    bit = lax.axis_size("tensor") // 2
    parts = {0: a}
    while bit:
        parts.update({m | bit: swap(p, "tensor", bit) for m, p in list(parts.items())})
        bit //= 2
    return [parts[m] for m in range(len(parts))]


def per_device(hidden_in, prev_logits, routes, block_ids, cotangent, gain_attn, w_qkv, w_out, gain_moe, w_router, w_prev, w_const, v_const, w_gate_up, w_down):
    tokens, width = hidden_in.shape
    types = w_router.shape[1]
    experts = lax.axis_size("expert")
    heads = w_out.shape[0] // HEAD_DIM
    hidden = w_down.shape[1]
    total_tokens = tokens * lax.axis_size(("dp", "expert"))
    t_index, x_index = lax.axis_index("tensor"), lax.axis_index("expert")
    t_idx = jnp.stack([t_index, t_index % 2]).astype(jnp.int32)
    x_idx = jnp.stack([x_index, t_index % 2]).astype(jnp.int32)

    gain_first = gain_attn.astype(F32)[None]
    gain_second = gain_moe.astype(F32)[None]
    consts = w_const.transpose(1, 0, 2).reshape(width, 4)
    wcat = jnp.pad(jnp.concatenate([w_router, consts], axis=1), ((0, 0), (0, LANES - types - 4)))
    aux = jnp.concatenate([prev_logits, routes.astype(BF16)], axis=1)
    aux = jnp.pad(aux, ((0, 0), (0, LANES - types - 2)))
    wprev = jnp.pad(w_prev, ((0, LANES - types), (0, LANES - types)))
    wprevt = jnp.pad(w_prev.T, ((0, LANES - types), (0, LANES - types)))
    vt = jnp.pad(v_const.T, ((0, 0), (0, LANES - 2)))
    vrows = jnp.pad(v_const.astype(F32), ((0, 6), (0, 0)))
    erows = -(-types // 16) * 16
    eye = jnp.eye(erows, LANES, dtype=BF16)
    lanes = jnp.arange(LANES, dtype=jnp.int32)
    chosen = (routes[:, :, None] == lanes[None, None, :]).astype(F32)
    count = jnp.sum(chosen, axis=(0, 1))[None]
    bq, bk = block_ids, block_ids.reshape(tokens, 1)

    w_halves = w_qkv.T.reshape(-1, 2, width // 2).transpose(1, 0, 2)

    wgu, wd = w_gate_up[0].reshape(width, 2 * hidden), w_down[0]
    fused = experts == 2 and lax.axis_size("dp") == 4 and lax.axis_size("tensor") == 4
    if fused:
        part = jnp.broadcast_to(count, (8, LANES))
        h1, qkvt, ot, lse, x1, h2, lg, prob_part, count, *peer = front_pass(
            hidden_in, gain_first, w_qkv.T, bq, bk, w_out, gain_second, wcat, aux, wprev, part, wgu, wd, heads, types
        )
        wgus, wds, count = [wgu, peer[0]], [wd, peer[1]], count[:1]
    else:
        wgus = [wgu] + [swap(wgu, "expert", s) for s in range(1, experts)]
        wds = [wd] + [swap(wd, "expert", s) for s in range(1, experts)]
        h1, qkvt, ot, lse = attention_forward(hidden_in, gain_first, w_qkv.T, bq, bk, heads)
        ots, wos = gather_group(ot), gather_group(w_out)
        x1, h2, lg, prob_part = post_attention(t_idx, hidden_in, ots, wos, gain_second, wcat, aux, wprev, types)
        count = sum_over(tie(count, wds[-1]), ("expert", "dp"))
    srows = -(-(types + 4) // 8) * 8
    prow = -(-types // 8) * 8

    def small_rows(g1, g2, g3, g4):
        wide = lambda a: jnp.pad(a, ((0, 0), (0, width - LANES)))
        return jnp.concatenate([g1[:srows], g2[:8], g3, wide(g4[:prow]), wide(prob_part)], axis=0)

    if fused:
        dx1, da, gp, f, gu, down, *g = layer_pass(
            h2, cotangent, lg, aux, x1, wgus, wds, eye, count, gain_second, wcat, vt, wprevt, types, total_tokens
        )
        dh1, gain_all, grads, grad_gate_up, grad_down, small = attention_backward(
            da, w_out, qkvt, ot, lse, bq, bk, w_halves, h1, heads, gu, down, small_rows(*g)
        )
    else:
        keep, send, gh, du, dlt = experts_pass(x_idx, h2, cotangent, lg, aux, wgus, wds, eye, types)
        mine, theirs = group_sum(pair_sum(keep, send))
        dlt = sum_over(dlt, ("tensor",))
        fkeep, fsend = down_pass(x_idx, gh, wds)
        gu_parts = [tn(h2, du[e]).astype(BF16) for e in range(experts)]
        down_parts = [tn(cotangent, gh[e]).astype(BF16) for e in range(experts)]
        f_mine, f_theirs = group_sum(pair_sum(fkeep, fsend))
        first, second = jnp.where(t_index % 2 == 0, f_mine, f_theirs), jnp.where(t_index % 2 == 0, f_theirs, f_mine)
        f = jnp.stack([first, second])
        dx1, da, gp, *g = middle_pass(
            x_idx, mine, theirs, x1, cotangent, lg, aux, dlt, eye, count, gain_second, wcat, vt, wprevt, types, experts, total_tokens
        )
        dh1, gain_part, grads = attention_backward(da, w_out, qkvt, ot, lse, bq, bk, w_halves, h1, heads)
        grads = scatter_sum(grads, ("dp", "expert")).astype(F32)
        gu_got = [swap(gu_parts[e], "expert", e) for e in range(1, experts)]
        down_got = [swap(down_parts[e], "expert", e) for e in range(1, experts)]
        grad_gate_up = scatter_sum(add_all(gu_parts[0], gu_got), ("dp",)).astype(F32)
        grad_down = scatter_sum(add_all(down_parts[0], down_got), ("dp",)).astype(F32)
        gain_all = sum_over(gain_part, ("tensor", "expert", "dp"))
        small = sum_over(small_rows(*g), ("expert", "dp"))

    grad_gain = gain_all[0] / gain_first[0]
    grad_input = last_pass(dh1, hidden_in, dx1, gain_first)
    output = output_pass(f, x1, h2, lg, aux, vrows, types, experts)
    grad_qkv, grad_out = grads[:, : w_qkv.shape[1]], grads[:, w_qkv.shape[1] :].T

    prob_all = small[srows + 16 + prow, :types]
    count_all = count[0, :types]
    balance_loss = types * jnp.sum((count_all / (2.0 * total_tokens)) * prob_all / total_tokens)
    load = jnp.stack([count_all / (2.0 * tokens), prob_all / tokens])
    return (
        output,
        grad_input,
        gp[:, :types],
        grad_gain,
        grad_qkv,
        grad_out,
        small[srows + 8],
        small[:types].T,
        small[srows + 16 : srows + 16 + types, :types],
        small[types : types + 4].reshape(2, 2, width).transpose(0, 2, 1),
        small[srows : srows + 2],
        grad_gate_up.reshape(1, -1, 2, hidden),
        grad_down.T[None],
        balance_loss,
        load,
    )


def solution(mesh):
    tok = P(("dp", "expert"), None)
    return jax.shard_map(
        per_device,
        mesh=mesh,
        in_specs=(
            tok,
            tok,
            tok,
            tok,
            tok,
            P(),
            P(None, "tensor"),
            P("tensor", None),
            P(),
            P(),
            P(),
            P(),
            P(),
            P("expert", None, None, "tensor"),
            P("expert", "tensor", None),
        ),
        out_specs=(
            tok,
            tok,
            tok,
            P(),
            P(("dp", "expert"), "tensor"),
            P("tensor", ("dp", "expert")),
            P(),
            P(),
            P(),
            P(),
            P(),
            P("expert", "dp", None, "tensor"),
            P("expert", "tensor", "dp"),
            P(),
            P(),
        ),
        check_vma=False,
    )
```

```python
import functools

import jax
import jax.numpy as jnp
from jax import lax
from jax.experimental import pallas as pl
from jax.experimental.pallas import tpu as pltpu
from jax.sharding import PartitionSpec as P

HEAD_DIM = 64
EPSILON = 1e-06
AUX_WEIGHT = 0.01
SCORE_SCALE = 0.125
MAX_BLOCK = 256
LANES = 128
QB = 256
QF = 512
TB = 256
NEG = -1e30
F32 = jnp.float32
BF16 = jnp.bfloat16
MESH = pl.DeviceIdType.MESH
VMEM_LIMIT = 54 * 1024 * 1024
COST = pl.CostEstimate(flops=1000, bytes_accessed=1000, transcendentals=0)


def params(**more):
    return pltpu.CompilerParams(vmem_limit_bytes=VMEM_LIMIT, **more)


def nn(a, b):
    return lax.dot_general(a, b, (((1,), (0,)), ((), ())), preferred_element_type=F32)


def nt(a, b):
    return lax.dot_general(a, b, (((1,), (1,)), ((), ())), preferred_element_type=F32)


def tn(a, b):
    return lax.dot_general(a, b, (((0,), (0,)), ((), ())), preferred_element_type=F32)


def split_hi_lo(a):
    hi = a.astype(BF16)
    return hi, (a - hi.astype(F32)).astype(BF16)


def rms_factor(values):
    return lax.rsqrt(jnp.mean(values * values, axis=-1, keepdims=True) + EPSILON)


def swap(a, axis, bit):
    n = lax.axis_size(axis)
    return lax.ppermute(a, axis, [(i, i ^ bit) for i in range(n)])


def sum_over(a, axes):
    for axis in axes:
        bit = 1
        while bit < lax.axis_size(axis):
            a = a + swap(a, axis, bit)
            bit *= 2
    return a


def key_range(q0, rows, tokens):
    return min(tokens, q0 + rows + MAX_BLOCK)


def project_rows(r0, heads, x_ref, gain_ref, wt_ref, h1_ref, qkvt_ref, kn_ref):
    d = HEAD_DIM
    rows = slice(r0, r0 + QF)
    xb = x_ref[rows, :].astype(F32)
    h1 = (xb * rms_factor(xb) * gain_ref[...]).astype(BF16)
    h1_ref[rows, :] = h1
    qkvt = nt(wt_ref[...], h1)
    for h in range(heads):
        base = h * 3 * d
        q = qkvt[base : base + d].astype(BF16).astype(F32) * SCORE_SCALE
        qkvt_ref[base : base + d, rows] = q.astype(BF16)
        qkvt_ref[base + d : base + 3 * d, rows] = qkvt[base + d : base + 3 * d].astype(BF16)
        kn_ref[h, rows, :] = qkvt[base + d : base + 2 * d].T.astype(BF16)


def attend_rows(q0, h, bq_ref, bk_ref, qkvt_ref, kn_ref, lse_ref):
    tokens = qkvt_ref.shape[1]
    d = HEAD_DIM
    base = h * 3 * d
    cols = slice(q0, q0 + QF)
    top = key_range(q0, QF, tokens)
    s = nn(kn_ref[h, :top, :], qkvt_ref[base : base + d, cols])
    parts = [jnp.where(bk_ref[q0:top, :] <= bq_ref[:, cols], s[q0:], NEG)]
    if q0:
        parts = [s[:q0]] + parts
    m = functools.reduce(jnp.maximum, [jnp.max(a, axis=0, keepdims=True) for a in parts])
    ps = [jnp.exp(a - m) for a in parts]
    total = functools.reduce(jnp.add, [jnp.sum(p, axis=0, keepdims=True) for p in ps])
    p = jnp.concatenate([p.astype(BF16) for p in ps], axis=0)
    acc = nn(qkvt_ref[base + 2 * d : base + 3 * d, :top], p)
    lse_ref[h : h + 1, cols] = m + jnp.log(total)
    return (acc / total).astype(BF16)


def attn_fwd_kernel(heads, x_ref, gain_ref, wt_ref, bq_ref, bk_ref, h1_ref, qkvt_ref, ot_ref, lse_ref, kn_ref):
    tokens = x_ref.shape[0]
    d = HEAD_DIM
    for r0 in range(0, tokens, QF):
        project_rows(r0, heads, x_ref, gain_ref, wt_ref, h1_ref, qkvt_ref, kn_ref)
    for h in range(heads):
        for q0 in range(0, tokens, QF):
            ot_ref[h * d : (h + 1) * d, q0 : q0 + QF] = attend_rows(q0, h, bq_ref, bk_ref, qkvt_ref, kn_ref, lse_ref)


def attention_forward(x, gain, w_t, bq, bk, heads):
    tokens, width = x.shape
    cols = w_t.shape[0]
    lse_rows = -(-heads // 8) * 8
    return pl.pallas_call(
        functools.partial(attn_fwd_kernel, heads),
        name="attn_fwd",
        out_shape=(
            jax.ShapeDtypeStruct((tokens, width), BF16),
            jax.ShapeDtypeStruct((cols, tokens), BF16),
            jax.ShapeDtypeStruct((heads * HEAD_DIM, tokens), BF16),
            jax.ShapeDtypeStruct((lse_rows, tokens), F32),
        ),
        scratch_shapes=[pltpu.VMEM((heads, tokens, HEAD_DIM), BF16)],
        compiler_params=params(),
        cost_estimate=COST,
    )(x, gain, w_t, bq, bk)


CHUNK = 256
F_LATE = 3


def neighbours():
    t = lax.axis_index("tensor")
    return t % 2, {"tensor": t + 1 - 2 * (t % 2)}, {"tensor": (t + 2) % 4}


def greet(devices):
    barrier = pltpu.get_barrier_semaphore()
    for device in devices:
        pl.semaphore_signal(barrier, inc=1, device_id=device, device_id_type=MESH)
    pl.semaphore_wait(barrier, len(devices))


def each(count, step):
    def body(i, carry):
        step(i)
        return carry

    lax.fori_loop(0, count, body, 0)


class GroupSum:
    def __init__(self, keep, send, first, second, result, sems):
        self.keep, self.send, self.first, self.second, self.result, self.sems = keep, send, first, second, result, sems
        self.half, self.partner, self.other = neighbours()

    def rows(self, i):
        return pl.ds(pl.multiple_of(i * CHUNK, CHUNK), CHUNK)

    def copy(self, stage, i, src, dst, device):
        return pltpu.make_async_remote_copy(
            src_ref=src,
            dst_ref=dst,
            send_sem=self.sems.at[0, stage, i],
            recv_sem=self.sems.at[1, stage, i],
            device_id=device,
            device_id_type=MESH,
        )

    def to_partner(self, i):
        r = self.rows(i)
        return self.copy(0, i, self.send.at[r, :], self.first.at[r, :], self.partner)

    def to_other(self, i):
        r = self.rows(i)
        return self.copy(1, i, self.keep.at[r, :], self.second.at[r, :], self.other)

    def back(self, i):
        place = self.result.at[self.half, self.rows(i), :]
        return self.copy(2, i, place, place, self.partner)

    def pair_only(self, i):
        self.to_partner(i).wait_recv()
        r = self.rows(i)
        self.keep[r, :] = (self.keep[r, :].astype(F32) + self.first[r, :].astype(F32)).astype(BF16)

    def pair(self, i):
        self.pair_only(i)
        self.to_other(i).start()

    def finish(self, i):
        self.to_other(i).wait_recv()
        r = self.rows(i)
        self.result[self.half, r, :] = (self.keep[r, :].astype(F32) + self.second[r, :].astype(F32)).astype(BF16)
        self.back(i).start()

    def close(self, i):
        self.back(i).wait_recv()
        if self.send is not None:
            self.to_partner(i).wait_send()
        self.to_other(i).wait_send()
        self.back(i).wait_send()


class SmallSum:
    def __init__(self, part, first, second, sems):
        self.part, self.first, self.second, self.sems = part, first, second, sems
        _, self.partner, self.other = neighbours()

    def copy(self, stage, i, landing, device):
        return pltpu.make_async_remote_copy(
            src_ref=self.part.at[stage, i],
            dst_ref=landing.at[i],
            send_sem=self.sems.at[0, stage, i],
            recv_sem=self.sems.at[1, stage, i],
            device_id=device,
            device_id_type=MESH,
        )

    def start(self, i):
        self.copy(0, i, self.first, self.partner).start()

    def pair(self, i):
        self.copy(0, i, self.first, self.partner).wait_recv()
        self.part[1, i] = self.part[0, i] + self.first[i]
        self.copy(1, i, self.second, self.other).start()

    def finish(self, i):
        self.copy(1, i, self.second, self.other).wait_recv()
        self.copy(0, i, self.first, self.partner).wait_send()
        self.copy(1, i, self.second, self.other).wait_send()
        return self.part[1, i] + self.second[i]


class HopSum:
    def __init__(self, partial, landed, sems, devices):
        self.partial, self.landed, self.sems, self.devices = partial, landed, sems, devices

    def hop(self, n):
        return pltpu.make_async_remote_copy(
            src_ref=self.partial.at[n],
            dst_ref=self.landed.at[n],
            send_sem=self.sems.at[0, n],
            recv_sem=self.sems.at[1, n],
            device_id=self.devices[n],
            device_id_type=MESH,
        )

    def start(self):
        self.hop(0).start()

    def add(self, n):
        self.hop(n).wait_recv()
        total = self.partial[n] + self.landed[n]
        if n + 1 < len(self.devices):
            self.partial[n + 1] = total
            self.hop(n + 1).start()
        return total

    def close(self):
        for n in range(len(self.devices)):
            self.hop(n).wait_send()


def hop_scratch(hops, rows, width):
    return [pltpu.VMEM((hops, rows, width), F32), pltpu.VMEM((hops, rows, width), F32), pltpu.SemaphoreType.DMA((2, hops))]


def replica(n):
    place = (lax.axis_index("dp") * 2 + lax.axis_index("expert") + n) % 8
    return {"dp": place // 2, "expert": place % 2}, place


def all_replicas():
    return [replica(n)[0] for n in range(1, 8)]


class ReplicaSum:
    def __init__(self, own, landed, result, sems):
        self.own, self.landed, self.result, self.sems = own, landed, result, sems

    def copy(self, stage, n):
        device, place = replica(n)
        _, me = replica(0)
        rows = lambda block: pl.ds(pl.multiple_of(block * 8, 8), 8)
        src, dst = ((self.own.at[rows(place), :], self.landed.at[me]), (self.result.at[rows(me), :], self.result.at[rows(me), :]))[stage]
        return pltpu.make_async_remote_copy(
            src_ref=src,
            dst_ref=dst,
            send_sem=self.sems.at[0, stage, n],
            recv_sem=self.sems.at[1, stage, n],
            device_id=device,
            device_id_type=MESH,
        )

    def start(self):
        for n in range(1, 8):
            self.copy(0, n).start()

    def share(self):
        _, me = replica(0)
        rows = pl.ds(pl.multiple_of(me * 8, 8), 8)
        self.landed[me] = self.own[rows, :]
        for n in range(1, 8):
            self.copy(0, n).wait_recv()
        total = self.landed[0]
        for n in range(1, 8):
            total = total + self.landed[n]
        self.result[rows, :] = total
        for n in range(1, 8):
            self.copy(1, n).start()

    def close(self):
        for n in range(1, 8):
            self.copy(1, n).wait_recv()
            for stage in range(2):
                self.copy(stage, n).wait_send()


class EverywhereSum:
    def __init__(self, first, second, fsems, ssems):
        self.first, self.second, self.fsems, self.ssems = first, second, fsems, ssems
        self.t = lax.axis_index("tensor")

    def copy(self, buffer, sems, place, n, device):
        return pltpu.make_async_remote_copy(
            src_ref=buffer.at[place],
            dst_ref=buffer.at[place],
            send_sem=sems.at[0, n],
            recv_sem=sems.at[1, n],
            device_id=device,
            device_id_type=MESH,
        )

    def outer(self):
        return [self.copy(self.first, self.fsems, replica(0)[1], n, replica(n)[0]) for n in range(1, 8)]

    def inner(self):
        return [self.copy(self.second, self.ssems, self.t, n, {"tensor": (self.t + n) % 4}) for n in range(1, 4)]

    def start(self, value):
        self.first[replica(0)[1]] = value
        for c in self.outer():
            c.start()

    def share(self):
        for c in self.outer():
            c.wait_recv()
        total = self.first[0]
        for n in range(1, 8):
            total = total + self.first[n]
        self.second[self.t] = total
        for c in self.inner():
            c.start()

    def finish(self):
        for c in self.inner():
            c.wait_recv()
        for c in self.outer() + self.inner():
            c.wait_send()
        return self.second[0] + self.second[1] + (self.second[2] + self.second[3])


def depth_place():
    z = lax.axis_index("dp")
    low, high = z % 2, z // 2
    order = [2 * (1 - high) + 1 - low, 2 * high + 1 - low, 2 * (1 - high) + low, z]
    return {"dp": z + 1 - 2 * low}, {"dp": (z + 2) % 4}, order


class DepthSum:
    def __init__(self, own, across, landed, xsems, zsems, sources, device):
        self.own, self.across, self.landed, self.xsems, self.zsems = own, across, landed, xsems, zsems
        self.sources, self.device = sources, device
        self.near, self.far, _ = depth_place()

    def x_copy(self, k):
        return pltpu.make_async_remote_copy(
            src_ref=self.sources[k],
            dst_ref=self.across.at[k],
            send_sem=self.xsems.at[0, k],
            recv_sem=self.xsems.at[1, k],
            device_id=self.device,
            device_id_type=MESH,
        )

    def z_copy(self, k):
        return pltpu.make_async_remote_copy(
            src_ref=self.own.at[k],
            dst_ref=self.landed.at[k],
            send_sem=self.zsems.at[0, k],
            recv_sem=self.zsems.at[1, k],
            device_id=self.near if k < 2 else self.far,
            device_id_type=MESH,
        )

    def pass_on(self, k):
        total = self.own[k].astype(F32)
        if self.sources[k] is not None:
            self.x_copy(k).wait_recv()
            total = total + self.across[k].astype(F32)
        for came in {2: (0,), 3: (1, 2)}.get(k, ()):
            self.z_copy(came).wait_recv()
            total = total + self.landed[came].astype(F32)
        if k < 3:
            self.own[k] = total.astype(BF16)
            self.z_copy(k).start()
        return total

    def close(self):
        for k in range(4):
            if self.sources[k] is not None:
                self.x_copy(k).wait_send()
            if k < 3:
                self.z_copy(k).wait_send()


def depth_scratch(rows, cols):
    return [
        pltpu.VMEM((4, rows, cols), BF16),
        pltpu.VMEM((4, rows, cols), BF16),
        pltpu.VMEM((3, rows, cols), BF16),
        pltpu.SemaphoreType.DMA((2, 4)),
        pltpu.SemaphoreType.DMA((2, 3)),
    ]


def sum_scratch(tokens, half_cols, sends=True):
    return [pltpu.VMEM((tokens, half_cols), BF16)] * (4 if sends else 3) + [pltpu.SemaphoreType.DMA((2, 3, tokens // CHUNK))]


def attn_bwd_kernel(heads, fused, da_ref, wo_ref, qkvt_ref, ot_ref, lse_ref, bq_ref, bk_ref, wq_ref, h1_ref, *refs):
    if fused:
        gu_ref, down_ref, small_ref, flate_ref = refs[:4]
        dres_ref, gain_ref, gsum_ref, gusum_ref, dosum_ref, smallsum_ref, fres_ref = refs[4:11]
        scratch = refs[11:]
    else:
        dres_ref, gain_ref, gsum_ref = refs[:3]
        scratch = refs[3:]
    dqkvt_ref, dot_ref, delta_ref, kn_ref, vn_ref, dk_ref, dv_ref, dkeep, dsend, dfirst, dsecond, dsems = scratch[:12]
    tokens, width = da_ref.shape
    d = HEAD_DIM
    cols_all = dqkvt_ref.shape[0]
    chunks = tokens // CHUNK
    dh = GroupSum(dkeep, dsend, dfirst, dsecond, dres_ref, dsems)
    half, partner, other = neighbours()
    if fused:
        glocal, *rest = scratch[12:]
        gparts, uparts, dparts, sparts, nparts, (lsems,) = rest[:5], rest[5:10], rest[10:15], rest[15:17], rest[17:21], rest[21:22]
        fsecond, fsems = rest[22:]
        ff = GroupSum(flate_ref, None, None, fsecond, fres_ref, fsems)
        hidden = dparts[0].shape[2]
        x = lax.axis_index("expert")
        near, far, order = depth_place()
        block, piece = width // 4, width // 8
        across = {"expert": 1 - x}
        t = lax.axis_index("tensor")
        greet([{"tensor": (t + n) % 4} for n in range(1, 4)] + all_replicas())

        def block_rows(k):
            return pl.ds(pl.multiple_of(order[k] * block, block), block)

        def pieces(k, place):
            return pl.ds(pl.multiple_of(order[k] * block + place * piece, piece), piece)

        gate_up = DepthSum(*uparts, [None] * 2 + [gu_ref.at[block_rows(k), pl.ds(2 * hidden, 2 * hidden)] for k in range(2, 4)], across)
        down = DepthSum(*dparts, [None] * 2 + [down_ref.at[block_rows(k), pl.ds(hidden, hidden)] for k in range(2, 4)], across)
        attn = DepthSum(*gparts, [glocal.at[pieces(k, 1 - x), :] for k in range(4)], across)
        small = ReplicaSum(small_ref, sparts[0], smallsum_ref, sparts[1])
        total_gain = EverywhereSum(*nparts)

        def local_copies(k):
            return [
                pltpu.make_async_copy(gu_ref.at[block_rows(k), pl.ds(0, 2 * hidden)], gate_up.own.at[k], lsems.at[0, k]),
                pltpu.make_async_copy(down_ref.at[block_rows(k), pl.ds(0, hidden)], down.own.at[k], lsems.at[1, k]),
            ]

        def pass_on(k):
            for c in local_copies(k):
                c.wait()
            return gate_up.pass_on(k), down.pass_on(k)

        for n in range(F_LATE):
            ff.to_other(n).start()
        small.start()
        for k in range(4):
            for c in local_copies(k):
                c.start()
            if k >= 2:
                gate_up.x_copy(k).start()
                down.x_copy(k).start()
    else:
        glocal = gsum_ref
        greet([partner, other])

    def project(i):
        rows = pl.ds(pl.multiple_of(i * CHUNK, CHUNK), CHUNK)
        dot = nt(wo_ref[...], da_ref[rows, :]).astype(BF16)
        dot_ref[:, rows] = dot
        prod = dot.astype(F32) * ot_ref[:, rows].astype(F32)
        for h in range(heads):
            base = h * 3 * d
            delta_ref[h : h + 1, rows] = jnp.sum(prod[h * d : (h + 1) * d], axis=0, keepdims=True)
            kn_ref[h, rows, :] = qkvt_ref[base + d : base + 2 * d, rows].astype(F32).T.astype(BF16)
            vn_ref[h, rows, :] = qkvt_ref[base + 2 * d : base + 3 * d, rows].astype(F32).T.astype(BF16)

    each(chunks, project)
    dk_ref[...] = jnp.zeros_like(dk_ref)
    dv_ref[...] = jnp.zeros_like(dv_ref)
    glocal[:, cols_all:] = nn(ot_ref[...], da_ref[...]).T.astype(BF16)

    def query_block(q0):
        def head(h):
            base = h * 3 * d
            orows = pl.ds(h * d, d)
            cols = slice(q0, q0 + QB)
            top = key_range(q0, QB, tokens)
            qt = qkvt_ref[pl.ds(base, d), cols]
            dot = dot_ref[orows, cols]
            s = nn(kn_ref[h, :top, :], qt)
            p = jnp.exp(s - lse_ref[pl.ds(h, 1), cols])
            last = jnp.where(bk_ref[q0:top, :] <= bq_ref[:, cols], p[q0:], 0.0)
            p = jnp.concatenate([p[:q0], last], axis=0) if q0 else last
            dp = nn(vn_ref[h, :top, :], dot)
            ds = (p * (dp - delta_ref[pl.ds(h, 1), cols])).astype(BF16)
            dv_ref[h, :, :top] += nt(dot, p.astype(BF16))
            dk_ref[h, :, :top] += nt(qt, ds)
            dq = nn(qkvt_ref[pl.ds(base + d, d), :top], ds)
            dqkvt_ref[pl.ds(base, d), cols] = (dq * SCORE_SCALE).astype(BF16)

        for h in range(heads):
            head(h)

    def input_grad(i):
        r = dh.rows(i)
        for h in range(heads):
            base = h * 3 * d
            dqkvt_ref[base + d : base + 2 * d, r] = dk_ref[h, :, r].astype(BF16)
            dqkvt_ref[base + 2 * d : base + 3 * d, r] = dv_ref[h, :, r].astype(BF16)
        dqkv = dqkvt_ref[:, r]
        dsend[r, :] = tn(dqkv, wq_ref[1 - half]).astype(BF16)
        dh.to_partner(i).start()
        dkeep[r, :] = tn(dqkv, wq_ref[half]).astype(BF16)
        dh.pair(i)

    if fused:
        pass_on(0)
        pass_on(1)
    for i in reversed(range(chunks)):
        query_block(i * QB)
        if i + 1 < chunks:
            input_grad(i + 1)
        if fused and i == chunks - 3:
            pass_on(2)
            small.share()
        if fused and i == 1:
            for n in range(F_LATE):
                ff.finish(n)
    input_grad(0)
    gain = jnp.zeros((1, width), F32)
    for c0 in range(0, cols_all, 3 * d):
        part = nn(dqkvt_ref[c0 : c0 + 3 * d, :], h1_ref[...])
        w = jnp.concatenate([wq_ref[0, c0 : c0 + 3 * d, :], wq_ref[1, c0 : c0 + 3 * d, :]], axis=1)
        gain = gain + jnp.sum(part * w.astype(F32), axis=0, keepdims=True)
        glocal[:, c0 : c0 + 3 * d] = part.T.astype(BF16)
    gain = jnp.broadcast_to(gain, gain_ref.shape)
    if fused:
        total_gain.start(gain)
        for k in range(4):
            attn.own[k] = glocal[pieces(k, x), :]
            attn.x_copy(k).start()
        dh.finish(chunks - 1)
        dh.finish(chunks - 2)
        attn.pass_on(0)
        attn.pass_on(1)
        total_gain.share()
        dh.finish(chunks - 3)
        gusum_ref[...], dosum_ref[...] = pass_on(3)
        attn.pass_on(2)
        each(chunks - 3, lambda i: dh.finish(chunks - 4 - i))
        gsum_ref[...] = attn.pass_on(3)
        gain_ref[...] = total_gain.finish()
        for n in range(F_LATE):
            ff.close(n)
        for part in (gate_up, down, attn, small):
            part.close()
    else:
        gain_ref[...] = gain
        each(chunks, lambda i: dh.finish(chunks - 1 - i))
    each(chunks, dh.close)


def attention_backward(da, w_out, qkvt, ot, lse, bq, bk, w_halves, h1, heads, gu=None, down=None, small=None, f_late=None):
    tokens, width = da.shape
    cols = qkvt.shape[0]
    fused = gu is not None
    out_shape = [jax.ShapeDtypeStruct((2, tokens, width // 2), BF16), jax.ShapeDtypeStruct((8, width), F32)]
    vmem = pl.BlockSpec(memory_space=pltpu.VMEM)
    in_specs = [vmem] * 9
    operands = [da, w_out, qkvt, ot, lse, bq, bk, w_halves, h1]
    rows = w_out.shape[0]
    scratch = [
        pltpu.VMEM((cols, tokens), BF16),
        pltpu.VMEM((rows, tokens), BF16),
        pltpu.VMEM((lse.shape[0], tokens), F32),
        pltpu.VMEM((heads, tokens, HEAD_DIM), BF16),
        pltpu.VMEM((heads, tokens, HEAD_DIM), BF16),
        pltpu.VMEM((heads, HEAD_DIM, tokens), F32),
        pltpu.VMEM((heads, HEAD_DIM, tokens), F32),
    ] + sum_scratch(tokens, width // 2)
    if fused:
        hidden = down.shape[1] // 2
        operands += [gu, down, small, f_late]
        in_specs += [pl.BlockSpec(memory_space=pl.ANY)] * 2 + [vmem] * 2
        out_shape += [
            jax.ShapeDtypeStruct((width // 8, cols + rows), F32),
            jax.ShapeDtypeStruct((width // 4, 2 * hidden), F32),
            jax.ShapeDtypeStruct((width // 4, hidden), F32),
            jax.ShapeDtypeStruct(small.shape, F32),
            jax.ShapeDtypeStruct((2, *f_late.shape), BF16),
        ]
        scratch += [pltpu.VMEM((width, cols + rows), BF16)]
        scratch += depth_scratch(width // 8, cols + rows)
        scratch += depth_scratch(width // 4, 2 * hidden) + depth_scratch(width // 4, hidden)
        scratch += [pltpu.VMEM((8, 8, width), F32), pltpu.SemaphoreType.DMA((2, 2, 8))]
        scratch += [
            pltpu.VMEM((8, 8, width), F32),
            pltpu.VMEM((4, 8, width), F32),
            pltpu.SemaphoreType.DMA((2, 8)),
            pltpu.SemaphoreType.DMA((2, 4)),
        ]
        scratch += [pltpu.SemaphoreType.DMA((2, 4))]
        scratch += [pltpu.VMEM(f_late.shape, BF16), pltpu.SemaphoreType.DMA((2, 3, F_LATE))]
    else:
        out_shape += [jax.ShapeDtypeStruct((width, cols + rows), BF16)]
    return pl.pallas_call(
        functools.partial(attn_bwd_kernel, heads, fused),
        name="attn_bwd",
        in_specs=in_specs,
        out_shape=out_shape,
        scratch_shapes=scratch,
        compiler_params=params(collective_id=1, has_side_effects=True),
        cost_estimate=COST,
    )(*operands)


def lane_iota(rows):
    return lax.broadcasted_iota(jnp.int32, (rows, LANES), 1)


def column(values, lane, number):
    return jnp.sum(jnp.where(lane == number, values, 0.0), axis=1, keepdims=True)


def routing(logits, aux, types):
    lane = lane_iota(logits.shape[0])
    is_type = lane < types
    shown = jnp.where(is_type, logits, NEG)
    e = jnp.exp(shown - jnp.max(shown, axis=1, keepdims=True))
    probs = e / jnp.sum(e, axis=1, keepdims=True)
    aux = aux.astype(F32)
    first = column(aux, lane, types).astype(jnp.int32)
    second = column(aux, lane, types + 1).astype(jnp.int32)
    mask = jnp.where((lane == first) | (lane == second), 1.0, 0.0)
    return lane, probs, mask


def const_mix(logits, lane, types, c):
    l0 = column(logits, lane, types + 2 * c)
    l1 = column(logits, lane, types + 2 * c + 1)
    top = jnp.maximum(l0, l1)
    e0, e1 = jnp.exp(l0 - top), jnp.exp(l1 - top)
    total = e0 + e1
    return e0 / total, e1 / total


def post_attn_kernel(types, group, idx_ref, x_ref, *refs):
    ots, wos = refs[:group], refs[group : 2 * group]
    gain_ref, wcat_ref, aux_ref, wprev_ref = refs[2 * group : 2 * group + 4]
    x1_ref, h2_ref, lg_ref, ps_ref, wo_scr, ot_scr = refs[2 * group + 4 :]
    rows = ots[0].shape[0]
    me = idx_ref[0]

    @pl.when(pl.program_id(0) == 0)
    def _():
        for m in range(group):
            wo_scr[pl.ds(pl.multiple_of((me ^ m) * rows, HEAD_DIM), rows), :] = wos[m][...]
        ps_ref[...] = jnp.zeros_like(ps_ref)

    for m in range(group):
        ot_scr[pl.ds(pl.multiple_of((me ^ m) * rows, HEAD_DIM), rows), :] = ots[m][...]
    x1 = x_ref[...].astype(F32) + tn(ot_scr[...], wo_scr[...])
    x1_ref[...] = x1
    h2 = (x1 * rms_factor(x1) * gain_ref[...]).astype(BF16)
    h2_ref[...] = h2
    lg = nn(h2, wcat_ref[...]) + nn(aux_ref[...], wprev_ref[...])
    lg_ref[...] = lg
    _, probs, _ = routing(lg, aux_ref[...], types)
    ps_ref[0:1, :] += jnp.sum(probs, axis=0, keepdims=True)


def post_attention(me, x, ots, wos, gain, wcat, aux, wprev, types):
    tokens, width = x.shape
    rows = ots[0].shape[0]
    group = len(ots)
    block = lambda i, *_: (i, 0)
    fixed = lambda i, *_: (0, 0)
    grid_spec = pltpu.PrefetchScalarGridSpec(
        num_scalar_prefetch=1,
        grid=(tokens // TB,),
        in_specs=[pl.BlockSpec((TB, width), block)]
        + [pl.BlockSpec((rows, TB), lambda i, *_: (0, i))] * group
        + [pl.BlockSpec((rows, width), fixed)] * group
        + [
            pl.BlockSpec((1, width), fixed),
            pl.BlockSpec((width, LANES), fixed),
            pl.BlockSpec((TB, LANES), block),
            pl.BlockSpec((LANES, LANES), fixed),
        ],
        out_specs=[
            pl.BlockSpec((TB, width), block),
            pl.BlockSpec((TB, width), block),
            pl.BlockSpec((TB, LANES), block),
            pl.BlockSpec((8, LANES), fixed),
        ],
        scratch_shapes=[pltpu.VMEM((group * rows, width), BF16), pltpu.VMEM((group * rows, TB), BF16)],
    )
    return pl.pallas_call(
        functools.partial(post_attn_kernel, types, group),
        name="post_attn",
        grid_spec=grid_spec,
        out_shape=(
            jax.ShapeDtypeStruct((tokens, width), F32),
            jax.ShapeDtypeStruct((tokens, width), BF16),
            jax.ShapeDtypeStruct((tokens, LANES), F32),
            jax.ShapeDtypeStruct((8, LANES), F32),
        ),
        compiler_params=params(),
        cost_estimate=COST,
    )(me, x, *ots, *wos, gain, wcat, aux, wprev)


def front_kernel(heads, types, x_ref, gain_ref, wt_ref, bq_ref, bk_ref, wo_ref, gain2_ref, wcat_ref, aux_ref, wprev_ref, part_ref, wgu_ref, wd_ref, h1_ref, qkvt_ref, ot_ref, lse_ref, x1_ref, h2_ref, lg_ref, ps_ref, count_ref, pgu_ref, pd_ref, *scratch):
    kn_ref, oall, wall, osems, wsems, esems, *counts = scratch
    tokens, width = x_ref.shape
    rows = ot_ref.shape[0]
    d = HEAD_DIM
    t = lax.axis_index("tensor")
    half, partner, other = neighbours()
    near, far, _ = depth_place()
    across = {"expert": 1 - lax.axis_index("expert")}
    low = lax.axis_index("dp") % 2
    greet([partner, other, across, near, far])
    count = HopSum(*counts, [across, near, far])
    count.partial[0] = part_ref[...]
    count.start()

    mine = pl.ds(pl.multiple_of(t * rows, d), rows)
    others = pl.ds(pl.multiple_of(((t + 2) % 4) * rows, d), rows)

    def spread(ref, cols, sems, n):
        return [
            pltpu.make_async_remote_copy(
                src_ref=ref.at[place, cols],
                dst_ref=ref.at[place, cols],
                send_sem=sems.at[0, stage, n],
                recv_sem=sems.at[1, stage, n],
                device_id=device,
                device_id_type=MESH,
            )
            for stage, (place, device) in enumerate(((mine, partner), (mine, other), (others, partner)))
        ]

    pieces = []
    for ref, land in ((wgu_ref, pgu_ref), (wd_ref, pd_ref)):
        step = ref.shape[0] // 4
        for n in range(2):
            pieces.append((ref, land, pl.ds(pl.multiple_of((2 * low + n) * step, step), step)))

    def weight_copy(n, stage):
        ref, land, place = pieces[n]
        return pltpu.make_async_remote_copy(
            src_ref=(land if stage else ref).at[place, :],
            dst_ref=land.at[place, :],
            send_sem=esems.at[0, stage, n],
            recv_sem=esems.at[1, stage, n],
            device_id=near if stage else across,
            device_id_type=MESH,
        )

    def weight_on(n):
        weight_copy(n, 0).wait_recv()
        weight_copy(n, 1).start()

    for n in range(4):
        weight_copy(n, 0).start()
    wall[mine, :] = wo_ref[...]
    every = slice(None)
    for c in spread(wall, every, wsems, 0)[:2]:
        c.start()

    for r0 in range(0, tokens, QF):
        project_rows(r0, heads, x_ref, gain_ref, wt_ref, h1_ref, qkvt_ref, kn_ref)
    count.add(0)
    ps_ref[...] = jnp.zeros_like(ps_ref)

    def block_cols(n):
        return slice(n * QF, (n + 1) * QF)

    def attend(n):
        o = jnp.concatenate([attend_rows(n * QF, h, bq_ref, bk_ref, qkvt_ref, kn_ref, lse_ref) for h in range(heads)], axis=0)
        ot_ref[:, block_cols(n)] = o
        oall[mine, block_cols(n)] = o
        for c in spread(oall, block_cols(n), osems, n)[:2]:
            c.start()

    def onward(ref, cols, sems, n):
        copies = spread(ref, cols, sems, n)
        copies[1].wait_recv()
        copies[2].start()

    def post(n):
        copies = spread(oall, block_cols(n), osems, n)
        copies[0].wait_recv()
        copies[2].wait_recv()
        for r0 in range(n * QF, (n + 1) * QF, TB):
            r = slice(r0, r0 + TB)
            x1 = x_ref[r, :].astype(F32) + tn(oall[:, r], wall[...])
            x1_ref[r, :] = x1
            h2 = (x1 * rms_factor(x1) * gain2_ref[...]).astype(BF16)
            h2_ref[r, :] = h2
            lg = nn(h2, wcat_ref[...]) + nn(aux_ref[r, :], wprev_ref[...])
            lg_ref[r, :] = lg
            _, probs, _ = routing(lg, aux_ref[r, :], types)
            ps_ref[0:1, :] += jnp.sum(probs, axis=0, keepdims=True)

    blocks = tokens // QF
    for n in range(blocks):
        attend(n)
        if n == 0:
            onward(wall, every, wsems, 0)
            count.add(1)
        if n == 1:
            weight_on(0)
            count_ref[...] = count.add(2)
        if n == 2:
            copies = spread(wall, every, wsems, 0)
            copies[0].wait_recv()
            copies[2].wait_recv()
            weight_on(1)
        if n >= 1:
            onward(oall, block_cols(n - 1), osems, n - 1)
        if n >= 2:
            post(n - 2)
    onward(oall, block_cols(blocks - 1), osems, blocks - 1)
    weight_on(2)
    post(blocks - 2)
    weight_on(3)
    post(blocks - 1)
    for n in range(4):
        weight_copy(n, 1).wait_recv()
        for stage in range(2):
            weight_copy(n, stage).wait_send()
    for c in spread(wall, every, wsems, 0):
        c.wait_send()
    for n in range(blocks):
        for c in spread(oall, block_cols(n), osems, n):
            c.wait_send()
    count.close()


def front_pass(x, gain, w_t, bq, bk, w_out, gain2, wcat, aux, wprev, part, wgu, wd, heads, types):
    tokens, width = x.shape
    cols, rows = w_t.shape[0], w_out.shape[0]
    lse_rows = -(-heads // 8) * 8
    blocks = tokens // QF
    vmem = pl.BlockSpec(memory_space=pltpu.VMEM)
    anywhere = pl.BlockSpec(memory_space=pl.ANY)
    return pl.pallas_call(
        functools.partial(front_kernel, heads, types),
        name="front",
        in_specs=[vmem] * 11 + [anywhere] * 2,
        out_specs=[vmem] * 9 + [anywhere] * 2,
        out_shape=(
            jax.ShapeDtypeStruct((tokens, width), BF16),
            jax.ShapeDtypeStruct((cols, tokens), BF16),
            jax.ShapeDtypeStruct((rows, tokens), BF16),
            jax.ShapeDtypeStruct((lse_rows, tokens), F32),
            jax.ShapeDtypeStruct((tokens, width), F32),
            jax.ShapeDtypeStruct((tokens, width), BF16),
            jax.ShapeDtypeStruct((tokens, LANES), F32),
            jax.ShapeDtypeStruct((8, LANES), F32),
            jax.ShapeDtypeStruct(part.shape, F32),
            jax.ShapeDtypeStruct(wgu.shape, BF16),
            jax.ShapeDtypeStruct(wd.shape, BF16),
        ),
        scratch_shapes=[
            pltpu.VMEM((heads, tokens, HEAD_DIM), BF16),
            pltpu.VMEM((4 * rows, tokens), BF16),
            pltpu.VMEM((4 * rows, width), BF16),
            pltpu.SemaphoreType.DMA((2, 3, blocks)),
            pltpu.SemaphoreType.DMA((2, 3, 1)),
            pltpu.SemaphoreType.DMA((2, 2, 4)),
        ]
        + hop_scratch(3, *part.shape),
        compiler_params=params(collective_id=3, has_side_effects=True),
        cost_estimate=COST,
    )(x, gain, w_t, bq, bk, w_out, gain2, wcat, aux, wprev, part, wgu, wd)


def expert_kernel(types, experts, halves, idx_ref, h2_ref, dy_ref, lg_ref, aux_ref, *refs):
    wgus, wds = refs[:experts], refs[experts : 2 * experts]
    eye_ref = refs[2 * experts]
    keep_ref, send_ref, gh_ref, du_ref, dlt_ref, acc_ref = refs[2 * experts + 1 :]
    me, half = idx_ref[0], idx_ref[1]
    hidden = wds[0].shape[0]
    h2, dy = h2_ref[...], dy_ref[...]
    lane, probs, mask = routing(lg_ref[...], aux_ref[...], types)
    gates = probs * mask
    dprobs = jnp.zeros_like(probs)
    for s in range(experts):
        e = me ^ s
        gate_col = column(gates, lane, e)
        u = nn(h2, wgus[s][...])
        dhr = nt(dy, wds[s][...])
        g, up = u[:, :hidden], u[:, hidden:]
        sig = 1.0 / (1.0 + jnp.exp(-g))
        silu = g * sig
        hid = silu * up
        gh_ref[s, :, :] = (hid * gate_col).astype(BF16)
        dg = jnp.sum(hid * dhr, axis=1, keepdims=True)
        dprobs = dprobs + jnp.where(lane == e, dg * mask, 0.0)
        dh = dhr * gate_col
        dgate = dh * up * sig * (1.0 + g * (1.0 - sig))
        dup = dh * silu
        du_ref[s, :, :hidden] = dgate.astype(BF16)
        du_ref[s, :, hidden:] = dup.astype(BF16)
        part = nt(du_ref[s, :, :], wgus[s][...])
        if s == 0:
            acc_ref[...] = part
        else:
            acc_ref[...] += part
    dlog = probs * (dprobs - jnp.sum(probs * dprobs, axis=1, keepdims=True))
    hi, lo = split_hi_lo(dlog)
    dlt_ref[...] = nt(eye_ref[...], hi) + nt(eye_ref[...], lo)
    half_cols = acc_ref.shape[1] // halves
    keep_ref[...] = acc_ref[:, pl.ds(pl.multiple_of(half * half_cols, LANES), half_cols)].astype(BF16)
    send_ref[...] = acc_ref[:, pl.ds(pl.multiple_of((1 - half) * half_cols, LANES), half_cols)].astype(BF16)


def experts_pass(idx, h2, dy, lg, aux, wgus, wds, eye, types):
    tokens, width = h2.shape
    experts = len(wgus)
    hidden = wds[0].shape[0]
    erows = eye.shape[0]
    block = lambda i, *_: (i, 0)
    fixed = lambda i, *_: (0, 0)
    grid_spec = pltpu.PrefetchScalarGridSpec(
        num_scalar_prefetch=1,
        grid=(tokens // TB,),
        in_specs=[
            pl.BlockSpec((TB, width), block),
            pl.BlockSpec((TB, width), block),
            pl.BlockSpec((TB, LANES), block),
            pl.BlockSpec((TB, LANES), block),
        ]
        + [pl.BlockSpec((width, 2 * hidden), fixed, pipeline_mode=pl.Buffered(1))] * experts
        + [pl.BlockSpec((hidden, width), fixed, pipeline_mode=pl.Buffered(1))] * experts
        + [pl.BlockSpec((erows, LANES), fixed)],
        out_specs=[
            pl.BlockSpec((TB, width // 2), block),
            pl.BlockSpec((TB, width // 2), block),
            pl.BlockSpec((experts, TB, hidden), lambda i, *_: (0, i, 0)),
            pl.BlockSpec((experts, TB, 2 * hidden), lambda i, *_: (0, i, 0)),
            pl.BlockSpec((erows, TB), lambda i, *_: (0, i)),
        ],
        scratch_shapes=[pltpu.VMEM((TB, width), F32)],
    )
    return pl.pallas_call(
        functools.partial(expert_kernel, types, experts, 2),
        name="experts",
        grid_spec=grid_spec,
        out_shape=(
            jax.ShapeDtypeStruct((tokens, width // 2), BF16),
            jax.ShapeDtypeStruct((tokens, width // 2), BF16),
            jax.ShapeDtypeStruct((experts, tokens, hidden), BF16),
            jax.ShapeDtypeStruct((experts, tokens, 2 * hidden), BF16),
            jax.ShapeDtypeStruct((erows, tokens), F32),
        ),
        compiler_params=params(),
        cost_estimate=COST,
    )(idx, h2, dy, lg, aux, *wgus, *wds, eye)


def down_kernel(experts, idx_ref, gh_ref, *refs):
    wds, (keep_ref, send_ref, acc_ref) = refs[:experts], refs[experts:]
    me, half = idx_ref[0], idx_ref[1]
    for s in range(experts):
        part = nn(gh_ref[s, :, :], wds[s][...])
        if s == 0:
            acc_ref[...] = part
        else:
            acc_ref[...] += part
    half_cols = keep_ref.shape[1]
    keep_ref[...] = acc_ref[:, pl.ds(pl.multiple_of(half * half_cols, LANES), half_cols)].astype(BF16)
    send_ref[...] = acc_ref[:, pl.ds(pl.multiple_of((1 - half) * half_cols, LANES), half_cols)].astype(BF16)


def down_pass(idx, gh, wds):
    experts, tokens, hidden = gh.shape
    width = wds[0].shape[1]
    block = lambda i, *_: (i, 0)
    fixed = lambda i, *_: (0, 0)
    grid_spec = pltpu.PrefetchScalarGridSpec(
        num_scalar_prefetch=1,
        grid=(tokens // TB,),
        in_specs=[pl.BlockSpec((experts, TB, hidden), lambda i, *_: (0, i, 0))]
        + [pl.BlockSpec((hidden, width), fixed, pipeline_mode=pl.Buffered(1))] * experts,
        out_specs=[pl.BlockSpec((TB, width // 2), block)] * 2,
        scratch_shapes=[pltpu.VMEM((TB, width), F32)],
    )
    return pl.pallas_call(
        functools.partial(down_kernel, experts),
        name="down",
        grid_spec=grid_spec,
        out_shape=(jax.ShapeDtypeStruct((tokens, width // 2), BF16),) * 2,
        compiler_params=params(),
        cost_estimate=COST,
    )(idx, gh, *wds)


def middle_kernel(types, ffn, total_tokens, idx_ref, mine_ref, theirs_ref, x1_ref, dy_ref, lg_ref, aux_ref, dlt_ref, eye_ref, count_ref, gain_ref, wcat_ref, vt_ref, wprevt_ref, dx1_ref, da_ref, gp_ref, g1_ref, g2_ref, g3_ref, g4_ref, scr_ref):
    half = idx_ref[1]
    half_cols = mine_ref.shape[1]
    scr_ref[:, pl.ds(pl.multiple_of(half * half_cols, LANES), half_cols)] = mine_ref[...]
    scr_ref[:, pl.ds(pl.multiple_of((1 - half) * half_cols, LANES), half_cols)] = theirs_ref[...]
    first = pl.program_id(0) == 0

    @pl.when(first)
    def _():
        for ref in (g1_ref, g2_ref, g3_ref, g4_ref):
            ref[...] = jnp.zeros_like(ref)

    gain = gain_ref[...]
    x1 = x1_ref[...]
    r2 = rms_factor(x1)
    n2 = x1 * r2
    h2 = (n2 * gain).astype(BF16)
    dyb = dy_ref[...]
    dy = dyb.astype(F32)
    lg = lg_ref[...]
    lane, probs, mask = routing(lg, aux_ref[...], types)
    gates = probs * mask
    a = jnp.sum(dy * h2.astype(F32), axis=1, keepdims=True)
    b = nn(dyb, vt_ref[...])
    coef = column(gates, lane, ffn + 1)
    dprobs = jnp.where(lane == ffn + 1, a, 0.0)
    dlc = jnp.zeros_like(probs)
    vcoef = jnp.zeros_like(probs)
    for c in range(2):
        m0, m1 = const_mix(lg, lane, types, c)
        g = column(gates, lane, ffn + 2 + c)
        bc = column(b, lane, c)
        dprobs = dprobs + jnp.where(lane == ffn + 2 + c, m0 * a + m1 * bc, 0.0)
        dm0, dm1 = g * a, g * bc
        inner = m0 * dm0 + m1 * dm1
        dlc = dlc + jnp.where(lane == types + 2 * c, m0 * (dm0 - inner), 0.0)
        dlc = dlc + jnp.where(lane == types + 2 * c + 1, m1 * (dm1 - inner), 0.0)
        coef = coef + g * m0
        vcoef = vcoef + jnp.where(lane == c, g * m1, 0.0)
    dprobs = dprobs * mask + count_ref[...] * (AUX_WEIGHT * types / (2.0 * total_tokens * total_tokens))
    dlog = probs * (dprobs - jnp.sum(probs * dprobs, axis=1, keepdims=True))
    hi, lo = split_hi_lo(dlt_ref[...])
    dl = dlog + dlc + tn(hi, eye_ref[...]) + tn(lo, eye_ref[...])
    dhi, dlo = split_hi_lo(dl)
    dh2 = scr_ref[...].astype(F32) + coef * dy + nt(dhi, wcat_ref[...]) + nt(dlo, wcat_ref[...])
    dn2 = dh2 * gain
    dx1 = dy + r2 * (dn2 - n2 * jnp.mean(dn2 * n2, axis=1, keepdims=True))
    dx1_ref[...] = dx1
    da_ref[...] = dx1.astype(BF16)
    gp_ref[...] = nn(dhi, wprevt_ref[...]) + nn(dlo, wprevt_ref[...])
    g1_ref[...] += tn(dhi, h2) + tn(dlo, h2)
    vhi, vlo = split_hi_lo(vcoef)
    g2_ref[...] += tn(vhi, dyb) + tn(vlo, dyb)
    g3_ref[0:1, :] += jnp.sum(dh2 * n2, axis=0, keepdims=True)
    g4_ref[...] += tn(aux_ref[...], dhi) + tn(aux_ref[...], dlo)


def middle_pass(idx, mine, theirs, x1, dy, lg, aux, dlt, eye, count, gain, wcat, vt, wprevt, types, ffn, total_tokens):
    tokens, width = x1.shape
    erows = dlt.shape[0]
    block = lambda i, *_: (i, 0)
    fixed = lambda i, *_: (0, 0)
    grid_spec = pltpu.PrefetchScalarGridSpec(
        num_scalar_prefetch=1,
        grid=(tokens // TB,),
        in_specs=[
            pl.BlockSpec((TB, width // 2), block),
            pl.BlockSpec((TB, width // 2), block),
            pl.BlockSpec((TB, width), block),
            pl.BlockSpec((TB, width), block),
            pl.BlockSpec((TB, LANES), block),
            pl.BlockSpec((TB, LANES), block),
            pl.BlockSpec((erows, TB), lambda i, *_: (0, i)),
            pl.BlockSpec((erows, LANES), fixed),
            pl.BlockSpec((1, LANES), fixed),
            pl.BlockSpec((1, width), fixed),
            pl.BlockSpec((width, LANES), fixed),
            pl.BlockSpec((width, LANES), fixed),
            pl.BlockSpec((LANES, LANES), fixed),
        ],
        out_specs=[
            pl.BlockSpec((TB, width), block),
            pl.BlockSpec((TB, width), block),
            pl.BlockSpec((TB, LANES), block),
            pl.BlockSpec((LANES, width), fixed),
            pl.BlockSpec((LANES, width), fixed),
            pl.BlockSpec((8, width), fixed),
            pl.BlockSpec((LANES, LANES), fixed),
        ],
        scratch_shapes=[pltpu.VMEM((TB, width), BF16)],
    )
    return pl.pallas_call(
        functools.partial(middle_kernel, types, ffn, total_tokens),
        name="middle",
        grid_spec=grid_spec,
        out_shape=(
            jax.ShapeDtypeStruct((tokens, width), F32),
            jax.ShapeDtypeStruct((tokens, width), BF16),
            jax.ShapeDtypeStruct((tokens, LANES), F32),
            jax.ShapeDtypeStruct((LANES, width), F32),
            jax.ShapeDtypeStruct((LANES, width), F32),
            jax.ShapeDtypeStruct((8, width), F32),
            jax.ShapeDtypeStruct((LANES, LANES), F32),
        ),
        compiler_params=params(),
        cost_estimate=COST,
    )(idx, mine, theirs, x1, dy, lg, aux, dlt, eye, count, gain, wcat, vt, wprevt)


def layer_kernel(types, experts, total_tokens, blocks, h2_ref, dy_ref, lg_ref, aux_ref, x1_ref, *refs):
    wgus, wds = refs[:experts], refs[experts : 2 * experts]
    eye_ref, count_ref, gain_ref, wcat_ref, vt_ref, wprevt_ref = refs[2 * experts : 2 * experts + 6]
    dx1_ref, da_ref, gp_ref, base_ref, flate_ref, gu_ref, down_ref, g1_ref, g2_ref, g3_ref, g4_ref = refs[2 * experts + 6 : 2 * experts + 17]
    scratch = refs[2 * experts + 17 :]
    early = blocks - F_LATE
    acc_gu, acc_down, du_ref, gh_ref, dres, fres = scratch[:6]
    dkeep, dsend, dfirst, dsecond, dsems, fkeep, fsend, ffirst, fsecond, fsems, lpart, lfirst, lsecond, lsems = scratch[6:20]
    xg, xd, xsems = scratch[20:]
    step = pl.program_id(0)
    hidden = wds[0].shape[0]
    lrows = lpart.shape[2]
    me = lax.axis_index("expert")
    half, partner, other = neighbours()
    half_cols = dkeep.shape[1]
    dx = GroupSum(dkeep, dsend, dfirst, dsecond, dres, dsems)
    ff = GroupSum(fkeep, fsend, ffirst, fsecond, fres, fsems)
    small = SmallSum(lpart, lfirst, lsecond, lsems)
    across = {"expert": 1 - me}
    _, _, order = depth_place()
    block = gu_ref.shape[0] // 4
    first_rows = [pl.ds(pl.multiple_of(order[k] * block, block), block) for k in range(2)]

    def first_copies(k):
        return [
            pltpu.make_async_remote_copy(
                src_ref=src.at[first_rows[k], pl.ds(cols, cols)],
                dst_ref=dst.at[k],
                send_sem=xsems.at[0, n, k],
                recv_sem=xsems.at[1, n, k],
                device_id=across,
                device_id_type=MESH,
            )
            for n, (src, dst, cols) in enumerate(((gu_ref, xg, 2 * hidden), (down_ref, xd, hidden)))
        ]

    @pl.when(step == 0)
    def _():
        greet((partner, other, across))
        for ref in (acc_gu, acc_down, g1_ref, g2_ref, g3_ref, g4_ref):
            ref[...] = jnp.zeros_like(ref)

    def own_cols(which):
        return pl.ds(pl.multiple_of(which * half_cols, LANES), half_cols)

    @pl.when(step < blocks)
    def _():
        i = step
        h2, dy = h2_ref[...], dy_ref[...]
        lane, probs, mask = routing(lg_ref[...], aux_ref[...], types)
        gates = probs * mask
        dprobs = jnp.zeros_like(probs)
        for s in range(experts):
            e = (me + s) % experts
            gate_col = column(gates, lane, e)
            u = nn(h2, wgus[s][...])
            dhr = nt(dy, wds[s][...])
            g, up = u[:, :hidden], u[:, hidden:]
            sig = 1.0 / (1.0 + jnp.exp(-g))
            silu = g * sig
            hid = silu * up
            gh_ref[:, s * hidden : (s + 1) * hidden] = (hid * gate_col).astype(BF16)
            dg = jnp.sum(hid * dhr, axis=1, keepdims=True)
            dprobs = dprobs + jnp.where(lane == e, dg * mask, 0.0)
            dh = dhr * gate_col
            base = 2 * s * hidden
            du_ref[:, base : base + hidden] = (dh * up * sig * (1.0 + g * (1.0 - sig))).astype(BF16)
            du_ref[:, base + hidden : base + 2 * hidden] = (dh * silu).astype(BF16)
        dlog = probs * (dprobs - jnp.sum(probs * dprobs, axis=1, keepdims=True))
        hi, lo = split_hi_lo(dlog)
        lpart[0, i] = (nt(eye_ref[...], hi) + nt(eye_ref[...], lo))[:lrows]
        small.start(i)
        rows = dx.rows(i)
        for which, place in ((1 - half, dsend), (half, dkeep)):
            cols = own_cols(which)
            total = nt(du_ref[:, : 2 * hidden], wgus[0][cols, :])
            for s in range(1, experts):
                total = total + nt(du_ref[:, 2 * s * hidden : 2 * (s + 1) * hidden], wgus[s][cols, :])
            place[rows, :] = total.astype(BF16)
            if place is dsend:
                dx.to_partner(i).start()
        for which, place in ((1 - half, fsend), (half, fkeep)):
            cols = own_cols(which)
            total = nn(gh_ref[:, :hidden], wds[0][:, cols])
            for s in range(1, experts):
                total = total + nn(gh_ref[:, s * hidden : (s + 1) * hidden], wds[s][:, cols])
            place[rows, :] = total.astype(BF16)
            if place is fsend:
                ff.to_partner(i).start()
        small.pair(i)
        dx.pair(i)
        acc_gu[...] += tn(h2, du_ref[...])

        @pl.when(i < early)
        def _():
            ff.pair(i)

        @pl.when(i >= early)
        def _():
            ff.pair_only(i)

        acc_down[...] += tn(dy, gh_ref[...])

    @pl.when(step == blocks)
    def _():
        gu_ref[...] = acc_gu[...].astype(BF16)
        down_ref[...] = acc_down[...].astype(BF16)
        for c in first_copies(0) + first_copies(1):
            c.start()
        dx.finish(0)

    @pl.when(step >= blocks)
    def _():
        i = step - blocks

        @pl.when(i + 1 < blocks)
        def _():
            dx.finish(i + 1)

        @pl.when(i < early)
        def _():
            ff.finish(i)

        rows = dx.rows(i)
        dlt = small.finish(i)
        gain = gain_ref[...]
        x1 = x1_ref[...]
        r2 = rms_factor(x1)
        n2 = x1 * r2
        h2 = h2_ref[...]
        dyb = dy_ref[...]
        dy = dyb.astype(F32)
        lg = lg_ref[...]
        lane, probs, mask = routing(lg, aux_ref[...], types)
        gates = probs * mask
        a = jnp.sum(dy * h2.astype(F32), axis=1, keepdims=True)
        b = nn(dyb, vt_ref[...])
        coef = column(gates, lane, experts + 1)
        dprobs = jnp.where(lane == experts + 1, a, 0.0)
        dlc = jnp.zeros_like(probs)
        vcoef = jnp.zeros_like(probs)
        for c in range(2):
            m0, m1 = const_mix(lg, lane, types, c)
            g = column(gates, lane, experts + 2 + c)
            bc = column(b, lane, c)
            dprobs = dprobs + jnp.where(lane == experts + 2 + c, m0 * a + m1 * bc, 0.0)
            dm0, dm1 = g * a, g * bc
            inner = m0 * dm0 + m1 * dm1
            dlc = dlc + jnp.where(lane == types + 2 * c, m0 * (dm0 - inner), 0.0)
            dlc = dlc + jnp.where(lane == types + 2 * c + 1, m1 * (dm1 - inner), 0.0)
            coef = coef + g * m0
            vcoef = vcoef + jnp.where(lane == c, g * m1, 0.0)
        dprobs = dprobs * mask + count_ref[...] * (AUX_WEIGHT * types / (2.0 * total_tokens * total_tokens))
        dlog = probs * (dprobs - jnp.sum(probs * dprobs, axis=1, keepdims=True))
        hi, lo = split_hi_lo(dlt)
        eye = eye_ref[:lrows, :]
        dl = dlog + dlc + tn(hi, eye) + tn(lo, eye)
        dhi, dlo = split_hi_lo(dl)
        vhi, vlo = split_hi_lo(vcoef)
        gp_ref[...] = nn(dhi, wprevt_ref[...]) + nn(dlo, wprevt_ref[...])
        g1_ref[...] += tn(dhi, h2) + tn(dlo, h2)
        g2_ref[...] += tn(vhi, dyb) + tn(vlo, dyb)
        g4_ref[...] += tn(aux_ref[...], dhi) + tn(aux_ref[...], dlo)
        dh2 = coef * dy + nt(dhi, wcat_ref[...]) + nt(dlo, wcat_ref[...])
        dx.close(i)
        dh2 = dh2 + jnp.concatenate([dres[0, rows, :], dres[1, rows, :]], axis=1).astype(F32)
        g3_ref[0:1, :] += jnp.sum(dh2 * n2, axis=0, keepdims=True)
        dn2 = dh2 * gain
        dx1 = dy + r2 * (dn2 - n2 * jnp.mean(dn2 * n2, axis=1, keepdims=True))
        dx1_ref[...] = dx1
        da_ref[...] = dx1.astype(BF16)
        vt = vt_ref[...]
        base_ref[...] = x1 + coef * h2.astype(F32) + nt(vhi, vt) + nt(vlo, vt)

        @pl.when(i < early)
        def _():
            ff.close(i)
            base_ref[...] += jnp.concatenate([fres[0, rows, :], fres[1, rows, :]], axis=1).astype(F32)

        @pl.when(i >= early)
        def _():
            ff.to_partner(i).wait_send()
            flate_ref[...] = fkeep[rows, :]

    @pl.when(step == 2 * blocks - 1)
    def _():
        for k in range(2):
            for c, ref, got in zip(first_copies(k), (gu_ref, down_ref), (xg, xd)):
                c.wait()
                own = (first_rows[k], slice(0, got.shape[2]))
                ref[own] = (ref[own].astype(F32) + got[k].astype(F32)).astype(BF16)


def layer_pass(h2, dy, lg, aux, x1, wgus, wds, eye, count, gain, wcat, vt, wprevt, types, total_tokens):
    tokens, width = h2.shape
    experts = len(wgus)
    hidden = wds[0].shape[0]
    blocks = tokens // CHUNK
    lrows = -(-types // 8) * 8
    both = lambda i: (i % blocks, 0)
    late = lambda i: (jnp.maximum(i - blocks, 0), 0)
    fixed = lambda i: (0, 0)
    once = dict(pipeline_mode=pl.Buffered(1))
    small_sums = [
        pltpu.VMEM((2, blocks, lrows, CHUNK), F32),
        pltpu.VMEM((blocks, lrows, CHUNK), F32),
        pltpu.VMEM((blocks, lrows, CHUNK), F32),
        pltpu.SemaphoreType.DMA((2, 2, blocks)),
    ]
    return pl.pallas_call(
        functools.partial(layer_kernel, types, experts, total_tokens, blocks),
        name="layer",
        grid=(2 * blocks,),
        in_specs=[
            pl.BlockSpec((CHUNK, width), both),
            pl.BlockSpec((CHUNK, width), both),
            pl.BlockSpec((CHUNK, LANES), both),
            pl.BlockSpec((CHUNK, LANES), both),
            pl.BlockSpec((CHUNK, width), late),
        ]
        + [pl.BlockSpec((width, 2 * hidden), fixed, **once)] * experts
        + [pl.BlockSpec((hidden, width), fixed, **once)] * experts
        + [
            pl.BlockSpec(eye.shape, fixed),
            pl.BlockSpec((1, LANES), fixed),
            pl.BlockSpec((1, width), fixed),
            pl.BlockSpec((width, LANES), fixed),
            pl.BlockSpec((width, LANES), fixed),
            pl.BlockSpec((LANES, LANES), fixed),
        ],
        out_specs=[
            pl.BlockSpec((CHUNK, width), late),
            pl.BlockSpec((CHUNK, width), late),
            pl.BlockSpec((CHUNK, LANES), late),
            pl.BlockSpec((CHUNK, width), late),
            pl.BlockSpec((CHUNK, width // 2), lambda i: (jnp.maximum(i - (2 * blocks - F_LATE), 0), 0)),
            pl.BlockSpec((width, 2 * experts * hidden), fixed, **once),
            pl.BlockSpec((width, experts * hidden), fixed, **once),
            pl.BlockSpec((LANES, width), fixed),
            pl.BlockSpec((LANES, width), fixed),
            pl.BlockSpec((8, width), fixed),
            pl.BlockSpec((LANES, LANES), fixed),
        ],
        out_shape=(
            jax.ShapeDtypeStruct((tokens, width), F32),
            jax.ShapeDtypeStruct((tokens, width), BF16),
            jax.ShapeDtypeStruct((tokens, LANES), F32),
            jax.ShapeDtypeStruct((tokens, width), F32),
            jax.ShapeDtypeStruct((F_LATE * CHUNK, width // 2), BF16),
            jax.ShapeDtypeStruct((width, 2 * experts * hidden), BF16),
            jax.ShapeDtypeStruct((width, experts * hidden), BF16),
            jax.ShapeDtypeStruct((LANES, width), F32),
            jax.ShapeDtypeStruct((LANES, width), F32),
            jax.ShapeDtypeStruct((8, width), F32),
            jax.ShapeDtypeStruct((LANES, LANES), F32),
        ),
        scratch_shapes=[
            pltpu.VMEM((width, 2 * experts * hidden), F32),
            pltpu.VMEM((width, experts * hidden), F32),
            pltpu.VMEM((CHUNK, 2 * experts * hidden), BF16),
            pltpu.VMEM((CHUNK, experts * hidden), BF16),
            pltpu.VMEM((2, tokens, width // 2), BF16),
            pltpu.VMEM((2, tokens - F_LATE * CHUNK, width // 2), BF16),
        ]
        + sum_scratch(tokens, width // 2)
        + sum_scratch(tokens, width // 2)
        + small_sums
        + [
            pltpu.VMEM((2, width // 4, 2 * hidden), BF16),
            pltpu.VMEM((2, width // 4, hidden), BF16),
            pltpu.SemaphoreType.DMA((2, 2, 2)),
        ],
        compiler_params=params(collective_id=2, has_side_effects=True),
        cost_estimate=COST,
    )(h2, dy, lg, aux, x1, *wgus, *wds, eye, count, gain, wcat, vt, wprevt)


def output_kernel(types, ffn, f_ref, x1_ref, h2_ref, lg_ref, aux_ref, v_ref, out_ref):
    halves = jnp.concatenate([f_ref[0], f_ref[1]], axis=1)
    lg = lg_ref[...]
    lane, probs, mask = routing(lg, aux_ref[...], types)
    gates = probs * mask
    coef = column(gates, lane, ffn + 1)
    out = x1_ref[...] + halves.astype(F32)
    for c in range(2):
        m0, m1 = const_mix(lg, lane, types, c)
        g = column(gates, lane, ffn + 2 + c)
        coef = coef + g * m0
        out = out + (g * m1) * v_ref[c : c + 1, :]
    out_ref[...] = out + coef * h2_ref[...].astype(F32)


def output_pass(f, x1, h2, lg, aux, v, types, ffn):
    tokens, width = x1.shape
    block = lambda i: (i, 0)
    return pl.pallas_call(
        functools.partial(output_kernel, types, ffn),
        name="output",
        grid=(tokens // TB,),
        in_specs=[
            pl.BlockSpec((2, TB, width // 2), lambda i: (0, i, 0)),
            pl.BlockSpec((TB, width), block),
            pl.BlockSpec((TB, width), block),
            pl.BlockSpec((TB, LANES), block),
            pl.BlockSpec((TB, LANES), block),
            pl.BlockSpec((8, width), lambda i: (0, 0)),
        ],
        out_specs=pl.BlockSpec((TB, width), block),
        out_shape=jax.ShapeDtypeStruct((tokens, width), F32),
        compiler_params=params(),
        cost_estimate=COST,
    )(f, x1, h2, lg, aux, v)


def last_kernel(d_ref, x_ref, dx1_ref, gain_ref, out_ref):
    halves = jnp.concatenate([d_ref[0], d_ref[1]], axis=1)
    x = x_ref[...].astype(F32)
    r1 = rms_factor(x)
    n1 = x * r1
    dn1 = halves.astype(F32) * gain_ref[...]
    out_ref[...] = dx1_ref[...] + r1 * (dn1 - n1 * jnp.mean(dn1 * n1, axis=1, keepdims=True))


def last_pass(dh1, x, dx1, gain):
    tokens, width = x.shape
    block = lambda i: (i, 0)
    return pl.pallas_call(
        last_kernel,
        name="last",
        grid=(tokens // TB,),
        in_specs=[
            pl.BlockSpec((2, TB, width // 2), lambda i: (0, i, 0)),
            pl.BlockSpec((TB, width), block),
            pl.BlockSpec((TB, width), block),
            pl.BlockSpec((1, width), lambda i: (0, 0)),
        ],
        out_specs=pl.BlockSpec((TB, width), block),
        out_shape=jax.ShapeDtypeStruct((tokens, width), F32),
        compiler_params=params(),
        cost_estimate=COST,
    )(dh1, x, dx1, gain)


def tail_kernel(first_late, d_ref, x_ref, dx1_ref, gain_ref, base_ref, f_ref, grad_ref, out_ref):
    last_kernel(d_ref, x_ref, dx1_ref, gain_ref, grad_ref)
    late = pl.program_id(0) >= first_late

    @pl.when(late)
    def _():
        out_ref[...] = base_ref[...] + jnp.concatenate([f_ref[0], f_ref[1]], axis=1).astype(F32)

    @pl.when(jnp.logical_not(late))
    def _():
        out_ref[...] = base_ref[...]


def tail_pass(dh1, x, dx1, gain, base, f_late):
    tokens, width = x.shape
    first_late = tokens // CHUNK - F_LATE
    block = lambda i: (i, 0)
    return pl.pallas_call(
        functools.partial(tail_kernel, first_late),
        name="tail",
        grid=(tokens // CHUNK,),
        in_specs=[
            pl.BlockSpec((2, CHUNK, width // 2), lambda i: (0, i, 0)),
            pl.BlockSpec((CHUNK, width), block),
            pl.BlockSpec((CHUNK, width), block),
            pl.BlockSpec((1, width), lambda i: (0, 0)),
            pl.BlockSpec((CHUNK, width), block),
            pl.BlockSpec((2, CHUNK, width // 2), lambda i: (0, jnp.maximum(i - first_late, 0), 0)),
        ],
        out_specs=[pl.BlockSpec((CHUNK, width), block)] * 2,
        out_shape=(jax.ShapeDtypeStruct((tokens, width), F32),) * 2,
        compiler_params=params(),
        cost_estimate=COST,
    )(dh1, x, dx1, gain, base, f_late)


def tie(value, *others):
    return lax.optimization_barrier((value, *others))[0]


def add_all(own, got):
    total = own.astype(F32)
    for g in got:
        total = total + g.astype(F32)
    return total.astype(BF16)


def pair_sum(keep, send):
    return (keep.astype(F32) + swap(send, "tensor", 1).astype(F32)).astype(BF16)


def group_sum(part):
    bit = 2
    while bit < lax.axis_size("tensor"):
        part = (part.astype(F32) + swap(part, "tensor", bit).astype(F32)).astype(BF16)
        bit *= 2
    return part, swap(part, "tensor", 1)


def scatter_sum(a, axes):
    steps = []
    for axis in axes:
        bits = lax.axis_size(axis).bit_length() - 1
        steps += [(axis, b) for b in reversed(range(bits))]
    a = a.reshape((2,) * len(steps) + (-1, a.shape[-1]))
    order = [s for axis in reversed(axes) for s in reversed(steps) if s[0] == axis]
    left = list(steps)
    for axis, bit in order:
        dim = left.index((axis, bit))
        mine = (lax.axis_index(axis) >> bit) & 1
        got = swap(lax.dynamic_index_in_dim(a, 1 - mine, dim, keepdims=False), axis, 1 << bit)
        a = (lax.dynamic_index_in_dim(a, mine, dim, keepdims=False).astype(F32) + got.astype(F32)).astype(BF16)
        left.remove((axis, bit))
    return a


def gather_group(a):
    out = [a]
    bit = lax.axis_size("tensor") // 2
    parts = {0: a}
    while bit:
        parts.update({m | bit: swap(p, "tensor", bit) for m, p in list(parts.items())})
        bit //= 2
    return [parts[m] for m in range(len(parts))]


def per_device(hidden_in, prev_logits, routes, block_ids, cotangent, gain_attn, w_qkv, w_out, gain_moe, w_router, w_prev, w_const, v_const, w_gate_up, w_down):
    tokens, width = hidden_in.shape
    types = w_router.shape[1]
    experts = lax.axis_size("expert")
    heads = w_out.shape[0] // HEAD_DIM
    hidden = w_down.shape[1]
    total_tokens = tokens * lax.axis_size(("dp", "expert"))
    t_index, x_index = lax.axis_index("tensor"), lax.axis_index("expert")
    t_idx = jnp.stack([t_index, t_index % 2]).astype(jnp.int32)
    x_idx = jnp.stack([x_index, t_index % 2]).astype(jnp.int32)

    gain_first = gain_attn.astype(F32)[None]
    gain_second = gain_moe.astype(F32)[None]
    consts = w_const.transpose(1, 0, 2).reshape(width, 4)
    wcat = jnp.pad(jnp.concatenate([w_router, consts], axis=1), ((0, 0), (0, LANES - types - 4)))
    aux = jnp.concatenate([prev_logits, routes.astype(BF16)], axis=1)
    aux = jnp.pad(aux, ((0, 0), (0, LANES - types - 2)))
    wprev = jnp.pad(w_prev, ((0, LANES - types), (0, LANES - types)))
    wprevt = jnp.pad(w_prev.T, ((0, LANES - types), (0, LANES - types)))
    vt = jnp.pad(v_const.T, ((0, 0), (0, LANES - 2)))
    vrows = jnp.pad(v_const.astype(F32), ((0, 6), (0, 0)))
    erows = -(-types // 16) * 16
    eye = jnp.eye(erows, LANES, dtype=BF16)
    lanes = jnp.arange(LANES, dtype=jnp.int32)
    chosen = (routes[:, :, None] == lanes[None, None, :]).astype(F32)
    count = jnp.sum(chosen, axis=(0, 1))[None]
    bq, bk = block_ids, block_ids.reshape(tokens, 1)

    w_halves = w_qkv.T.reshape(-1, 2, width // 2).transpose(1, 0, 2)

    wgu, wd = w_gate_up[0].reshape(width, 2 * hidden), w_down[0]
    fused = experts == 2 and lax.axis_size("dp") == 4 and lax.axis_size("tensor") == 4
    if fused:
        part = jnp.broadcast_to(count, (8, LANES))
        h1, qkvt, ot, lse, x1, h2, lg, prob_part, count, *peer = front_pass(
            hidden_in, gain_first, w_qkv.T, bq, bk, w_out, gain_second, wcat, aux, wprev, part, wgu, wd, heads, types
        )
        wgus, wds, count = [wgu, peer[0]], [wd, peer[1]], count[:1]
    else:
        wgus = [wgu] + [swap(wgu, "expert", s) for s in range(1, experts)]
        wds = [wd] + [swap(wd, "expert", s) for s in range(1, experts)]
        h1, qkvt, ot, lse = attention_forward(hidden_in, gain_first, w_qkv.T, bq, bk, heads)
        ots, wos = gather_group(ot), gather_group(w_out)
        x1, h2, lg, prob_part = post_attention(t_idx, hidden_in, ots, wos, gain_second, wcat, aux, wprev, types)
        count = sum_over(tie(count, wds[-1]), ("expert", "dp"))
    srows = -(-(types + 4) // 8) * 8
    prow = -(-types // 8) * 8

    def small_rows(g1, g2, g3, g4):
        wide = lambda a: jnp.pad(a, ((0, 0), (0, width - LANES)))
        rows = jnp.concatenate([g1[:srows], g2[:8], g3, wide(g4[:prow]), wide(prob_part)], axis=0)
        return jnp.pad(rows, ((0, 64 - rows.shape[0]), (0, 0)))

    if fused:
        dx1, da, gp, base, f_late, gu, down, *g = layer_pass(
            h2, cotangent, lg, aux, x1, wgus, wds, eye, count, gain_second, wcat, vt, wprevt, types, total_tokens
        )
        dh1, gain_all, grads, grad_gate_up, grad_down, small, f_late = attention_backward(
            da, w_out, qkvt, ot, lse, bq, bk, w_halves, h1, heads, gu, down, small_rows(*g), f_late
        )
        grad_input, output = tail_pass(dh1, hidden_in, dx1, gain_first, base, f_late)
    else:
        keep, send, gh, du, dlt = experts_pass(x_idx, h2, cotangent, lg, aux, wgus, wds, eye, types)
        mine, theirs = group_sum(pair_sum(keep, send))
        dlt = sum_over(dlt, ("tensor",))
        fkeep, fsend = down_pass(x_idx, gh, wds)
        gu_parts = [tn(h2, du[e]).astype(BF16) for e in range(experts)]
        down_parts = [tn(cotangent, gh[e]).astype(BF16) for e in range(experts)]
        f_mine, f_theirs = group_sum(pair_sum(fkeep, fsend))
        first, second = jnp.where(t_index % 2 == 0, f_mine, f_theirs), jnp.where(t_index % 2 == 0, f_theirs, f_mine)
        f = jnp.stack([first, second])
        dx1, da, gp, *g = middle_pass(
            x_idx, mine, theirs, x1, cotangent, lg, aux, dlt, eye, count, gain_second, wcat, vt, wprevt, types, experts, total_tokens
        )
        dh1, gain_part, grads = attention_backward(da, w_out, qkvt, ot, lse, bq, bk, w_halves, h1, heads)
        grads = scatter_sum(grads, ("dp", "expert")).astype(F32)
        gu_got = [swap(gu_parts[e], "expert", e) for e in range(1, experts)]
        down_got = [swap(down_parts[e], "expert", e) for e in range(1, experts)]
        grad_gate_up = scatter_sum(add_all(gu_parts[0], gu_got), ("dp",)).astype(F32)
        grad_down = scatter_sum(add_all(down_parts[0], down_got), ("dp",)).astype(F32)
        gain_all = sum_over(gain_part, ("tensor", "expert", "dp"))
        small = sum_over(small_rows(*g), ("expert", "dp"))
        grad_input = last_pass(dh1, hidden_in, dx1, gain_first)
        output = output_pass(f, x1, h2, lg, aux, vrows, types, experts)

    grad_gain = gain_all[0] / gain_first[0]
    grad_qkv, grad_out = grads[:, : w_qkv.shape[1]], grads[:, w_qkv.shape[1] :].T

    prob_all = small[srows + 16 + prow, :types]
    count_all = count[0, :types]
    balance_loss = types * jnp.sum((count_all / (2.0 * total_tokens)) * prob_all / total_tokens)
    load = jnp.stack([count_all / (2.0 * tokens), prob_all / tokens])
    return (
        output,
        grad_input,
        gp[:, :types],
        grad_gain,
        grad_qkv,
        grad_out,
        small[srows + 8],
        small[:types].T,
        small[srows + 16 : srows + 16 + types, :types],
        small[types : types + 4].reshape(2, 2, width).transpose(0, 2, 1),
        small[srows : srows + 2],
        grad_gate_up.reshape(1, -1, 2, hidden),
        grad_down.T[None],
        balance_loss,
        load,
    )


def solution(mesh):
    tok = P(("dp", "expert"), None)
    return jax.shard_map(
        per_device,
        mesh=mesh,
        in_specs=(
            tok,
            tok,
            tok,
            tok,
            tok,
            P(),
            P(None, "tensor"),
            P("tensor", None),
            P(),
            P(),
            P(),
            P(),
            P(),
            P("expert", None, None, "tensor"),
            P("expert", "tensor", None),
        ),
        out_specs=(
            tok,
            tok,
            tok,
            P(),
            P(("dp", "expert"), "tensor"),
            P("tensor", ("dp", "expert")),
            P(),
            P(),
            P(),
            P(),
            P(),
            P("expert", "dp", None, "tensor"),
            P("expert", "tensor", "dp"),
            P(),
            P(),
        ),
        check_vma=False,
    )
```

```python
import functools

import jax
import jax.numpy as jnp
from jax import lax
from jax.experimental import pallas as pl
from jax.experimental.pallas import tpu as pltpu
from jax.sharding import PartitionSpec as P

HEAD_DIM = 64
EPSILON = 1e-06
AUX_WEIGHT = 0.01
SCORE_SCALE = 0.125
MAX_BLOCK = 256
LANES = 128
QB = 256
QF = 512
TB = 256
NEG = -1e30
F32 = jnp.float32
BF16 = jnp.bfloat16
MESH = pl.DeviceIdType.MESH
VMEM_LIMIT = 54 * 1024 * 1024
COST = pl.CostEstimate(flops=1000, bytes_accessed=1000, transcendentals=0)


def params(**more):
    return pltpu.CompilerParams(vmem_limit_bytes=VMEM_LIMIT, **more)


def nn(a, b):
    return lax.dot_general(a, b, (((1,), (0,)), ((), ())), preferred_element_type=F32)


def nt(a, b):
    return lax.dot_general(a, b, (((1,), (1,)), ((), ())), preferred_element_type=F32)


def tn(a, b):
    return lax.dot_general(a, b, (((0,), (0,)), ((), ())), preferred_element_type=F32)


def split_hi_lo(a):
    hi = a.astype(BF16)
    return hi, (a - hi.astype(F32)).astype(BF16)


def rms_factor(values):
    return lax.rsqrt(jnp.mean(values * values, axis=-1, keepdims=True) + EPSILON)


def swap(a, axis, bit):
    n = lax.axis_size(axis)
    return lax.ppermute(a, axis, [(i, i ^ bit) for i in range(n)])


def sum_over(a, axes):
    for axis in axes:
        bit = 1
        while bit < lax.axis_size(axis):
            a = a + swap(a, axis, bit)
            bit *= 2
    return a


def key_range(q0, rows, tokens):
    return min(tokens, q0 + rows + MAX_BLOCK)


def project_rows(r0, heads, x_ref, gain_ref, wt_ref, h1_ref, qkvt_ref, kn_ref):
    d = HEAD_DIM
    rows = slice(r0, r0 + QF)
    xb = x_ref[rows, :].astype(F32)
    h1 = (xb * rms_factor(xb) * gain_ref[...]).astype(BF16)
    h1_ref[rows, :] = h1
    qkvt = nt(wt_ref[...], h1)
    for h in range(heads):
        base = h * 3 * d
        q = qkvt[base : base + d].astype(BF16).astype(F32) * SCORE_SCALE
        qkvt_ref[base : base + d, rows] = q.astype(BF16)
        qkvt_ref[base + d : base + 3 * d, rows] = qkvt[base + d : base + 3 * d].astype(BF16)
        kn_ref[h, rows, :] = qkvt[base + d : base + 2 * d].T.astype(BF16)


def attend_rows(q0, h, bq_ref, bk_ref, qkvt_ref, kn_ref, lse_ref):
    tokens = qkvt_ref.shape[1]
    d = HEAD_DIM
    base = h * 3 * d
    cols = slice(q0, q0 + QF)
    top = key_range(q0, QF, tokens)
    s = nn(kn_ref[h, :top, :], qkvt_ref[base : base + d, cols])
    parts = [jnp.where(bk_ref[q0:top, :] <= bq_ref[:, cols], s[q0:], NEG)]
    if q0:
        parts = [s[:q0]] + parts
    m = functools.reduce(jnp.maximum, [jnp.max(a, axis=0, keepdims=True) for a in parts])
    ps = [jnp.exp(a - m) for a in parts]
    total = functools.reduce(jnp.add, [jnp.sum(p, axis=0, keepdims=True) for p in ps])
    p = jnp.concatenate([p.astype(BF16) for p in ps], axis=0)
    acc = nn(qkvt_ref[base + 2 * d : base + 3 * d, :top], p)
    lse_ref[h : h + 1, cols] = m + jnp.log(total)
    return (acc / total).astype(BF16)


def attn_fwd_kernel(heads, x_ref, gain_ref, wt_ref, bq_ref, bk_ref, h1_ref, qkvt_ref, ot_ref, lse_ref, kn_ref):
    tokens = x_ref.shape[0]
    d = HEAD_DIM
    for r0 in range(0, tokens, QF):
        project_rows(r0, heads, x_ref, gain_ref, wt_ref, h1_ref, qkvt_ref, kn_ref)
    for h in range(heads):
        for q0 in range(0, tokens, QF):
            ot_ref[h * d : (h + 1) * d, q0 : q0 + QF] = attend_rows(q0, h, bq_ref, bk_ref, qkvt_ref, kn_ref, lse_ref)


def attention_forward(x, gain, w_t, bq, bk, heads):
    tokens, width = x.shape
    cols = w_t.shape[0]
    lse_rows = -(-heads // 8) * 8
    return pl.pallas_call(
        functools.partial(attn_fwd_kernel, heads),
        name="attn_fwd",
        out_shape=(
            jax.ShapeDtypeStruct((tokens, width), BF16),
            jax.ShapeDtypeStruct((cols, tokens), BF16),
            jax.ShapeDtypeStruct((heads * HEAD_DIM, tokens), BF16),
            jax.ShapeDtypeStruct((lse_rows, tokens), F32),
        ),
        scratch_shapes=[pltpu.VMEM((heads, tokens, HEAD_DIM), BF16)],
        compiler_params=params(),
        cost_estimate=COST,
    )(x, gain, w_t, bq, bk)


CHUNK = 256
F_LATE = 6
X_EARLY = 1


def neighbours():
    t = lax.axis_index("tensor")
    return t % 2, {"tensor": t + 1 - 2 * (t % 2)}, {"tensor": (t + 2) % 4}


def greet(devices):
    barrier = pltpu.get_barrier_semaphore()
    for device in devices:
        pl.semaphore_signal(barrier, inc=1, device_id=device, device_id_type=MESH)
    pl.semaphore_wait(barrier, len(devices))


def each(count, step):
    def body(i, carry):
        step(i)
        return carry

    lax.fori_loop(0, count, body, 0)


class GroupSum:
    def __init__(self, keep, send, first, second, result, sems):
        self.keep, self.send, self.first, self.second, self.result, self.sems = keep, send, first, second, result, sems
        self.half, self.partner, self.other = neighbours()

    def rows(self, i):
        return pl.ds(pl.multiple_of(i * CHUNK, CHUNK), CHUNK)

    def copy(self, stage, i, src, dst, device):
        return pltpu.make_async_remote_copy(
            src_ref=src,
            dst_ref=dst,
            send_sem=self.sems.at[0, stage, i],
            recv_sem=self.sems.at[1, stage, i],
            device_id=device,
            device_id_type=MESH,
        )

    def to_partner(self, i):
        r = self.rows(i)
        return self.copy(0, i, self.send.at[r, :], self.first.at[r, :], self.partner)

    def to_other(self, i):
        r = self.rows(i)
        return self.copy(1, i, self.keep.at[r, :], self.second.at[r, :], self.other)

    def back(self, i):
        place = self.result.at[self.half, self.rows(i), :]
        return self.copy(2, i, place, place, self.partner)

    def pair_only(self, i):
        self.to_partner(i).wait_recv()
        r = self.rows(i)
        self.keep[r, :] = (self.keep[r, :].astype(F32) + self.first[r, :].astype(F32)).astype(BF16)

    def pair(self, i):
        self.pair_only(i)
        self.to_other(i).start()

    def finish(self, i):
        self.to_other(i).wait_recv()
        r = self.rows(i)
        self.result[self.half, r, :] = (self.keep[r, :].astype(F32) + self.second[r, :].astype(F32)).astype(BF16)
        self.back(i).start()

    def close(self, i):
        self.back(i).wait_recv()
        if self.send is not None:
            self.to_partner(i).wait_send()
        self.to_other(i).wait_send()
        self.back(i).wait_send()


class SmallSum:
    def __init__(self, part, first, second, sems):
        self.part, self.first, self.second, self.sems = part, first, second, sems
        _, self.partner, self.other = neighbours()

    def copy(self, stage, i, landing, device):
        return pltpu.make_async_remote_copy(
            src_ref=self.part.at[stage, i],
            dst_ref=landing.at[i],
            send_sem=self.sems.at[0, stage, i],
            recv_sem=self.sems.at[1, stage, i],
            device_id=device,
            device_id_type=MESH,
        )

    def start(self, i):
        self.copy(0, i, self.first, self.partner).start()

    def pair(self, i):
        self.copy(0, i, self.first, self.partner).wait_recv()
        self.part[1, i] = self.part[0, i] + self.first[i]
        self.copy(1, i, self.second, self.other).start()

    def finish(self, i):
        self.copy(1, i, self.second, self.other).wait_recv()
        self.copy(0, i, self.first, self.partner).wait_send()
        self.copy(1, i, self.second, self.other).wait_send()
        return self.part[1, i] + self.second[i]


class HopSum:
    def __init__(self, partial, landed, sems, devices):
        self.partial, self.landed, self.sems, self.devices = partial, landed, sems, devices

    def hop(self, n):
        return pltpu.make_async_remote_copy(
            src_ref=self.partial.at[n],
            dst_ref=self.landed.at[n],
            send_sem=self.sems.at[0, n],
            recv_sem=self.sems.at[1, n],
            device_id=self.devices[n],
            device_id_type=MESH,
        )

    def start(self):
        self.hop(0).start()

    def add(self, n):
        self.hop(n).wait_recv()
        total = self.partial[n] + self.landed[n]
        if n + 1 < len(self.devices):
            self.partial[n + 1] = total
            self.hop(n + 1).start()
        return total

    def close(self):
        for n in range(len(self.devices)):
            self.hop(n).wait_send()


def hop_scratch(hops, rows, width):
    return [pltpu.VMEM((hops, rows, width), F32), pltpu.VMEM((hops, rows, width), F32), pltpu.SemaphoreType.DMA((2, hops))]


def replica(n):
    place = (lax.axis_index("dp") * 2 + lax.axis_index("expert") + n) % 8
    return {"dp": place // 2, "expert": place % 2}, place


def all_replicas():
    return [replica(n)[0] for n in range(1, 8)]


class ReplicaSum:
    def __init__(self, own, landed, result, sems):
        self.own, self.landed, self.result, self.sems = own, landed, result, sems

    def copy(self, stage, n):
        device, place = replica(n)
        _, me = replica(0)
        rows = lambda block: pl.ds(pl.multiple_of(block * 8, 8), 8)
        src, dst = ((self.own.at[rows(place), :], self.landed.at[me]), (self.result.at[rows(me), :], self.result.at[rows(me), :]))[stage]
        return pltpu.make_async_remote_copy(
            src_ref=src,
            dst_ref=dst,
            send_sem=self.sems.at[0, stage, n],
            recv_sem=self.sems.at[1, stage, n],
            device_id=device,
            device_id_type=MESH,
        )

    def start(self):
        for n in range(1, 8):
            self.copy(0, n).start()

    def share(self):
        _, me = replica(0)
        rows = pl.ds(pl.multiple_of(me * 8, 8), 8)
        self.landed[me] = self.own[rows, :]
        for n in range(1, 8):
            self.copy(0, n).wait_recv()
        total = self.landed[0]
        for n in range(1, 8):
            total = total + self.landed[n]
        self.result[rows, :] = total
        for n in range(1, 8):
            self.copy(1, n).start()

    def close(self):
        for n in range(1, 8):
            self.copy(1, n).wait_recv()
            for stage in range(2):
                self.copy(stage, n).wait_send()


class EverywhereSum:
    def __init__(self, first, second, fsems, ssems):
        self.first, self.second, self.fsems, self.ssems = first, second, fsems, ssems
        self.t = lax.axis_index("tensor")

    def copy(self, buffer, sems, place, n, device):
        return pltpu.make_async_remote_copy(
            src_ref=buffer.at[place],
            dst_ref=buffer.at[place],
            send_sem=sems.at[0, n],
            recv_sem=sems.at[1, n],
            device_id=device,
            device_id_type=MESH,
        )

    def outer(self):
        return [self.copy(self.first, self.fsems, replica(0)[1], n, replica(n)[0]) for n in range(1, 8)]

    def inner(self):
        return [self.copy(self.second, self.ssems, self.t, n, {"tensor": (self.t + n) % 4}) for n in range(1, 4)]

    def start(self, value):
        self.first[replica(0)[1]] = value
        for c in self.outer():
            c.start()

    def share(self):
        for c in self.outer():
            c.wait_recv()
        total = self.first[0]
        for n in range(1, 8):
            total = total + self.first[n]
        self.second[self.t] = total
        for c in self.inner():
            c.start()

    def finish(self):
        for c in self.inner():
            c.wait_recv()
        for c in self.outer() + self.inner():
            c.wait_send()
        return self.second[0] + self.second[1] + (self.second[2] + self.second[3])


def depth_place():
    z = lax.axis_index("dp")
    low, high = z % 2, z // 2
    order = [2 * (1 - high) + 1 - low, 2 * high + 1 - low, 2 * (1 - high) + low, z]
    return {"dp": z + 1 - 2 * low}, {"dp": (z + 2) % 4}, order


class DepthSum:
    def __init__(self, own, across, landed, xsems, zsems, sources, device):
        self.own, self.across, self.landed, self.xsems, self.zsems = own, across, landed, xsems, zsems
        self.sources, self.device = sources, device
        self.near, self.far, _ = depth_place()

    def x_copy(self, k):
        return pltpu.make_async_remote_copy(
            src_ref=self.sources[k],
            dst_ref=self.across.at[k],
            send_sem=self.xsems.at[0, k],
            recv_sem=self.xsems.at[1, k],
            device_id=self.device,
            device_id_type=MESH,
        )

    def z_copy(self, k):
        return pltpu.make_async_remote_copy(
            src_ref=self.own.at[k],
            dst_ref=self.landed.at[k],
            send_sem=self.zsems.at[0, k],
            recv_sem=self.zsems.at[1, k],
            device_id=self.near if k < 2 else self.far,
            device_id_type=MESH,
        )

    def pass_on(self, k):
        total = self.own[k].astype(F32)
        if self.sources[k] is not None:
            self.x_copy(k).wait_recv()
            total = total + self.across[k].astype(F32)
        for came in {2: (0,), 3: (1, 2)}.get(k, ()):
            self.z_copy(came).wait_recv()
            total = total + self.landed[came].astype(F32)
        if k < 3:
            self.own[k] = total.astype(BF16)
            self.z_copy(k).start()
        return total

    def close(self):
        for k in range(4):
            if self.sources[k] is not None:
                self.x_copy(k).wait_send()
            if k < 3:
                self.z_copy(k).wait_send()


def depth_scratch(rows, cols):
    return [
        pltpu.VMEM((4, rows, cols), BF16),
        pltpu.VMEM((4, rows, cols), BF16),
        pltpu.VMEM((3, rows, cols), BF16),
        pltpu.SemaphoreType.DMA((2, 4)),
        pltpu.SemaphoreType.DMA((2, 3)),
    ]


def sum_scratch(tokens, half_cols, sends=True):
    return [pltpu.VMEM((tokens, half_cols), BF16)] * (4 if sends else 3) + [pltpu.SemaphoreType.DMA((2, 3, tokens // CHUNK))]


def attn_bwd_kernel(heads, fused, da_ref, wo_ref, qkvt_ref, ot_ref, lse_ref, bq_ref, bk_ref, wq_ref, h1_ref, *refs):
    if fused:
        gu_ref, down_ref, small_ref, flate_ref = refs[:4]
        dres_ref, gain_ref, gsum_ref, gusum_ref, dosum_ref, smallsum_ref, fres_ref = refs[4:11]
        scratch = refs[11:]
    else:
        dres_ref, gain_ref, gsum_ref = refs[:3]
        scratch = refs[3:]
    dqkvt_ref, dot_ref, delta_ref, kn_ref, vn_ref, dk_ref, dv_ref, dkeep, dsend, dfirst, dsecond, dsems = scratch[:12]
    tokens, width = da_ref.shape
    d = HEAD_DIM
    cols_all = dqkvt_ref.shape[0]
    chunks = tokens // CHUNK
    dh = GroupSum(dkeep, dsend, dfirst, dsecond, dres_ref, dsems)
    half, partner, other = neighbours()
    if fused:
        glocal, *rest = scratch[12:]
        gparts, uparts, dparts, sparts, nparts, (lsems,) = rest[:5], rest[5:10], rest[10:15], rest[15:17], rest[17:21], rest[21:22]
        fsecond, fsems = rest[22:]
        ff = GroupSum(flate_ref, None, None, fsecond, fres_ref, fsems)
        hidden = dparts[0].shape[2]
        x = lax.axis_index("expert")
        near, far, order = depth_place()
        block, piece = width // 4, width // 8
        across = {"expert": 1 - x}
        t = lax.axis_index("tensor")
        greet([{"tensor": (t + n) % 4} for n in range(1, 4)] + all_replicas())

        def block_rows(k):
            return pl.ds(pl.multiple_of(order[k] * block, block), block)

        def pieces(k, place):
            return pl.ds(pl.multiple_of(order[k] * block + place * piece, piece), piece)

        gate_up = DepthSum(*uparts, [None] * X_EARLY + [gu_ref.at[block_rows(k), pl.ds(2 * hidden, 2 * hidden)] for k in range(X_EARLY, 4)], across)
        down = DepthSum(*dparts, [None] * X_EARLY + [down_ref.at[block_rows(k), pl.ds(hidden, hidden)] for k in range(X_EARLY, 4)], across)
        attn = DepthSum(*gparts, [glocal.at[pieces(k, 1 - x), :] for k in range(4)], across)
        small = ReplicaSum(small_ref, sparts[0], smallsum_ref, sparts[1])
        total_gain = EverywhereSum(*nparts)

        def local_copies(k):
            return [
                pltpu.make_async_copy(gu_ref.at[block_rows(k), pl.ds(0, 2 * hidden)], gate_up.own.at[k], lsems.at[0, k]),
                pltpu.make_async_copy(down_ref.at[block_rows(k), pl.ds(0, hidden)], down.own.at[k], lsems.at[1, k]),
            ]

        def pass_on(k):
            for c in local_copies(k):
                c.wait()
            return gate_up.pass_on(k), down.pass_on(k)

        for n in range(F_LATE):
            ff.to_other(n).start()
        small.start()
        for k in range(4):
            for c in local_copies(k):
                c.start()
            if k >= X_EARLY:
                gate_up.x_copy(k).start()
                down.x_copy(k).start()
    else:
        glocal = gsum_ref
        greet([partner, other])

    def project(i):
        rows = pl.ds(pl.multiple_of(i * CHUNK, CHUNK), CHUNK)
        dot = nt(wo_ref[...], da_ref[rows, :]).astype(BF16)
        dot_ref[:, rows] = dot
        prod = dot.astype(F32) * ot_ref[:, rows].astype(F32)
        for h in range(heads):
            base = h * 3 * d
            delta_ref[h : h + 1, rows] = jnp.sum(prod[h * d : (h + 1) * d], axis=0, keepdims=True)
            kn_ref[h, rows, :] = qkvt_ref[base + d : base + 2 * d, rows].astype(F32).T.astype(BF16)
            vn_ref[h, rows, :] = qkvt_ref[base + 2 * d : base + 3 * d, rows].astype(F32).T.astype(BF16)

    each(chunks, project)
    dk_ref[...] = jnp.zeros_like(dk_ref)
    dv_ref[...] = jnp.zeros_like(dv_ref)
    glocal[:, cols_all:] = nn(ot_ref[...], da_ref[...]).T.astype(BF16)

    def query_block(q0):
        def head(h):
            base = h * 3 * d
            orows = pl.ds(h * d, d)
            cols = slice(q0, q0 + QB)
            top = key_range(q0, QB, tokens)
            qt = qkvt_ref[pl.ds(base, d), cols]
            dot = dot_ref[orows, cols]
            s = nn(kn_ref[h, :top, :], qt)
            p = jnp.exp(s - lse_ref[pl.ds(h, 1), cols])
            last = jnp.where(bk_ref[q0:top, :] <= bq_ref[:, cols], p[q0:], 0.0)
            p = jnp.concatenate([p[:q0], last], axis=0) if q0 else last
            dp = nn(vn_ref[h, :top, :], dot)
            ds = (p * (dp - delta_ref[pl.ds(h, 1), cols])).astype(BF16)
            dv_ref[h, :, :top] += nt(dot, p.astype(BF16))
            dk_ref[h, :, :top] += nt(qt, ds)
            dq = nn(qkvt_ref[pl.ds(base + d, d), :top], ds)
            dqkvt_ref[pl.ds(base, d), cols] = (dq * SCORE_SCALE).astype(BF16)

        for h in range(heads):
            head(h)

    def input_grad(i):
        r = dh.rows(i)
        for h in range(heads):
            base = h * 3 * d
            dqkvt_ref[base + d : base + 2 * d, r] = dk_ref[h, :, r].astype(BF16)
            dqkvt_ref[base + 2 * d : base + 3 * d, r] = dv_ref[h, :, r].astype(BF16)
        dqkv = dqkvt_ref[:, r]
        dsend[r, :] = tn(dqkv, wq_ref[1 - half]).astype(BF16)
        dh.to_partner(i).start()
        dkeep[r, :] = tn(dqkv, wq_ref[half]).astype(BF16)
        dh.pair(i)

    if fused:
        pass_on(0)
    for i in reversed(range(chunks)):
        query_block(i * QB)
        if i + 1 < chunks:
            input_grad(i + 1)
        if fused and i == chunks - 3:
            pass_on(1)
        if fused and i == chunks - 5:
            pass_on(2)
        if fused and i == chunks - 5:
            small.share()
        if fused and i == 1:
            for n in range(F_LATE):
                ff.finish(n)
    input_grad(0)
    gain = jnp.zeros((1, width), F32)
    for c0 in range(0, cols_all, 3 * d):
        part = nn(dqkvt_ref[c0 : c0 + 3 * d, :], h1_ref[...])
        w = jnp.concatenate([wq_ref[0, c0 : c0 + 3 * d, :], wq_ref[1, c0 : c0 + 3 * d, :]], axis=1)
        gain = gain + jnp.sum(part * w.astype(F32), axis=0, keepdims=True)
        glocal[:, c0 : c0 + 3 * d] = part.T.astype(BF16)
    gain = jnp.concatenate([gain[:, c : c + LANES] for c in range(0, width, LANES)] + [jnp.zeros((8 - width // LANES, LANES), F32)], axis=0)
    if fused:
        total_gain.start(gain)
        for k in range(4):
            attn.own[k] = glocal[pieces(k, x), :]
            attn.x_copy(k).start()
        each(2, lambda i: dh.finish(chunks - 1 - i))
        attn.pass_on(0)
        attn.pass_on(1)
        total_gain.share()
        each(1, lambda i: dh.finish(chunks - 3 - i))
        gusum_ref[...], dosum_ref[...] = pass_on(3)
        attn.pass_on(2)
        each(5, lambda i: dh.finish(chunks - 4 - i))
        gsum_ref[...] = attn.pass_on(3)
        gain_ref[...] = total_gain.finish()
        for n in range(F_LATE):
            ff.close(n)
        for part in (gate_up, down, attn, small):
            part.close()
    else:
        gain_ref[...] = gain
        each(chunks, lambda i: dh.finish(chunks - 1 - i))
    each(chunks, dh.close)


def attention_backward(da, w_out, qkvt, ot, lse, bq, bk, w_halves, h1, heads, gu=None, down=None, small=None, f_late=None):
    tokens, width = da.shape
    cols = qkvt.shape[0]
    fused = gu is not None
    out_shape = [jax.ShapeDtypeStruct((2, tokens, width // 2), BF16), jax.ShapeDtypeStruct((8, LANES), F32)]
    vmem = pl.BlockSpec(memory_space=pltpu.VMEM)
    in_specs = [vmem] * 9
    operands = [da, w_out, qkvt, ot, lse, bq, bk, w_halves, h1]
    rows = w_out.shape[0]
    scratch = [
        pltpu.VMEM((cols, tokens), BF16),
        pltpu.VMEM((rows, tokens), BF16),
        pltpu.VMEM((lse.shape[0], tokens), F32),
        pltpu.VMEM((heads, tokens, HEAD_DIM), BF16),
        pltpu.VMEM((heads, tokens, HEAD_DIM), BF16),
        pltpu.VMEM((heads, HEAD_DIM, tokens), F32),
        pltpu.VMEM((heads, HEAD_DIM, tokens), F32),
    ] + sum_scratch(tokens, width // 2)
    if fused:
        hidden = down.shape[1] // 2
        operands += [gu, down, small, f_late]
        in_specs += [pl.BlockSpec(memory_space=pl.ANY)] * 2 + [vmem] * 2
        out_shape += [
            jax.ShapeDtypeStruct((width // 8, cols + rows), F32),
            jax.ShapeDtypeStruct((width // 4, 2 * hidden), F32),
            jax.ShapeDtypeStruct((width // 4, hidden), F32),
            jax.ShapeDtypeStruct(small.shape, F32),
            jax.ShapeDtypeStruct((2, *f_late.shape), BF16),
        ]
        scratch += [pltpu.VMEM((width, cols + rows), BF16)]
        scratch += depth_scratch(width // 8, cols + rows)
        scratch += depth_scratch(width // 4, 2 * hidden) + depth_scratch(width // 4, hidden)
        scratch += [pltpu.VMEM((8, 8, width), F32), pltpu.SemaphoreType.DMA((2, 2, 8))]
        scratch += [
            pltpu.VMEM((8, 8, LANES), F32),
            pltpu.VMEM((4, 8, LANES), F32),
            pltpu.SemaphoreType.DMA((2, 8)),
            pltpu.SemaphoreType.DMA((2, 4)),
        ]
        scratch += [pltpu.SemaphoreType.DMA((2, 4))]
        scratch += [pltpu.VMEM(f_late.shape, BF16), pltpu.SemaphoreType.DMA((2, 3, F_LATE))]
    else:
        out_shape += [jax.ShapeDtypeStruct((width, cols + rows), BF16)]
    return pl.pallas_call(
        functools.partial(attn_bwd_kernel, heads, fused),
        name="attn_bwd",
        in_specs=in_specs,
        out_shape=out_shape,
        scratch_shapes=scratch,
        compiler_params=params(collective_id=1, has_side_effects=True),
        cost_estimate=COST,
    )(*operands)


def lane_iota(rows):
    return lax.broadcasted_iota(jnp.int32, (rows, LANES), 1)


def column(values, lane, number):
    return jnp.sum(jnp.where(lane == number, values, 0.0), axis=1, keepdims=True)


def routing(logits, aux, types):
    lane = lane_iota(logits.shape[0])
    is_type = lane < types
    shown = jnp.where(is_type, logits, NEG)
    e = jnp.exp(shown - jnp.max(shown, axis=1, keepdims=True))
    probs = e / jnp.sum(e, axis=1, keepdims=True)
    aux = aux.astype(F32)
    first = column(aux, lane, types).astype(jnp.int32)
    second = column(aux, lane, types + 1).astype(jnp.int32)
    mask = jnp.where((lane == first) | (lane == second), 1.0, 0.0)
    return lane, probs, mask


def const_mix(logits, lane, types, c):
    l0 = column(logits, lane, types + 2 * c)
    l1 = column(logits, lane, types + 2 * c + 1)
    top = jnp.maximum(l0, l1)
    e0, e1 = jnp.exp(l0 - top), jnp.exp(l1 - top)
    total = e0 + e1
    return e0 / total, e1 / total


def post_attn_kernel(types, group, idx_ref, x_ref, *refs):
    ots, wos = refs[:group], refs[group : 2 * group]
    gain_ref, wcat_ref, aux_ref, wprev_ref = refs[2 * group : 2 * group + 4]
    x1_ref, h2_ref, lg_ref, ps_ref, wo_scr, ot_scr = refs[2 * group + 4 :]
    rows = ots[0].shape[0]
    me = idx_ref[0]

    @pl.when(pl.program_id(0) == 0)
    def _():
        for m in range(group):
            wo_scr[pl.ds(pl.multiple_of((me ^ m) * rows, HEAD_DIM), rows), :] = wos[m][...]
        ps_ref[...] = jnp.zeros_like(ps_ref)

    for m in range(group):
        ot_scr[pl.ds(pl.multiple_of((me ^ m) * rows, HEAD_DIM), rows), :] = ots[m][...]
    x1 = x_ref[...].astype(F32) + tn(ot_scr[...], wo_scr[...])
    x1_ref[...] = x1
    h2 = (x1 * rms_factor(x1) * gain_ref[...]).astype(BF16)
    h2_ref[...] = h2
    lg = nn(h2, wcat_ref[...]) + nn(aux_ref[...], wprev_ref[...])
    lg_ref[...] = lg
    _, probs, _ = routing(lg, aux_ref[...], types)
    ps_ref[0:1, :] += jnp.sum(probs, axis=0, keepdims=True)


def post_attention(me, x, ots, wos, gain, wcat, aux, wprev, types):
    tokens, width = x.shape
    rows = ots[0].shape[0]
    group = len(ots)
    block = lambda i, *_: (i, 0)
    fixed = lambda i, *_: (0, 0)
    grid_spec = pltpu.PrefetchScalarGridSpec(
        num_scalar_prefetch=1,
        grid=(tokens // TB,),
        in_specs=[pl.BlockSpec((TB, width), block)]
        + [pl.BlockSpec((rows, TB), lambda i, *_: (0, i))] * group
        + [pl.BlockSpec((rows, width), fixed)] * group
        + [
            pl.BlockSpec((1, width), fixed),
            pl.BlockSpec((width, LANES), fixed),
            pl.BlockSpec((TB, LANES), block),
            pl.BlockSpec((LANES, LANES), fixed),
        ],
        out_specs=[
            pl.BlockSpec((TB, width), block),
            pl.BlockSpec((TB, width), block),
            pl.BlockSpec((TB, LANES), block),
            pl.BlockSpec((8, LANES), fixed),
        ],
        scratch_shapes=[pltpu.VMEM((group * rows, width), BF16), pltpu.VMEM((group * rows, TB), BF16)],
    )
    return pl.pallas_call(
        functools.partial(post_attn_kernel, types, group),
        name="post_attn",
        grid_spec=grid_spec,
        out_shape=(
            jax.ShapeDtypeStruct((tokens, width), F32),
            jax.ShapeDtypeStruct((tokens, width), BF16),
            jax.ShapeDtypeStruct((tokens, LANES), F32),
            jax.ShapeDtypeStruct((8, LANES), F32),
        ),
        compiler_params=params(),
        cost_estimate=COST,
    )(me, x, *ots, *wos, gain, wcat, aux, wprev)


def front_kernel(heads, types, x_ref, gain_ref, wt_ref, bq_ref, bk_ref, wo_ref, gain2_ref, wcat_ref, aux_ref, wprev_ref, part_ref, wgu_ref, wd_ref, h1_ref, qkvt_ref, ot_ref, lse_ref, x1_ref, h2_ref, lg_ref, ps_ref, count_ref, pgu_ref, pd_ref, *scratch):
    kn_ref, oall, wall, osems, wsems, esems, *counts = scratch
    tokens, width = x_ref.shape
    rows = ot_ref.shape[0]
    d = HEAD_DIM
    t = lax.axis_index("tensor")
    half, partner, other = neighbours()
    near, far, _ = depth_place()
    across = {"expert": 1 - lax.axis_index("expert")}
    low = lax.axis_index("dp") % 2
    greet([partner, other, across, near, far])
    count = HopSum(*counts, [across, near, far])
    count.partial[0] = part_ref[...]
    count.start()

    mine = pl.ds(pl.multiple_of(t * rows, d), rows)
    others = pl.ds(pl.multiple_of(((t + 2) % 4) * rows, d), rows)

    def spread(ref, cols, sems, n):
        return [
            pltpu.make_async_remote_copy(
                src_ref=ref.at[place, cols],
                dst_ref=ref.at[place, cols],
                send_sem=sems.at[0, stage, n],
                recv_sem=sems.at[1, stage, n],
                device_id=device,
                device_id_type=MESH,
            )
            for stage, (place, device) in enumerate(((mine, partner), (mine, other), (others, partner)))
        ]

    pieces = []
    for ref, land in ((wgu_ref, pgu_ref), (wd_ref, pd_ref)):
        step = ref.shape[0] // 4
        for n in range(2):
            pieces.append((ref, land, pl.ds(pl.multiple_of((2 * low + n) * step, step), step)))

    def weight_copy(n, stage):
        ref, land, place = pieces[n]
        return pltpu.make_async_remote_copy(
            src_ref=(land if stage else ref).at[place, :],
            dst_ref=land.at[place, :],
            send_sem=esems.at[0, stage, n],
            recv_sem=esems.at[1, stage, n],
            device_id=near if stage else across,
            device_id_type=MESH,
        )

    def weight_on(n):
        weight_copy(n, 0).wait_recv()
        weight_copy(n, 1).start()

    for n in range(4):
        weight_copy(n, 0).start()
    wall[mine, :] = wo_ref[...]
    every = slice(None)
    for c in spread(wall, every, wsems, 0)[:2]:
        c.start()

    for r0 in range(0, tokens, QF):
        project_rows(r0, heads, x_ref, gain_ref, wt_ref, h1_ref, qkvt_ref, kn_ref)
    count.add(0)
    ps_ref[...] = jnp.zeros_like(ps_ref)

    def block_cols(n):
        return slice(n * QF, (n + 1) * QF)

    def attend(n):
        o = jnp.concatenate([attend_rows(n * QF, h, bq_ref, bk_ref, qkvt_ref, kn_ref, lse_ref) for h in range(heads)], axis=0)
        ot_ref[:, block_cols(n)] = o
        oall[mine, block_cols(n)] = o
        for c in spread(oall, block_cols(n), osems, n)[:2]:
            c.start()

    def onward(ref, cols, sems, n):
        copies = spread(ref, cols, sems, n)
        copies[1].wait_recv()
        copies[2].start()

    def post(n):
        copies = spread(oall, block_cols(n), osems, n)
        copies[0].wait_recv()
        copies[2].wait_recv()
        for r0 in range(n * QF, (n + 1) * QF, TB):
            r = slice(r0, r0 + TB)
            x1 = x_ref[r, :].astype(F32) + tn(oall[:, r], wall[...])
            x1_ref[r, :] = x1
            h2 = (x1 * rms_factor(x1) * gain2_ref[...]).astype(BF16)
            h2_ref[r, :] = h2
            lg = nn(h2, wcat_ref[...]) + nn(aux_ref[r, :], wprev_ref[...])
            lg_ref[r, :] = lg
            _, probs, _ = routing(lg, aux_ref[r, :], types)
            ps_ref[0:1, :] += jnp.sum(probs, axis=0, keepdims=True)

    blocks = tokens // QF
    for n in range(blocks):
        attend(n)
        if n == 0:
            onward(wall, every, wsems, 0)
            count.add(1)
        if n == 1:
            weight_on(0)
            count_ref[...] = count.add(2)
        if n == 2:
            copies = spread(wall, every, wsems, 0)
            copies[0].wait_recv()
            copies[2].wait_recv()
            weight_on(1)
        if n >= 1:
            onward(oall, block_cols(n - 1), osems, n - 1)
        if n >= 2:
            post(n - 2)
    onward(oall, block_cols(blocks - 1), osems, blocks - 1)
    weight_on(2)
    post(blocks - 2)
    weight_on(3)
    post(blocks - 1)
    for n in range(4):
        weight_copy(n, 1).wait_recv()
        for stage in range(2):
            weight_copy(n, stage).wait_send()
    for c in spread(wall, every, wsems, 0):
        c.wait_send()
    for n in range(blocks):
        for c in spread(oall, block_cols(n), osems, n):
            c.wait_send()
    count.close()


def front_pass(x, gain, w_t, bq, bk, w_out, gain2, wcat, aux, wprev, part, wgu, wd, heads, types):
    tokens, width = x.shape
    cols, rows = w_t.shape[0], w_out.shape[0]
    lse_rows = -(-heads // 8) * 8
    blocks = tokens // QF
    vmem = pl.BlockSpec(memory_space=pltpu.VMEM)
    anywhere = pl.BlockSpec(memory_space=pl.ANY)
    return pl.pallas_call(
        functools.partial(front_kernel, heads, types),
        name="front",
        in_specs=[vmem] * 11 + [anywhere] * 2,
        out_specs=[vmem] * 9 + [anywhere] * 2,
        out_shape=(
            jax.ShapeDtypeStruct((tokens, width), BF16),
            jax.ShapeDtypeStruct((cols, tokens), BF16),
            jax.ShapeDtypeStruct((rows, tokens), BF16),
            jax.ShapeDtypeStruct((lse_rows, tokens), F32),
            jax.ShapeDtypeStruct((tokens, width), F32),
            jax.ShapeDtypeStruct((tokens, width), BF16),
            jax.ShapeDtypeStruct((tokens, LANES), F32),
            jax.ShapeDtypeStruct((8, LANES), F32),
            jax.ShapeDtypeStruct(part.shape, F32),
            jax.ShapeDtypeStruct(wgu.shape, BF16),
            jax.ShapeDtypeStruct(wd.shape, BF16),
        ),
        scratch_shapes=[
            pltpu.VMEM((heads, tokens, HEAD_DIM), BF16),
            pltpu.VMEM((4 * rows, tokens), BF16),
            pltpu.VMEM((4 * rows, width), BF16),
            pltpu.SemaphoreType.DMA((2, 3, blocks)),
            pltpu.SemaphoreType.DMA((2, 3, 1)),
            pltpu.SemaphoreType.DMA((2, 2, 4)),
        ]
        + hop_scratch(3, *part.shape),
        compiler_params=params(collective_id=3, has_side_effects=True),
        cost_estimate=COST,
    )(x, gain, w_t, bq, bk, w_out, gain2, wcat, aux, wprev, part, wgu, wd)


def expert_kernel(types, experts, halves, idx_ref, h2_ref, dy_ref, lg_ref, aux_ref, *refs):
    wgus, wds = refs[:experts], refs[experts : 2 * experts]
    eye_ref = refs[2 * experts]
    keep_ref, send_ref, gh_ref, du_ref, dlt_ref, acc_ref = refs[2 * experts + 1 :]
    me, half = idx_ref[0], idx_ref[1]
    hidden = wds[0].shape[0]
    h2, dy = h2_ref[...], dy_ref[...]
    lane, probs, mask = routing(lg_ref[...], aux_ref[...], types)
    gates = probs * mask
    dprobs = jnp.zeros_like(probs)
    for s in range(experts):
        e = me ^ s
        gate_col = column(gates, lane, e)
        u = nn(h2, wgus[s][...])
        dhr = nt(dy, wds[s][...])
        g, up = u[:, :hidden], u[:, hidden:]
        sig = 1.0 / (1.0 + jnp.exp(-g))
        silu = g * sig
        hid = silu * up
        gh_ref[s, :, :] = (hid * gate_col).astype(BF16)
        dg = jnp.sum(hid * dhr, axis=1, keepdims=True)
        dprobs = dprobs + jnp.where(lane == e, dg * mask, 0.0)
        dh = dhr * gate_col
        dgate = dh * up * sig * (1.0 + g * (1.0 - sig))
        dup = dh * silu
        du_ref[s, :, :hidden] = dgate.astype(BF16)
        du_ref[s, :, hidden:] = dup.astype(BF16)
        part = nt(du_ref[s, :, :], wgus[s][...])
        if s == 0:
            acc_ref[...] = part
        else:
            acc_ref[...] += part
    dlog = probs * (dprobs - jnp.sum(probs * dprobs, axis=1, keepdims=True))
    hi, lo = split_hi_lo(dlog)
    dlt_ref[...] = nt(eye_ref[...], hi) + nt(eye_ref[...], lo)
    half_cols = acc_ref.shape[1] // halves
    keep_ref[...] = acc_ref[:, pl.ds(pl.multiple_of(half * half_cols, LANES), half_cols)].astype(BF16)
    send_ref[...] = acc_ref[:, pl.ds(pl.multiple_of((1 - half) * half_cols, LANES), half_cols)].astype(BF16)


def experts_pass(idx, h2, dy, lg, aux, wgus, wds, eye, types):
    tokens, width = h2.shape
    experts = len(wgus)
    hidden = wds[0].shape[0]
    erows = eye.shape[0]
    block = lambda i, *_: (i, 0)
    fixed = lambda i, *_: (0, 0)
    grid_spec = pltpu.PrefetchScalarGridSpec(
        num_scalar_prefetch=1,
        grid=(tokens // TB,),
        in_specs=[
            pl.BlockSpec((TB, width), block),
            pl.BlockSpec((TB, width), block),
            pl.BlockSpec((TB, LANES), block),
            pl.BlockSpec((TB, LANES), block),
        ]
        + [pl.BlockSpec((width, 2 * hidden), fixed, pipeline_mode=pl.Buffered(1))] * experts
        + [pl.BlockSpec((hidden, width), fixed, pipeline_mode=pl.Buffered(1))] * experts
        + [pl.BlockSpec((erows, LANES), fixed)],
        out_specs=[
            pl.BlockSpec((TB, width // 2), block),
            pl.BlockSpec((TB, width // 2), block),
            pl.BlockSpec((experts, TB, hidden), lambda i, *_: (0, i, 0)),
            pl.BlockSpec((experts, TB, 2 * hidden), lambda i, *_: (0, i, 0)),
            pl.BlockSpec((erows, TB), lambda i, *_: (0, i)),
        ],
        scratch_shapes=[pltpu.VMEM((TB, width), F32)],
    )
    return pl.pallas_call(
        functools.partial(expert_kernel, types, experts, 2),
        name="experts",
        grid_spec=grid_spec,
        out_shape=(
            jax.ShapeDtypeStruct((tokens, width // 2), BF16),
            jax.ShapeDtypeStruct((tokens, width // 2), BF16),
            jax.ShapeDtypeStruct((experts, tokens, hidden), BF16),
            jax.ShapeDtypeStruct((experts, tokens, 2 * hidden), BF16),
            jax.ShapeDtypeStruct((erows, tokens), F32),
        ),
        compiler_params=params(),
        cost_estimate=COST,
    )(idx, h2, dy, lg, aux, *wgus, *wds, eye)


def down_kernel(experts, idx_ref, gh_ref, *refs):
    wds, (keep_ref, send_ref, acc_ref) = refs[:experts], refs[experts:]
    me, half = idx_ref[0], idx_ref[1]
    for s in range(experts):
        part = nn(gh_ref[s, :, :], wds[s][...])
        if s == 0:
            acc_ref[...] = part
        else:
            acc_ref[...] += part
    half_cols = keep_ref.shape[1]
    keep_ref[...] = acc_ref[:, pl.ds(pl.multiple_of(half * half_cols, LANES), half_cols)].astype(BF16)
    send_ref[...] = acc_ref[:, pl.ds(pl.multiple_of((1 - half) * half_cols, LANES), half_cols)].astype(BF16)


def down_pass(idx, gh, wds):
    experts, tokens, hidden = gh.shape
    width = wds[0].shape[1]
    block = lambda i, *_: (i, 0)
    fixed = lambda i, *_: (0, 0)
    grid_spec = pltpu.PrefetchScalarGridSpec(
        num_scalar_prefetch=1,
        grid=(tokens // TB,),
        in_specs=[pl.BlockSpec((experts, TB, hidden), lambda i, *_: (0, i, 0))]
        + [pl.BlockSpec((hidden, width), fixed, pipeline_mode=pl.Buffered(1))] * experts,
        out_specs=[pl.BlockSpec((TB, width // 2), block)] * 2,
        scratch_shapes=[pltpu.VMEM((TB, width), F32)],
    )
    return pl.pallas_call(
        functools.partial(down_kernel, experts),
        name="down",
        grid_spec=grid_spec,
        out_shape=(jax.ShapeDtypeStruct((tokens, width // 2), BF16),) * 2,
        compiler_params=params(),
        cost_estimate=COST,
    )(idx, gh, *wds)


def middle_kernel(types, ffn, total_tokens, idx_ref, mine_ref, theirs_ref, x1_ref, dy_ref, lg_ref, aux_ref, dlt_ref, eye_ref, count_ref, gain_ref, wcat_ref, vt_ref, wprevt_ref, dx1_ref, da_ref, gp_ref, g1_ref, g2_ref, g3_ref, g4_ref, scr_ref):
    half = idx_ref[1]
    half_cols = mine_ref.shape[1]
    scr_ref[:, pl.ds(pl.multiple_of(half * half_cols, LANES), half_cols)] = mine_ref[...]
    scr_ref[:, pl.ds(pl.multiple_of((1 - half) * half_cols, LANES), half_cols)] = theirs_ref[...]
    first = pl.program_id(0) == 0

    @pl.when(first)
    def _():
        for ref in (g1_ref, g2_ref, g3_ref, g4_ref):
            ref[...] = jnp.zeros_like(ref)

    gain = gain_ref[...]
    x1 = x1_ref[...]
    r2 = rms_factor(x1)
    n2 = x1 * r2
    h2 = (n2 * gain).astype(BF16)
    dyb = dy_ref[...]
    dy = dyb.astype(F32)
    lg = lg_ref[...]
    lane, probs, mask = routing(lg, aux_ref[...], types)
    gates = probs * mask
    a = jnp.sum(dy * h2.astype(F32), axis=1, keepdims=True)
    b = nn(dyb, vt_ref[...])
    coef = column(gates, lane, ffn + 1)
    dprobs = jnp.where(lane == ffn + 1, a, 0.0)
    dlc = jnp.zeros_like(probs)
    vcoef = jnp.zeros_like(probs)
    for c in range(2):
        m0, m1 = const_mix(lg, lane, types, c)
        g = column(gates, lane, ffn + 2 + c)
        bc = column(b, lane, c)
        dprobs = dprobs + jnp.where(lane == ffn + 2 + c, m0 * a + m1 * bc, 0.0)
        dm0, dm1 = g * a, g * bc
        inner = m0 * dm0 + m1 * dm1
        dlc = dlc + jnp.where(lane == types + 2 * c, m0 * (dm0 - inner), 0.0)
        dlc = dlc + jnp.where(lane == types + 2 * c + 1, m1 * (dm1 - inner), 0.0)
        coef = coef + g * m0
        vcoef = vcoef + jnp.where(lane == c, g * m1, 0.0)
    dprobs = dprobs * mask + count_ref[...] * (AUX_WEIGHT * types / (2.0 * total_tokens * total_tokens))
    dlog = probs * (dprobs - jnp.sum(probs * dprobs, axis=1, keepdims=True))
    hi, lo = split_hi_lo(dlt_ref[...])
    dl = dlog + dlc + tn(hi, eye_ref[...]) + tn(lo, eye_ref[...])
    dhi, dlo = split_hi_lo(dl)
    dh2 = scr_ref[...].astype(F32) + coef * dy + nt(dhi, wcat_ref[...]) + nt(dlo, wcat_ref[...])
    dn2 = dh2 * gain
    dx1 = dy + r2 * (dn2 - n2 * jnp.mean(dn2 * n2, axis=1, keepdims=True))
    dx1_ref[...] = dx1
    da_ref[...] = dx1.astype(BF16)
    gp_ref[...] = nn(dhi, wprevt_ref[...]) + nn(dlo, wprevt_ref[...])
    g1_ref[...] += tn(dhi, h2) + tn(dlo, h2)
    vhi, vlo = split_hi_lo(vcoef)
    g2_ref[...] += tn(vhi, dyb) + tn(vlo, dyb)
    g3_ref[0:1, :] += jnp.sum(dh2 * n2, axis=0, keepdims=True)
    g4_ref[...] += tn(aux_ref[...], dhi) + tn(aux_ref[...], dlo)


def middle_pass(idx, mine, theirs, x1, dy, lg, aux, dlt, eye, count, gain, wcat, vt, wprevt, types, ffn, total_tokens):
    tokens, width = x1.shape
    erows = dlt.shape[0]
    block = lambda i, *_: (i, 0)
    fixed = lambda i, *_: (0, 0)
    grid_spec = pltpu.PrefetchScalarGridSpec(
        num_scalar_prefetch=1,
        grid=(tokens // TB,),
        in_specs=[
            pl.BlockSpec((TB, width // 2), block),
            pl.BlockSpec((TB, width // 2), block),
            pl.BlockSpec((TB, width), block),
            pl.BlockSpec((TB, width), block),
            pl.BlockSpec((TB, LANES), block),
            pl.BlockSpec((TB, LANES), block),
            pl.BlockSpec((erows, TB), lambda i, *_: (0, i)),
            pl.BlockSpec((erows, LANES), fixed),
            pl.BlockSpec((1, LANES), fixed),
            pl.BlockSpec((1, width), fixed),
            pl.BlockSpec((width, LANES), fixed),
            pl.BlockSpec((width, LANES), fixed),
            pl.BlockSpec((LANES, LANES), fixed),
        ],
        out_specs=[
            pl.BlockSpec((TB, width), block),
            pl.BlockSpec((TB, width), block),
            pl.BlockSpec((TB, LANES), block),
            pl.BlockSpec((LANES, width), fixed),
            pl.BlockSpec((LANES, width), fixed),
            pl.BlockSpec((8, width), fixed),
            pl.BlockSpec((LANES, LANES), fixed),
        ],
        scratch_shapes=[pltpu.VMEM((TB, width), BF16)],
    )
    return pl.pallas_call(
        functools.partial(middle_kernel, types, ffn, total_tokens),
        name="middle",
        grid_spec=grid_spec,
        out_shape=(
            jax.ShapeDtypeStruct((tokens, width), F32),
            jax.ShapeDtypeStruct((tokens, width), BF16),
            jax.ShapeDtypeStruct((tokens, LANES), F32),
            jax.ShapeDtypeStruct((LANES, width), F32),
            jax.ShapeDtypeStruct((LANES, width), F32),
            jax.ShapeDtypeStruct((8, width), F32),
            jax.ShapeDtypeStruct((LANES, LANES), F32),
        ),
        compiler_params=params(),
        cost_estimate=COST,
    )(idx, mine, theirs, x1, dy, lg, aux, dlt, eye, count, gain, wcat, vt, wprevt)


def layer_kernel(types, experts, total_tokens, blocks, h2_ref, dy_ref, lg_ref, aux_ref, x1_ref, *refs):
    wgus, wds = refs[:experts], refs[experts : 2 * experts]
    eye_ref, count_ref, gain_ref, wcat_ref, vt_ref, wprevt_ref = refs[2 * experts : 2 * experts + 6]
    dx1_ref, da_ref, gp_ref, base_ref, flate_ref, gu_ref, down_ref, g1_ref, g2_ref, g3_ref, g4_ref = refs[2 * experts + 6 : 2 * experts + 17]
    scratch = refs[2 * experts + 17 :]
    early = blocks - F_LATE
    acc_gu, acc_down, du_ref, gh_ref, dres, fres = scratch[:6]
    dkeep, dsend, dfirst, dsecond, dsems, fkeep, fsend, ffirst, fsecond, fsems, lpart, lfirst, lsecond, lsems = scratch[6:20]
    xg, xd, xsems = scratch[20:]
    step = pl.program_id(0)
    hidden = wds[0].shape[0]
    lrows = lpart.shape[2]
    me = lax.axis_index("expert")
    half, partner, other = neighbours()
    half_cols = dkeep.shape[1]
    dx = GroupSum(dkeep, dsend, dfirst, dsecond, dres, dsems)
    ff = GroupSum(fkeep, fsend, ffirst, fsecond, fres, fsems)
    small = SmallSum(lpart, lfirst, lsecond, lsems)
    across = {"expert": 1 - me}
    _, _, order = depth_place()
    block = gu_ref.shape[0] // 4
    first_rows = [pl.ds(pl.multiple_of(order[k] * block, block), block) for k in range(X_EARLY)]

    def first_copies(k):
        return [
            pltpu.make_async_remote_copy(
                src_ref=src.at[first_rows[k], pl.ds(cols, cols)],
                dst_ref=dst.at[k],
                send_sem=xsems.at[0, n, k],
                recv_sem=xsems.at[1, n, k],
                device_id=across,
                device_id_type=MESH,
            )
            for n, (src, dst, cols) in enumerate(((gu_ref, xg, 2 * hidden), (down_ref, xd, hidden)))
        ]

    @pl.when(step == 0)
    def _():
        greet((partner, other, across))
        for ref in (acc_gu, acc_down, g1_ref, g2_ref, g3_ref, g4_ref):
            ref[...] = jnp.zeros_like(ref)

    @pl.when(jnp.logical_and(step > 0, step <= blocks))
    def _():
        i = step - 1
        small.pair(i)
        dx.pair(i)

        @pl.when(i < early)
        def _():
            ff.pair(i)

        @pl.when(i >= early)
        def _():
            ff.pair_only(i)

    @pl.when(step < blocks)
    def _():
        i = step
        h2, dy = h2_ref[...], dy_ref[...]
        lane, probs, mask = routing(lg_ref[...], aux_ref[...], types)
        gates = probs * mask
        dprobs = jnp.zeros_like(probs)
        for s in range(experts):
            e = (me + s) % experts
            gate_col = column(gates, lane, e)
            u = nn(h2, wgus[s][...])
            dhr = nt(dy, wds[s][...])
            g, up = u[:, :hidden], u[:, hidden:]
            sig = 1.0 / (1.0 + jnp.exp(-g))
            silu = g * sig
            hid = silu * up
            gh_ref[:, s * hidden : (s + 1) * hidden] = (hid * gate_col).astype(BF16)
            dg = jnp.sum(hid * dhr, axis=1, keepdims=True)
            dprobs = dprobs + jnp.where(lane == e, dg * mask, 0.0)
            dh = dhr * gate_col
            base = 2 * s * hidden
            du_ref[:, base : base + hidden] = (dh * up * (sig + silu * (1.0 - sig))).astype(BF16)
            du_ref[:, base + hidden : base + 2 * hidden] = (dh * silu).astype(BF16)
        dlog = probs * (dprobs - jnp.sum(probs * dprobs, axis=1, keepdims=True))
        hi, lo = split_hi_lo(dlog)
        lpart[0, i] = (nt(eye_ref[...], hi) + nt(eye_ref[...], lo))[:lrows]
        small.start(i)
        rows = dx.rows(i)

        def place(total, group, keep, send):
            low, high = total[:, :half_cols], total[:, half_cols:]
            send[rows, :] = jnp.where(half == 0, high, low).astype(BF16)
            group.to_partner(i).start()
            keep[rows, :] = jnp.where(half == 0, low, high).astype(BF16)

        total = nt(du_ref[:, : 2 * hidden], wgus[0][...])
        for s in range(1, experts):
            total = total + nt(du_ref[:, 2 * s * hidden : 2 * (s + 1) * hidden], wgus[s][...])
        place(total, dx, dkeep, dsend)
        total = nn(gh_ref[:, :hidden], wds[0][...])
        for s in range(1, experts):
            total = total + nn(gh_ref[:, s * hidden : (s + 1) * hidden], wds[s][...])
        place(total, ff, fkeep, fsend)
        acc_gu[...] += tn(h2, du_ref[...])
        acc_down[...] += tn(dy, gh_ref[...])

    @pl.when(step == blocks)
    def _():
        gu_ref[...] = acc_gu[...].astype(BF16)
        down_ref[...] = acc_down[...].astype(BF16)
        for k in range(X_EARLY):
            for c in first_copies(k):
                c.start()
        dx.finish(0)

    @pl.when(step >= blocks)
    def _():
        i = step - blocks

        @pl.when(i + 1 < blocks)
        def _():
            dx.finish(i + 1)

        @pl.when(i < early)
        def _():
            ff.finish(i)

        rows = dx.rows(i)
        dlt = small.finish(i)
        gain = gain_ref[...]
        x1 = x1_ref[...]
        r2 = rms_factor(x1)
        n2 = x1 * r2
        h2 = h2_ref[...]
        dyb = dy_ref[...]
        dy = dyb.astype(F32)
        lg = lg_ref[...]
        lane, probs, mask = routing(lg, aux_ref[...], types)
        gates = probs * mask
        a = jnp.sum(dy * h2.astype(F32), axis=1, keepdims=True)
        b = nn(dyb, vt_ref[...])
        coef = column(gates, lane, experts + 1)
        dprobs = jnp.where(lane == experts + 1, a, 0.0)
        dlc = jnp.zeros_like(probs)
        vcoef = jnp.zeros_like(probs)
        for c in range(2):
            m0, m1 = const_mix(lg, lane, types, c)
            g = column(gates, lane, experts + 2 + c)
            bc = column(b, lane, c)
            dprobs = dprobs + jnp.where(lane == experts + 2 + c, m0 * a + m1 * bc, 0.0)
            dm0, dm1 = g * a, g * bc
            inner = m0 * dm0 + m1 * dm1
            dlc = dlc + jnp.where(lane == types + 2 * c, m0 * (dm0 - inner), 0.0)
            dlc = dlc + jnp.where(lane == types + 2 * c + 1, m1 * (dm1 - inner), 0.0)
            coef = coef + g * m0
            vcoef = vcoef + jnp.where(lane == c, g * m1, 0.0)
        dprobs = dprobs * mask + count_ref[...] * (AUX_WEIGHT * types / (2.0 * total_tokens * total_tokens))
        dlog = probs * (dprobs - jnp.sum(probs * dprobs, axis=1, keepdims=True))
        hi, lo = split_hi_lo(dlt)
        eye = eye_ref[:lrows, :]
        dl = dlog + dlc + tn(hi, eye) + tn(lo, eye)
        dhi, dlo = split_hi_lo(dl)
        vhi, vlo = split_hi_lo(vcoef)
        gp_ref[...] = nn(dhi, wprevt_ref[...]) + nn(dlo, wprevt_ref[...])
        g1_ref[...] += tn(dhi, h2) + tn(dlo, h2)
        g2_ref[...] += tn(vhi, dyb) + tn(vlo, dyb)
        g4_ref[...] += tn(aux_ref[...], dhi) + tn(aux_ref[...], dlo)
        dh2 = coef * dy + nt(dhi, wcat_ref[...]) + nt(dlo, wcat_ref[...])
        dx.close(i)
        dh2 = dh2 + jnp.concatenate([dres[0, rows, :], dres[1, rows, :]], axis=1).astype(F32)
        g3_ref[0:1, :] += jnp.sum(dh2 * n2, axis=0, keepdims=True)
        dn2 = dh2 * gain
        dx1 = dy + r2 * (dn2 - n2 * jnp.mean(dn2 * n2, axis=1, keepdims=True))
        dx1_ref[...] = dx1
        da_ref[...] = dx1.astype(BF16)
        vt = vt_ref[...]
        base_ref[...] = x1 + coef * h2.astype(F32) + nt(vhi, vt) + nt(vlo, vt)

        @pl.when(i < early)
        def _():
            ff.close(i)
            base_ref[...] += jnp.concatenate([fres[0, rows, :], fres[1, rows, :]], axis=1).astype(F32)

        @pl.when(i >= early)
        def _():
            ff.to_partner(i).wait_send()
            flate_ref[...] = fkeep[rows, :]

    @pl.when(step == 2 * blocks - 1)
    def _():
        for k in range(X_EARLY):
            for c, ref, got in zip(first_copies(k), (gu_ref, down_ref), (xg, xd)):
                c.wait()
                own = (first_rows[k], slice(0, got.shape[2]))
                ref[own] = (ref[own].astype(F32) + got[k].astype(F32)).astype(BF16)


def layer_pass(h2, dy, lg, aux, x1, wgus, wds, eye, count, gain, wcat, vt, wprevt, types, total_tokens):
    tokens, width = h2.shape
    experts = len(wgus)
    hidden = wds[0].shape[0]
    blocks = tokens // CHUNK
    lrows = -(-types // 8) * 8
    both = lambda i: (i % blocks, 0)
    late = lambda i: (jnp.maximum(i - blocks, 0), 0)
    fixed = lambda i: (0, 0)
    once = dict(pipeline_mode=pl.Buffered(1))
    small_sums = [
        pltpu.VMEM((2, blocks, lrows, CHUNK), F32),
        pltpu.VMEM((blocks, lrows, CHUNK), F32),
        pltpu.VMEM((blocks, lrows, CHUNK), F32),
        pltpu.SemaphoreType.DMA((2, 2, blocks)),
    ]
    return pl.pallas_call(
        functools.partial(layer_kernel, types, experts, total_tokens, blocks),
        name="layer",
        grid=(2 * blocks,),
        in_specs=[
            pl.BlockSpec((CHUNK, width), both),
            pl.BlockSpec((CHUNK, width), both),
            pl.BlockSpec((CHUNK, LANES), both),
            pl.BlockSpec((CHUNK, LANES), both),
            pl.BlockSpec((CHUNK, width), late),
        ]
        + [pl.BlockSpec((width, 2 * hidden), fixed, **once)] * experts
        + [pl.BlockSpec((hidden, width), fixed, **once)] * experts
        + [
            pl.BlockSpec(eye.shape, fixed),
            pl.BlockSpec((1, LANES), fixed),
            pl.BlockSpec((1, width), fixed),
            pl.BlockSpec((width, LANES), fixed),
            pl.BlockSpec((width, LANES), fixed),
            pl.BlockSpec((LANES, LANES), fixed),
        ],
        out_specs=[
            pl.BlockSpec((CHUNK, width), late),
            pl.BlockSpec((CHUNK, width), late),
            pl.BlockSpec((CHUNK, LANES), late),
            pl.BlockSpec((CHUNK, width), late),
            pl.BlockSpec((CHUNK, width // 2), lambda i: (jnp.maximum(i - (2 * blocks - F_LATE), 0), 0)),
            pl.BlockSpec((width, 2 * experts * hidden), fixed, **once),
            pl.BlockSpec((width, experts * hidden), fixed, **once),
            pl.BlockSpec((LANES, width), fixed),
            pl.BlockSpec((LANES, width), fixed),
            pl.BlockSpec((8, width), fixed),
            pl.BlockSpec((LANES, LANES), fixed),
        ],
        out_shape=(
            jax.ShapeDtypeStruct((tokens, width), F32),
            jax.ShapeDtypeStruct((tokens, width), BF16),
            jax.ShapeDtypeStruct((tokens, LANES), F32),
            jax.ShapeDtypeStruct((tokens, width), F32),
            jax.ShapeDtypeStruct((F_LATE * CHUNK, width // 2), BF16),
            jax.ShapeDtypeStruct((width, 2 * experts * hidden), BF16),
            jax.ShapeDtypeStruct((width, experts * hidden), BF16),
            jax.ShapeDtypeStruct((LANES, width), F32),
            jax.ShapeDtypeStruct((LANES, width), F32),
            jax.ShapeDtypeStruct((8, width), F32),
            jax.ShapeDtypeStruct((LANES, LANES), F32),
        ),
        scratch_shapes=[
            pltpu.VMEM((width, 2 * experts * hidden), F32),
            pltpu.VMEM((width, experts * hidden), F32),
            pltpu.VMEM((CHUNK, 2 * experts * hidden), BF16),
            pltpu.VMEM((CHUNK, experts * hidden), BF16),
            pltpu.VMEM((2, tokens, width // 2), BF16),
            pltpu.VMEM((2, tokens - F_LATE * CHUNK, width // 2), BF16),
        ]
        + sum_scratch(tokens, width // 2)
        + sum_scratch(tokens, width // 2)
        + small_sums
        + [
            pltpu.VMEM((X_EARLY, width // 4, 2 * hidden), BF16),
            pltpu.VMEM((X_EARLY, width // 4, hidden), BF16),
            pltpu.SemaphoreType.DMA((2, 2, X_EARLY)),
        ],
        compiler_params=params(collective_id=2, has_side_effects=True),
        cost_estimate=COST,
    )(h2, dy, lg, aux, x1, *wgus, *wds, eye, count, gain, wcat, vt, wprevt)


def output_kernel(types, ffn, f_ref, x1_ref, h2_ref, lg_ref, aux_ref, v_ref, out_ref):
    halves = jnp.concatenate([f_ref[0], f_ref[1]], axis=1)
    lg = lg_ref[...]
    lane, probs, mask = routing(lg, aux_ref[...], types)
    gates = probs * mask
    coef = column(gates, lane, ffn + 1)
    out = x1_ref[...] + halves.astype(F32)
    for c in range(2):
        m0, m1 = const_mix(lg, lane, types, c)
        g = column(gates, lane, ffn + 2 + c)
        coef = coef + g * m0
        out = out + (g * m1) * v_ref[c : c + 1, :]
    out_ref[...] = out + coef * h2_ref[...].astype(F32)


def output_pass(f, x1, h2, lg, aux, v, types, ffn):
    tokens, width = x1.shape
    block = lambda i: (i, 0)
    return pl.pallas_call(
        functools.partial(output_kernel, types, ffn),
        name="output",
        grid=(tokens // TB,),
        in_specs=[
            pl.BlockSpec((2, TB, width // 2), lambda i: (0, i, 0)),
            pl.BlockSpec((TB, width), block),
            pl.BlockSpec((TB, width), block),
            pl.BlockSpec((TB, LANES), block),
            pl.BlockSpec((TB, LANES), block),
            pl.BlockSpec((8, width), lambda i: (0, 0)),
        ],
        out_specs=pl.BlockSpec((TB, width), block),
        out_shape=jax.ShapeDtypeStruct((tokens, width), F32),
        compiler_params=params(),
        cost_estimate=COST,
    )(f, x1, h2, lg, aux, v)


def last_kernel(d_ref, x_ref, dx1_ref, gain_ref, out_ref):
    halves = jnp.concatenate([d_ref[0], d_ref[1]], axis=1)
    x = x_ref[...].astype(F32)
    r1 = rms_factor(x)
    n1 = x * r1
    dn1 = halves.astype(F32) * gain_ref[...]
    out_ref[...] = dx1_ref[...] + r1 * (dn1 - n1 * jnp.mean(dn1 * n1, axis=1, keepdims=True))


def last_pass(dh1, x, dx1, gain):
    tokens, width = x.shape
    block = lambda i: (i, 0)
    return pl.pallas_call(
        last_kernel,
        name="last",
        grid=(tokens // TB,),
        in_specs=[
            pl.BlockSpec((2, TB, width // 2), lambda i: (0, i, 0)),
            pl.BlockSpec((TB, width), block),
            pl.BlockSpec((TB, width), block),
            pl.BlockSpec((1, width), lambda i: (0, 0)),
        ],
        out_specs=pl.BlockSpec((TB, width), block),
        out_shape=jax.ShapeDtypeStruct((tokens, width), F32),
        compiler_params=params(),
        cost_estimate=COST,
    )(dh1, x, dx1, gain)


def tail_kernel(first_late, d_ref, x_ref, dx1_ref, gain_ref, base_ref, f_ref, grad_ref, out_ref):
    last_kernel(d_ref, x_ref, dx1_ref, gain_ref, grad_ref)
    late = pl.program_id(0) >= first_late

    @pl.when(late)
    def _():
        out_ref[...] = base_ref[...] + jnp.concatenate([f_ref[0], f_ref[1]], axis=1).astype(F32)

    @pl.when(jnp.logical_not(late))
    def _():
        out_ref[...] = base_ref[...]


def tail_pass(dh1, x, dx1, gain, base, f_late):
    tokens, width = x.shape
    first_late = tokens // CHUNK - F_LATE
    block = lambda i: (i, 0)
    return pl.pallas_call(
        functools.partial(tail_kernel, first_late),
        name="tail",
        grid=(tokens // CHUNK,),
        in_specs=[
            pl.BlockSpec((2, CHUNK, width // 2), lambda i: (0, i, 0)),
            pl.BlockSpec((CHUNK, width), block),
            pl.BlockSpec((CHUNK, width), block),
            pl.BlockSpec((1, width), lambda i: (0, 0)),
            pl.BlockSpec((CHUNK, width), block),
            pl.BlockSpec((2, CHUNK, width // 2), lambda i: (0, jnp.maximum(i - first_late, 0), 0)),
        ],
        out_specs=[pl.BlockSpec((CHUNK, width), block)] * 2,
        out_shape=(jax.ShapeDtypeStruct((tokens, width), F32),) * 2,
        compiler_params=params(),
        cost_estimate=COST,
    )(dh1, x, dx1, gain, base, f_late)


def tie(value, *others):
    return lax.optimization_barrier((value, *others))[0]


def add_all(own, got):
    total = own.astype(F32)
    for g in got:
        total = total + g.astype(F32)
    return total.astype(BF16)


def pair_sum(keep, send):
    return (keep.astype(F32) + swap(send, "tensor", 1).astype(F32)).astype(BF16)


def group_sum(part):
    bit = 2
    while bit < lax.axis_size("tensor"):
        part = (part.astype(F32) + swap(part, "tensor", bit).astype(F32)).astype(BF16)
        bit *= 2
    return part, swap(part, "tensor", 1)


def scatter_sum(a, axes):
    steps = []
    for axis in axes:
        bits = lax.axis_size(axis).bit_length() - 1
        steps += [(axis, b) for b in reversed(range(bits))]
    a = a.reshape((2,) * len(steps) + (-1, a.shape[-1]))
    order = [s for axis in reversed(axes) for s in reversed(steps) if s[0] == axis]
    left = list(steps)
    for axis, bit in order:
        dim = left.index((axis, bit))
        mine = (lax.axis_index(axis) >> bit) & 1
        got = swap(lax.dynamic_index_in_dim(a, 1 - mine, dim, keepdims=False), axis, 1 << bit)
        a = (lax.dynamic_index_in_dim(a, mine, dim, keepdims=False).astype(F32) + got.astype(F32)).astype(BF16)
        left.remove((axis, bit))
    return a


def gather_group(a):
    out = [a]
    bit = lax.axis_size("tensor") // 2
    parts = {0: a}
    while bit:
        parts.update({m | bit: swap(p, "tensor", bit) for m, p in list(parts.items())})
        bit //= 2
    return [parts[m] for m in range(len(parts))]


def per_device(hidden_in, prev_logits, routes, block_ids, cotangent, gain_attn, w_qkv, w_out, gain_moe, w_router, w_prev, w_const, v_const, w_gate_up, w_down):
    tokens, width = hidden_in.shape
    types = w_router.shape[1]
    experts = lax.axis_size("expert")
    heads = w_out.shape[0] // HEAD_DIM
    hidden = w_down.shape[1]
    total_tokens = tokens * lax.axis_size(("dp", "expert"))
    t_index, x_index = lax.axis_index("tensor"), lax.axis_index("expert")
    t_idx = jnp.stack([t_index, t_index % 2]).astype(jnp.int32)
    x_idx = jnp.stack([x_index, t_index % 2]).astype(jnp.int32)

    gain_first = gain_attn.astype(F32)[None]
    gain_second = gain_moe.astype(F32)[None]
    consts = w_const.transpose(1, 0, 2).reshape(width, 4)
    wcat = jnp.pad(jnp.concatenate([w_router, consts], axis=1), ((0, 0), (0, LANES - types - 4)))
    aux = jnp.concatenate([prev_logits, routes.astype(BF16)], axis=1)
    aux = jnp.pad(aux, ((0, 0), (0, LANES - types - 2)))
    wprev = jnp.pad(w_prev, ((0, LANES - types), (0, LANES - types)))
    wprevt = jnp.pad(w_prev.T, ((0, LANES - types), (0, LANES - types)))
    vt = jnp.pad(v_const.T, ((0, 0), (0, LANES - 2)))
    vrows = jnp.pad(v_const.astype(F32), ((0, 6), (0, 0)))
    erows = -(-types // 16) * 16
    eye = jnp.eye(erows, LANES, dtype=BF16)
    lanes = jnp.arange(LANES, dtype=jnp.int32)
    chosen = (routes[:, :, None] == lanes[None, None, :]).astype(F32)
    count = jnp.sum(chosen, axis=(0, 1))[None]
    bq, bk = block_ids, block_ids.reshape(tokens, 1)

    w_halves = w_qkv.T.reshape(-1, 2, width // 2).transpose(1, 0, 2)

    wgu, wd = w_gate_up[0].reshape(width, 2 * hidden), w_down[0]
    fused = experts == 2 and lax.axis_size("dp") == 4 and lax.axis_size("tensor") == 4
    if fused:
        part = jnp.broadcast_to(count, (8, LANES))
        h1, qkvt, ot, lse, x1, h2, lg, prob_part, count, *peer = front_pass(
            hidden_in, gain_first, w_qkv.T, bq, bk, w_out, gain_second, wcat, aux, wprev, part, wgu, wd, heads, types
        )
        wgus, wds, count = [wgu, peer[0]], [wd, peer[1]], count[:1]
    else:
        wgus = [wgu] + [swap(wgu, "expert", s) for s in range(1, experts)]
        wds = [wd] + [swap(wd, "expert", s) for s in range(1, experts)]
        h1, qkvt, ot, lse = attention_forward(hidden_in, gain_first, w_qkv.T, bq, bk, heads)
        ots, wos = gather_group(ot), gather_group(w_out)
        x1, h2, lg, prob_part = post_attention(t_idx, hidden_in, ots, wos, gain_second, wcat, aux, wprev, types)
        count = sum_over(tie(count, wds[-1]), ("expert", "dp"))
    srows = -(-(types + 4) // 8) * 8
    prow = -(-types // 8) * 8

    def small_rows(g1, g2, g3, g4):
        wide = lambda a: jnp.pad(a, ((0, 0), (0, width - LANES)))
        rows = jnp.concatenate([g1[:srows], g2[:8], g3, wide(g4[:prow]), wide(prob_part)], axis=0)
        return jnp.pad(rows, ((0, 64 - rows.shape[0]), (0, 0)))

    if fused:
        dx1, da, gp, base, f_late, gu, down, *g = layer_pass(
            h2, cotangent, lg, aux, x1, wgus, wds, eye, count, gain_second, wcat, vt, wprevt, types, total_tokens
        )
        dh1, gain_all, grads, grad_gate_up, grad_down, small, f_late = attention_backward(
            da, w_out, qkvt, ot, lse, bq, bk, w_halves, h1, heads, gu, down, small_rows(*g), f_late
        )
        grad_input, output = tail_pass(dh1, hidden_in, dx1, gain_first, base, f_late)
    else:
        keep, send, gh, du, dlt = experts_pass(x_idx, h2, cotangent, lg, aux, wgus, wds, eye, types)
        mine, theirs = group_sum(pair_sum(keep, send))
        dlt = sum_over(dlt, ("tensor",))
        fkeep, fsend = down_pass(x_idx, gh, wds)
        gu_parts = [tn(h2, du[e]).astype(BF16) for e in range(experts)]
        down_parts = [tn(cotangent, gh[e]).astype(BF16) for e in range(experts)]
        f_mine, f_theirs = group_sum(pair_sum(fkeep, fsend))
        first, second = jnp.where(t_index % 2 == 0, f_mine, f_theirs), jnp.where(t_index % 2 == 0, f_theirs, f_mine)
        f = jnp.stack([first, second])
        dx1, da, gp, *g = middle_pass(
            x_idx, mine, theirs, x1, cotangent, lg, aux, dlt, eye, count, gain_second, wcat, vt, wprevt, types, experts, total_tokens
        )
        dh1, gain_part, grads = attention_backward(da, w_out, qkvt, ot, lse, bq, bk, w_halves, h1, heads)
        grads = scatter_sum(grads, ("dp", "expert")).astype(F32)
        gu_got = [swap(gu_parts[e], "expert", e) for e in range(1, experts)]
        down_got = [swap(down_parts[e], "expert", e) for e in range(1, experts)]
        grad_gate_up = scatter_sum(add_all(gu_parts[0], gu_got), ("dp",)).astype(F32)
        grad_down = scatter_sum(add_all(down_parts[0], down_got), ("dp",)).astype(F32)
        gain_all = sum_over(gain_part, ("tensor", "expert", "dp"))
        small = sum_over(small_rows(*g), ("expert", "dp"))
        grad_input = last_pass(dh1, hidden_in, dx1, gain_first)
        output = output_pass(f, x1, h2, lg, aux, vrows, types, experts)

    grad_gain = gain_all.reshape(-1)[:width] / gain_first[0]
    grad_qkv, grad_out = grads[:, : w_qkv.shape[1]], grads[:, w_qkv.shape[1] :].T

    prob_all = small[srows + 16 + prow, :types]
    count_all = count[0, :types]
    balance_loss = types * jnp.sum((count_all / (2.0 * total_tokens)) * prob_all / total_tokens)
    load = jnp.stack([count_all / (2.0 * tokens), prob_all / tokens])
    return (
        output,
        grad_input,
        gp[:, :types],
        grad_gain,
        grad_qkv,
        grad_out,
        small[srows + 8],
        small[:types].T,
        small[srows + 16 : srows + 16 + types, :types],
        small[types : types + 4].reshape(2, 2, width).transpose(0, 2, 1),
        small[srows : srows + 2],
        grad_gate_up.reshape(1, -1, 2, hidden),
        grad_down.T[None],
        balance_loss,
        load,
    )


def solution(mesh):
    tok = P(("dp", "expert"), None)
    return jax.shard_map(
        per_device,
        mesh=mesh,
        in_specs=(
            tok,
            tok,
            tok,
            tok,
            tok,
            P(),
            P(None, "tensor"),
            P("tensor", None),
            P(),
            P(),
            P(),
            P(),
            P(),
            P("expert", None, None, "tensor"),
            P("expert", "tensor", None),
        ),
        out_specs=(
            tok,
            tok,
            tok,
            P(),
            P(("dp", "expert"), "tensor"),
            P("tensor", ("dp", "expert")),
            P(),
            P(),
            P(),
            P(),
            P(),
            P("expert", "dp", None, "tensor"),
            P("expert", "tensor", "dp"),
            P(),
            P(),
        ),
        check_vma=False,
    )
```

```python
import functools

import jax
import jax.numpy as jnp
from jax import lax
from jax.experimental import pallas as pl
from jax.experimental.pallas import tpu as pltpu
from jax.sharding import PartitionSpec as P

HEAD_DIM = 64
EPSILON = 1e-06
AUX_WEIGHT = 0.01
SCORE_SCALE = 0.125
MAX_BLOCK = 256
LANES = 128
QB = 256
QF = 512
TB = 256
NEG = -1e30
F32 = jnp.float32
BF16 = jnp.bfloat16
MESH = pl.DeviceIdType.MESH
VMEM_LIMIT = 54 * 1024 * 1024
COST = pl.CostEstimate(flops=1000, bytes_accessed=1000, transcendentals=0)


def params(**more):
    return pltpu.CompilerParams(vmem_limit_bytes=VMEM_LIMIT, **more)


def nn(a, b):
    return lax.dot_general(a, b, (((1,), (0,)), ((), ())), preferred_element_type=F32)


def nt(a, b):
    return lax.dot_general(a, b, (((1,), (1,)), ((), ())), preferred_element_type=F32)


def tn(a, b):
    return lax.dot_general(a, b, (((0,), (0,)), ((), ())), preferred_element_type=F32)


def split_hi_lo(a):
    hi = a.astype(BF16)
    return hi, (a - hi.astype(F32)).astype(BF16)


def rms_factor(values):
    return lax.rsqrt(jnp.mean(values * values, axis=-1, keepdims=True) + EPSILON)


def swap(a, axis, bit):
    n = lax.axis_size(axis)
    return lax.ppermute(a, axis, [(i, i ^ bit) for i in range(n)])


def sum_over(a, axes):
    for axis in axes:
        bit = 1
        while bit < lax.axis_size(axis):
            a = a + swap(a, axis, bit)
            bit *= 2
    return a


def key_range(q0, rows, tokens):
    return min(tokens, q0 + rows + MAX_BLOCK)


def project_rows(r0, heads, x_ref, gain_ref, wt_ref, h1_ref, qkvt_ref, kn_ref):
    d = HEAD_DIM
    rows = slice(r0, r0 + QF)
    xb = x_ref[rows, :].astype(F32)
    h1 = (xb * rms_factor(xb) * gain_ref[...]).astype(BF16)
    h1_ref[rows, :] = h1
    qkvt = nt(wt_ref[...], h1)
    for h in range(heads):
        base = h * 3 * d
        q = qkvt[base : base + d].astype(BF16).astype(F32) * SCORE_SCALE
        qkvt_ref[base : base + d, rows] = q.astype(BF16)
        qkvt_ref[base + d : base + 3 * d, rows] = qkvt[base + d : base + 3 * d].astype(BF16)
        kn_ref[h, rows, :] = qkvt[base + d : base + 2 * d].T.astype(BF16)


def attend_rows(q0, h, bq_ref, bk_ref, qkvt_ref, kn_ref, lse_ref):
    tokens = qkvt_ref.shape[1]
    d = HEAD_DIM
    base = h * 3 * d
    cols = slice(q0, q0 + QF)
    top = key_range(q0, QF, tokens)
    s = nn(kn_ref[h, :top, :], qkvt_ref[base : base + d, cols])
    parts = [jnp.where(bk_ref[q0:top, :] <= bq_ref[:, cols], s[q0:], NEG)]
    if q0:
        parts = [s[:q0]] + parts
    m = functools.reduce(jnp.maximum, [jnp.max(a, axis=0, keepdims=True) for a in parts])
    ps = [jnp.exp(a - m) for a in parts]
    total = functools.reduce(jnp.add, [jnp.sum(p, axis=0, keepdims=True) for p in ps])
    p = jnp.concatenate([p.astype(BF16) for p in ps], axis=0)
    acc = nn(qkvt_ref[base + 2 * d : base + 3 * d, :top], p)
    lse_ref[h : h + 1, cols] = m + jnp.log(total)
    return (acc / total).astype(BF16)


def attn_fwd_kernel(heads, x_ref, gain_ref, wt_ref, bq_ref, bk_ref, h1_ref, qkvt_ref, ot_ref, lse_ref, kn_ref):
    tokens = x_ref.shape[0]
    d = HEAD_DIM
    for r0 in range(0, tokens, QF):
        project_rows(r0, heads, x_ref, gain_ref, wt_ref, h1_ref, qkvt_ref, kn_ref)
    for h in range(heads):
        for q0 in range(0, tokens, QF):
            ot_ref[h * d : (h + 1) * d, q0 : q0 + QF] = attend_rows(q0, h, bq_ref, bk_ref, qkvt_ref, kn_ref, lse_ref)


def attention_forward(x, gain, w_t, bq, bk, heads):
    tokens, width = x.shape
    cols = w_t.shape[0]
    lse_rows = -(-heads // 8) * 8
    return pl.pallas_call(
        functools.partial(attn_fwd_kernel, heads),
        name="attn_fwd",
        out_shape=(
            jax.ShapeDtypeStruct((tokens, width), BF16),
            jax.ShapeDtypeStruct((cols, tokens), BF16),
            jax.ShapeDtypeStruct((heads * HEAD_DIM, tokens), BF16),
            jax.ShapeDtypeStruct((lse_rows, tokens), F32),
        ),
        scratch_shapes=[pltpu.VMEM((heads, tokens, HEAD_DIM), BF16)],
        compiler_params=params(),
        cost_estimate=COST,
    )(x, gain, w_t, bq, bk)


CHUNK = 256
F_LATE = 6
X_EARLY = 1


def neighbours():
    t = lax.axis_index("tensor")
    return t % 2, {"tensor": t + 1 - 2 * (t % 2)}, {"tensor": (t + 2) % 4}


def greet(devices):
    barrier = pltpu.get_barrier_semaphore()
    for device in devices:
        pl.semaphore_signal(barrier, inc=1, device_id=device, device_id_type=MESH)
    pl.semaphore_wait(barrier, len(devices))


def each(count, step):
    def body(i, carry):
        step(i)
        return carry

    lax.fori_loop(0, count, body, 0)


class GroupSum:
    def __init__(self, keep, send, first, second, result, sems):
        self.keep, self.send, self.first, self.second, self.result, self.sems = keep, send, first, second, result, sems
        self.half, self.partner, self.other = neighbours()

    def rows(self, i):
        return pl.ds(pl.multiple_of(i * CHUNK, CHUNK), CHUNK)

    def copy(self, stage, i, src, dst, device):
        return pltpu.make_async_remote_copy(
            src_ref=src,
            dst_ref=dst,
            send_sem=self.sems.at[0, stage, i],
            recv_sem=self.sems.at[1, stage, i],
            device_id=device,
            device_id_type=MESH,
        )

    def to_partner(self, i):
        r = self.rows(i)
        return self.copy(0, i, self.send.at[r, :], self.first.at[r, :], self.partner)

    def to_other(self, i):
        r = self.rows(i)
        return self.copy(1, i, self.keep.at[r, :], self.second.at[r, :], self.other)

    def back(self, i):
        place = self.result.at[self.half, self.rows(i), :]
        return self.copy(2, i, place, place, self.partner)

    def pair_only(self, i):
        self.to_partner(i).wait_recv()
        r = self.rows(i)
        self.keep[r, :] = (self.keep[r, :].astype(F32) + self.first[r, :].astype(F32)).astype(BF16)

    def pair(self, i):
        self.pair_only(i)
        self.to_other(i).start()

    def finish(self, i):
        self.to_other(i).wait_recv()
        r = self.rows(i)
        self.result[self.half, r, :] = (self.keep[r, :].astype(F32) + self.second[r, :].astype(F32)).astype(BF16)
        self.back(i).start()

    def close(self, i):
        self.back(i).wait_recv()
        if self.send is not None:
            self.to_partner(i).wait_send()
        self.to_other(i).wait_send()
        self.back(i).wait_send()


class SmallSum:
    def __init__(self, part, first, second, sems):
        self.part, self.first, self.second, self.sems = part, first, second, sems
        _, self.partner, self.other = neighbours()

    def copy(self, stage, i, landing, device):
        return pltpu.make_async_remote_copy(
            src_ref=self.part.at[stage, i],
            dst_ref=landing.at[i],
            send_sem=self.sems.at[0, stage, i],
            recv_sem=self.sems.at[1, stage, i],
            device_id=device,
            device_id_type=MESH,
        )

    def start(self, i):
        self.copy(0, i, self.first, self.partner).start()

    def pair(self, i):
        self.copy(0, i, self.first, self.partner).wait_recv()
        self.part[1, i] = self.part[0, i] + self.first[i]
        self.copy(1, i, self.second, self.other).start()

    def finish(self, i):
        self.copy(1, i, self.second, self.other).wait_recv()
        self.copy(0, i, self.first, self.partner).wait_send()
        self.copy(1, i, self.second, self.other).wait_send()
        return self.part[1, i] + self.second[i]


class HopSum:
    def __init__(self, partial, landed, sems, devices):
        self.partial, self.landed, self.sems, self.devices = partial, landed, sems, devices

    def hop(self, n):
        return pltpu.make_async_remote_copy(
            src_ref=self.partial.at[n],
            dst_ref=self.landed.at[n],
            send_sem=self.sems.at[0, n],
            recv_sem=self.sems.at[1, n],
            device_id=self.devices[n],
            device_id_type=MESH,
        )

    def start(self):
        self.hop(0).start()

    def add(self, n):
        self.hop(n).wait_recv()
        total = self.partial[n] + self.landed[n]
        if n + 1 < len(self.devices):
            self.partial[n + 1] = total
            self.hop(n + 1).start()
        return total

    def close(self):
        for n in range(len(self.devices)):
            self.hop(n).wait_send()


def hop_scratch(hops, rows, width):
    return [pltpu.VMEM((hops, rows, width), F32), pltpu.VMEM((hops, rows, width), F32), pltpu.SemaphoreType.DMA((2, hops))]


def replica(n):
    place = (lax.axis_index("dp") * 2 + lax.axis_index("expert") + n) % 8
    return {"dp": place // 2, "expert": place % 2}, place


def all_replicas():
    return [replica(n)[0] for n in range(1, 8)]


class ReplicaSum:
    def __init__(self, own, landed, result, sems):
        self.own, self.landed, self.result, self.sems = own, landed, result, sems

    def copy(self, stage, n):
        device, place = replica(n)
        _, me = replica(0)
        rows = lambda block: pl.ds(pl.multiple_of(block * 8, 8), 8)
        src, dst = ((self.own.at[rows(place), :], self.landed.at[me]), (self.result.at[rows(me), :], self.result.at[rows(me), :]))[stage]
        return pltpu.make_async_remote_copy(
            src_ref=src,
            dst_ref=dst,
            send_sem=self.sems.at[0, stage, n],
            recv_sem=self.sems.at[1, stage, n],
            device_id=device,
            device_id_type=MESH,
        )

    def start(self):
        for n in range(1, 8):
            self.copy(0, n).start()

    def share(self):
        _, me = replica(0)
        rows = pl.ds(pl.multiple_of(me * 8, 8), 8)
        self.landed[me] = self.own[rows, :]
        for n in range(1, 8):
            self.copy(0, n).wait_recv()
        total = self.landed[0]
        for n in range(1, 8):
            total = total + self.landed[n]
        self.result[rows, :] = total
        for n in range(1, 8):
            self.copy(1, n).start()

    def close(self):
        for n in range(1, 8):
            self.copy(1, n).wait_recv()
            for stage in range(2):
                self.copy(stage, n).wait_send()


class EverywhereSum:
    def __init__(self, first, second, fsems, ssems):
        self.first, self.second, self.fsems, self.ssems = first, second, fsems, ssems
        self.t = lax.axis_index("tensor")

    def copy(self, buffer, sems, place, n, device):
        return pltpu.make_async_remote_copy(
            src_ref=buffer.at[place],
            dst_ref=buffer.at[place],
            send_sem=sems.at[0, n],
            recv_sem=sems.at[1, n],
            device_id=device,
            device_id_type=MESH,
        )

    def outer(self):
        return [self.copy(self.first, self.fsems, replica(0)[1], n, replica(n)[0]) for n in range(1, 8)]

    def inner(self):
        return [self.copy(self.second, self.ssems, self.t, n, {"tensor": (self.t + n) % 4}) for n in range(1, 4)]

    def start(self, value):
        self.first[replica(0)[1]] = value
        for c in self.outer():
            c.start()

    def share(self):
        for c in self.outer():
            c.wait_recv()
        total = self.first[0]
        for n in range(1, 8):
            total = total + self.first[n]
        self.second[self.t] = total
        for c in self.inner():
            c.start()

    def finish(self):
        for c in self.inner():
            c.wait_recv()
        for c in self.outer() + self.inner():
            c.wait_send()
        return self.second[0] + self.second[1] + (self.second[2] + self.second[3])


def depth_place():
    z = lax.axis_index("dp")
    low, high = z % 2, z // 2
    order = [2 * (1 - high) + 1 - low, 2 * high + 1 - low, 2 * (1 - high) + low, z]
    return {"dp": z + 1 - 2 * low}, {"dp": (z + 2) % 4}, order


class DepthSum:
    def __init__(self, own, across, landed, xsems, zsems, sources, device):
        self.own, self.across, self.landed, self.xsems, self.zsems = own, across, landed, xsems, zsems
        self.sources, self.device = sources, device
        self.near, self.far, _ = depth_place()

    def x_copy(self, k):
        return pltpu.make_async_remote_copy(
            src_ref=self.sources[k],
            dst_ref=self.across.at[k],
            send_sem=self.xsems.at[0, k],
            recv_sem=self.xsems.at[1, k],
            device_id=self.device,
            device_id_type=MESH,
        )

    def z_copy(self, k):
        return pltpu.make_async_remote_copy(
            src_ref=self.own.at[k],
            dst_ref=self.landed.at[k],
            send_sem=self.zsems.at[0, k],
            recv_sem=self.zsems.at[1, k],
            device_id=self.near if k < 2 else self.far,
            device_id_type=MESH,
        )

    def pass_on(self, k):
        total = self.own[k].astype(F32)
        if self.sources[k] is not None:
            self.x_copy(k).wait_recv()
            total = total + self.across[k].astype(F32)
        for came in {2: (0,), 3: (1, 2)}.get(k, ()):
            self.z_copy(came).wait_recv()
            total = total + self.landed[came].astype(F32)
        if k < 3:
            self.own[k] = total.astype(BF16)
            self.z_copy(k).start()
        return total

    def close(self):
        for k in range(4):
            if self.sources[k] is not None:
                self.x_copy(k).wait_send()
            if k < 3:
                self.z_copy(k).wait_send()


def depth_scratch(rows, cols):
    return [
        pltpu.VMEM((4, rows, cols), BF16),
        pltpu.VMEM((4, rows, cols), BF16),
        pltpu.VMEM((3, rows, cols), BF16),
        pltpu.SemaphoreType.DMA((2, 4)),
        pltpu.SemaphoreType.DMA((2, 3)),
    ]


def sum_scratch(tokens, half_cols, sends=True):
    return [pltpu.VMEM((tokens, half_cols), BF16)] * (4 if sends else 3) + [pltpu.SemaphoreType.DMA((2, 3, tokens // CHUNK))]


def attn_bwd_kernel(heads, fused, da_ref, wo_ref, qkvt_ref, ot_ref, lse_ref, bq_ref, bk_ref, wq_ref, h1_ref, *refs):
    if fused:
        gu_ref, down_ref, small_ref, flate_ref = refs[:4]
        dres_ref, gain_ref, gsum_ref, gusum_ref, dosum_ref, smallsum_ref, fres_ref = refs[4:11]
        scratch = refs[11:]
    else:
        dres_ref, gain_ref, gsum_ref = refs[:3]
        scratch = refs[3:]
    dqkvt_ref, dot_ref, delta_ref, kn_ref, vn_ref, dk_ref, dv_ref, dkeep, dsend, dfirst, dsecond, dsems = scratch[:12]
    tokens, width = da_ref.shape
    d = HEAD_DIM
    cols_all = dqkvt_ref.shape[0]
    chunks = tokens // CHUNK
    dh = GroupSum(dkeep, dsend, dfirst, dsecond, dres_ref, dsems)
    half, partner, other = neighbours()
    if fused:
        glocal, *rest = scratch[12:]
        gparts, uparts, dparts, sparts, nparts, (lsems,) = rest[:5], rest[5:10], rest[10:15], rest[15:17], rest[17:21], rest[21:22]
        fsecond, fsems = rest[22:]
        ff = GroupSum(flate_ref, None, None, fsecond, fres_ref, fsems)
        hidden = dparts[0].shape[2]
        x = lax.axis_index("expert")
        near, far, order = depth_place()
        block, piece = width // 4, width // 8
        across = {"expert": 1 - x}
        t = lax.axis_index("tensor")
        greet([{"tensor": (t + n) % 4} for n in range(1, 4)] + all_replicas())

        def block_rows(k):
            return pl.ds(pl.multiple_of(order[k] * block, block), block)

        def pieces(k, place):
            return pl.ds(pl.multiple_of(order[k] * block + place * piece, piece), piece)

        gate_up = DepthSum(*uparts, [None] * X_EARLY + [gu_ref.at[block_rows(k), pl.ds(2 * hidden, 2 * hidden)] for k in range(X_EARLY, 4)], across)
        down = DepthSum(*dparts, [None] * X_EARLY + [down_ref.at[block_rows(k), pl.ds(hidden, hidden)] for k in range(X_EARLY, 4)], across)
        attn = DepthSum(*gparts, [glocal.at[pieces(k, 1 - x), :] for k in range(4)], across)
        small = ReplicaSum(small_ref, sparts[0], smallsum_ref, sparts[1])
        total_gain = EverywhereSum(*nparts)

        def local_copies(k):
            return [
                pltpu.make_async_copy(gu_ref.at[block_rows(k), pl.ds(0, 2 * hidden)], gate_up.own.at[k], lsems.at[0, k]),
                pltpu.make_async_copy(down_ref.at[block_rows(k), pl.ds(0, hidden)], down.own.at[k], lsems.at[1, k]),
            ]

        def pass_on(k):
            for c in local_copies(k):
                c.wait()
            return gate_up.pass_on(k), down.pass_on(k)

        for n in range(F_LATE):
            ff.to_other(n).start()
        small.start()
        for k in range(4):
            for c in local_copies(k):
                c.start()
            if k >= X_EARLY:
                gate_up.x_copy(k).start()
                down.x_copy(k).start()
    else:
        glocal = gsum_ref
        greet([partner, other])

    def project(i):
        rows = pl.ds(pl.multiple_of(i * CHUNK, CHUNK), CHUNK)
        dot = nt(wo_ref[...], da_ref[rows, :]).astype(BF16)
        dot_ref[:, rows] = dot
        prod = dot.astype(F32) * ot_ref[:, rows].astype(F32)
        for h in range(heads):
            base = h * 3 * d
            delta_ref[h : h + 1, rows] = jnp.sum(prod[h * d : (h + 1) * d], axis=0, keepdims=True)
            kn_ref[h, rows, :] = qkvt_ref[base + d : base + 2 * d, rows].astype(F32).T.astype(BF16)
            vn_ref[h, rows, :] = qkvt_ref[base + 2 * d : base + 3 * d, rows].astype(F32).T.astype(BF16)

    each(chunks, project)
    dk_ref[...] = jnp.zeros_like(dk_ref)
    dv_ref[...] = jnp.zeros_like(dv_ref)
    glocal[:, cols_all:] = nn(ot_ref[...], da_ref[...]).T.astype(BF16)

    def query_block(q0):
        def head(h):
            base = h * 3 * d
            orows = pl.ds(h * d, d)
            cols = slice(q0, q0 + QB)
            top = key_range(q0, QB, tokens)
            qt = qkvt_ref[pl.ds(base, d), cols]
            dot = dot_ref[orows, cols]
            s = nn(kn_ref[h, :top, :], qt)
            p = jnp.exp(s - lse_ref[pl.ds(h, 1), cols])
            last = jnp.where(bk_ref[q0:top, :] <= bq_ref[:, cols], p[q0:], 0.0)
            p = jnp.concatenate([p[:q0], last], axis=0) if q0 else last
            dp = nn(vn_ref[h, :top, :], dot)
            ds = (p * (dp - delta_ref[pl.ds(h, 1), cols])).astype(BF16)
            dv_ref[h, :, :top] += nt(dot, p.astype(BF16))
            dk_ref[h, :, :top] += nt(qt, ds)
            dq = nn(qkvt_ref[pl.ds(base + d, d), :top], ds)
            dqkvt_ref[pl.ds(base, d), cols] = (dq * SCORE_SCALE).astype(BF16)

        for h in range(heads):
            head(h)

    def input_grad(i):
        r = dh.rows(i)
        for h in range(heads):
            base = h * 3 * d
            dqkvt_ref[base + d : base + 2 * d, r] = dk_ref[h, :, r].astype(BF16)
            dqkvt_ref[base + 2 * d : base + 3 * d, r] = dv_ref[h, :, r].astype(BF16)
        dqkv = dqkvt_ref[:, r]
        dsend[r, :] = tn(dqkv, wq_ref[1 - half]).astype(BF16)
        dh.to_partner(i).start()
        dkeep[r, :] = tn(dqkv, wq_ref[half]).astype(BF16)
        dh.pair(i)

    if fused:
        pass_on(0)
    for i in reversed(range(chunks)):
        query_block(i * QB)
        if i + 1 < chunks:
            input_grad(i + 1)
        if fused and i == chunks - 3:
            pass_on(1)
        if fused and i == chunks - 5:
            pass_on(2)
        if fused and i == chunks - 5:
            small.share()
        if fused and i == 1:
            for n in range(F_LATE):
                ff.finish(n)
    input_grad(0)
    gain = jnp.zeros((1, width), F32)
    for c0 in range(0, cols_all, 3 * d):
        part = nn(dqkvt_ref[c0 : c0 + 3 * d, :], h1_ref[...])
        w = jnp.concatenate([wq_ref[0, c0 : c0 + 3 * d, :], wq_ref[1, c0 : c0 + 3 * d, :]], axis=1)
        gain = gain + jnp.sum(part * w.astype(F32), axis=0, keepdims=True)
        glocal[:, c0 : c0 + 3 * d] = part.T.astype(BF16)
    gain = jnp.concatenate([gain[:, c : c + LANES] for c in range(0, width, LANES)] + [jnp.zeros((8 - width // LANES, LANES), F32)], axis=0)
    if fused:
        total_gain.start(gain)
        for k in range(4):
            attn.own[k] = glocal[pieces(k, x), :]
            attn.x_copy(k).start()
        each(2, lambda i: dh.finish(chunks - 1 - i))
        attn.pass_on(0)
        attn.pass_on(1)
        total_gain.share()
        each(1, lambda i: dh.finish(chunks - 3 - i))
        gusum_ref[...], dosum_ref[...] = pass_on(3)
        attn.pass_on(2)
        each(5, lambda i: dh.finish(chunks - 4 - i))
        gsum_ref[...] = attn.pass_on(3)
        gain_ref[...] = total_gain.finish()
        for n in range(F_LATE):
            ff.close(n)
        for part in (gate_up, down, attn, small):
            part.close()
    else:
        gain_ref[...] = gain
        each(chunks, lambda i: dh.finish(chunks - 1 - i))
    each(chunks, dh.close)


def attention_backward(da, w_out, qkvt, ot, lse, bq, bk, w_halves, h1, heads, gu=None, down=None, small=None, f_late=None):
    tokens, width = da.shape
    cols = qkvt.shape[0]
    fused = gu is not None
    out_shape = [jax.ShapeDtypeStruct((2, tokens, width // 2), BF16), jax.ShapeDtypeStruct((8, LANES), F32)]
    vmem = pl.BlockSpec(memory_space=pltpu.VMEM)
    in_specs = [vmem] * 9
    operands = [da, w_out, qkvt, ot, lse, bq, bk, w_halves, h1]
    rows = w_out.shape[0]
    scratch = [
        pltpu.VMEM((cols, tokens), BF16),
        pltpu.VMEM((rows, tokens), BF16),
        pltpu.VMEM((lse.shape[0], tokens), F32),
        pltpu.VMEM((heads, tokens, HEAD_DIM), BF16),
        pltpu.VMEM((heads, tokens, HEAD_DIM), BF16),
        pltpu.VMEM((heads, HEAD_DIM, tokens), F32),
        pltpu.VMEM((heads, HEAD_DIM, tokens), F32),
    ] + sum_scratch(tokens, width // 2)
    if fused:
        hidden = down.shape[1] // 2
        operands += [gu, down, small, f_late]
        in_specs += [pl.BlockSpec(memory_space=pl.ANY)] * 2 + [vmem] * 2
        out_shape += [
            jax.ShapeDtypeStruct((width // 8, cols + rows), F32),
            jax.ShapeDtypeStruct((width // 4, 2 * hidden), F32),
            jax.ShapeDtypeStruct((width // 4, hidden), F32),
            jax.ShapeDtypeStruct(small.shape, F32),
            jax.ShapeDtypeStruct((2, *f_late.shape), BF16),
        ]
        scratch += [pltpu.VMEM((width, cols + rows), BF16)]
        scratch += depth_scratch(width // 8, cols + rows)
        scratch += depth_scratch(width // 4, 2 * hidden) + depth_scratch(width // 4, hidden)
        scratch += [pltpu.VMEM((8, 8, width), F32), pltpu.SemaphoreType.DMA((2, 2, 8))]
        scratch += [
            pltpu.VMEM((8, 8, LANES), F32),
            pltpu.VMEM((4, 8, LANES), F32),
            pltpu.SemaphoreType.DMA((2, 8)),
            pltpu.SemaphoreType.DMA((2, 4)),
        ]
        scratch += [pltpu.SemaphoreType.DMA((2, 4))]
        scratch += [pltpu.VMEM(f_late.shape, BF16), pltpu.SemaphoreType.DMA((2, 3, F_LATE))]
    else:
        out_shape += [jax.ShapeDtypeStruct((width, cols + rows), BF16)]
    return pl.pallas_call(
        functools.partial(attn_bwd_kernel, heads, fused),
        name="attn_bwd",
        in_specs=in_specs,
        out_shape=out_shape,
        scratch_shapes=scratch,
        compiler_params=params(collective_id=1, has_side_effects=True),
        cost_estimate=COST,
    )(*operands)


def lane_iota(rows):
    return lax.broadcasted_iota(jnp.int32, (rows, LANES), 1)


def column(values, lane, number):
    return jnp.sum(jnp.where(lane == number, values, 0.0), axis=1, keepdims=True)


def routing(logits, aux, types):
    lane = lane_iota(logits.shape[0])
    is_type = lane < types
    shown = jnp.where(is_type, logits, NEG)
    e = jnp.exp(shown - jnp.max(shown, axis=1, keepdims=True))
    probs = e / jnp.sum(e, axis=1, keepdims=True)
    aux = aux.astype(F32)
    first = column(aux, lane, types).astype(jnp.int32)
    second = column(aux, lane, types + 1).astype(jnp.int32)
    mask = jnp.where((lane == first) | (lane == second), 1.0, 0.0)
    return lane, probs, mask


def const_mix(logits, lane, types, c):
    l0 = column(logits, lane, types + 2 * c)
    l1 = column(logits, lane, types + 2 * c + 1)
    top = jnp.maximum(l0, l1)
    e0, e1 = jnp.exp(l0 - top), jnp.exp(l1 - top)
    total = e0 + e1
    return e0 / total, e1 / total


def post_attn_kernel(types, group, idx_ref, x_ref, *refs):
    ots, wos = refs[:group], refs[group : 2 * group]
    gain_ref, wcat_ref, aux_ref, wprev_ref = refs[2 * group : 2 * group + 4]
    x1_ref, h2_ref, lg_ref, ps_ref, wo_scr, ot_scr = refs[2 * group + 4 :]
    rows = ots[0].shape[0]
    me = idx_ref[0]

    @pl.when(pl.program_id(0) == 0)
    def _():
        for m in range(group):
            wo_scr[pl.ds(pl.multiple_of((me ^ m) * rows, HEAD_DIM), rows), :] = wos[m][...]
        ps_ref[...] = jnp.zeros_like(ps_ref)

    for m in range(group):
        ot_scr[pl.ds(pl.multiple_of((me ^ m) * rows, HEAD_DIM), rows), :] = ots[m][...]
    x1 = x_ref[...].astype(F32) + tn(ot_scr[...], wo_scr[...])
    x1_ref[...] = x1
    h2 = (x1 * rms_factor(x1) * gain_ref[...]).astype(BF16)
    h2_ref[...] = h2
    lg = nn(h2, wcat_ref[...]) + nn(aux_ref[...], wprev_ref[...])
    lg_ref[...] = lg
    _, probs, _ = routing(lg, aux_ref[...], types)
    ps_ref[0:1, :] += jnp.sum(probs, axis=0, keepdims=True)


def post_attention(me, x, ots, wos, gain, wcat, aux, wprev, types):
    tokens, width = x.shape
    rows = ots[0].shape[0]
    group = len(ots)
    block = lambda i, *_: (i, 0)
    fixed = lambda i, *_: (0, 0)
    grid_spec = pltpu.PrefetchScalarGridSpec(
        num_scalar_prefetch=1,
        grid=(tokens // TB,),
        in_specs=[pl.BlockSpec((TB, width), block)]
        + [pl.BlockSpec((rows, TB), lambda i, *_: (0, i))] * group
        + [pl.BlockSpec((rows, width), fixed)] * group
        + [
            pl.BlockSpec((1, width), fixed),
            pl.BlockSpec((width, LANES), fixed),
            pl.BlockSpec((TB, LANES), block),
            pl.BlockSpec((LANES, LANES), fixed),
        ],
        out_specs=[
            pl.BlockSpec((TB, width), block),
            pl.BlockSpec((TB, width), block),
            pl.BlockSpec((TB, LANES), block),
            pl.BlockSpec((8, LANES), fixed),
        ],
        scratch_shapes=[pltpu.VMEM((group * rows, width), BF16), pltpu.VMEM((group * rows, TB), BF16)],
    )
    return pl.pallas_call(
        functools.partial(post_attn_kernel, types, group),
        name="post_attn",
        grid_spec=grid_spec,
        out_shape=(
            jax.ShapeDtypeStruct((tokens, width), F32),
            jax.ShapeDtypeStruct((tokens, width), BF16),
            jax.ShapeDtypeStruct((tokens, LANES), F32),
            jax.ShapeDtypeStruct((8, LANES), F32),
        ),
        compiler_params=params(),
        cost_estimate=COST,
    )(me, x, *ots, *wos, gain, wcat, aux, wprev)


def front_kernel(heads, types, x_ref, gain_ref, wt_ref, bq_ref, bk_ref, wo_ref, gain2_ref, wcat_ref, aux_ref, wprev_ref, part_ref, wgu_ref, wd_ref, h1_ref, qkvt_ref, ot_ref, lse_ref, x1_ref, h2_ref, lg_ref, ps_ref, count_ref, pgu_ref, pd_ref, *scratch):
    kn_ref, oall, wall, osems, wsems, esems, *counts = scratch
    tokens, width = x_ref.shape
    rows = ot_ref.shape[0]
    d = HEAD_DIM
    t = lax.axis_index("tensor")
    half, partner, other = neighbours()
    near, far, _ = depth_place()
    across = {"expert": 1 - lax.axis_index("expert")}
    low = lax.axis_index("dp") % 2
    greet([partner, other, across, near, far])
    count = HopSum(*counts, [across, near, far])
    count.partial[0] = part_ref[...]
    count.start()

    mine = pl.ds(pl.multiple_of(t * rows, d), rows)
    others = pl.ds(pl.multiple_of(((t + 2) % 4) * rows, d), rows)

    def spread(ref, cols, sems, n):
        return [
            pltpu.make_async_remote_copy(
                src_ref=ref.at[place, cols],
                dst_ref=ref.at[place, cols],
                send_sem=sems.at[0, stage, n],
                recv_sem=sems.at[1, stage, n],
                device_id=device,
                device_id_type=MESH,
            )
            for stage, (place, device) in enumerate(((mine, partner), (mine, other), (others, partner)))
        ]

    pieces = []
    for ref, land in ((wgu_ref, pgu_ref), (wd_ref, pd_ref)):
        step = ref.shape[0] // 4
        for n in range(2):
            pieces.append((ref, land, pl.ds(pl.multiple_of((2 * low + n) * step, step), step)))

    def weight_copy(n, stage):
        ref, land, place = pieces[n]
        return pltpu.make_async_remote_copy(
            src_ref=(land if stage else ref).at[place, :],
            dst_ref=land.at[place, :],
            send_sem=esems.at[0, stage, n],
            recv_sem=esems.at[1, stage, n],
            device_id=near if stage else across,
            device_id_type=MESH,
        )

    def weight_on(n):
        weight_copy(n, 0).wait_recv()
        weight_copy(n, 1).start()

    for n in range(4):
        weight_copy(n, 0).start()
    wall[mine, :] = wo_ref[...]
    every = slice(None)
    for c in spread(wall, every, wsems, 0)[:2]:
        c.start()

    for r0 in range(0, tokens, QF):
        project_rows(r0, heads, x_ref, gain_ref, wt_ref, h1_ref, qkvt_ref, kn_ref)
    count.add(0)
    ps_ref[...] = jnp.zeros_like(ps_ref)

    def block_cols(n):
        return slice(n * QF, (n + 1) * QF)

    def attend(n):
        o = jnp.concatenate([attend_rows(n * QF, h, bq_ref, bk_ref, qkvt_ref, kn_ref, lse_ref) for h in range(heads)], axis=0)
        ot_ref[:, block_cols(n)] = o
        oall[mine, block_cols(n)] = o
        for c in spread(oall, block_cols(n), osems, n)[:2]:
            c.start()

    def onward(ref, cols, sems, n):
        copies = spread(ref, cols, sems, n)
        copies[1].wait_recv()
        copies[2].start()

    def post(n):
        copies = spread(oall, block_cols(n), osems, n)
        copies[0].wait_recv()
        copies[2].wait_recv()
        for r0 in range(n * QF, (n + 1) * QF, TB):
            r = slice(r0, r0 + TB)
            x1 = x_ref[r, :].astype(F32) + tn(oall[:, r], wall[...])
            x1_ref[r, :] = x1
            h2 = (x1 * rms_factor(x1) * gain2_ref[...]).astype(BF16)
            h2_ref[r, :] = h2
            lg = nn(h2, wcat_ref[...]) + nn(aux_ref[r, :], wprev_ref[...])
            lg_ref[r, :] = lg
            _, probs, _ = routing(lg, aux_ref[r, :], types)
            ps_ref[0:1, :] += jnp.sum(probs, axis=0, keepdims=True)

    blocks = tokens // QF
    for n in range(blocks):
        attend(n)
        if n == 0:
            onward(wall, every, wsems, 0)
            count.add(1)
        if n == 1:
            weight_on(0)
            count_ref[...] = count.add(2)
        if n == 2:
            copies = spread(wall, every, wsems, 0)
            copies[0].wait_recv()
            copies[2].wait_recv()
            weight_on(1)
        if n >= 1:
            onward(oall, block_cols(n - 1), osems, n - 1)
        if n >= 2:
            post(n - 2)
    onward(oall, block_cols(blocks - 1), osems, blocks - 1)
    weight_on(2)
    post(blocks - 2)
    weight_on(3)
    post(blocks - 1)
    for n in range(4):
        weight_copy(n, 1).wait_recv()
        for stage in range(2):
            weight_copy(n, stage).wait_send()
    for c in spread(wall, every, wsems, 0):
        c.wait_send()
    for n in range(blocks):
        for c in spread(oall, block_cols(n), osems, n):
            c.wait_send()
    count.close()


def front_pass(x, gain, w_t, bq, bk, w_out, gain2, wcat, aux, wprev, part, wgu, wd, heads, types):
    tokens, width = x.shape
    cols, rows = w_t.shape[0], w_out.shape[0]
    lse_rows = -(-heads // 8) * 8
    blocks = tokens // QF
    vmem = pl.BlockSpec(memory_space=pltpu.VMEM)
    anywhere = pl.BlockSpec(memory_space=pl.ANY)
    return pl.pallas_call(
        functools.partial(front_kernel, heads, types),
        name="front",
        in_specs=[vmem] * 11 + [anywhere] * 2,
        out_specs=[vmem] * 9 + [anywhere] * 2,
        out_shape=(
            jax.ShapeDtypeStruct((tokens, width), BF16),
            jax.ShapeDtypeStruct((cols, tokens), BF16),
            jax.ShapeDtypeStruct((rows, tokens), BF16),
            jax.ShapeDtypeStruct((lse_rows, tokens), F32),
            jax.ShapeDtypeStruct((tokens, width), F32),
            jax.ShapeDtypeStruct((tokens, width), BF16),
            jax.ShapeDtypeStruct((tokens, LANES), F32),
            jax.ShapeDtypeStruct((8, LANES), F32),
            jax.ShapeDtypeStruct(part.shape, F32),
            jax.ShapeDtypeStruct(wgu.shape, BF16),
            jax.ShapeDtypeStruct(wd.shape, BF16),
        ),
        scratch_shapes=[
            pltpu.VMEM((heads, tokens, HEAD_DIM), BF16),
            pltpu.VMEM((4 * rows, tokens), BF16),
            pltpu.VMEM((4 * rows, width), BF16),
            pltpu.SemaphoreType.DMA((2, 3, blocks)),
            pltpu.SemaphoreType.DMA((2, 3, 1)),
            pltpu.SemaphoreType.DMA((2, 2, 4)),
        ]
        + hop_scratch(3, *part.shape),
        compiler_params=params(collective_id=3, has_side_effects=True),
        cost_estimate=COST,
    )(x, gain, w_t, bq, bk, w_out, gain2, wcat, aux, wprev, part, wgu, wd)


def expert_kernel(types, experts, halves, idx_ref, h2_ref, dy_ref, lg_ref, aux_ref, *refs):
    wgus, wds = refs[:experts], refs[experts : 2 * experts]
    eye_ref = refs[2 * experts]
    keep_ref, send_ref, gh_ref, du_ref, dlt_ref, acc_ref = refs[2 * experts + 1 :]
    me, half = idx_ref[0], idx_ref[1]
    hidden = wds[0].shape[0]
    h2, dy = h2_ref[...], dy_ref[...]
    lane, probs, mask = routing(lg_ref[...], aux_ref[...], types)
    gates = probs * mask
    dprobs = jnp.zeros_like(probs)
    for s in range(experts):
        e = me ^ s
        gate_col = column(gates, lane, e)
        u = nn(h2, wgus[s][...])
        dhr = nt(dy, wds[s][...])
        g, up = u[:, :hidden], u[:, hidden:]
        sig = 1.0 / (1.0 + jnp.exp(-g))
        silu = g * sig
        hid = silu * up
        gh_ref[s, :, :] = (hid * gate_col).astype(BF16)
        dg = jnp.sum(hid * dhr, axis=1, keepdims=True)
        dprobs = dprobs + jnp.where(lane == e, dg * mask, 0.0)
        dh = dhr * gate_col
        dgate = dh * up * sig * (1.0 + g * (1.0 - sig))
        dup = dh * silu
        du_ref[s, :, :hidden] = dgate.astype(BF16)
        du_ref[s, :, hidden:] = dup.astype(BF16)
        part = nt(du_ref[s, :, :], wgus[s][...])
        if s == 0:
            acc_ref[...] = part
        else:
            acc_ref[...] += part
    dlog = probs * (dprobs - jnp.sum(probs * dprobs, axis=1, keepdims=True))
    hi, lo = split_hi_lo(dlog)
    dlt_ref[...] = nt(eye_ref[...], hi) + nt(eye_ref[...], lo)
    half_cols = acc_ref.shape[1] // halves
    keep_ref[...] = acc_ref[:, pl.ds(pl.multiple_of(half * half_cols, LANES), half_cols)].astype(BF16)
    send_ref[...] = acc_ref[:, pl.ds(pl.multiple_of((1 - half) * half_cols, LANES), half_cols)].astype(BF16)


def experts_pass(idx, h2, dy, lg, aux, wgus, wds, eye, types):
    tokens, width = h2.shape
    experts = len(wgus)
    hidden = wds[0].shape[0]
    erows = eye.shape[0]
    block = lambda i, *_: (i, 0)
    fixed = lambda i, *_: (0, 0)
    grid_spec = pltpu.PrefetchScalarGridSpec(
        num_scalar_prefetch=1,
        grid=(tokens // TB,),
        in_specs=[
            pl.BlockSpec((TB, width), block),
            pl.BlockSpec((TB, width), block),
            pl.BlockSpec((TB, LANES), block),
            pl.BlockSpec((TB, LANES), block),
        ]
        + [pl.BlockSpec((width, 2 * hidden), fixed, pipeline_mode=pl.Buffered(1))] * experts
        + [pl.BlockSpec((hidden, width), fixed, pipeline_mode=pl.Buffered(1))] * experts
        + [pl.BlockSpec((erows, LANES), fixed)],
        out_specs=[
            pl.BlockSpec((TB, width // 2), block),
            pl.BlockSpec((TB, width // 2), block),
            pl.BlockSpec((experts, TB, hidden), lambda i, *_: (0, i, 0)),
            pl.BlockSpec((experts, TB, 2 * hidden), lambda i, *_: (0, i, 0)),
            pl.BlockSpec((erows, TB), lambda i, *_: (0, i)),
        ],
        scratch_shapes=[pltpu.VMEM((TB, width), F32)],
    )
    return pl.pallas_call(
        functools.partial(expert_kernel, types, experts, 2),
        name="experts",
        grid_spec=grid_spec,
        out_shape=(
            jax.ShapeDtypeStruct((tokens, width // 2), BF16),
            jax.ShapeDtypeStruct((tokens, width // 2), BF16),
            jax.ShapeDtypeStruct((experts, tokens, hidden), BF16),
            jax.ShapeDtypeStruct((experts, tokens, 2 * hidden), BF16),
            jax.ShapeDtypeStruct((erows, tokens), F32),
        ),
        compiler_params=params(),
        cost_estimate=COST,
    )(idx, h2, dy, lg, aux, *wgus, *wds, eye)


def down_kernel(experts, idx_ref, gh_ref, *refs):
    wds, (keep_ref, send_ref, acc_ref) = refs[:experts], refs[experts:]
    me, half = idx_ref[0], idx_ref[1]
    for s in range(experts):
        part = nn(gh_ref[s, :, :], wds[s][...])
        if s == 0:
            acc_ref[...] = part
        else:
            acc_ref[...] += part
    half_cols = keep_ref.shape[1]
    keep_ref[...] = acc_ref[:, pl.ds(pl.multiple_of(half * half_cols, LANES), half_cols)].astype(BF16)
    send_ref[...] = acc_ref[:, pl.ds(pl.multiple_of((1 - half) * half_cols, LANES), half_cols)].astype(BF16)


def down_pass(idx, gh, wds):
    experts, tokens, hidden = gh.shape
    width = wds[0].shape[1]
    block = lambda i, *_: (i, 0)
    fixed = lambda i, *_: (0, 0)
    grid_spec = pltpu.PrefetchScalarGridSpec(
        num_scalar_prefetch=1,
        grid=(tokens // TB,),
        in_specs=[pl.BlockSpec((experts, TB, hidden), lambda i, *_: (0, i, 0))]
        + [pl.BlockSpec((hidden, width), fixed, pipeline_mode=pl.Buffered(1))] * experts,
        out_specs=[pl.BlockSpec((TB, width // 2), block)] * 2,
        scratch_shapes=[pltpu.VMEM((TB, width), F32)],
    )
    return pl.pallas_call(
        functools.partial(down_kernel, experts),
        name="down",
        grid_spec=grid_spec,
        out_shape=(jax.ShapeDtypeStruct((tokens, width // 2), BF16),) * 2,
        compiler_params=params(),
        cost_estimate=COST,
    )(idx, gh, *wds)


def middle_kernel(types, ffn, total_tokens, idx_ref, mine_ref, theirs_ref, x1_ref, dy_ref, lg_ref, aux_ref, dlt_ref, eye_ref, count_ref, gain_ref, wcat_ref, vt_ref, wprevt_ref, dx1_ref, da_ref, gp_ref, g1_ref, g2_ref, g3_ref, g4_ref, scr_ref):
    half = idx_ref[1]
    half_cols = mine_ref.shape[1]
    scr_ref[:, pl.ds(pl.multiple_of(half * half_cols, LANES), half_cols)] = mine_ref[...]
    scr_ref[:, pl.ds(pl.multiple_of((1 - half) * half_cols, LANES), half_cols)] = theirs_ref[...]
    first = pl.program_id(0) == 0

    @pl.when(first)
    def _():
        for ref in (g1_ref, g2_ref, g3_ref, g4_ref):
            ref[...] = jnp.zeros_like(ref)

    gain = gain_ref[...]
    x1 = x1_ref[...]
    r2 = rms_factor(x1)
    n2 = x1 * r2
    h2 = (n2 * gain).astype(BF16)
    dyb = dy_ref[...]
    dy = dyb.astype(F32)
    lg = lg_ref[...]
    lane, probs, mask = routing(lg, aux_ref[...], types)
    gates = probs * mask
    a = jnp.sum(dy * h2.astype(F32), axis=1, keepdims=True)
    b = nn(dyb, vt_ref[...])
    coef = column(gates, lane, ffn + 1)
    dprobs = jnp.where(lane == ffn + 1, a, 0.0)
    dlc = jnp.zeros_like(probs)
    vcoef = jnp.zeros_like(probs)
    for c in range(2):
        m0, m1 = const_mix(lg, lane, types, c)
        g = column(gates, lane, ffn + 2 + c)
        bc = column(b, lane, c)
        dprobs = dprobs + jnp.where(lane == ffn + 2 + c, m0 * a + m1 * bc, 0.0)
        dm0, dm1 = g * a, g * bc
        inner = m0 * dm0 + m1 * dm1
        dlc = dlc + jnp.where(lane == types + 2 * c, m0 * (dm0 - inner), 0.0)
        dlc = dlc + jnp.where(lane == types + 2 * c + 1, m1 * (dm1 - inner), 0.0)
        coef = coef + g * m0
        vcoef = vcoef + jnp.where(lane == c, g * m1, 0.0)
    dprobs = dprobs * mask + count_ref[...] * (AUX_WEIGHT * types / (2.0 * total_tokens * total_tokens))
    dlog = probs * (dprobs - jnp.sum(probs * dprobs, axis=1, keepdims=True))
    hi, lo = split_hi_lo(dlt_ref[...])
    dl = dlog + dlc + tn(hi, eye_ref[...]) + tn(lo, eye_ref[...])
    dhi, dlo = split_hi_lo(dl)
    dh2 = scr_ref[...].astype(F32) + coef * dy + nt(dhi, wcat_ref[...]) + nt(dlo, wcat_ref[...])
    dn2 = dh2 * gain
    dx1 = dy + r2 * (dn2 - n2 * jnp.mean(dn2 * n2, axis=1, keepdims=True))
    dx1_ref[...] = dx1
    da_ref[...] = dx1.astype(BF16)
    gp_ref[...] = nn(dhi, wprevt_ref[...]) + nn(dlo, wprevt_ref[...])
    g1_ref[...] += tn(dhi, h2) + tn(dlo, h2)
    vhi, vlo = split_hi_lo(vcoef)
    g2_ref[...] += tn(vhi, dyb) + tn(vlo, dyb)
    g3_ref[0:1, :] += jnp.sum(dh2 * n2, axis=0, keepdims=True)
    g4_ref[...] += tn(aux_ref[...], dhi) + tn(aux_ref[...], dlo)


def middle_pass(idx, mine, theirs, x1, dy, lg, aux, dlt, eye, count, gain, wcat, vt, wprevt, types, ffn, total_tokens):
    tokens, width = x1.shape
    erows = dlt.shape[0]
    block = lambda i, *_: (i, 0)
    fixed = lambda i, *_: (0, 0)
    grid_spec = pltpu.PrefetchScalarGridSpec(
        num_scalar_prefetch=1,
        grid=(tokens // TB,),
        in_specs=[
            pl.BlockSpec((TB, width // 2), block),
            pl.BlockSpec((TB, width // 2), block),
            pl.BlockSpec((TB, width), block),
            pl.BlockSpec((TB, width), block),
            pl.BlockSpec((TB, LANES), block),
            pl.BlockSpec((TB, LANES), block),
            pl.BlockSpec((erows, TB), lambda i, *_: (0, i)),
            pl.BlockSpec((erows, LANES), fixed),
            pl.BlockSpec((1, LANES), fixed),
            pl.BlockSpec((1, width), fixed),
            pl.BlockSpec((width, LANES), fixed),
            pl.BlockSpec((width, LANES), fixed),
            pl.BlockSpec((LANES, LANES), fixed),
        ],
        out_specs=[
            pl.BlockSpec((TB, width), block),
            pl.BlockSpec((TB, width), block),
            pl.BlockSpec((TB, LANES), block),
            pl.BlockSpec((LANES, width), fixed),
            pl.BlockSpec((LANES, width), fixed),
            pl.BlockSpec((8, width), fixed),
            pl.BlockSpec((LANES, LANES), fixed),
        ],
        scratch_shapes=[pltpu.VMEM((TB, width), BF16)],
    )
    return pl.pallas_call(
        functools.partial(middle_kernel, types, ffn, total_tokens),
        name="middle",
        grid_spec=grid_spec,
        out_shape=(
            jax.ShapeDtypeStruct((tokens, width), F32),
            jax.ShapeDtypeStruct((tokens, width), BF16),
            jax.ShapeDtypeStruct((tokens, LANES), F32),
            jax.ShapeDtypeStruct((LANES, width), F32),
            jax.ShapeDtypeStruct((LANES, width), F32),
            jax.ShapeDtypeStruct((8, width), F32),
            jax.ShapeDtypeStruct((LANES, LANES), F32),
        ),
        compiler_params=params(),
        cost_estimate=COST,
    )(idx, mine, theirs, x1, dy, lg, aux, dlt, eye, count, gain, wcat, vt, wprevt)


def layer_kernel(types, experts, total_tokens, blocks, h2_ref, dy_ref, lg_ref, aux_ref, x1_ref, *refs):
    wgus, wds = refs[:experts], refs[experts : 2 * experts]
    eye_ref, count_ref, gain_ref, wcat_ref, vt_ref, wprevt_ref, ps_ref = refs[2 * experts : 2 * experts + 7]
    dx1_ref, da_ref, gp_ref, base_ref, flate_ref, gu_ref, down_ref, rows_ref = refs[2 * experts + 7 : 2 * experts + 15]
    scratch = refs[2 * experts + 15 :]
    early = blocks - F_LATE
    acc_gu, acc_down, du_ref, gh_ref, dres, fres = scratch[:6]
    dkeep, dsend, dfirst, dsecond, dsems, fkeep, fsend, ffirst, fsecond, fsems, lpart, lfirst, lsecond, lsems = scratch[6:20]
    xg, xd, xsems, g1_ref, g2_ref, g3_ref, g4_ref = scratch[20:]
    step = pl.program_id(0)
    hidden = wds[0].shape[0]
    lrows = lpart.shape[2]
    me = lax.axis_index("expert")
    half, partner, other = neighbours()
    half_cols = dkeep.shape[1]
    dx = GroupSum(dkeep, dsend, dfirst, dsecond, dres, dsems)
    ff = GroupSum(fkeep, fsend, ffirst, fsecond, fres, fsems)
    small = SmallSum(lpart, lfirst, lsecond, lsems)
    across = {"expert": 1 - me}
    _, _, order = depth_place()
    block = gu_ref.shape[0] // 4
    first_rows = [pl.ds(pl.multiple_of(order[k] * block, block), block) for k in range(X_EARLY)]

    def first_copies(k):
        return [
            pltpu.make_async_remote_copy(
                src_ref=src.at[first_rows[k], pl.ds(cols, cols)],
                dst_ref=dst.at[k],
                send_sem=xsems.at[0, n, k],
                recv_sem=xsems.at[1, n, k],
                device_id=across,
                device_id_type=MESH,
            )
            for n, (src, dst, cols) in enumerate(((gu_ref, xg, 2 * hidden), (down_ref, xd, hidden)))
        ]

    @pl.when(step == 0)
    def _():
        greet((partner, other, across))
        for ref in (acc_gu, acc_down, g1_ref, g2_ref, g3_ref, g4_ref):
            ref[...] = jnp.zeros_like(ref)

    @pl.when(jnp.logical_and(step > 0, step <= blocks))
    def _():
        i = step - 1
        small.pair(i)
        dx.pair(i)

        @pl.when(i < early)
        def _():
            ff.pair(i)

        @pl.when(i >= early)
        def _():
            ff.pair_only(i)

    @pl.when(step < blocks)
    def _():
        i = step
        h2, dy = h2_ref[...], dy_ref[...]
        lane, probs, mask = routing(lg_ref[...], aux_ref[...], types)
        gates = probs * mask
        dprobs = jnp.zeros_like(probs)
        for s in range(experts):
            e = (me + s) % experts
            gate_col = column(gates, lane, e)
            u = nn(h2, wgus[s][...])
            dhr = nt(dy, wds[s][...])
            g, up = u[:, :hidden], u[:, hidden:]
            sig = 1.0 / (1.0 + jnp.exp(-g))
            silu = g * sig
            hid = silu * up
            gh_ref[:, s * hidden : (s + 1) * hidden] = (hid * gate_col).astype(BF16)
            dg = jnp.sum(hid * dhr, axis=1, keepdims=True)
            dprobs = dprobs + jnp.where(lane == e, dg * mask, 0.0)
            dh = dhr * gate_col
            base = 2 * s * hidden
            du_ref[:, base : base + hidden] = (dh * up * (sig + silu * (1.0 - sig))).astype(BF16)
            du_ref[:, base + hidden : base + 2 * hidden] = (dh * silu).astype(BF16)
        dlog = probs * (dprobs - jnp.sum(probs * dprobs, axis=1, keepdims=True))
        hi, lo = split_hi_lo(dlog)
        lpart[0, i] = (nt(eye_ref[...], hi) + nt(eye_ref[...], lo))[:lrows]
        small.start(i)
        rows = dx.rows(i)

        def place(total, group, keep, send):
            low, high = total[:, :half_cols], total[:, half_cols:]
            send[rows, :] = jnp.where(half == 0, high, low).astype(BF16)
            group.to_partner(i).start()
            keep[rows, :] = jnp.where(half == 0, low, high).astype(BF16)

        total = nt(du_ref[:, : 2 * hidden], wgus[0][...])
        for s in range(1, experts):
            total = total + nt(du_ref[:, 2 * s * hidden : 2 * (s + 1) * hidden], wgus[s][...])
        place(total, dx, dkeep, dsend)
        total = nn(gh_ref[:, :hidden], wds[0][...])
        for s in range(1, experts):
            total = total + nn(gh_ref[:, s * hidden : (s + 1) * hidden], wds[s][...])
        place(total, ff, fkeep, fsend)
        acc_gu[...] += tn(h2, du_ref[...])
        acc_down[...] += tn(dy, gh_ref[...])

    @pl.when(step == blocks)
    def _():
        gu_ref[...] = acc_gu[...].astype(BF16)
        down_ref[...] = acc_down[...].astype(BF16)
        for k in range(X_EARLY):
            for c in first_copies(k):
                c.start()
        dx.finish(0)

    @pl.when(step >= blocks)
    def _():
        i = step - blocks

        @pl.when(i + 1 < blocks)
        def _():
            dx.finish(i + 1)

        @pl.when(i < early)
        def _():
            ff.finish(i)

        rows = dx.rows(i)
        dlt = small.finish(i)
        gain = gain_ref[...]
        x1 = x1_ref[...]
        r2 = rms_factor(x1)
        n2 = x1 * r2
        h2 = h2_ref[...]
        dyb = dy_ref[...]
        dy = dyb.astype(F32)
        lg = lg_ref[...]
        lane, probs, mask = routing(lg, aux_ref[...], types)
        gates = probs * mask
        a = jnp.sum(dy * h2.astype(F32), axis=1, keepdims=True)
        b = nn(dyb, vt_ref[...])
        coef = column(gates, lane, experts + 1)
        dprobs = jnp.where(lane == experts + 1, a, 0.0)
        dlc = jnp.zeros_like(probs)
        vcoef = jnp.zeros_like(probs)
        for c in range(2):
            m0, m1 = const_mix(lg, lane, types, c)
            g = column(gates, lane, experts + 2 + c)
            bc = column(b, lane, c)
            dprobs = dprobs + jnp.where(lane == experts + 2 + c, m0 * a + m1 * bc, 0.0)
            dm0, dm1 = g * a, g * bc
            inner = m0 * dm0 + m1 * dm1
            dlc = dlc + jnp.where(lane == types + 2 * c, m0 * (dm0 - inner), 0.0)
            dlc = dlc + jnp.where(lane == types + 2 * c + 1, m1 * (dm1 - inner), 0.0)
            coef = coef + g * m0
            vcoef = vcoef + jnp.where(lane == c, g * m1, 0.0)
        dprobs = dprobs * mask + count_ref[...] * (AUX_WEIGHT * types / (2.0 * total_tokens * total_tokens))
        dlog = probs * (dprobs - jnp.sum(probs * dprobs, axis=1, keepdims=True))
        hi, lo = split_hi_lo(dlt)
        eye = eye_ref[:lrows, :]
        dl = dlog + dlc + tn(hi, eye) + tn(lo, eye)
        dhi, dlo = split_hi_lo(dl)
        vhi, vlo = split_hi_lo(vcoef)
        gp_ref[...] = nn(dhi, wprevt_ref[...]) + nn(dlo, wprevt_ref[...])
        g1_ref[...] += tn(dhi, h2) + tn(dlo, h2)
        g2_ref[...] += tn(vhi, dyb) + tn(vlo, dyb)
        g4_ref[...] += tn(aux_ref[...], dhi) + tn(aux_ref[...], dlo)
        dh2 = coef * dy + nt(dhi, wcat_ref[...]) + nt(dlo, wcat_ref[...])
        dx.close(i)
        dh2 = dh2 + jnp.concatenate([dres[0, rows, :], dres[1, rows, :]], axis=1).astype(F32)
        g3_ref[0:1, :] += jnp.sum(dh2 * n2, axis=0, keepdims=True)
        dn2 = dh2 * gain
        dx1 = dy + r2 * (dn2 - n2 * jnp.mean(dn2 * n2, axis=1, keepdims=True))
        dx1_ref[...] = dx1
        da_ref[...] = dx1.astype(BF16)
        vt = vt_ref[...]
        base_ref[...] = x1 + coef * h2.astype(F32) + nt(vhi, vt) + nt(vlo, vt)

        @pl.when(i < early)
        def _():
            ff.close(i)
            base_ref[...] += jnp.concatenate([fres[0, rows, :], fres[1, rows, :]], axis=1).astype(F32)

        @pl.when(i >= early)
        def _():
            ff.to_partner(i).wait_send()
            flate_ref[...] = fkeep[rows, :]

    @pl.when(step == 2 * blocks - 1)
    def _():
        srows, prow = -(-(types + 4) // 8) * 8, -(-types // 8) * 8
        rows_ref[...] = jnp.zeros_like(rows_ref)
        rows_ref[0:srows, :] = g1_ref[0:srows, :]
        rows_ref[srows : srows + 8, :] = g2_ref[0:8, :]
        rows_ref[srows + 8 : srows + 16, :] = g3_ref[...]
        rows_ref[srows + 16 : srows + 16 + prow, 0:LANES] = g4_ref[0:prow, :]
        rows_ref[srows + 16 + prow : srows + 24 + prow, 0:LANES] = ps_ref[...]
        for k in range(X_EARLY):
            for c, ref, got in zip(first_copies(k), (gu_ref, down_ref), (xg, xd)):
                c.wait()
                own = (first_rows[k], slice(0, got.shape[2]))
                ref[own] = (ref[own].astype(F32) + got[k].astype(F32)).astype(BF16)


def layer_pass(h2, dy, lg, aux, x1, wgus, wds, eye, count, gain, wcat, vt, wprevt, ps, types, total_tokens):
    tokens, width = h2.shape
    experts = len(wgus)
    hidden = wds[0].shape[0]
    blocks = tokens // CHUNK
    lrows = -(-types // 8) * 8
    both = lambda i: (i % blocks, 0)
    late = lambda i: (jnp.maximum(i - blocks, 0), 0)
    fixed = lambda i: (0, 0)
    once = dict(pipeline_mode=pl.Buffered(1))
    small_sums = [
        pltpu.VMEM((2, blocks, lrows, CHUNK), F32),
        pltpu.VMEM((blocks, lrows, CHUNK), F32),
        pltpu.VMEM((blocks, lrows, CHUNK), F32),
        pltpu.SemaphoreType.DMA((2, 2, blocks)),
    ]
    return pl.pallas_call(
        functools.partial(layer_kernel, types, experts, total_tokens, blocks),
        name="layer",
        grid=(2 * blocks,),
        in_specs=[
            pl.BlockSpec((CHUNK, width), both),
            pl.BlockSpec((CHUNK, width), both),
            pl.BlockSpec((CHUNK, LANES), both),
            pl.BlockSpec((CHUNK, LANES), both),
            pl.BlockSpec((CHUNK, width), late),
        ]
        + [pl.BlockSpec((width, 2 * hidden), fixed, **once)] * experts
        + [pl.BlockSpec((hidden, width), fixed, **once)] * experts
        + [
            pl.BlockSpec(eye.shape, fixed),
            pl.BlockSpec((1, LANES), fixed),
            pl.BlockSpec((1, width), fixed),
            pl.BlockSpec((width, LANES), fixed),
            pl.BlockSpec((width, LANES), fixed),
            pl.BlockSpec((LANES, LANES), fixed),
            pl.BlockSpec((8, LANES), fixed),
        ],
        out_specs=[
            pl.BlockSpec((CHUNK, width), late),
            pl.BlockSpec((CHUNK, width), late),
            pl.BlockSpec((CHUNK, LANES), late),
            pl.BlockSpec((CHUNK, width), late),
            pl.BlockSpec((CHUNK, width // 2), lambda i: (jnp.maximum(i - (2 * blocks - F_LATE), 0), 0)),
            pl.BlockSpec((width, 2 * experts * hidden), fixed, **once),
            pl.BlockSpec((width, experts * hidden), fixed, **once),
            pl.BlockSpec((64, width), fixed),
        ],
        out_shape=(
            jax.ShapeDtypeStruct((tokens, width), F32),
            jax.ShapeDtypeStruct((tokens, width), BF16),
            jax.ShapeDtypeStruct((tokens, LANES), F32),
            jax.ShapeDtypeStruct((tokens, width), F32),
            jax.ShapeDtypeStruct((F_LATE * CHUNK, width // 2), BF16),
            jax.ShapeDtypeStruct((width, 2 * experts * hidden), BF16),
            jax.ShapeDtypeStruct((width, experts * hidden), BF16),
            jax.ShapeDtypeStruct((64, width), F32),
        ),
        scratch_shapes=[
            pltpu.VMEM((width, 2 * experts * hidden), F32),
            pltpu.VMEM((width, experts * hidden), F32),
            pltpu.VMEM((CHUNK, 2 * experts * hidden), BF16),
            pltpu.VMEM((CHUNK, experts * hidden), BF16),
            pltpu.VMEM((2, tokens, width // 2), BF16),
            pltpu.VMEM((2, tokens - F_LATE * CHUNK, width // 2), BF16),
        ]
        + sum_scratch(tokens, width // 2)
        + sum_scratch(tokens, width // 2)
        + small_sums
        + [
            pltpu.VMEM((X_EARLY, width // 4, 2 * hidden), BF16),
            pltpu.VMEM((X_EARLY, width // 4, hidden), BF16),
            pltpu.SemaphoreType.DMA((2, 2, X_EARLY)),
            pltpu.VMEM((LANES, width), F32),
            pltpu.VMEM((LANES, width), F32),
            pltpu.VMEM((8, width), F32),
            pltpu.VMEM((LANES, LANES), F32),
        ],
        compiler_params=params(collective_id=2, has_side_effects=True),
        cost_estimate=COST,
    )(h2, dy, lg, aux, x1, *wgus, *wds, eye, count, gain, wcat, vt, wprevt, ps)


def output_kernel(types, ffn, f_ref, x1_ref, h2_ref, lg_ref, aux_ref, v_ref, out_ref):
    halves = jnp.concatenate([f_ref[0], f_ref[1]], axis=1)
    lg = lg_ref[...]
    lane, probs, mask = routing(lg, aux_ref[...], types)
    gates = probs * mask
    coef = column(gates, lane, ffn + 1)
    out = x1_ref[...] + halves.astype(F32)
    for c in range(2):
        m0, m1 = const_mix(lg, lane, types, c)
        g = column(gates, lane, ffn + 2 + c)
        coef = coef + g * m0
        out = out + (g * m1) * v_ref[c : c + 1, :]
    out_ref[...] = out + coef * h2_ref[...].astype(F32)


def output_pass(f, x1, h2, lg, aux, v, types, ffn):
    tokens, width = x1.shape
    block = lambda i: (i, 0)
    return pl.pallas_call(
        functools.partial(output_kernel, types, ffn),
        name="output",
        grid=(tokens // TB,),
        in_specs=[
            pl.BlockSpec((2, TB, width // 2), lambda i: (0, i, 0)),
            pl.BlockSpec((TB, width), block),
            pl.BlockSpec((TB, width), block),
            pl.BlockSpec((TB, LANES), block),
            pl.BlockSpec((TB, LANES), block),
            pl.BlockSpec((8, width), lambda i: (0, 0)),
        ],
        out_specs=pl.BlockSpec((TB, width), block),
        out_shape=jax.ShapeDtypeStruct((tokens, width), F32),
        compiler_params=params(),
        cost_estimate=COST,
    )(f, x1, h2, lg, aux, v)


def last_kernel(d_ref, x_ref, dx1_ref, gain_ref, out_ref):
    halves = jnp.concatenate([d_ref[0], d_ref[1]], axis=1)
    x = x_ref[...].astype(F32)
    r1 = rms_factor(x)
    n1 = x * r1
    dn1 = halves.astype(F32) * gain_ref[...]
    out_ref[...] = dx1_ref[...] + r1 * (dn1 - n1 * jnp.mean(dn1 * n1, axis=1, keepdims=True))


def last_pass(dh1, x, dx1, gain):
    tokens, width = x.shape
    block = lambda i: (i, 0)
    return pl.pallas_call(
        last_kernel,
        name="last",
        grid=(tokens // TB,),
        in_specs=[
            pl.BlockSpec((2, TB, width // 2), lambda i: (0, i, 0)),
            pl.BlockSpec((TB, width), block),
            pl.BlockSpec((TB, width), block),
            pl.BlockSpec((1, width), lambda i: (0, 0)),
        ],
        out_specs=pl.BlockSpec((TB, width), block),
        out_shape=jax.ShapeDtypeStruct((tokens, width), F32),
        compiler_params=params(),
        cost_estimate=COST,
    )(dh1, x, dx1, gain)


def tail_kernel(first_late, d_ref, x_ref, dx1_ref, gain_ref, base_ref, f_ref, grad_ref, out_ref):
    last_kernel(d_ref, x_ref, dx1_ref, gain_ref, grad_ref)
    late = pl.program_id(0) >= first_late

    @pl.when(late)
    def _():
        out_ref[...] = base_ref[...] + jnp.concatenate([f_ref[0], f_ref[1]], axis=1).astype(F32)

    @pl.when(jnp.logical_not(late))
    def _():
        out_ref[...] = base_ref[...]


def tail_pass(dh1, x, dx1, gain, base, f_late):
    tokens, width = x.shape
    first_late = tokens // CHUNK - F_LATE
    block = lambda i: (i, 0)
    return pl.pallas_call(
        functools.partial(tail_kernel, first_late),
        name="tail",
        grid=(tokens // CHUNK,),
        in_specs=[
            pl.BlockSpec((2, CHUNK, width // 2), lambda i: (0, i, 0)),
            pl.BlockSpec((CHUNK, width), block),
            pl.BlockSpec((CHUNK, width), block),
            pl.BlockSpec((1, width), lambda i: (0, 0)),
            pl.BlockSpec((CHUNK, width), block),
            pl.BlockSpec((2, CHUNK, width // 2), lambda i: (0, jnp.maximum(i - first_late, 0), 0)),
        ],
        out_specs=[pl.BlockSpec((CHUNK, width), block)] * 2,
        out_shape=(jax.ShapeDtypeStruct((tokens, width), F32),) * 2,
        compiler_params=params(),
        cost_estimate=COST,
    )(dh1, x, dx1, gain, base, f_late)


def tie(value, *others):
    return lax.optimization_barrier((value, *others))[0]


def add_all(own, got):
    total = own.astype(F32)
    for g in got:
        total = total + g.astype(F32)
    return total.astype(BF16)


def pair_sum(keep, send):
    return (keep.astype(F32) + swap(send, "tensor", 1).astype(F32)).astype(BF16)


def group_sum(part):
    bit = 2
    while bit < lax.axis_size("tensor"):
        part = (part.astype(F32) + swap(part, "tensor", bit).astype(F32)).astype(BF16)
        bit *= 2
    return part, swap(part, "tensor", 1)


def scatter_sum(a, axes):
    steps = []
    for axis in axes:
        bits = lax.axis_size(axis).bit_length() - 1
        steps += [(axis, b) for b in reversed(range(bits))]
    a = a.reshape((2,) * len(steps) + (-1, a.shape[-1]))
    order = [s for axis in reversed(axes) for s in reversed(steps) if s[0] == axis]
    left = list(steps)
    for axis, bit in order:
        dim = left.index((axis, bit))
        mine = (lax.axis_index(axis) >> bit) & 1
        got = swap(lax.dynamic_index_in_dim(a, 1 - mine, dim, keepdims=False), axis, 1 << bit)
        a = (lax.dynamic_index_in_dim(a, mine, dim, keepdims=False).astype(F32) + got.astype(F32)).astype(BF16)
        left.remove((axis, bit))
    return a


def gather_group(a):
    out = [a]
    bit = lax.axis_size("tensor") // 2
    parts = {0: a}
    while bit:
        parts.update({m | bit: swap(p, "tensor", bit) for m, p in list(parts.items())})
        bit //= 2
    return [parts[m] for m in range(len(parts))]


def per_device(hidden_in, prev_logits, routes, block_ids, cotangent, gain_attn, w_qkv, w_out, gain_moe, w_router, w_prev, w_const, v_const, w_gate_up, w_down):
    tokens, width = hidden_in.shape
    types = w_router.shape[1]
    experts = lax.axis_size("expert")
    heads = w_out.shape[0] // HEAD_DIM
    hidden = w_down.shape[1]
    total_tokens = tokens * lax.axis_size(("dp", "expert"))
    t_index, x_index = lax.axis_index("tensor"), lax.axis_index("expert")
    t_idx = jnp.stack([t_index, t_index % 2]).astype(jnp.int32)
    x_idx = jnp.stack([x_index, t_index % 2]).astype(jnp.int32)

    gain_first = gain_attn.astype(F32)[None]
    gain_second = gain_moe.astype(F32)[None]
    consts = w_const.transpose(1, 0, 2).reshape(width, 4)
    wcat = jnp.pad(jnp.concatenate([w_router, consts], axis=1), ((0, 0), (0, LANES - types - 4)))
    aux = jnp.concatenate([prev_logits, routes.astype(BF16)], axis=1)
    aux = jnp.pad(aux, ((0, 0), (0, LANES - types - 2)))
    wprev = jnp.pad(w_prev, ((0, LANES - types), (0, LANES - types)))
    wprevt = jnp.pad(w_prev.T, ((0, LANES - types), (0, LANES - types)))
    vt = jnp.pad(v_const.T, ((0, 0), (0, LANES - 2)))
    vrows = jnp.pad(v_const.astype(F32), ((0, 6), (0, 0)))
    erows = -(-types // 16) * 16
    eye = jnp.eye(erows, LANES, dtype=BF16)
    lanes = jnp.arange(LANES, dtype=jnp.int32)
    chosen = (routes[:, :, None] == lanes[None, None, :]).astype(F32)
    count = jnp.sum(chosen, axis=(0, 1))[None]
    bq, bk = block_ids, block_ids.reshape(tokens, 1)

    w_halves = w_qkv.T.reshape(-1, 2, width // 2).transpose(1, 0, 2)

    wgu, wd = w_gate_up[0].reshape(width, 2 * hidden), w_down[0]
    fused = experts == 2 and lax.axis_size("dp") == 4 and lax.axis_size("tensor") == 4
    if fused:
        part = jnp.broadcast_to(count, (8, LANES))
        h1, qkvt, ot, lse, x1, h2, lg, prob_part, count, *peer = front_pass(
            hidden_in, gain_first, w_qkv.T, bq, bk, w_out, gain_second, wcat, aux, wprev, part, wgu, wd, heads, types
        )
        wgus, wds, count = [wgu, peer[0]], [wd, peer[1]], count[:1]
    else:
        wgus = [wgu] + [swap(wgu, "expert", s) for s in range(1, experts)]
        wds = [wd] + [swap(wd, "expert", s) for s in range(1, experts)]
        h1, qkvt, ot, lse = attention_forward(hidden_in, gain_first, w_qkv.T, bq, bk, heads)
        ots, wos = gather_group(ot), gather_group(w_out)
        x1, h2, lg, prob_part = post_attention(t_idx, hidden_in, ots, wos, gain_second, wcat, aux, wprev, types)
        count = sum_over(tie(count, wds[-1]), ("expert", "dp"))
    srows = -(-(types + 4) // 8) * 8
    prow = -(-types // 8) * 8

    def small_rows(g1, g2, g3, g4):
        wide = lambda a: jnp.pad(a, ((0, 0), (0, width - LANES)))
        rows = jnp.concatenate([g1[:srows], g2[:8], g3, wide(g4[:prow]), wide(prob_part)], axis=0)
        return jnp.pad(rows, ((0, 64 - rows.shape[0]), (0, 0)))

    if fused:
        dx1, da, gp, base, f_late, gu, down, packed = layer_pass(
            h2, cotangent, lg, aux, x1, wgus, wds, eye, count, gain_second, wcat, vt, wprevt, prob_part, types, total_tokens
        )
        dh1, gain_all, grads, grad_gate_up, grad_down, small, f_late = attention_backward(
            da, w_out, qkvt, ot, lse, bq, bk, w_halves, h1, heads, gu, down, packed, f_late
        )
        grad_input, output = tail_pass(dh1, hidden_in, dx1, gain_first, base, f_late)
    else:
        keep, send, gh, du, dlt = experts_pass(x_idx, h2, cotangent, lg, aux, wgus, wds, eye, types)
        mine, theirs = group_sum(pair_sum(keep, send))
        dlt = sum_over(dlt, ("tensor",))
        fkeep, fsend = down_pass(x_idx, gh, wds)
        gu_parts = [tn(h2, du[e]).astype(BF16) for e in range(experts)]
        down_parts = [tn(cotangent, gh[e]).astype(BF16) for e in range(experts)]
        f_mine, f_theirs = group_sum(pair_sum(fkeep, fsend))
        first, second = jnp.where(t_index % 2 == 0, f_mine, f_theirs), jnp.where(t_index % 2 == 0, f_theirs, f_mine)
        f = jnp.stack([first, second])
        dx1, da, gp, *g = middle_pass(
            x_idx, mine, theirs, x1, cotangent, lg, aux, dlt, eye, count, gain_second, wcat, vt, wprevt, types, experts, total_tokens
        )
        dh1, gain_part, grads = attention_backward(da, w_out, qkvt, ot, lse, bq, bk, w_halves, h1, heads)
        grads = scatter_sum(grads, ("dp", "expert")).astype(F32)
        gu_got = [swap(gu_parts[e], "expert", e) for e in range(1, experts)]
        down_got = [swap(down_parts[e], "expert", e) for e in range(1, experts)]
        grad_gate_up = scatter_sum(add_all(gu_parts[0], gu_got), ("dp",)).astype(F32)
        grad_down = scatter_sum(add_all(down_parts[0], down_got), ("dp",)).astype(F32)
        gain_all = sum_over(gain_part, ("tensor", "expert", "dp"))
        small = sum_over(small_rows(*g), ("expert", "dp"))
        grad_input = last_pass(dh1, hidden_in, dx1, gain_first)
        output = output_pass(f, x1, h2, lg, aux, vrows, types, experts)

    grad_gain = gain_all.reshape(-1)[:width] / gain_first[0]
    grad_qkv, grad_out = grads[:, : w_qkv.shape[1]], grads[:, w_qkv.shape[1] :].T

    prob_all = small[srows + 16 + prow, :types]
    count_all = count[0, :types]
    balance_loss = types * jnp.sum((count_all / (2.0 * total_tokens)) * prob_all / total_tokens)
    load = jnp.stack([count_all / (2.0 * tokens), prob_all / tokens])
    return (
        output,
        grad_input,
        gp[:, :types],
        grad_gain,
        grad_qkv,
        grad_out,
        small[srows + 8],
        small[:types].T,
        small[srows + 16 : srows + 16 + types, :types],
        small[types : types + 4].reshape(2, 2, width).transpose(0, 2, 1),
        small[srows : srows + 2],
        grad_gate_up.reshape(1, -1, 2, hidden),
        grad_down.T[None],
        balance_loss,
        load,
    )


def solution(mesh):
    tok = P(("dp", "expert"), None)
    return jax.shard_map(
        per_device,
        mesh=mesh,
        in_specs=(
            tok,
            tok,
            tok,
            tok,
            tok,
            P(),
            P(None, "tensor"),
            P("tensor", None),
            P(),
            P(),
            P(),
            P(),
            P(),
            P("expert", None, None, "tensor"),
            P("expert", "tensor", None),
        ),
        out_specs=(
            tok,
            tok,
            tok,
            P(),
            P(("dp", "expert"), "tensor"),
            P("tensor", ("dp", "expert")),
            P(),
            P(),
            P(),
            P(),
            P(),
            P("expert", "dp", None, "tensor"),
            P("expert", "tensor", "dp"),
            P(),
            P(),
        ),
        check_vma=False,
    )
```
